256 devices in a mesh: seq: 32 (over x, y, z_hi), head: 8 (over z_lo, core).
Axes of the slice: x: 4, y: 4, z: 8 (z_hi: 2, z_lo: 4; z = z_hi * 4 + z_lo), core: 2. Of those that a mesh axis runs over, the one named last changes fastest.
Arguments:
- queries: bfloat16 [8192, 8192], P('seq', 'head'), may hold values from -6 to 6
- resp_kv: bfloat16 [8192, 2048], P('seq', 'head'), may hold values from -6 to 6
- prompt_cache: bfloat16 [16384, 2048], P(('seq', 'head')), may hold values from -6 to 6
- grad_out: bfloat16 [8192, 8192], P('seq', 'head'), may hold values from -96 to 96
- group_counts: int32 [8], replicated, may hold values from 1 to 16, 32 in all
- prompt_slot: int32 [8], replicated, may hold values from 0 to 7, each once
- slot_response: int32 [32], replicated, may hold values from 0 to 31, each once
- resp_len: int32 [32], P('seq'), may hold values from 1 to 256, as said below
- weight_code: int32 [32], P('seq'), may hold values from 1 to 16
Outputs:
- grad_queries: bfloat16 [8192, 8192], P('seq', 'head')
- grad_resp_kv: bfloat16 [8192, 2048], P('seq', 'head')
- grad_prompt_cache: bfloat16 [16384, 2048], P(('seq', 'head'))
The draws below stay inside these ranges and needn't reach their ends.
Inputs may be any that keep to these rules, and one draw needn't show every extreme that they name: `group_counts`: they sum to 32, and the largest is 16. `prompt_slot`: each stored prompt belongs to exactly one group. `slot_response`: each response number stands in exactly one slot. `resp_len`: some slot holds a full response.
All inputs are finite; a program needn't handle non-finite values.
Results may differ from the reference program's by a relative error of at most 0.022.
Values may be sent and summed in bfloat16 or wider, within the bound.
A program may use at most 64 MiB of HBM per device.

```python
import math
import jax
import jax.numpy as jnp
import numpy as np
from jax import lax

H = 64
KVH = 8
HD = 128
PLEN = 2048
RLEN = 256
PROMPTS = 8
RESPONSES = 32
RESP_MOST = 16
RESP_ROWS = 8192


def draw_queries(key, part):
    key = jax.random.fold_in(key, 5)
    row_count = RESPONSES * RLEN
    drawn = jnp.clip(jax.random.normal(key, (row_count, H * HD), jnp.float32), -4.0, 4.0)
    return drawn.astype(jnp.bfloat16)


def draw_prompt_cache(key, part):
    key = jax.random.fold_in(key, 9)
    row_count = PROMPTS * PLEN
    col_count = KVH * 2 * HD
    drawn = jnp.clip(jax.random.normal(key, (row_count, col_count), jnp.float32), -4.0, 4.0)
    return drawn.astype(jnp.bfloat16)


def draw_resp_len(key, part):
    key = jax.random.fold_in(key, 13)
    first_key, second_key = jax.random.split(key)
    lengths = jax.random.randint(first_key, (RESPONSES,), 1, RLEN + 1)
    chosen_slot = jax.random.randint(second_key, (), 0, RESPONSES)
    return jnp.where(jnp.arange(RESPONSES) == chosen_slot, RLEN, lengths).astype(jnp.int32)


def set_ends(entries, key, least, high):
    dims = entries.shape
    spot = [jax.random.randint(jax.random.fold_in(key, axis), (), 0, dims[axis]) for axis in range(len(dims))]
    entries = entries.at[tuple(spot)].set(least)
    longest = dims.index(max(dims))
    spot[longest] = (spot[longest] + 1) % dims[longest]
    return entries.at[tuple(spot)].set(high)


def shard_levels(own_key, extent, cuts, smallest, high):
    def one(axis_at, parts):
        draws = jax.random.uniform(jax.random.fold_in(jax.random.fold_in(own_key, 6), axis_at), (parts,), jnp.float32, smallest / len(cuts), high / len(cuts))
        return jnp.repeat(jnp.exp(draws), extent[axis_at] // parts).reshape((-1,) + (1,) * (len(extent) - axis_at - 1))

    level = one(*cuts[0])
    for cut in cuts[1:]:
        level = level * one(*cut)
    return level


def split_up(amount, total, reach, lean):
    loads = [(1 << 20) // math.isqrt(standing ** lean) + 1 for standing in range(2, amount + 1)]
    surplus, holding = total - reach - (amount - 1), [1] * (amount - 1)
    while surplus > 0:
        free = [i for i in range(amount - 1) if holding[i] < reach]
        whole, budget = sum([loads[i] for i in free]), surplus
        for i in free:
            addition = min(reach - holding[i], max(1, budget * loads[i] // whole), surplus)
            holding[i] = holding[i] + addition
            surplus = surplus - addition
    return np.array([reach] + holding)


def uneven(stream_key, count, total, bound, skew):
    if count == 2:
        one = jax.random.randint(stream_key, (), max(1, total - bound), min(bound, total - 1) + 1)
        return jnp.stack([one, total - one])
    sizes = jnp.asarray(split_up(count, total, bound, skew), jnp.int32)
    pairs = (count - 1) // 2
    donor, taker = sizes[1:1 + 2 * pairs:2], sizes[2:2 + 2 * pairs:2]
    slack = jnp.minimum(donor - 1, bound - taker)
    moved = jax.random.randint(jax.random.fold_in(stream_key, 1), (pairs,), 0, 1 << 20) % (slack + 1)
    sizes = sizes.at[1:1 + 2 * pairs:2].set(donor - moved).at[2:2 + 2 * pairs:2].set(taker + moved)
    return sizes[jax.random.permutation(jax.random.fold_in(stream_key, 2), count)]


def centred(rng, shape, spread, bound, cuts=(), kind=jnp.bfloat16):
    entries = jax.random.normal(rng, shape, jnp.float32) * spread
    if len(cuts) > 0:
        entries = shard_levels(rng, shape, cuts, -0.22, 0.18) * entries
    return jnp.clip(entries, min=-bound, max=bound).astype(kind)


def setup_inputs(seed: int = 0) -> dict:
    seeds = jax.random.split(jax.random.key(seed), 10)
    return {
        "queries": draw_queries(jax.random.fold_in(seeds[9], 71), 0),
        "resp_kv": centred(seeds[1], (RESP_ROWS, KVH * 2 * HD), 1.0, 6.0, ((0, 32), (1, 8))),
        "prompt_cache": draw_prompt_cache(jax.random.fold_in(seeds[9], 71), 0),
        "grad_out": centred(seeds[3], (RESP_ROWS, H * HD), 16.0, 96.0, ((0, 32), (1, 8))),
        "group_counts": uneven(seeds[4], PROMPTS, RESPONSES, RESP_MOST, 2).astype(jnp.int32),
        "prompt_slot": jax.random.permutation(seeds[5], PROMPTS).astype(jnp.int32),
        "slot_response": jax.random.permutation(seeds[6], RESPONSES).astype(jnp.int32),
        "resp_len": draw_resp_len(jax.random.fold_in(seeds[9], 71), 0),
        "weight_code": set_ends(jax.random.randint(seeds[8], (RESPONSES,), 1, 17), jax.random.fold_in(seeds[8], 1), 1, 16).astype(jnp.int32),
    }


def attend(query_rows, cotangent_rows, key_rows, value_rows, positions):
    inv_root = HD ** -0.5
    scores = jnp.dot(query_rows, key_rows.T, preferred_element_type=jnp.float32) * inv_root
    key_index = jnp.arange(key_rows.shape[0], dtype=jnp.int32)
    visible = (key_index[None, :] < PLEN) | (key_index[None, :] - PLEN <= positions[:, None])
    scores = jnp.where(visible, scores, -jnp.inf)
    row_max = jnp.max(scores, axis=1, keepdims=True)
    raw_weights = jnp.exp(scores - row_max)
    row_sum = jnp.sum(raw_weights, axis=1, keepdims=True)
    attn_probs = raw_weights / row_sum
    probs_half = attn_probs.astype(jnp.bfloat16)
    out_half = jnp.dot(probs_half, value_rows, preferred_element_type=jnp.float32).astype(jnp.bfloat16)
    row_delta = jnp.sum(cotangent_rows.astype(jnp.float32) * out_half.astype(jnp.float32), axis=1, keepdims=True)
    grad_probs = jnp.dot(cotangent_rows, value_rows.T, preferred_element_type=jnp.float32)
    grad_scores = (attn_probs * (grad_probs - row_delta) * inv_root).astype(jnp.bfloat16)
    grad_query = jnp.dot(grad_scores, key_rows, preferred_element_type=jnp.float32).astype(jnp.bfloat16)
    grad_key = jnp.dot(grad_scores.T, query_rows, preferred_element_type=jnp.float32)
    grad_value = jnp.dot(probs_half.T, cotangent_rows, preferred_element_type=jnp.float32)
    return grad_query, grad_key, grad_value


def reference(queries, resp_kv, prompt_cache, grad_out, group_counts, prompt_slot, slot_response, resp_len, weight_code):
    per_group = H // KVH
    kv_width = KVH * 2 * HD
    group_ends = jnp.cumsum(group_counts)
    positions = jnp.arange(RLEN * per_group, dtype=jnp.int32) // per_group

    def one_slot(prompt_sum, stored_slot):
        response = slot_response[stored_slot]
        owner_group = jnp.sum((group_ends <= response).astype(jnp.int32))
        first_row = (prompt_slot[owner_group] * PLEN).astype(jnp.int32)
        first_resp = (stored_slot * RLEN).astype(jnp.int32)
        prompt_kv = lax.dynamic_slice_in_dim(prompt_cache, first_row, PLEN, 0)
        own_kv = lax.dynamic_slice_in_dim(resp_kv, first_resp, RLEN, 0)
        kv_all = jnp.concatenate([prompt_kv, own_kv], 0).reshape(PLEN + RLEN, KVH, 2, HD).transpose(1, 2, 0, 3)
        query_heads = lax.dynamic_slice_in_dim(queries, first_resp, RLEN, 0)
        query_heads = query_heads.reshape(RLEN, KVH, per_group, HD).transpose(1, 0, 2, 3).reshape(KVH, RLEN * per_group, HD)
        live_rows = jnp.arange(RLEN, dtype=jnp.int32) < resp_len[stored_slot]
        factor = jnp.where(live_rows, weight_code[stored_slot].astype(jnp.float32) / 8.0, 0.0)
        cotangent = lax.dynamic_slice_in_dim(grad_out, first_resp, RLEN, 0).astype(jnp.float32)
        cotangent = (cotangent * factor[:, None]).astype(jnp.bfloat16)
        cotangent = cotangent.reshape(RLEN, KVH, per_group, HD).transpose(1, 0, 2, 3).reshape(KVH, RLEN * per_group, HD)

        def per_head(bundle):
            return attend(bundle[0], bundle[1], bundle[2][0], bundle[2][1], positions)

        grad_query, grad_key, grad_value = lax.map(per_head, (query_heads, cotangent, kv_all))
        grad_query = grad_query.reshape(KVH, RLEN, per_group, HD).transpose(1, 0, 2, 3).reshape(RLEN, H * HD)
        flat_grads = jnp.stack([grad_key, grad_value], 1).transpose(2, 0, 1, 3).reshape(PLEN + RLEN, kv_width)
        current = lax.dynamic_slice_in_dim(prompt_sum, first_row, PLEN, 0)
        prompt_sum = lax.dynamic_update_slice_in_dim(prompt_sum, current + flat_grads[:PLEN], first_row, 0)
        return prompt_sum, (grad_query, flat_grads[PLEN:].astype(jnp.bfloat16))

    start_sum = jnp.zeros((PROMPTS * PLEN, kv_width), jnp.float32)
    prompt_sum, (query_grads, resp_grads) = lax.scan(one_slot, start_sum, jnp.arange(RESPONSES, dtype=jnp.int32))
    return (query_grads.reshape(RESPONSES * RLEN, H * HD), resp_grads.reshape(RESPONSES * RLEN, kv_width), prompt_sum.astype(jnp.bfloat16))
```

```python
import functools
import math

import jax
import jax.numpy as jnp
from jax import lax
from jax.experimental import pallas as pl
from jax.experimental.pallas import tpu as pltpu
from jax.sharding import PartitionSpec as P

HD = 128
PLEN = 2048
PROMPTS = 8
PLANE = 16
COLUMN = 16
CHUNK = PLEN // PLANE
PIECE = CHUNK // 2
WIDTH = 2 * HD
MESH = pl.DeviceIdType.MESH
VMEM_LIMIT = 56 * 1024 * 1024


def place():
    seq = lax.axis_index("seq")
    head = lax.axis_index("head")
    plane = seq // 2
    half = lax.rem(seq, 2)
    return plane, half, head, half * 8 + head


def in_plane(other):
    _, half, head, _ = place()
    return {"seq": 2 * other + half, "head": head}


def in_column(other):
    plane, _, _, _ = place()
    return {"seq": 2 * plane + other // 8, "head": lax.rem(other, 8)}


def greet():
    plane, _, _, column = place()
    barrier = pltpu.get_barrier_semaphore()

    def signal(step, carry):
        pl.semaphore_signal(
            barrier, inc=1, device_id=in_column(lax.rem(column + step, COLUMN)), device_id_type=MESH
        )
        pl.semaphore_signal(
            barrier, inc=1, device_id=in_plane(lax.rem(plane + step, PLANE)), device_id_type=MESH
        )
        return carry

    lax.fori_loop(1, 16, signal, 0)
    pl.semaphore_wait(barrier, 30)


def remote(src, dst, send_sem, recv_sem, device):
    return pltpu.make_async_remote_copy(
        src_ref=src,
        dst_ref=dst,
        send_sem=send_sem,
        recv_sem=recv_sem,
        device_id=device,
        device_id_type=MESH,
    )


def gather_kernel(
    wanted_ref, cache_ref, out_ref, by_head, held, staged, a_send, a_recv, b_send, b_recv, c_send, c_recv, local_sem
):
    plane, half, head, column = place()
    greet()

    def cache_part(target):
        return cache_ref.at[:, pl.ds(pl.multiple_of(lax.rem(target, 8) * WIDTH, WIDTH), WIDTH)]

    def column_copy(target):
        return remote(cache_part(target), by_head.at[column], a_send.at[target], a_recv.at[column], in_column(target))

    def column_arrival(source):
        return remote(cache_part(source), by_head.at[source], a_send.at[source], a_recv.at[source], in_column(source))

    def held_part(source):
        return held.at[source // 2, pl.ds(pl.multiple_of(lax.rem(source, 2) * PIECE, PIECE), PIECE)]

    def spread_copy(target):
        return remote(by_head.at[target], held_part(plane), b_send.at[target], b_recv.at[plane], in_plane(target))

    def spread_arrival(source):
        return remote(by_head.at[source], held_part(source), b_send.at[source], b_recv.at[source], in_plane(source))

    def chunk_copy(target):
        return remote(staged.at[target], out_ref.at[plane], c_send.at[target], c_recv.at[plane], in_plane(target))

    def chunk_arrival(source):
        return remote(staged.at[source], out_ref.at[source], c_send.at[source], c_recv.at[source], in_plane(source))

    def start_column(step, carry):
        column_copy(lax.rem(column + step, COLUMN)).start()
        return carry

    lax.fori_loop(1, COLUMN, start_column, 0)
    own = pltpu.make_async_copy(cache_part(column), by_head.at[column], local_sem)
    own.start()
    own.wait()

    def pass_on(step, carry):
        source = lax.rem(column + COLUMN - step, COLUMN)

        @pl.when(step > 0)
        def _():
            column_arrival(source).wait_recv()

        @pl.when(source != plane)
        def _():
            spread_copy(source).start()

        @pl.when(source == plane)
        def _():
            mine = pltpu.make_async_copy(by_head.at[plane], held_part(plane), local_sem)
            mine.start()
            mine.wait()

        return carry

    lax.fori_loop(0, COLUMN, pass_on, 0)

    def take_spread(step, carry):
        spread_arrival(lax.rem(plane + PLANE - step, PLANE)).wait_recv()
        return carry

    lax.fori_loop(1, PLANE, take_spread, 0)

    def send_chunk(step, carry):
        target = lax.rem(plane + step, PLANE)
        staged[target] = held[wanted_ref[2 * target + half]]
        chunk_copy(target).start()
        return carry

    lax.fori_loop(1, PLANE, send_chunk, 0)
    out_ref[plane] = held[wanted_ref[2 * plane + half]]

    def finish(step, carry):
        chunk_arrival(lax.rem(plane + PLANE - step, PLANE)).wait_recv()
        column_copy(lax.rem(column + step, COLUMN)).wait_send()
        target = lax.rem(plane + step, PLANE)
        spread_copy(target).wait_send()
        chunk_copy(target).wait_send()
        return carry

    lax.fori_loop(1, PLANE, finish, 0)


def return_kernel(
    order_ref,
    keep_ref,
    last_ref,
    some_ref,
    grads_ref,
    out_ref,
    terms,
    running,
    summed,
    spread,
    parts,
    c_send,
    c_recv,
    b_send,
    b_recv,
    a_send,
    a_recv,
    local_sem,
):
    plane, half, head, column = place()
    greet()

    def chunk_copy(target):
        return remote(grads_ref.at[target], terms.at[plane], c_send.at[target], c_recv.at[plane], in_plane(target))

    def chunk_arrival(source):
        return remote(grads_ref.at[source], terms.at[source], c_send.at[source], c_recv.at[source], in_plane(source))

    def summed_part(target):
        return summed.at[target // 2, pl.ds(pl.multiple_of(lax.rem(target, 2) * PIECE, PIECE), PIECE)]

    def spread_copy(target):
        return remote(summed_part(target), spread.at[plane], b_send.at[target], b_recv.at[plane], in_plane(target))

    def spread_arrival(source):
        return remote(summed_part(source), spread.at[source], b_send.at[source], b_recv.at[source], in_plane(source))

    def column_copy(target):
        return remote(spread.at[target], parts.at[column], a_send.at[target], a_recv.at[column], in_column(target))

    def column_arrival(source):
        return remote(spread.at[source], parts.at[source], a_send.at[source], a_recv.at[source], in_column(source))

    def send_chunk(step, carry):
        chunk_copy(lax.rem(plane + step, PLANE)).start()
        return carry

    lax.fori_loop(1, PLANE, send_chunk, 0)
    terms[plane] = grads_ref[plane]

    def take_chunk(step, carry):
        chunk_arrival(lax.rem(plane + PLANE - step, PLANE)).wait_recv()
        return carry

    lax.fori_loop(1, PLANE, take_chunk, 0)

    def add_rows(block, carry):
        rows = pl.ds(pl.multiple_of(block * 16, 16), 16)
        total = jnp.zeros((16, WIDTH), jnp.float32)
        for i in range(PLANE):
            total = total * keep_ref[i] + terms[order_ref[i], rows].astype(jnp.float32)
            running[i, rows] = total
        for p in range(PROMPTS):
            summed[p, rows] = (running[last_ref[p], rows] * some_ref[p]).astype(jnp.bfloat16)
        return carry

    lax.fori_loop(0, CHUNK // 16, add_rows, 0)

    def send_spread(step, carry):
        spread_copy(lax.rem(plane + step, PLANE)).start()
        return carry

    lax.fori_loop(1, PLANE, send_spread, 0)
    mine = pltpu.make_async_copy(summed_part(plane), spread.at[plane], local_sem)
    mine.start()
    mine.wait()

    def pass_on(step, carry):
        source = lax.rem(plane + PLANE - step, PLANE)

        @pl.when(step > 0)
        def _():
            spread_arrival(source).wait_recv()

        @pl.when(source != column)
        def _():
            column_copy(source).start()

        @pl.when(source == column)
        def _():
            own = pltpu.make_async_copy(spread.at[column], parts.at[column], local_sem)
            own.start()
            own.wait()

        return carry

    lax.fori_loop(0, PLANE, pass_on, 0)

    def finish(step, carry):
        column_arrival(lax.rem(column + COLUMN - step, COLUMN)).wait_recv()
        target = lax.rem(plane + step, PLANE)
        chunk_copy(target).wait_send()
        spread_copy(target).wait_send()
        column_copy(lax.rem(column + step, COLUMN)).wait_send()
        return carry

    lax.fori_loop(1, PLANE, finish, 0)
    for h in range(8):
        both = parts[h].astype(jnp.float32) + parts[8 + h].astype(jnp.float32)
        out_ref[:, h * WIDTH : (h + 1) * WIDTH] = both.astype(jnp.bfloat16)


def attend_kernel(
    len_ref,
    code_ref,
    q_ref,
    go_ref,
    kv_ref,
    own_ref,
    dq_ref,
    dkv_ref,
    down_ref,
    keys,
    values,
    scores,
    dk_sum,
    dv_sum,
):
    step = pl.program_id(0)
    rows = q_ref.shape[0]
    total = PLEN + rows
    scale = HD**-0.5
    log2e = math.log2(math.e)

    @pl.when(step == 0)
    def _():
        keys[:PLEN] = kv_ref[:, :HD]
        keys[PLEN:] = own_ref[:, :HD]
        values[:PLEN] = kv_ref[:, HD:]
        values[PLEN:] = own_ref[:, HD:]
        dk_sum[...] = jnp.zeros_like(dk_sum)
        dv_sum[...] = jnp.zeros_like(dv_sum)

    query = q_ref[...]
    position = lax.broadcasted_iota(jnp.int32, (rows, HD), 0)
    factor = jnp.where(position < len_ref[0], code_ref[0].astype(jnp.float32) / 8.0, 0.0)
    cotangent = (go_ref[...].astype(jnp.float32) * factor).astype(jnp.bfloat16)

    nt = (((1,), (1,)), ((), ()))
    nn = (((1,), (0,)), ((), ()))
    tn = (((0,), (0,)), ((), ()))
    block = 256
    count = total // block
    top = None
    for b in range(count):
        at = slice(b * block, (b + 1) * block)
        part = lax.dot_general(keys[at], query, nt, preferred_element_type=jnp.float32)
        if b == count - 1:
            key_at = lax.broadcasted_iota(jnp.int32, (block, rows), 0)
            seen_from = lax.broadcasted_iota(jnp.int32, (block, rows), 1)
            part = jnp.where(key_at <= seen_from, part, -1e30)
        scores[at] = part
        high = jnp.max(part.reshape(block // 8, 8, rows), axis=0)
        top = high if top is None else jnp.maximum(top, high)
    top = jnp.max(top, axis=0, keepdims=True)
    weight_sum = None
    for b in range(count):
        at = slice(b * block, (b + 1) * block)
        raw = jnp.exp2((scores[at] - top) * (scale * log2e))
        scores[at] = raw
        low = jnp.sum(raw.reshape(block // 8, 8, rows), axis=0)
        weight_sum = low if weight_sum is None else weight_sum + low
    inverse = 1.0 / jnp.sum(weight_sum, axis=0, keepdims=True)
    inverse_rows = jnp.transpose(jnp.broadcast_to(inverse, (HD, rows)))
    scaled = (cotangent.astype(jnp.float32) * inverse_rows).astype(jnp.bfloat16)
    delta = None
    pieces = []
    for b in range(count):
        at = slice(b * block, (b + 1) * block)
        raw = scores[at]
        grad = lax.dot_general(values[at], scaled, nt, preferred_element_type=jnp.float32)
        pieces.append(grad)
        term = jnp.sum((raw * grad).reshape(block // 8, 8, rows), axis=0)
        delta = term if delta is None else delta + term
        dv_sum[at] += lax.dot_general(raw.astype(jnp.bfloat16), scaled, nn, preferred_element_type=jnp.float32)
    delta = jnp.sum(delta, axis=0, keepdims=True) * inverse
    query_grad = jnp.zeros((rows, HD), jnp.float32)
    for b in range(count):
        at = slice(b * block, (b + 1) * block)
        half = (scores[at] * (pieces[b] - delta)).astype(jnp.bfloat16)
        dk_sum[at] += lax.dot_general(half, query, nn, preferred_element_type=jnp.float32)
        query_grad = query_grad + lax.dot_general(half, keys[at], tn, preferred_element_type=jnp.float32)
    dq_ref[...] = (query_grad * scale).astype(jnp.bfloat16)

    @pl.when(step == pl.num_programs(0) - 1)
    def _():
        dkv_ref[:, :HD] = (dk_sum[:PLEN] * scale).astype(jnp.bfloat16)
        dkv_ref[:, HD:] = dv_sum[:PLEN].astype(jnp.bfloat16)
        down_ref[:, :HD] = (dk_sum[PLEN:] * scale).astype(jnp.bfloat16)
        down_ref[:, HD:] = dv_sum[PLEN:].astype(jnp.bfloat16)


def local(
    queries, resp_kv, prompt_cache, grad_out, group_counts, prompt_slot, slot_response, resp_len, weight_code
):
    half = lax.rem(lax.axis_index("seq"), 2)
    ends = jnp.cumsum(group_counts)
    group = jnp.sum((ends[None, :] <= slot_response[:, None]).astype(jnp.int32), axis=1)
    number = jnp.arange(PROMPTS, dtype=jnp.int32)
    wanted = jnp.sum(jnp.where(group[:, None] == number[None, :], prompt_slot[None, :], 0), axis=1)

    both = wanted.reshape(PLANE, 2)
    mine = jnp.where(half == 0, both[:, 0], both[:, 1])
    slot = jnp.arange(PLANE, dtype=jnp.int32)
    before = (mine[None, :] < mine[:, None]) | ((mine[None, :] == mine[:, None]) & (slot[None, :] < slot[:, None]))
    rank = jnp.sum(before.astype(jnp.int32), axis=1)
    is_at = rank[None, :] == slot[:, None]
    order = jnp.sum(jnp.where(is_at, slot[None, :], 0), axis=1)
    sorted_prompt = jnp.sum(jnp.where(is_at, mine[None, :], 0), axis=1)
    earlier = jnp.concatenate([jnp.full((1,), -1, jnp.int32), sorted_prompt[:-1]])
    keep = (sorted_prompt == earlier).astype(jnp.float32)
    upto = jnp.sum((mine[None, :] <= number[:, None]).astype(jnp.int32), axis=1)
    last = jnp.maximum(upto - 1, 0)
    some = jnp.any(mine[None, :] == number[:, None], axis=1).astype(jnp.float32)

    vmem = pl.BlockSpec(memory_space=pltpu.VMEM)
    smem = pl.BlockSpec(memory_space=pltpu.SMEM)
    sems = [pltpu.SemaphoreType.DMA((16,))] * 6 + [pltpu.SemaphoreType.DMA]
    bf16 = jnp.bfloat16
    prompt_kv = pl.pallas_call(
        gather_kernel,
        out_shape=jax.ShapeDtypeStruct((PLANE, CHUNK, WIDTH), bf16),
        in_specs=[smem, vmem],
        out_specs=vmem,
        scratch_shapes=[
            pltpu.VMEM((COLUMN, PIECE, WIDTH), bf16),
            pltpu.VMEM((PROMPTS, CHUNK, WIDTH), bf16),
            pltpu.VMEM((PLANE, CHUNK, WIDTH), bf16),
        ]
        + sems,
        compiler_params=pltpu.CompilerParams(
            collective_id=0, has_side_effects=True, vmem_limit_bytes=VMEM_LIMIT
        ),
    )(wanted, prompt_cache)

    rows, columns = queries.shape
    total = PLEN + rows
    heads = columns // HD
    by_head = pl.BlockSpec((rows, HD), lambda i: (0, i))
    grad_queries, prompt_grads, grad_resp_kv = pl.pallas_call(
        attend_kernel,
        grid=(heads,),
        out_shape=[
            jax.ShapeDtypeStruct((rows, columns), bf16),
            jax.ShapeDtypeStruct((PLEN, WIDTH), bf16),
            jax.ShapeDtypeStruct((rows, WIDTH), bf16),
        ],
        in_specs=[smem, smem, by_head, by_head, vmem, vmem],
        out_specs=[by_head, vmem, vmem],
        scratch_shapes=[
            pltpu.VMEM((total, HD), bf16),
            pltpu.VMEM((total, HD), bf16),
            pltpu.VMEM((total, rows), jnp.float32),
            pltpu.VMEM((total, HD), jnp.float32),
            pltpu.VMEM((total, HD), jnp.float32),
        ],
        compiler_params=pltpu.CompilerParams(vmem_limit_bytes=VMEM_LIMIT),
    )(resp_len, weight_code, queries, grad_out, prompt_kv.reshape(PLEN, WIDTH), resp_kv)

    grad_prompt_cache = pl.pallas_call(
        return_kernel,
        out_shape=jax.ShapeDtypeStruct(prompt_cache.shape, bf16),
        in_specs=[smem, smem, smem, smem, vmem],
        out_specs=vmem,
        scratch_shapes=[
            pltpu.VMEM((PLANE, CHUNK, WIDTH), bf16),
            pltpu.VMEM((PLANE, CHUNK, WIDTH), jnp.float32),
            pltpu.VMEM((PROMPTS, CHUNK, WIDTH), bf16),
            pltpu.VMEM((PLANE, PIECE, WIDTH), bf16),
            pltpu.VMEM((COLUMN, PIECE, WIDTH), bf16),
        ]
        + sems,
        compiler_params=pltpu.CompilerParams(
            collective_id=1, has_side_effects=True, vmem_limit_bytes=VMEM_LIMIT
        ),
    )(order, keep, last, some, prompt_grads.reshape(PLANE, CHUNK, WIDTH))
    return grad_queries, grad_resp_kv, grad_prompt_cache


def solution(mesh):
    placed = (
        P("seq", "head"),
        P("seq", "head"),
        P(("seq", "head"), None),
        P("seq", "head"),
        P(),
        P(),
        P(),
        P("seq"),
        P("seq"),
    )
    return jax.shard_map(
        local,
        mesh=mesh,
        in_specs=placed,
        out_specs=(P("seq", "head"), P("seq", "head"), P(("seq", "head"), None)),
        check_vma=False,
    )
```

```python
import math

import jax
import jax.numpy as jnp
from jax import lax
from jax.experimental import pallas as pl
from jax.experimental.pallas import tpu as pltpu
from jax.sharding import PartitionSpec as P

HD = 128
PLEN = 2048
RLEN = 256
HEADS = 8
PROMPTS = 8
RING = 16
CHUNK = PLEN // RING
PIECE = CHUNK // 2
BLOCK = 256
BLOCKS = PLEN // BLOCK
PER_BLOCK = BLOCK // CHUNK
ROWS = HEADS * RLEN
KEYS = PLEN + RLEN
WIDTH = 2 * HD
SCALE = HD**-0.5
LOG2E = math.log2(math.e)
MESH = pl.DeviceIdType.MESH
VMEM_LIMIT = 60 * 1024 * 1024
NN = (((1,), (0,)), ((), ()))
F32 = jnp.float32
BF16 = jnp.bfloat16


def around(index):
    return lax.rem(index + 2 * RING, RING)


def head_rows(j):
    return slice(j * RLEN, (j + 1) * RLEN)


def head_columns(j):
    return slice(j * HD, (j + 1) * HD)


def chunk_rows(step):
    return pl.ds(pl.multiple_of(step * CHUNK, CHUNK), CHUNK)


def fold(values, op):
    return op(values.reshape(values.shape[0] // 8, 8, values.shape[1]), axis=0)


def dot(a, b):
    return lax.dot_general(a, b, NN, preferred_element_type=F32)


def kernel(
    counts_ref,
    prompt_slot_ref,
    response_ref,
    len_ref,
    code_ref,
    q_ref,
    own_ref,
    cache_ref,
    go_ref,
    dq_ref,
    down_ref,
    dcache_ref,
    wanted,
    previous,
    last,
    q_in,
    go_in,
    own_in,
    by_head,
    held_keys,
    held_values,
    staged,
    keys,
    values,
    q_rows,
    q_cols,
    cot_cols,
    cot_scaled_cols,
    cot_scaled_rows,
    scores,
    raw,
    top,
    delta,
    inverse,
    dq_cols,
    grads,
    terms,
    running,
    summed,
    spread,
    parts,
    in_sem,
    own_sem,
    a_send,
    a_recv,
    b_send,
    b_recv,
    c_send,
    c_recv,
    rc_send,
    rc_recv,
    rb_send,
    rb_recv,
    ra_send,
    ra_recv,
):
    seq = lax.axis_index("seq")
    head = lax.axis_index("head")
    plane = seq // 2
    half = lax.rem(seq, 2)
    column = half * 8 + head

    def in_plane(other):
        return {"seq": 2 * other + half, "head": head}

    def in_column(other):
        return {"seq": 2 * plane + other // 8, "head": lax.rem(other, 8)}

    def remote(src, dst, send_sem, recv_sem, device):
        return pltpu.make_async_remote_copy(
            src_ref=src, dst_ref=dst, send_sem=send_sem, recv_sem=recv_sem, device_id=device, device_id_type=MESH
        )

    def local_copy(src, dst):
        copy = pltpu.make_async_copy(src, dst, own_sem)
        copy.start()
        copy.wait()

    loads = [
        pltpu.make_async_copy(q_ref, q_in, in_sem.at[0]),
        pltpu.make_async_copy(go_ref, go_in, in_sem.at[1]),
        pltpu.make_async_copy(own_ref, own_in, in_sem.at[2]),
    ]
    for load in loads:
        load.start()

    barrier = pltpu.get_barrier_semaphore()

    def greet(step, carry):
        pl.semaphore_signal(barrier, inc=1, device_id=in_column(around(column + step)), device_id_type=MESH)
        pl.semaphore_signal(barrier, inc=1, device_id=in_plane(around(plane + step)), device_id_type=MESH)
        return carry

    lax.fori_loop(1, RING, greet, 0)
    pl.semaphore_wait(barrier, 2 * (RING - 1))

    def cache_part(part, target):
        at = lax.rem(target, 8) * WIDTH + part * HD
        return cache_ref.at[:, pl.ds(pl.multiple_of(at, HD), HD)]

    def column_copy(part, step):
        target = around(column + step)
        return remote(
            cache_part(part, target),
            by_head.at[part, step],
            a_send.at[part, step],
            a_recv.at[part, step],
            in_column(target),
        )

    for part in range(2):

        def start_column(step, carry):
            column_copy(part, step).start()
            return carry

        lax.fori_loop(1, RING, start_column, 0)

    held = (held_keys, held_values)

    def held_piece(part, source):
        return held[part].at[source // 2, pl.ds(pl.multiple_of(lax.rem(source, 2) * PIECE, PIECE), PIECE)]

    def spread_copy(part, step, by_step):
        return remote(
            by_head.at[part, by_step],
            held_piece(part, plane),
            b_send.at[part, step],
            b_recv.at[part, step],
            in_plane(around(plane + step)),
        )

    def pass_on(part):
        local_copy(cache_part(part, column), by_head.at[part, 0])

        def one(by_step, carry):
            @pl.when(by_step > 0)
            def _():
                column_copy(part, by_step).wait_recv()

            target = around(column - by_step)
            step = around(target - plane)

            @pl.when(step != 0)
            def _():
                spread_copy(part, step, by_step).start()

            @pl.when(step == 0)
            def _():
                local_copy(by_head.at[part, by_step], held_piece(part, plane))

            return carry

        lax.fori_loop(0, RING, one, 0)

    gathered = (keys, values)

    def chunk_copy(part, step):
        return remote(
            staged.at[part, step],
            gathered[part].at[chunk_rows(step)],
            c_send.at[part, step],
            c_recv.at[part, step],
            in_plane(around(plane + step)),
        )

    def send_chunks(part):
        def take(step, carry):
            source = around(plane - step)
            remote(
                by_head.at[part, 0],
                held_piece(part, source),
                b_send.at[part, step],
                b_recv.at[part, step],
                in_plane(source),
            ).wait_recv()
            return carry

        lax.fori_loop(1, RING, take, 0)

        def send(step, carry):
            staged[part, step] = held[part][wanted[step]]
            chunk_copy(part, step).start()
            return carry

        lax.fori_loop(1, RING, send, 0)
        gathered[part][:CHUNK] = held[part][wanted[0]]

    def find_prompt(step, carry):
        response = response_ref[2 * around(plane + step) + half]
        end = jnp.int32(0)
        group = jnp.int32(0)
        for i in range(PROMPTS):
            end = end + counts_ref[i]
            group = group + (end <= response).astype(jnp.int32)
        wanted[step] = prompt_slot_ref[jnp.minimum(group, PROMPTS - 1)]
        return carry

    lax.fori_loop(0, RING, find_prompt, 0)

    def find_previous(step, carry):
        def look(other, found):
            same = (wanted[other] == wanted[step]) & (other < step)
            return jnp.where(same, other, found)

        previous[step] = lax.fori_loop(0, RING, look, jnp.int32(RING))
        return carry

    lax.fori_loop(0, RING, find_previous, 0)

    def find_last(prompt, carry):
        def look(other, found):
            return jnp.where(wanted[other] == prompt, other, found)

        last[prompt] = lax.fori_loop(0, RING, look, jnp.int32(RING))
        return carry

    lax.fori_loop(0, PROMPTS, find_last, 0)

    for load in loads:
        load.wait()
    position = lax.broadcasted_iota(jnp.int32, (RLEN, HD), 0)
    factor = jnp.where(position < len_ref[0], code_ref[0].astype(F32) / 8.0, 0.0)
    for j in range(HEADS):
        query = q_in[:, head_columns(j)]
        q_rows[head_rows(j)] = query
        q_cols[:, head_rows(j)] = jnp.transpose(query)
        cotangent = go_in[:, head_columns(j)].astype(F32) * factor
        cot_cols[:, head_rows(j)] = jnp.transpose(cotangent).astype(BF16)
    keys[PLEN:] = own_in[:, :HD]
    values[PLEN:] = own_in[:, HD:]
    running[RING] = jnp.zeros((CHUNK, HD), F32)
    dq_cols[...] = jnp.zeros_like(dq_cols)

    def block_rows(b):
        return pl.ds(pl.multiple_of(b * BLOCK, BLOCK), BLOCK)

    def score(b, own):
        block = keys[block_rows(b)]
        for j in range(HEADS):
            at = head_rows(j)
            part = dot(block, q_cols[:, at])
            if own:
                key_at = lax.broadcasted_iota(jnp.int32, (BLOCK, RLEN), 0)
                seen_from = lax.broadcasted_iota(jnp.int32, (BLOCK, RLEN), 1)
                part = jnp.where(key_at <= seen_from, part, -1e30)
            scores[b, :, at] = part
            high = fold(part, jnp.max)
            top[:, at] = high if own else jnp.maximum(top[:, at], high)

    score(BLOCKS, True)

    pass_on(0)
    send_chunks(0)
    pass_on(1)
    send_chunks(1)

    def arrive(part, b):
        def one(i, carry):
            step = b * PER_BLOCK + i

            @pl.when(step > 0)
            def _():
                chunk_copy(part, step).wait_recv()

            return carry

        lax.fori_loop(0, PER_BLOCK, one, 0)

    def score_block(b, carry):
        arrive(0, b)
        score(b, False)
        return carry

    lax.fori_loop(0, BLOCKS, score_block, 0)

    for j in range(HEADS):
        at = head_rows(j)
        highest = jnp.max(top[:, at], axis=0, keepdims=True)

        def weigh(b, total):
            weights = jnp.exp2((scores[b, :, at] - highest) * (SCALE * LOG2E))
            raw[b, :, at] = weights.astype(BF16)
            return total + fold(weights, jnp.sum)

        total = lax.fori_loop(0, BLOCKS + 1, weigh, jnp.zeros((8, RLEN), F32))
        over = 1.0 / jnp.sum(total, axis=0, keepdims=True)
        inverse[:, at] = jnp.broadcast_to(over, (8, RLEN))
        scaled = cot_cols[:, at].astype(F32) * over
        cot_scaled_cols[:, at] = scaled.astype(BF16)
        cot_scaled_rows[at] = jnp.transpose(scaled).astype(BF16)

    def return_copy(part, step):
        return remote(
            grads.at[part, step],
            terms.at[part, step],
            rc_send.at[part, step],
            rc_recv.at[part, step],
            in_plane(around(plane - step)),
        )

    def send_back(part, b, block):
        for i in range(PER_BLOCK):
            grads[part, b * PER_BLOCK + i] = block[i * CHUNK : (i + 1) * CHUNK]

        def one(i, carry):
            step = b * PER_BLOCK + i

            @pl.when(step > 0)
            def _():
                return_copy(part, step).start()

            return carry

        lax.fori_loop(0, PER_BLOCK, one, 0)

    def value_part(b, first):
        block = values[block_rows(b)]
        for j in range(HEADS):
            at = head_rows(j)
            grad = dot(block, cot_scaled_cols[:, at])
            scores[b, :, at] = grad
            term = fold(grad * raw[b, :, at].astype(F32), jnp.sum)
            delta[:, at] = term if first else delta[:, at] + term
        return dot(raw[b], cot_scaled_rows[...]).astype(BF16)

    down_ref[:, HD:] = value_part(BLOCKS, True)

    def value_block(b, carry):
        arrive(1, b)
        send_back(1, b, value_part(b, False))
        return carry

    lax.fori_loop(0, BLOCKS, value_block, 0)
    for j in range(HEADS):
        at = head_rows(j)
        delta[:, at] = jnp.sum(delta[:, at], axis=0, keepdims=True) * inverse[:, at]

    def key_part(b):
        turned = jnp.transpose(keys[block_rows(b)])
        for j in range(HEADS):
            at = head_rows(j)
            weights = raw[b, :, at].astype(F32)
            shift = delta[0:1, at]
            change = (weights * (scores[b, :, at] - shift)).astype(BF16)
            raw[b, :, at] = change
            dq_cols[:, at] += dot(turned, change)
        return (dot(raw[b], q_rows[...]) * SCALE).astype(BF16)

    def key_block(b, carry):
        send_back(0, b, key_part(b))
        return carry

    lax.fori_loop(0, BLOCKS, key_block, 0)

    def return_spread(part, step):
        target = around(plane + step)
        piece = summed.at[
            part, target // 2, pl.ds(pl.multiple_of(lax.rem(target, 2) * PIECE, PIECE), PIECE)
        ]
        return remote(
            piece, spread.at[part, step], rb_send.at[part, step], rb_recv.at[part, step], in_plane(target)
        )

    def add_up(part):
        def take(step, carry):
            return_copy(part, step).wait_recv()
            return carry

        lax.fori_loop(1, RING, take, 0)
        terms[part, 0] = grads[part, 0]

        def add(step, carry):
            running[step] = running[previous[step]] + terms[part, step].astype(F32)
            return carry

        lax.fori_loop(0, RING, add, 0)

        def close(prompt, carry):
            summed[part, prompt] = running[last[prompt]].astype(BF16)
            return carry

        lax.fori_loop(0, PROMPTS, close, 0)

        def send(step, carry):
            return_spread(part, step).start()
            return carry

        lax.fori_loop(1, RING, send, 0)
        spread[part, 0] = summed[
            part, plane // 2, pl.ds(pl.multiple_of(lax.rem(plane, 2) * PIECE, PIECE), PIECE)
        ]

    def return_column(part, step, by_step):
        return remote(
            spread.at[part, by_step],
            parts.at[part, column],
            ra_send.at[part, step],
            ra_recv.at[part, step],
            in_column(around(column + step)),
        )

    def return_on(part):
        def one(by_step, carry):
            @pl.when(by_step > 0)
            def _():
                return_spread(part, by_step).wait_recv()

            step = around(plane - by_step - column)

            @pl.when(step != 0)
            def _():
                return_column(part, step, by_step).start()

            @pl.when(step == 0)
            def _():
                local_copy(spread.at[part, by_step], parts.at[part, column])

            return carry

        lax.fori_loop(0, RING, one, 0)

    add_up(1)

    down_ref[:, :HD] = key_part(BLOCKS)
    for j in range(HEADS):
        dq_ref[:, head_columns(j)] = (jnp.transpose(dq_cols[:, head_rows(j)]) * SCALE).astype(BF16)

    return_on(1)
    add_up(0)
    return_on(0)

    for part in (1, 0):

        def collect(step, carry):
            source = around(column - step)
            remote(
                spread.at[part, 0],
                parts.at[part, source],
                ra_send.at[part, step],
                ra_recv.at[part, step],
                in_column(source),
            ).wait_recv()
            return carry

        lax.fori_loop(1, RING, collect, 0)
        for h in range(8):
            both = parts[part, h].astype(F32) + parts[part, 8 + h].astype(F32)
            dcache_ref[:, h * WIDTH + part * HD : h * WIDTH + (part + 1) * HD] = both.astype(BF16)

    for part in range(2):

        def finish(step, carry):
            column_copy(part, step).wait_send()
            spread_copy(part, step, 0).wait_send()
            chunk_copy(part, step).wait_send()
            return_copy(part, step).wait_send()
            return_spread(part, step).wait_send()
            return_column(part, step, 0).wait_send()
            return carry

        lax.fori_loop(1, RING, finish, 0)


def local(
    queries, resp_kv, prompt_cache, grad_out, group_counts, prompt_slot, slot_response, resp_len, weight_code
):
    vmem = pl.BlockSpec(memory_space=pltpu.VMEM)
    smem = pl.BlockSpec(memory_space=pltpu.SMEM)
    hbm = pl.BlockSpec(memory_space=pltpu.HBM)
    scratch = [
        pltpu.SMEM((RING,), jnp.int32),
        pltpu.SMEM((RING,), jnp.int32),
        pltpu.SMEM((PROMPTS,), jnp.int32),
        pltpu.VMEM((RLEN, HEADS * HD), BF16),
        pltpu.VMEM((RLEN, HEADS * HD), BF16),
        pltpu.VMEM((RLEN, WIDTH), BF16),
        pltpu.VMEM((2, RING, PIECE, HD), BF16),
        pltpu.VMEM((PROMPTS, CHUNK, HD), BF16),
        pltpu.VMEM((PROMPTS, CHUNK, HD), BF16),
        pltpu.VMEM((2, RING, CHUNK, HD), BF16),
        pltpu.VMEM((KEYS, HD), BF16),
        pltpu.VMEM((KEYS, HD), BF16),
        pltpu.VMEM((ROWS, HD), BF16),
        pltpu.VMEM((HD, ROWS), BF16),
        pltpu.VMEM((HD, ROWS), BF16),
        pltpu.VMEM((HD, ROWS), BF16),
        pltpu.VMEM((ROWS, HD), BF16),
        pltpu.VMEM((BLOCKS + 1, BLOCK, ROWS), F32),
        pltpu.VMEM((BLOCKS + 1, BLOCK, ROWS), BF16),
        pltpu.VMEM((8, ROWS), F32),
        pltpu.VMEM((8, ROWS), F32),
        pltpu.VMEM((8, ROWS), F32),
        pltpu.VMEM((HD, ROWS), F32),
        pltpu.VMEM((2, RING, CHUNK, HD), BF16),
        pltpu.VMEM((2, RING, CHUNK, HD), BF16),
        pltpu.VMEM((RING + 1, CHUNK, HD), F32),
        pltpu.VMEM((2, PROMPTS, CHUNK, HD), BF16),
        pltpu.VMEM((2, RING, PIECE, HD), BF16),
        pltpu.VMEM((2, RING, PIECE, HD), BF16),
        pltpu.SemaphoreType.DMA((3,)),
        pltpu.SemaphoreType.DMA,
    ] + [pltpu.SemaphoreType.DMA((2, RING))] * 12
    products = 5 * ROWS * KEYS * HD
    return pl.pallas_call(
        kernel,
        out_shape=[
            jax.ShapeDtypeStruct(queries.shape, BF16),
            jax.ShapeDtypeStruct(resp_kv.shape, BF16),
            jax.ShapeDtypeStruct(prompt_cache.shape, BF16),
        ],
        in_specs=[smem] * 5 + [hbm] * 4,
        out_specs=[vmem] * 3,
        scratch_shapes=scratch,
        compiler_params=pltpu.CompilerParams(
            collective_id=0, has_side_effects=True, vmem_limit_bytes=VMEM_LIMIT
        ),
        cost_estimate=pl.CostEstimate(flops=2 * products, bytes_accessed=3 << 20, transcendentals=ROWS * KEYS),
    )(
        group_counts,
        prompt_slot,
        slot_response,
        resp_len,
        weight_code,
        queries,
        resp_kv,
        prompt_cache,
        grad_out,
    )


def solution(mesh):
    placed = (
        P("seq", "head"),
        P("seq", "head"),
        P(("seq", "head"), None),
        P("seq", "head"),
        P(),
        P(),
        P(),
        P("seq"),
        P("seq"),
    )
    return jax.shard_map(
        local,
        mesh=mesh,
        in_specs=placed,
        out_specs=(P("seq", "head"), P("seq", "head"), P(("seq", "head"), None)),
        check_vma=False,
    )
```

```python
import math

import jax
import jax.numpy as jnp
from jax import lax
from jax.experimental import pallas as pl
from jax.experimental.pallas import tpu as pltpu
from jax.sharding import PartitionSpec as P

HD = 128
PLEN = 2048
RLEN = 256
HEADS = 8
PROMPTS = 8
RING = 16
CHUNK = PLEN // RING
PIECE = CHUNK // 2
BLOCK = 256
BLOCKS = PLEN // BLOCK
PER_BLOCK = BLOCK // CHUNK
ROWS = HEADS * RLEN
KEYS = PLEN + RLEN
WIDTH = 2 * HD
SCALE = HD**-0.5
LOG2E = math.log2(math.e)
MESH = pl.DeviceIdType.MESH
VMEM_LIMIT = 60 * 1024 * 1024
NN = (((1,), (0,)), ((), ()))
F32 = jnp.float32
BF16 = jnp.bfloat16


RELAYS = ((9, 13, 12), (11, 15, 12), (6, 7, 3), (14, 15, 3))


def around(index):
    return lax.rem(index + 2 * RING, RING)


def plus(plane, offset):
    return lax.rem(plane // 4 + offset // 4, 4) * 4 + lax.rem(plane + lax.rem(offset, 4), 4)


def minus(plane, offset):
    return lax.rem(plane // 4 + 4 - offset // 4, 4) * 4 + lax.rem(plane + 4 - lax.rem(offset, 4), 4)


def opposite(offset):
    return (-(offset // 4) % 4) * 4 + -offset % 4


def is_relayed(offset):
    found = offset == RELAYS[0][0]
    for relay in RELAYS[1:]:
        found = found | (offset == relay[0])
    return found


def head_rows(j):
    return slice(j * RLEN, (j + 1) * RLEN)


def head_columns(j):
    return slice(j * HD, (j + 1) * HD)


def chunk_rows(step):
    return pl.ds(pl.multiple_of(step * CHUNK, CHUNK), CHUNK)


def fold(values, op):
    return op(values.reshape(values.shape[0] // 8, 8, values.shape[1]), axis=0)


def dot(a, b):
    return lax.dot_general(a, b, NN, preferred_element_type=F32)


def kernel(
    counts_ref,
    prompt_slot_ref,
    response_ref,
    len_ref,
    code_ref,
    q_ref,
    own_ref,
    cache_ref,
    go_ref,
    dq_ref,
    down_ref,
    dcache_ref,
    wanted,
    previous,
    last,
    q_in,
    go_in,
    own_in,
    by_head,
    held_keys,
    held_values,
    staged,
    keys,
    values,
    q_rows,
    q_cols,
    cot_cols,
    cot_scaled_cols,
    cot_scaled_rows,
    scores,
    raw,
    top,
    delta,
    inverse,
    dq_cols,
    grads,
    terms,
    running,
    summed,
    spread,
    parts,
    b_mid,
    c_mid,
    rc_mid,
    rb_mid,
    in_sem,
    a_send,
    a_recv,
    b_send,
    b_recv,
    c_send,
    c_recv,
    rc_send,
    rc_recv,
    rb_send,
    rb_recv,
    ra_send,
    ra_recv,
    b_mid_recv,
    b_mid_send,
    c_mid_recv,
    c_mid_send,
    rc_mid_recv,
    rc_mid_send,
    rb_mid_recv,
    rb_mid_send,
):
    seq = lax.axis_index("seq")
    head = lax.axis_index("head")
    plane = seq // 2
    half = lax.rem(seq, 2)
    column = half * 8 + head

    def in_plane(other):
        return {"seq": 2 * other + half, "head": head}

    def in_column(other):
        return {"seq": 2 * plane + other // 8, "head": lax.rem(other, 8)}

    def remote(src, dst, send_sem, recv_sem, device):
        return pltpu.make_async_remote_copy(
            src_ref=src, dst_ref=dst, send_sem=send_sem, recv_sem=recv_sem, device_id=device, device_id_type=MESH
        )

    loads = [
        pltpu.make_async_copy(q_ref, q_in, in_sem.at[0]),
        pltpu.make_async_copy(go_ref, go_in, in_sem.at[1]),
        pltpu.make_async_copy(own_ref, own_in, in_sem.at[2]),
    ]
    for part in range(2):
        at = pl.ds(pl.multiple_of(head * WIDTH + part * HD, HD), HD)
        loads.append(pltpu.make_async_copy(cache_ref.at[:, at], by_head.at[part, 0], in_sem.at[3 + part]))
    for load in loads:
        load.start()

    barrier = pltpu.get_barrier_semaphore()

    def greet(step, carry):
        pl.semaphore_signal(barrier, inc=1, device_id=in_column(around(column + step)), device_id_type=MESH)
        pl.semaphore_signal(barrier, inc=1, device_id=in_plane(plus(plane, step)), device_id_type=MESH)
        return carry

    lax.fori_loop(1, RING, greet, 0)
    pl.semaphore_wait(barrier, 2 * (RING - 1))

    def cache_part(part, target):
        at = lax.rem(target, 8) * WIDTH + part * HD
        return cache_ref.at[:, pl.ds(pl.multiple_of(at, HD), HD)]

    def column_copy(part, step):
        target = around(column + step)
        return remote(
            cache_part(part, target),
            by_head.at[part, step],
            a_send.at[part, step],
            a_recv.at[part, step],
            in_column(target),
        )

    for part in range(2):

        def start_column(step, carry):
            column_copy(part, step).start()
            return carry

        lax.fori_loop(1, RING, start_column, 0)

    held = (held_keys, held_values)

    def held_piece(part, source):
        return held[part].at[source // 2, pl.ds(pl.multiple_of(lax.rem(source, 2) * PIECE, PIECE), PIECE)]

    def spread_copy(part, step, by_step):
        return remote(
            by_head.at[part, by_step],
            held_piece(part, plane),
            b_send.at[part, step],
            b_recv.at[part, step],
            in_plane(plus(plane, step)),
        )

    def spread_first(part, r, by_step):
        offset, between, _ = RELAYS[r]
        return remote(
            by_head.at[part, by_step],
            b_mid.at[part, r],
            b_send.at[part, offset],
            b_mid_recv.at[part, r],
            in_plane(plus(plane, between)),
        )

    def spread_second(part, r):
        offset, between, on = RELAYS[r]
        return remote(
            b_mid.at[part, r],
            held_piece(part, minus(plane, between)),
            b_mid_send.at[part, r],
            b_recv.at[part, offset],
            in_plane(plus(plane, on)),
        )

    def pass_on(part):
        def one(by_step, carry):
            @pl.when(by_step > 0)
            def _():
                column_copy(part, by_step).wait_recv()

            target = around(column - by_step)
            step = lax.rem(target // 4 - plane // 4 + 4, 4) * 4 + lax.rem(target - plane + RING, 4)

            for r in range(len(RELAYS)):

                @pl.when(step == RELAYS[r][0])
                def _():
                    spread_first(part, r, by_step).start()

            @pl.when((step != 0) & jnp.logical_not(is_relayed(step)))
            def _():
                spread_copy(part, step, by_step).start()

            @pl.when(step == 0)
            def _():
                held[part][
                    plane // 2, pl.ds(pl.multiple_of(lax.rem(plane, 2) * PIECE, PIECE), PIECE)
                ] = by_head[part, by_step]

            return carry

        lax.fori_loop(0, RING, one, 0)
        for r in range(len(RELAYS)):
            spread_first(part, r, 0).wait_recv()
            spread_second(part, r).start()

    gathered = (keys, values)

    def chunk_copy(part, step):
        return remote(
            staged.at[part, step],
            gathered[part].at[chunk_rows(step)],
            c_send.at[part, step],
            c_recv.at[part, step],
            in_plane(plus(plane, step)),
        )

    def chunk_first(part, r):
        offset, between, _ = RELAYS[r]
        return remote(
            staged.at[part, offset],
            c_mid.at[part, r],
            c_send.at[part, offset],
            c_mid_recv.at[part, r],
            in_plane(plus(plane, between)),
        )

    def chunk_second(part, r):
        offset, _, on = RELAYS[r]
        return remote(
            c_mid.at[part, r],
            gathered[part].at[chunk_rows(offset)],
            c_mid_send.at[part, r],
            c_recv.at[part, offset],
            in_plane(plus(plane, on)),
        )

    def send_chunks(part):
        def take(step, carry):
            source = minus(plane, step)
            remote(
                by_head.at[part, 0],
                held_piece(part, source),
                b_send.at[part, step],
                b_recv.at[part, step],
                in_plane(source),
            ).wait_recv()
            return carry

        lax.fori_loop(1, RING, take, 0)

        for r in range(len(RELAYS)):
            offset = RELAYS[r][0]
            staged[part, offset] = held[part][wanted[offset]]
            chunk_first(part, r).start()

        def send(step, carry):
            @pl.when(jnp.logical_not(is_relayed(step)))
            def _():
                staged[part, step] = held[part][wanted[step]]
                chunk_copy(part, step).start()

            return carry

        lax.fori_loop(1, RING, send, 0)
        gathered[part][:CHUNK] = held[part][wanted[0]]

    def send_on_chunks(part):
        for r in range(len(RELAYS)):
            chunk_first(part, r).wait_recv()
            chunk_second(part, r).start()

    def find_prompt(step, carry):
        response = response_ref[2 * plus(plane, step) + half]
        end = jnp.int32(0)
        group = jnp.int32(0)
        for i in range(PROMPTS):
            end = end + counts_ref[i]
            group = group + (end <= response).astype(jnp.int32)
        wanted[step] = prompt_slot_ref[jnp.minimum(group, PROMPTS - 1)]
        return carry

    lax.fori_loop(0, RING, find_prompt, 0)

    def find_previous(step, carry):
        def look(other, found):
            same = (wanted[other] == wanted[step]) & (other < step)
            return jnp.where(same, other, found)

        previous[step] = lax.fori_loop(0, RING, look, jnp.int32(RING))
        return carry

    lax.fori_loop(0, RING, find_previous, 0)

    def find_last(prompt, carry):
        def look(other, found):
            return jnp.where(wanted[other] == prompt, other, found)

        last[prompt] = lax.fori_loop(0, RING, look, jnp.int32(RING))
        return carry

    lax.fori_loop(0, PROMPTS, find_last, 0)

    for load in loads:
        load.wait()
    position = lax.broadcasted_iota(jnp.int32, (RLEN, HD), 0)
    factor = jnp.where(position < len_ref[0], code_ref[0].astype(F32) / 8.0, 0.0)
    for j in range(HEADS):
        query = q_in[:, head_columns(j)]
        q_rows[head_rows(j)] = query
        q_cols[:, head_rows(j)] = jnp.transpose(query)
        cotangent = go_in[:, head_columns(j)].astype(F32) * factor
        cot_cols[:, head_rows(j)] = jnp.transpose(cotangent).astype(BF16)
    keys[PLEN:] = own_in[:, :HD]
    values[PLEN:] = own_in[:, HD:]
    running[RING] = jnp.zeros((CHUNK, HD), F32)
    dq_cols[...] = jnp.zeros_like(dq_cols)

    def block_rows(b):
        return pl.ds(pl.multiple_of(b * BLOCK, BLOCK), BLOCK)

    def score(b, own):
        block = keys[block_rows(b)]
        for j in range(HEADS):
            at = head_rows(j)
            part = dot(block, q_cols[:, at])
            if own:
                key_at = lax.broadcasted_iota(jnp.int32, (BLOCK, RLEN), 0)
                seen_from = lax.broadcasted_iota(jnp.int32, (BLOCK, RLEN), 1)
                part = jnp.where(key_at <= seen_from, part, -1e30)
            scores[b, :, at] = part
            high = fold(part, jnp.max)
            top[:, at] = high if own else jnp.maximum(top[:, at], high)

    score(BLOCKS, True)

    pass_on(0)
    send_chunks(0)
    pass_on(1)
    send_on_chunks(0)
    send_chunks(1)
    send_on_chunks(1)

    def arrive(part, b):
        def one(i, carry):
            step = b * PER_BLOCK + i

            @pl.when(step > 0)
            def _():
                chunk_copy(part, step).wait_recv()

            return carry

        lax.fori_loop(0, PER_BLOCK, one, 0)

    def score_block(b, carry):
        arrive(0, b)
        score(b, False)
        return carry

    lax.fori_loop(0, BLOCKS, score_block, 0)

    for j in range(HEADS):
        at = head_rows(j)
        highest = jnp.max(top[:, at], axis=0, keepdims=True)

        def weigh(b, total):
            weights = jnp.exp2((scores[b, :, at] - highest) * (SCALE * LOG2E))
            raw[b, :, at] = weights.astype(BF16)
            return total + fold(weights, jnp.sum)

        total = lax.fori_loop(0, BLOCKS + 1, weigh, jnp.zeros((8, RLEN), F32))
        over = 1.0 / jnp.sum(total, axis=0, keepdims=True)
        inverse[:, at] = jnp.broadcast_to(over, (8, RLEN))
        scaled = cot_cols[:, at].astype(F32) * over
        cot_scaled_cols[:, at] = scaled.astype(BF16)
        cot_scaled_rows[at] = jnp.transpose(scaled).astype(BF16)

    def return_copy(part, step):
        return remote(
            grads.at[part, step],
            terms.at[part, step],
            rc_send.at[part, step],
            rc_recv.at[part, step],
            in_plane(minus(plane, step)),
        )

    def return_first(part, r):
        offset, between, _ = RELAYS[r]
        step = opposite(offset)
        return remote(
            grads.at[part, step],
            rc_mid.at[part, r],
            rc_send.at[part, step],
            rc_mid_recv.at[part, r],
            in_plane(plus(plane, between)),
        )

    def return_second(part, r):
        offset, _, on = RELAYS[r]
        step = opposite(offset)
        return remote(
            rc_mid.at[part, r],
            terms.at[part, step],
            rc_mid_send.at[part, r],
            rc_recv.at[part, step],
            in_plane(plus(plane, on)),
        )

    def return_through(part):
        for r in range(len(RELAYS)):
            return_first(part, r).wait_recv()
            return_second(part, r).start()

    def send_back(part, b, block):
        for i in range(PER_BLOCK):
            grads[part, b * PER_BLOCK + i] = block[i * CHUNK : (i + 1) * CHUNK]

        def one(i, carry):
            step = b * PER_BLOCK + i

            for r in range(len(RELAYS)):

                @pl.when(step == opposite(RELAYS[r][0]))
                def _():
                    return_first(part, r).start()

            @pl.when((step > 0) & jnp.logical_not(is_relayed(step)))
            def _():
                return_copy(part, step).start()

            return carry

        lax.fori_loop(0, PER_BLOCK, one, 0)

    def value_part(b, first):
        block = values[block_rows(b)]
        for j in range(HEADS):
            at = head_rows(j)
            grad = dot(block, cot_scaled_cols[:, at])
            scores[b, :, at] = grad
            term = fold(grad * raw[b, :, at].astype(F32), jnp.sum)
            delta[:, at] = term if first else delta[:, at] + term
        return dot(raw[b], cot_scaled_rows[...]).astype(BF16)

    down_ref[:, HD:] = value_part(BLOCKS, True)

    def value_block(b, carry):
        arrive(1, b)
        send_back(1, b, value_part(b, False))
        return carry

    lax.fori_loop(0, BLOCKS, value_block, 0)
    for j in range(HEADS):
        at = head_rows(j)
        delta[:, at] = jnp.sum(delta[:, at], axis=0, keepdims=True) * inverse[:, at]

    def key_part(b):
        turned = jnp.transpose(keys[block_rows(b)])
        for j in range(HEADS):
            at = head_rows(j)
            weights = raw[b, :, at].astype(F32)
            shift = delta[0:1, at]
            change = (weights * (scores[b, :, at] - shift)).astype(BF16)
            raw[b, :, at] = change
            dq_cols[:, at] += dot(turned, change)
        return (dot(raw[b], q_rows[...]) * SCALE).astype(BF16)

    def key_block(i, carry):
        b = lax.rem(i + 3, BLOCKS)
        send_back(0, b, key_part(b))
        return carry

    lax.fori_loop(0, 2, key_block, 0)
    return_through(1)
    lax.fori_loop(2, 6, key_block, 0)

    def return_spread(part, step):
        target = plus(plane, step)
        piece = summed.at[
            part, target // 2, pl.ds(pl.multiple_of(lax.rem(target, 2) * PIECE, PIECE), PIECE)
        ]
        return remote(
            piece, spread.at[part, step], rb_send.at[part, step], rb_recv.at[part, step], in_plane(target)
        )

    def return_spread_first(part, r):
        offset, between, _ = RELAYS[r]
        target = plus(plane, offset)
        piece = summed.at[
            part, target // 2, pl.ds(pl.multiple_of(lax.rem(target, 2) * PIECE, PIECE), PIECE)
        ]
        return remote(
            piece,
            rb_mid.at[part, r],
            rb_send.at[part, offset],
            rb_mid_recv.at[part, r],
            in_plane(plus(plane, between)),
        )

    def return_spread_second(part, r):
        offset, _, on = RELAYS[r]
        return remote(
            rb_mid.at[part, r],
            spread.at[part, offset],
            rb_mid_send.at[part, r],
            rb_recv.at[part, offset],
            in_plane(plus(plane, on)),
        )

    def add_up(part):
        def take(step, carry):
            return_copy(part, step).wait_recv()
            return carry

        lax.fori_loop(1, RING, take, 0)
        terms[part, 0] = grads[part, 0]

        def add(step, carry):
            running[step] = running[previous[step]] + terms[part, step].astype(F32)
            return carry

        lax.fori_loop(0, RING, add, 0)

        def close(prompt, carry):
            summed[part, prompt] = running[last[prompt]].astype(BF16)
            return carry

        lax.fori_loop(0, PROMPTS, close, 0)

        for r in range(len(RELAYS)):
            return_spread_first(part, r).start()

        def send(step, carry):
            @pl.when(jnp.logical_not(is_relayed(step)))
            def _():
                return_spread(part, step).start()

            return carry

        lax.fori_loop(1, RING, send, 0)
        spread[part, 0] = summed[
            part, plane // 2, pl.ds(pl.multiple_of(lax.rem(plane, 2) * PIECE, PIECE), PIECE)
        ]

    def return_column(part, step, by_step):
        return remote(
            spread.at[part, by_step],
            parts.at[part, column],
            ra_send.at[part, step],
            ra_recv.at[part, step],
            in_column(around(column + step)),
        )

    def return_on(part):
        for r in range(len(RELAYS)):
            return_spread_first(part, r).wait_recv()
            return_spread_second(part, r).start()

        def one(by_step, carry):
            @pl.when(by_step > 0)
            def _():
                return_spread(part, by_step).wait_recv()

            step = around(minus(plane, by_step) - column)

            @pl.when(step != 0)
            def _():
                return_column(part, step, by_step).start()

            @pl.when(step == 0)
            def _():
                parts[part, column] = spread[part, by_step]

            return carry

        lax.fori_loop(0, RING, one, 0)

    add_up(1)
    lax.fori_loop(6, BLOCKS, key_block, 0)
    return_on(1)
    return_through(0)

    down_ref[:, :HD] = key_part(BLOCKS)
    for j in range(HEADS):
        dq_ref[:, head_columns(j)] = (jnp.transpose(dq_cols[:, head_rows(j)]) * SCALE).astype(BF16)

    add_up(0)
    return_on(0)

    for part in (1, 0):

        def collect(step, carry):
            source = around(column - step)
            remote(
                spread.at[part, 0],
                parts.at[part, source],
                ra_send.at[part, step],
                ra_recv.at[part, step],
                in_column(source),
            ).wait_recv()
            return carry

        lax.fori_loop(1, RING, collect, 0)
        for h in range(8):
            both = parts[part, h].astype(F32) + parts[part, 8 + h].astype(F32)
            dcache_ref[:, h * WIDTH + part * HD : h * WIDTH + (part + 1) * HD] = both.astype(BF16)

    for part in range(2):

        def finish(step, carry):
            column_copy(part, step).wait_send()
            spread_copy(part, step, 0).wait_send()
            chunk_copy(part, step).wait_send()
            return_copy(part, step).wait_send()
            return_spread(part, step).wait_send()
            return_column(part, step, 0).wait_send()
            return carry

        lax.fori_loop(1, RING, finish, 0)
        for r in range(len(RELAYS)):
            spread_second(part, r).wait_send()
            chunk_second(part, r).wait_send()
            return_second(part, r).wait_send()
            return_spread_second(part, r).wait_send()


def local(
    queries, resp_kv, prompt_cache, grad_out, group_counts, prompt_slot, slot_response, resp_len, weight_code
):
    vmem = pl.BlockSpec(memory_space=pltpu.VMEM)
    smem = pl.BlockSpec(memory_space=pltpu.SMEM)
    hbm = pl.BlockSpec(memory_space=pltpu.HBM)
    scratch = [
        pltpu.SMEM((RING,), jnp.int32),
        pltpu.SMEM((RING,), jnp.int32),
        pltpu.SMEM((PROMPTS,), jnp.int32),
        pltpu.VMEM((RLEN, HEADS * HD), BF16),
        pltpu.VMEM((RLEN, HEADS * HD), BF16),
        pltpu.VMEM((RLEN, WIDTH), BF16),
        pltpu.VMEM((2, RING, PIECE, HD), BF16),
        pltpu.VMEM((PROMPTS, CHUNK, HD), BF16),
        pltpu.VMEM((PROMPTS, CHUNK, HD), BF16),
        pltpu.VMEM((2, RING, CHUNK, HD), BF16),
        pltpu.VMEM((KEYS, HD), BF16),
        pltpu.VMEM((KEYS, HD), BF16),
        pltpu.VMEM((ROWS, HD), BF16),
        pltpu.VMEM((HD, ROWS), BF16),
        pltpu.VMEM((HD, ROWS), BF16),
        pltpu.VMEM((HD, ROWS), BF16),
        pltpu.VMEM((ROWS, HD), BF16),
        pltpu.VMEM((BLOCKS + 1, BLOCK, ROWS), F32),
        pltpu.VMEM((BLOCKS + 1, BLOCK, ROWS), BF16),
        pltpu.VMEM((8, ROWS), F32),
        pltpu.VMEM((8, ROWS), F32),
        pltpu.VMEM((8, ROWS), F32),
        pltpu.VMEM((HD, ROWS), F32),
        pltpu.VMEM((2, RING, CHUNK, HD), BF16),
        pltpu.VMEM((2, RING, CHUNK, HD), BF16),
        pltpu.VMEM((RING + 1, CHUNK, HD), F32),
        pltpu.VMEM((2, PROMPTS, CHUNK, HD), BF16),
        pltpu.VMEM((2, RING, PIECE, HD), BF16),
        pltpu.VMEM((2, RING, PIECE, HD), BF16),
        pltpu.VMEM((2, len(RELAYS), PIECE, HD), BF16),
        pltpu.VMEM((2, len(RELAYS), CHUNK, HD), BF16),
        pltpu.VMEM((2, len(RELAYS), CHUNK, HD), BF16),
        pltpu.VMEM((2, len(RELAYS), PIECE, HD), BF16),
        pltpu.SemaphoreType.DMA((5,)),
    ] + [pltpu.SemaphoreType.DMA((2, RING))] * 12 + [pltpu.SemaphoreType.DMA((2, len(RELAYS)))] * 8
    products = 5 * ROWS * KEYS * HD
    return pl.pallas_call(
        kernel,
        out_shape=[
            jax.ShapeDtypeStruct(queries.shape, BF16),
            jax.ShapeDtypeStruct(resp_kv.shape, BF16),
            jax.ShapeDtypeStruct(prompt_cache.shape, BF16),
        ],
        in_specs=[smem] * 5 + [hbm] * 4,
        out_specs=[vmem] * 3,
        scratch_shapes=scratch,
        compiler_params=pltpu.CompilerParams(
            collective_id=0, has_side_effects=True, vmem_limit_bytes=VMEM_LIMIT
        ),
        cost_estimate=pl.CostEstimate(flops=2 * products, bytes_accessed=3 << 20, transcendentals=ROWS * KEYS),
    )(
        group_counts,
        prompt_slot,
        slot_response,
        resp_len,
        weight_code,
        queries,
        resp_kv,
        prompt_cache,
        grad_out,
    )


def solution(mesh):
    placed = (
        P("seq", "head"),
        P("seq", "head"),
        P(("seq", "head"), None),
        P("seq", "head"),
        P(),
        P(),
        P(),
        P("seq"),
        P("seq"),
    )
    return jax.shard_map(
        local,
        mesh=mesh,
        in_specs=placed,
        out_specs=(P("seq", "head"), P("seq", "head"), P(("seq", "head"), None)),
        check_vma=False,
    )
```

```python
import math

import jax
import jax.numpy as jnp
from jax import lax
from jax.experimental import pallas as pl
from jax.experimental.pallas import tpu as pltpu
from jax.sharding import PartitionSpec as P

HD = 128
PLEN = 2048
RLEN = 256
HEADS = 8
PROMPTS = 8
RING = 16
CHUNK = PLEN // RING
PIECE = CHUNK // 2
BLOCK = 256
BLOCKS = PLEN // BLOCK
PER_BLOCK = BLOCK // CHUNK
ROWS = HEADS * RLEN
KEYS = PLEN + RLEN
WIDTH = 2 * HD
SCALE = HD**-0.5
LOG2E = math.log2(math.e)
MESH = pl.DeviceIdType.MESH
VMEM_LIMIT = 60 * 1024 * 1024
NN = (((1,), (0,)), ((), ()))
F32 = jnp.float32
BF16 = jnp.bfloat16


OFFSETS = (10, 6, 9, 14, 11, 5, 15, 7, 13, 2, 8, 1, 4, 3, 12)


def around(index):
    return lax.rem(index + 2 * RING, RING)


def plus(plane, offset):
    return lax.rem(plane // 4 + offset // 4, 4) * 4 + lax.rem(plane + lax.rem(offset, 4), 4)


def minus(plane, offset):
    return lax.rem(plane // 4 + 4 - offset // 4, 4) * 4 + lax.rem(plane + 4 - lax.rem(offset, 4), 4)


def column_step(i):
    return 8 + (i // 2) * (1 - 2 * lax.rem(i, 2))


def head_rows(j):
    return slice(j * RLEN, (j + 1) * RLEN)


def head_columns(j):
    return slice(j * HD, (j + 1) * HD)


def chunk_rows(step):
    return pl.ds(pl.multiple_of(step * CHUNK, CHUNK), CHUNK)


def fold(values, op):
    return op(values.reshape(values.shape[0] // 8, 8, values.shape[1]), axis=0)


def dot(a, b):
    return lax.dot_general(a, b, NN, preferred_element_type=F32)


def kernel(
    counts_ref,
    prompt_slot_ref,
    response_ref,
    len_ref,
    code_ref,
    q_ref,
    own_ref,
    cache_ref,
    go_ref,
    dq_ref,
    down_ref,
    parts,
    wanted,
    previous,
    last,
    q_in,
    go_in,
    own_in,
    by_head,
    held_keys,
    held_values,
    staged,
    keys,
    values,
    q_rows,
    q_cols,
    cot_cols,
    cot_scaled_cols,
    cot_scaled_rows,
    scores,
    raw,
    top,
    delta,
    inverse,
    dq_cols,
    grads,
    terms,
    running,
    summed,
    spread,
    in_sem,
    a_send,
    a_recv,
    b_send,
    b_recv,
    c_send,
    c_recv,
    rc_send,
    rc_recv,
    rb_send,
    rb_recv,
    ra_send,
    ra_recv,
):
    seq = lax.axis_index("seq")
    head = lax.axis_index("head")
    plane = seq // 2
    half = lax.rem(seq, 2)
    column = half * 8 + head

    def in_plane(other):
        return {"seq": 2 * other + half, "head": head}

    def in_column(other):
        return {"seq": 2 * plane + other // 8, "head": lax.rem(other, 8)}

    def remote(src, dst, send_sem, recv_sem, device):
        return pltpu.make_async_remote_copy(
            src_ref=src, dst_ref=dst, send_sem=send_sem, recv_sem=recv_sem, device_id=device, device_id_type=MESH
        )

    def all_at_once(buffer, sem):
        pltpu.make_async_copy(buffer.at[pl.ds(1, RING - 1)], buffer.at[pl.ds(1, RING - 1)], sem).wait()

    loads = [
        pltpu.make_async_copy(q_ref, q_in, in_sem.at[0]),
        pltpu.make_async_copy(go_ref, go_in, in_sem.at[1]),
        pltpu.make_async_copy(own_ref, own_in, in_sem.at[2]),
    ]
    for part in range(2):
        at = pl.ds(pl.multiple_of(head * WIDTH + part * HD, HD), HD)
        loads.append(pltpu.make_async_copy(cache_ref.at[:, at], by_head.at[part, 0], in_sem.at[3 + part]))
    for load in loads:
        load.start()

    barrier = pltpu.get_barrier_semaphore()

    def greet(step, carry):
        pl.semaphore_signal(barrier, inc=1, device_id=in_column(around(column + step)), device_id_type=MESH)
        pl.semaphore_signal(barrier, inc=1, device_id=in_plane(plus(plane, step)), device_id_type=MESH)
        return carry

    lax.fori_loop(1, RING, greet, 0)
    pl.semaphore_wait(barrier, 2 * (RING - 1))

    def cache_part(part, target):
        at = lax.rem(target, 8) * WIDTH + part * HD
        return cache_ref.at[:, pl.ds(pl.multiple_of(at, HD), HD)]

    def column_copy(part, step):
        target = around(column + step)
        return remote(
            cache_part(part, target),
            by_head.at[part, step],
            a_send.at[part],
            a_recv.at[part, step],
            in_column(target),
        )

    for part in range(2):

        def start_column(i, carry):
            column_copy(part, column_step(i)).start()
            return carry

        lax.fori_loop(1, RING, start_column, 0)

    held = (held_keys, held_values)

    def held_piece(part, source):
        return held[part].at[source // 2, pl.ds(pl.multiple_of(lax.rem(source, 2) * PIECE, PIECE), PIECE)]

    def spread_copy(part, step, by_step):
        return remote(
            by_head.at[part, by_step],
            held_piece(part, plane),
            b_send.at[part],
            b_recv.at[part, 0],
            in_plane(plus(plane, step)),
        )

    def pass_on(part):
        def one(i, carry):
            by_step = column_step(i) * jnp.minimum(i, 1)

            @pl.when(i > 0)
            def _():
                column_copy(part, by_step).wait_recv()

            target = around(column - by_step)
            step = lax.rem(target // 4 - plane // 4 + 4, 4) * 4 + lax.rem(target - plane + RING, 4)

            @pl.when(step != 0)
            def _():
                spread_copy(part, step, by_step).start()

            @pl.when(step == 0)
            def _():
                held[part][
                    plane // 2, pl.ds(pl.multiple_of(lax.rem(plane, 2) * PIECE, PIECE), PIECE)
                ] = by_head[part, by_step]

            return carry

        lax.fori_loop(0, RING, one, 0)

    gathered = (keys, values)

    def chunk_copy(part, step):
        return remote(
            staged.at[part, step],
            gathered[part].at[chunk_rows(step)],
            c_send.at[part],
            c_recv.at[part, step],
            in_plane(plus(plane, step)),
        )

    def send_chunks(part):
        all_at_once(by_head.at[part], b_recv.at[part, 0])
        for step in OFFSETS:
            staged[part, step] = held[part][wanted[step]]
            chunk_copy(part, step).start()
        gathered[part][:CHUNK] = held[part][wanted[0]]

    ends = []
    for i in range(PROMPTS):
        ends.append(counts_ref[i] + (ends[-1] if ends else 0))
    prompts = []
    for step in range(RING):
        response = response_ref[2 * plus(plane, step) + half]
        group = jnp.int32(0)
        for end in ends[:-1]:
            group = group + (end <= response).astype(jnp.int32)
        prompts.append(prompt_slot_ref[group])
        wanted[step] = prompts[-1]
    for step in range(RING):
        found = jnp.int32(RING)
        for other in range(step):
            found = jnp.where(prompts[other] == prompts[step], other, found)
        previous[step] = found
    for prompt in range(PROMPTS):
        found = jnp.int32(RING)
        for step in range(RING):
            found = jnp.where(prompts[step] == prompt, step, found)
        last[prompt] = found

    for load in loads:
        load.wait()
    position = lax.broadcasted_iota(jnp.int32, (RLEN, HD), 0)
    factor = jnp.where(position < len_ref[0], code_ref[0].astype(F32) / 8.0, 0.0)
    for j in range(HEADS):
        query = q_in[:, head_columns(j)]
        q_rows[head_rows(j)] = query
        q_cols[:, head_rows(j)] = jnp.transpose(query)
        cotangent = go_in[:, head_columns(j)].astype(F32) * factor
        cot_cols[:, head_rows(j)] = jnp.transpose(cotangent).astype(BF16)
    keys[PLEN:] = own_in[:, :HD]
    values[PLEN:] = own_in[:, HD:]
    running[RING] = jnp.zeros((CHUNK, HD), F32)
    dq_cols[...] = jnp.zeros_like(dq_cols)

    def block_rows(b):
        return pl.ds(pl.multiple_of(b * BLOCK, BLOCK), BLOCK)

    def score(b, own):
        block = keys[block_rows(b)]
        for j in range(HEADS):
            at = head_rows(j)
            part = dot(block, q_cols[:, at])
            if own:
                key_at = lax.broadcasted_iota(jnp.int32, (BLOCK, RLEN), 0)
                seen_from = lax.broadcasted_iota(jnp.int32, (BLOCK, RLEN), 1)
                part = jnp.where(key_at <= seen_from, part, -1e30)
            scores[b, :, at] = part
            high = fold(part, jnp.max)
            top[:, at] = high if own else jnp.maximum(top[:, at], high)

    pass_on(0)
    send_chunks(0)
    pass_on(1)
    score(BLOCKS, True)
    send_chunks(1)

    def arrive(part, b):
        def one(i, carry):
            step = b * PER_BLOCK + i

            @pl.when(step > 0)
            def _():
                chunk_copy(part, step).wait_recv()

            return carry

        lax.fori_loop(0, PER_BLOCK, one, 0)

    def score_block(b, carry):
        arrive(0, b)
        score(b, False)
        return carry

    lax.fori_loop(0, BLOCKS, score_block, 0)

    for j in range(HEADS):
        at = head_rows(j)
        highest = jnp.max(top[:, at], axis=0, keepdims=True)

        def weigh(b, total):
            weights = jnp.exp2((scores[b, :, at] - highest) * (SCALE * LOG2E))
            raw[b, :, at] = weights.astype(BF16)
            return total + fold(weights, jnp.sum)

        total = lax.fori_loop(0, BLOCKS + 1, weigh, jnp.zeros((8, RLEN), F32))
        over = 1.0 / jnp.sum(total, axis=0, keepdims=True)
        inverse[:, at] = jnp.broadcast_to(over, (8, RLEN))
        scaled = cot_cols[:, at].astype(F32) * over
        cot_scaled_cols[:, at] = scaled.astype(BF16)
        cot_scaled_rows[at] = jnp.transpose(scaled).astype(BF16)

    def return_copy(part, step):
        return remote(
            grads.at[part, step],
            terms.at[part, step],
            rc_send.at[part],
            rc_recv.at[part, 0],
            in_plane(minus(plane, step)),
        )

    def send_back(part, b, block):
        for i in range(PER_BLOCK):
            grads[part, b * PER_BLOCK + i] = block[i * CHUNK : (i + 1) * CHUNK]

        def one(i, carry):
            step = b * PER_BLOCK + i

            @pl.when(step > 0)
            def _():
                return_copy(part, step).start()

            return carry

        lax.fori_loop(0, PER_BLOCK, one, 0)

    def value_part(b, first):
        block = values[block_rows(b)]
        for j in range(HEADS):
            at = head_rows(j)
            grad = dot(block, cot_scaled_cols[:, at])
            scores[b, :, at] = grad
            term = fold(grad * raw[b, :, at].astype(F32), jnp.sum)
            delta[:, at] = term if first else delta[:, at] + term
        return dot(raw[b], cot_scaled_rows[...]).astype(BF16)

    down_ref[:, HD:] = value_part(BLOCKS, True)

    def value_block(b, carry):
        arrive(1, b)
        send_back(1, b, value_part(b, False))
        return carry

    lax.fori_loop(0, BLOCKS, value_block, 0)
    for j in range(HEADS):
        at = head_rows(j)
        delta[:, at] = jnp.sum(delta[:, at], axis=0, keepdims=True) * inverse[:, at]

    def key_part(b):
        turned = jnp.transpose(keys[block_rows(b)])
        for j in range(HEADS):
            at = head_rows(j)
            weights = raw[b, :, at].astype(F32)
            shift = delta[0:1, at]
            change = (weights * (scores[b, :, at] - shift)).astype(BF16)
            raw[b, :, at] = change
            dq_cols[:, at] += dot(turned, change)
        return (dot(raw[b], q_rows[...]) * SCALE).astype(BF16)

    def key_block(b, carry):
        send_back(0, b, key_part(b))
        return carry

    lax.fori_loop(0, 6, key_block, 0)

    def return_spread(part, step):
        target = plus(plane, step)
        piece = summed.at[
            part, target // 2, pl.ds(pl.multiple_of(lax.rem(target, 2) * PIECE, PIECE), PIECE)
        ]
        return remote(
            piece, spread.at[part, step], rb_send.at[part], rb_recv.at[part, step], in_plane(target)
        )

    def add_up(part):
        all_at_once(grads.at[part], rc_recv.at[part, 0])
        terms[part, 0] = grads[part, 0]

        def add(step, carry):
            running[step] = running[previous[step]] + terms[part, step].astype(F32)
            return carry

        lax.fori_loop(0, RING, add, 0)

        def close(prompt, carry):
            summed[part, prompt] = running[last[prompt]].astype(BF16)
            return carry

        lax.fori_loop(0, PROMPTS, close, 0)

        for step in OFFSETS:
            return_spread(part, step).start()
        spread[part, 0] = summed[
            part, plane // 2, pl.ds(pl.multiple_of(lax.rem(plane, 2) * PIECE, PIECE), PIECE)
        ]

    def return_column(part, step, by_step):
        return remote(
            spread.at[part, by_step],
            parts.at[part, column],
            ra_send.at[part],
            ra_recv.at[part, 0],
            in_column(around(column + step)),
        )

    def return_on(part):
        for by_step in (0,) + OFFSETS:
            if by_step:
                return_spread(part, by_step).wait_recv()
            step = around(minus(plane, by_step) - column)

            @pl.when(step != 0)
            def _():
                return_column(part, step, by_step).start()

            @pl.when(step == 0)
            def _():
                parts[part, column] = spread[part, by_step]

    add_up(1)
    lax.fori_loop(6, BLOCKS, key_block, 0)

    down_ref[:, :HD] = key_part(BLOCKS)
    return_on(1)
    for j in range(HEADS):
        dq_ref[:, head_columns(j)] = (jnp.transpose(dq_cols[:, head_rows(j)]) * SCALE).astype(BF16)
    add_up(0)
    return_on(0)

    for part in range(2):
        all_at_once(by_head.at[part], a_send.at[part])
        all_at_once(by_head.at[part], b_send.at[part])
        all_at_once(staged.at[part], c_send.at[part])
        all_at_once(grads.at[part], rc_send.at[part])
        all_at_once(spread.at[part], rb_send.at[part])
        all_at_once(spread.at[part], ra_send.at[part])
        all_at_once(spread.at[part], ra_recv.at[part, 0])


def finish_kernel(dq_ref, down_ref, parts_ref, dq_out, down_out, dcache_out, parts, total, sems):
    gets = pltpu.make_async_copy(parts_ref, parts, sems.at[0])
    gets.start()
    passed = [
        pltpu.make_async_copy(dq_ref, dq_out, sems.at[1]),
        pltpu.make_async_copy(down_ref, down_out, sems.at[2]),
    ]
    for copy in passed:
        copy.start()
    gets.wait()
    for h in range(8):
        for part in range(2):
            both = parts[part, h].astype(F32) + parts[part, 8 + h].astype(F32)
            total[:, h * WIDTH + part * HD : h * WIDTH + (part + 1) * HD] = both.astype(BF16)
    put = pltpu.make_async_copy(total, dcache_out, sems.at[3])
    put.start()
    for copy in passed:
        copy.wait()
    put.wait()


def local(
    queries, resp_kv, prompt_cache, grad_out, group_counts, prompt_slot, slot_response, resp_len, weight_code
):
    vmem = pl.BlockSpec(memory_space=pltpu.VMEM)
    smem = pl.BlockSpec(memory_space=pltpu.SMEM)
    hbm = pl.BlockSpec(memory_space=pltpu.HBM)
    scratch = [
        pltpu.SMEM((RING,), jnp.int32),
        pltpu.SMEM((RING,), jnp.int32),
        pltpu.SMEM((PROMPTS,), jnp.int32),
        pltpu.VMEM((RLEN, HEADS * HD), BF16),
        pltpu.VMEM((RLEN, HEADS * HD), BF16),
        pltpu.VMEM((RLEN, WIDTH), BF16),
        pltpu.VMEM((2, RING, PIECE, HD), BF16),
        pltpu.VMEM((PROMPTS, CHUNK, HD), BF16),
        pltpu.VMEM((PROMPTS, CHUNK, HD), BF16),
        pltpu.VMEM((2, RING, CHUNK, HD), BF16),
        pltpu.VMEM((KEYS, HD), BF16),
        pltpu.VMEM((KEYS, HD), BF16),
        pltpu.VMEM((ROWS, HD), BF16),
        pltpu.VMEM((HD, ROWS), BF16),
        pltpu.VMEM((HD, ROWS), BF16),
        pltpu.VMEM((HD, ROWS), BF16),
        pltpu.VMEM((ROWS, HD), BF16),
        pltpu.VMEM((BLOCKS + 1, BLOCK, ROWS), F32),
        pltpu.VMEM((BLOCKS + 1, BLOCK, ROWS), BF16),
        pltpu.VMEM((8, ROWS), F32),
        pltpu.VMEM((8, ROWS), F32),
        pltpu.VMEM((8, ROWS), F32),
        pltpu.VMEM((HD, ROWS), F32),
        pltpu.VMEM((2, RING, CHUNK, HD), BF16),
        pltpu.VMEM((2, RING, CHUNK, HD), BF16),
        pltpu.VMEM((RING + 1, CHUNK, HD), F32),
        pltpu.VMEM((2, PROMPTS, CHUNK, HD), BF16),
        pltpu.VMEM((2, RING, PIECE, HD), BF16),
        pltpu.SemaphoreType.DMA((5,)),
    ] + [pltpu.SemaphoreType.DMA((2,)), pltpu.SemaphoreType.DMA((2, RING))] * 6
    products = 5 * ROWS * KEYS * HD
    dq, down, parts = pl.pallas_call(
        kernel,
        out_shape=[
            jax.ShapeDtypeStruct(queries.shape, BF16),
            jax.ShapeDtypeStruct(resp_kv.shape, BF16),
            jax.ShapeDtypeStruct((2, RING, PIECE, HD), BF16),
        ],
        in_specs=[smem] * 5 + [hbm] * 4,
        out_specs=[vmem] * 3,
        scratch_shapes=scratch,
        compiler_params=pltpu.CompilerParams(
            collective_id=0, has_side_effects=True, vmem_limit_bytes=VMEM_LIMIT
        ),
        cost_estimate=pl.CostEstimate(flops=2 * products, bytes_accessed=3 << 20, transcendentals=ROWS * KEYS),
    )(
        group_counts,
        prompt_slot,
        slot_response,
        resp_len,
        weight_code,
        queries,
        resp_kv,
        prompt_cache,
        grad_out,
    )
    return pl.pallas_call(
        finish_kernel,
        out_shape=[
            jax.ShapeDtypeStruct(queries.shape, BF16),
            jax.ShapeDtypeStruct(resp_kv.shape, BF16),
            jax.ShapeDtypeStruct(prompt_cache.shape, BF16),
        ],
        in_specs=[hbm] * 3,
        out_specs=[hbm] * 3,
        scratch_shapes=[
            pltpu.VMEM((2, RING, PIECE, HD), BF16),
            pltpu.VMEM(prompt_cache.shape, BF16),
            pltpu.SemaphoreType.DMA((4,)),
        ],
        compiler_params=pltpu.CompilerParams(vmem_limit_bytes=VMEM_LIMIT),
    )(dq, down, parts)


def solution(mesh):
    placed = (
        P("seq", "head"),
        P("seq", "head"),
        P(("seq", "head"), None),
        P("seq", "head"),
        P(),
        P(),
        P(),
        P("seq"),
        P("seq"),
    )
    return jax.shard_map(
        local,
        mesh=mesh,
        in_specs=placed,
        out_specs=(P("seq", "head"), P("seq", "head"), P(("seq", "head"), None)),
        check_vma=False,
    )
```

```python
import math

import jax
import jax.numpy as jnp
from jax import lax
from jax.experimental import pallas as pl
from jax.experimental.pallas import tpu as pltpu
from jax.sharding import PartitionSpec as P

HD = 128
PLEN = 2048
RLEN = 256
HEADS = 8
PROMPTS = 8
RING = 16
CHUNK = PLEN // RING
PIECE = CHUNK // 2
BLOCK = 256
BLOCKS = PLEN // BLOCK
PER_BLOCK = BLOCK // CHUNK
ROWS = HEADS * RLEN
KEYS = PLEN + RLEN
WIDTH = 2 * HD
SCALE = HD**-0.5
LOG2E = math.log2(math.e)
MESH = pl.DeviceIdType.MESH
VMEM_LIMIT = 60 * 1024 * 1024
NN = (((1,), (0,)), ((), ()))
F32 = jnp.float32
BF16 = jnp.bfloat16


OFFSETS = (10, 6, 9, 14, 11, 5, 15, 7, 13, 2, 8, 1, 4, 3, 12)


def around(index):
    return lax.rem(index + 2 * RING, RING)


def plus(plane, offset):
    return lax.rem(plane // 4 + offset // 4, 4) * 4 + lax.rem(plane + lax.rem(offset, 4), 4)


def minus(plane, offset):
    return lax.rem(plane // 4 + 4 - offset // 4, 4) * 4 + lax.rem(plane + 4 - lax.rem(offset, 4), 4)


def column_step(i):
    return 8 + (i // 2) * (1 - 2 * lax.rem(i, 2))


def head_rows(j):
    return slice(j * RLEN, (j + 1) * RLEN)


def head_columns(j):
    return slice(j * HD, (j + 1) * HD)


def chunk_rows(step):
    return pl.ds(pl.multiple_of(step * CHUNK, CHUNK), CHUNK)


def fold(values, op):
    return op(values.reshape(values.shape[0] // 8, 8, values.shape[1]), axis=0)


def dot(a, b):
    return lax.dot_general(a, b, NN, preferred_element_type=F32)


def kernel(
    counts_ref,
    prompt_slot_ref,
    response_ref,
    len_ref,
    code_ref,
    q_ref,
    own_ref,
    cache_ref,
    go_ref,
    dq_ref,
    down_ref,
    parts,
    wanted,
    previous,
    last,
    q_in,
    go_in,
    own_in,
    by_head,
    held,
    staged,
    keys,
    values,
    q_rows,
    q_cols,
    cot_cols,
    cot_scaled_cols,
    cot_scaled_rows,
    scores,
    raw,
    top,
    delta,
    inverse,
    dq_cols,
    grads,
    terms,
    running,
    summed,
    spread,
    in_sem,
    a_send,
    a_recv,
    b_send,
    b_recv,
    c_send,
    c_recv,
    rc_send,
    rc_recv,
    rb_send,
    rb_recv,
    ra_send,
    ra_recv,
):
    seq = lax.axis_index("seq")
    head = lax.axis_index("head")
    plane = seq // 2
    half = lax.rem(seq, 2)
    column = half * 8 + head

    def in_plane(other):
        return {"seq": 2 * other + half, "head": head}

    def in_column(other):
        return {"seq": 2 * plane + other // 8, "head": lax.rem(other, 8)}

    def remote(src, dst, send_sem, recv_sem, device):
        return pltpu.make_async_remote_copy(
            src_ref=src, dst_ref=dst, send_sem=send_sem, recv_sem=recv_sem, device_id=device, device_id_type=MESH
        )

    def all_at_once(buffer, sem):
        pltpu.make_async_copy(buffer.at[pl.ds(1, RING - 1)], buffer.at[pl.ds(1, RING - 1)], sem).wait()

    loads = [
        pltpu.make_async_copy(q_ref, q_in, in_sem.at[0]),
        pltpu.make_async_copy(go_ref, go_in, in_sem.at[1]),
        pltpu.make_async_copy(own_ref, own_in, in_sem.at[2]),
    ]
    loads.append(
        pltpu.make_async_copy(
            cache_ref.at[:, pl.ds(pl.multiple_of(head * WIDTH, WIDTH), WIDTH)], by_head.at[0], in_sem.at[3]
        )
    )
    for load in loads:
        load.start()

    barrier = pltpu.get_barrier_semaphore()

    def greet(step, carry):
        pl.semaphore_signal(barrier, inc=1, device_id=in_column(around(column + step)), device_id_type=MESH)
        pl.semaphore_signal(barrier, inc=1, device_id=in_plane(plus(plane, step)), device_id_type=MESH)
        return carry

    lax.fori_loop(1, RING, greet, 0)
    pl.semaphore_wait(barrier, 2 * (RING - 1))

    def column_copy(step):
        target = around(column + step)
        at = pl.ds(pl.multiple_of(lax.rem(target, 8) * WIDTH, WIDTH), WIDTH)
        return remote(cache_ref.at[:, at], by_head.at[step], a_send, a_recv.at[step], in_column(target))

    def start_column(i, carry):
        column_copy(column_step(i)).start()
        return carry

    lax.fori_loop(1, RING, start_column, 0)

    held_rows = pl.ds(pl.multiple_of(lax.rem(plane, 2) * PIECE, PIECE), PIECE)

    def spread_copy(step, by_step):
        return remote(
            by_head.at[by_step], held.at[plane // 2, held_rows], b_send, b_recv, in_plane(plus(plane, step))
        )

    def pass_on():
        def one(i, carry):
            by_step = column_step(i) * jnp.minimum(i, 1)

            @pl.when(i > 0)
            def _():
                column_copy(by_step).wait_recv()

            target = around(column - by_step)
            step = lax.rem(target // 4 - plane // 4 + 4, 4) * 4 + lax.rem(target - plane + RING, 4)

            @pl.when(step != 0)
            def _():
                spread_copy(step, by_step).start()

            @pl.when(step == 0)
            def _():
                held[plane // 2, held_rows] = by_head[by_step]

            return carry

        lax.fori_loop(0, RING, one, 0)

    gathered = (keys, values)

    def chunk_copy(part, step):
        return remote(
            staged.at[part, step],
            gathered[part].at[chunk_rows(step)],
            c_send.at[part],
            c_recv.at[part, step],
            in_plane(plus(plane, step)),
        )

    def send_chunks(part):
        at = slice(part * HD, (part + 1) * HD)
        for step in OFFSETS:
            staged[part, step] = held[wanted[step], :, at]
            chunk_copy(part, step).start()
        gathered[part][:CHUNK] = held[wanted[0], :, at]

    ends = []
    for i in range(PROMPTS):
        ends.append(counts_ref[i] + (ends[-1] if ends else 0))
    prompts = []
    for step in range(RING):
        response = response_ref[2 * plus(plane, step) + half]
        group = jnp.int32(0)
        for end in ends[:-1]:
            group = group + (end <= response).astype(jnp.int32)
        prompts.append(prompt_slot_ref[group])
        wanted[step] = prompts[-1]
    for step in range(RING):
        found = jnp.int32(RING)
        for other in range(step):
            found = jnp.where(prompts[other] == prompts[step], other, found)
        previous[step] = found
    for prompt in range(PROMPTS):
        found = jnp.int32(RING)
        for step in range(RING):
            found = jnp.where(prompts[step] == prompt, step, found)
        last[prompt] = found

    for load in loads:
        load.wait()
    position = lax.broadcasted_iota(jnp.int32, (RLEN, HD), 0)
    factor = jnp.where(position < len_ref[0], code_ref[0].astype(F32) / 8.0, 0.0)
    for j in range(HEADS):
        query = q_in[:, head_columns(j)]
        q_rows[head_rows(j)] = query
        q_cols[:, head_rows(j)] = jnp.transpose(query)
        cotangent = go_in[:, head_columns(j)].astype(F32) * factor
        cot_cols[:, head_rows(j)] = jnp.transpose(cotangent).astype(BF16)
    keys[PLEN:] = own_in[:, :HD]
    values[PLEN:] = own_in[:, HD:]
    running[RING] = jnp.zeros((CHUNK, HD), F32)
    dq_cols[...] = jnp.zeros_like(dq_cols)

    def block_rows(b):
        return pl.ds(pl.multiple_of(b * BLOCK, BLOCK), BLOCK)

    def score(b, own):
        block = keys[block_rows(b)]
        for j in range(HEADS):
            at = head_rows(j)
            part = dot(block, q_cols[:, at])
            if own:
                key_at = lax.broadcasted_iota(jnp.int32, (BLOCK, RLEN), 0)
                seen_from = lax.broadcasted_iota(jnp.int32, (BLOCK, RLEN), 1)
                part = jnp.where(key_at <= seen_from, part, -1e30)
            scores[b, :, at] = part
            high = fold(part, jnp.max)
            top[:, at] = high if own else jnp.maximum(top[:, at], high)

    pass_on()
    all_at_once(by_head, b_recv)
    send_chunks(0)
    send_chunks(1)
    score(BLOCKS, True)

    def arrive(part, b):
        def one(i, carry):
            step = b * PER_BLOCK + i

            @pl.when(step > 0)
            def _():
                chunk_copy(part, step).wait_recv()

            return carry

        lax.fori_loop(0, PER_BLOCK, one, 0)

    def score_block(b, carry):
        arrive(0, b)
        score(b, False)
        return carry

    lax.fori_loop(0, BLOCKS, score_block, 0)

    for j in range(HEADS):
        at = head_rows(j)
        highest = jnp.max(top[:, at], axis=0, keepdims=True)

        def weigh(b, total):
            weights = jnp.exp2((scores[b, :, at] - highest) * (SCALE * LOG2E))
            raw[b, :, at] = weights.astype(BF16)
            return total + fold(weights, jnp.sum)

        total = lax.fori_loop(0, BLOCKS + 1, weigh, jnp.zeros((8, RLEN), F32))
        over = 1.0 / jnp.sum(total, axis=0, keepdims=True)
        inverse[:, at] = jnp.broadcast_to(over, (8, RLEN))
        scaled = cot_cols[:, at].astype(F32) * over
        cot_scaled_cols[:, at] = scaled.astype(BF16)
        cot_scaled_rows[at] = jnp.transpose(scaled).astype(BF16)

    def return_copy(part, step):
        return remote(
            grads.at[part, step],
            terms.at[part, step],
            rc_send.at[part],
            rc_recv.at[part, 0],
            in_plane(minus(plane, step)),
        )

    def send_back(part, b, block):
        for i in range(PER_BLOCK):
            grads[part, b * PER_BLOCK + i] = block[i * CHUNK : (i + 1) * CHUNK]

        def one(i, carry):
            step = b * PER_BLOCK + i

            @pl.when(step > 0)
            def _():
                return_copy(part, step).start()

            return carry

        lax.fori_loop(0, PER_BLOCK, one, 0)

    def value_part(b, first):
        block = values[block_rows(b)]
        for j in range(HEADS):
            at = head_rows(j)
            grad = dot(block, cot_scaled_cols[:, at])
            scores[b, :, at] = grad
            term = fold(grad * raw[b, :, at].astype(F32), jnp.sum)
            delta[:, at] = term if first else delta[:, at] + term
        return dot(raw[b], cot_scaled_rows[...]).astype(BF16)

    down_ref[:, HD:] = value_part(BLOCKS, True)

    def value_block(b, carry):
        arrive(1, b)
        send_back(1, b, value_part(b, False))
        return carry

    lax.fori_loop(0, BLOCKS, value_block, 0)
    for j in range(HEADS):
        at = head_rows(j)
        delta[:, at] = jnp.sum(delta[:, at], axis=0, keepdims=True) * inverse[:, at]

    def key_part(b):
        turned = jnp.transpose(keys[block_rows(b)])
        for j in range(HEADS):
            at = head_rows(j)
            weights = raw[b, :, at].astype(F32)
            shift = delta[0:1, at]
            change = (weights * (scores[b, :, at] - shift)).astype(BF16)
            raw[b, :, at] = change
            dq_cols[:, at] += dot(turned, change)
        return (dot(raw[b], q_rows[...]) * SCALE).astype(BF16)

    def key_block(b, carry):
        send_back(0, b, key_part(b))
        return carry

    lax.fori_loop(0, 6, key_block, 0)

    def return_spread(part, step):
        target = plus(plane, step)
        piece = summed.at[
            part, target // 2, pl.ds(pl.multiple_of(lax.rem(target, 2) * PIECE, PIECE), PIECE)
        ]
        return remote(
            piece, spread.at[part, step], rb_send.at[part], rb_recv.at[part, step], in_plane(target)
        )

    def add_up(part):
        all_at_once(grads.at[part], rc_recv.at[part, 0])
        terms[part, 0] = grads[part, 0]

        def add(step, carry):
            running[step] = running[previous[step]] + terms[part, step].astype(F32)
            return carry

        lax.fori_loop(0, RING, add, 0)

        def close(prompt, carry):
            summed[part, prompt] = running[last[prompt]].astype(BF16)
            return carry

        lax.fori_loop(0, PROMPTS, close, 0)

        for step in OFFSETS:
            return_spread(part, step).start()
        spread[part, 0] = summed[
            part, plane // 2, pl.ds(pl.multiple_of(lax.rem(plane, 2) * PIECE, PIECE), PIECE)
        ]

    def return_column(part, step, by_step):
        return remote(
            spread.at[part, by_step],
            parts.at[part, column],
            ra_send.at[part],
            ra_recv.at[part, 0],
            in_column(around(column + step)),
        )

    def return_on(part):
        for by_step in (0,) + OFFSETS:
            if by_step:
                return_spread(part, by_step).wait_recv()
            step = around(minus(plane, by_step) - column)

            @pl.when(step != 0)
            def _():
                return_column(part, step, by_step).start()

            @pl.when(step == 0)
            def _():
                parts[part, column] = spread[part, by_step]

    add_up(1)
    lax.fori_loop(6, BLOCKS, key_block, 0)

    down_ref[:, :HD] = key_part(BLOCKS)
    return_on(1)
    for j in range(HEADS):
        dq_ref[:, head_columns(j)] = (jnp.transpose(dq_cols[:, head_rows(j)]) * SCALE).astype(BF16)
    add_up(0)
    return_on(0)

    all_at_once(by_head, a_send)
    all_at_once(by_head, b_send)
    for part in range(2):
        all_at_once(staged.at[part], c_send.at[part])
        all_at_once(grads.at[part], rc_send.at[part])
        all_at_once(spread.at[part], rb_send.at[part])
        all_at_once(spread.at[part], ra_send.at[part])
        all_at_once(spread.at[part], ra_recv.at[part, 0])


def finish_kernel(dq_ref, down_ref, parts_ref, dq_out, down_out, dcache_out, dq, down, parts, total, get_sems, put_sems):
    gets = [
        pltpu.make_async_copy(parts_ref, parts, get_sems.at[0]),
        pltpu.make_async_copy(dq_ref, dq, get_sems.at[1]),
        pltpu.make_async_copy(down_ref, down, get_sems.at[2]),
    ]
    puts = [
        pltpu.make_async_copy(total, dcache_out, put_sems.at[0]),
        pltpu.make_async_copy(dq, dq_out, put_sems.at[1]),
        pltpu.make_async_copy(down, down_out, put_sems.at[2]),
    ]
    for get in gets:
        get.start()
    gets[0].wait()
    for h in range(8):
        for part in range(2):
            both = parts[part, h].astype(F32) + parts[part, 8 + h].astype(F32)
            total[:, h * WIDTH + part * HD : h * WIDTH + (part + 1) * HD] = both.astype(BF16)
    puts[0].start()
    for get, put in zip(gets[1:], puts[1:]):
        get.wait()
        put.start()
    for put in puts:
        put.wait()


def local(
    queries, resp_kv, prompt_cache, grad_out, group_counts, prompt_slot, slot_response, resp_len, weight_code
):
    vmem = pl.BlockSpec(memory_space=pltpu.VMEM)
    smem = pl.BlockSpec(memory_space=pltpu.SMEM)
    hbm = pl.BlockSpec(memory_space=pltpu.HBM)
    scratch = [
        pltpu.SMEM((RING,), jnp.int32),
        pltpu.SMEM((RING,), jnp.int32),
        pltpu.SMEM((PROMPTS,), jnp.int32),
        pltpu.VMEM((RLEN, HEADS * HD), BF16),
        pltpu.VMEM((RLEN, HEADS * HD), BF16),
        pltpu.VMEM((RLEN, WIDTH), BF16),
        pltpu.VMEM((RING, PIECE, WIDTH), BF16),
        pltpu.VMEM((PROMPTS, CHUNK, WIDTH), BF16),
        pltpu.VMEM((2, RING, CHUNK, HD), BF16),
        pltpu.VMEM((KEYS, HD), BF16),
        pltpu.VMEM((KEYS, HD), BF16),
        pltpu.VMEM((ROWS, HD), BF16),
        pltpu.VMEM((HD, ROWS), BF16),
        pltpu.VMEM((HD, ROWS), BF16),
        pltpu.VMEM((HD, ROWS), BF16),
        pltpu.VMEM((ROWS, HD), BF16),
        pltpu.VMEM((BLOCKS + 1, BLOCK, ROWS), F32),
        pltpu.VMEM((BLOCKS + 1, BLOCK, ROWS), BF16),
        pltpu.VMEM((8, ROWS), F32),
        pltpu.VMEM((8, ROWS), F32),
        pltpu.VMEM((8, ROWS), F32),
        pltpu.VMEM((HD, ROWS), F32),
        pltpu.VMEM((2, RING, CHUNK, HD), BF16),
        pltpu.VMEM((2, RING, CHUNK, HD), BF16),
        pltpu.VMEM((RING + 1, CHUNK, HD), F32),
        pltpu.VMEM((2, PROMPTS, CHUNK, HD), BF16),
        pltpu.VMEM((2, RING, PIECE, HD), BF16),
        pltpu.SemaphoreType.DMA((5,)),
        pltpu.SemaphoreType.DMA,
        pltpu.SemaphoreType.DMA((RING,)),
        pltpu.SemaphoreType.DMA,
        pltpu.SemaphoreType.DMA,
    ] + [pltpu.SemaphoreType.DMA((2,)), pltpu.SemaphoreType.DMA((2, RING))] * 4
    products = 5 * ROWS * KEYS * HD
    dq, down, parts = pl.pallas_call(
        kernel,
        out_shape=[
            jax.ShapeDtypeStruct(queries.shape, BF16),
            jax.ShapeDtypeStruct(resp_kv.shape, BF16),
            jax.ShapeDtypeStruct((2, RING, PIECE, HD), BF16),
        ],
        in_specs=[smem] * 5 + [hbm] * 4,
        out_specs=[vmem] * 3,
        scratch_shapes=scratch,
        compiler_params=pltpu.CompilerParams(
            collective_id=0, has_side_effects=True, vmem_limit_bytes=VMEM_LIMIT
        ),
        cost_estimate=pl.CostEstimate(flops=2 * products, bytes_accessed=3 << 20, transcendentals=ROWS * KEYS),
    )(
        group_counts,
        prompt_slot,
        slot_response,
        resp_len,
        weight_code,
        queries,
        resp_kv,
        prompt_cache,
        grad_out,
    )
    return pl.pallas_call(
        finish_kernel,
        out_shape=[
            jax.ShapeDtypeStruct(queries.shape, BF16),
            jax.ShapeDtypeStruct(resp_kv.shape, BF16),
            jax.ShapeDtypeStruct(prompt_cache.shape, BF16),
        ],
        in_specs=[hbm] * 3,
        out_specs=[hbm] * 3,
        scratch_shapes=[
            pltpu.VMEM(queries.shape, BF16),
            pltpu.VMEM(resp_kv.shape, BF16),
            pltpu.VMEM((2, RING, PIECE, HD), BF16),
            pltpu.VMEM(prompt_cache.shape, BF16),
            pltpu.SemaphoreType.DMA((3,)),
            pltpu.SemaphoreType.DMA((3,)),
        ],
        compiler_params=pltpu.CompilerParams(vmem_limit_bytes=VMEM_LIMIT),
    )(dq, down, parts)


def solution(mesh):
    placed = (
        P("seq", "head"),
        P("seq", "head"),
        P(("seq", "head"), None),
        P("seq", "head"),
        P(),
        P(),
        P(),
        P("seq"),
        P("seq"),
    )
    return jax.shard_map(
        local,
        mesh=mesh,
        in_specs=placed,
        out_specs=(P("seq", "head"), P("seq", "head"), P(("seq", "head"), None)),
        check_vma=False,
    )
```

```python
import math

import jax
import jax.numpy as jnp
from jax import lax
from jax.experimental import pallas as pl
from jax.experimental.pallas import tpu as pltpu
from jax.sharding import PartitionSpec as P

HD = 128
PLEN = 2048
RLEN = 256
HEADS = 8
PROMPTS = 8
RING = 16
CHUNK = PLEN // RING
UNITS = 4
UNIT = 16
BLOCK = 256
BLOCKS = PLEN // BLOCK
PER_BLOCK = BLOCK // CHUNK
ROWS = HEADS * RLEN
KEYS = PLEN + RLEN
WIDTH = 2 * HD
SCALE = HD**-0.5
LOG2E = math.log2(math.e)
MESH = pl.DeviceIdType.MESH
VMEM_LIMIT = 60 * 1024 * 1024
NN = (((1,), (0,)), ((), ()))
F32 = jnp.float32
BF16 = jnp.bfloat16


OFFSETS = (10, 6, 9, 14, 11, 5, 15, 7, 13, 2, 8, 1, 4, 3, 12)


def around(index):
    return lax.rem(index + 2 * RING, RING)


def plus(plane, offset):
    return lax.rem(plane // 4 + offset // 4, 4) * 4 + lax.rem(plane + lax.rem(offset, 4), 4)


def minus(plane, offset):
    return lax.rem(plane // 4 + 4 - offset // 4, 4) * 4 + lax.rem(plane + 4 - lax.rem(offset, 4), 4)


def unit_offset(column, u):
    return 4 * u + lax.rem(column + u, 4)


def column_step(i):
    return 8 + (i // 2) * (1 - 2 * lax.rem(i, 2))


def head_rows(j):
    return slice(j * RLEN, (j + 1) * RLEN)


def head_columns(j):
    return slice(j * HD, (j + 1) * HD)


def chunk_rows(step):
    return pl.ds(pl.multiple_of(step * CHUNK, CHUNK), CHUNK)


def fold(values, op):
    return op(values.reshape(values.shape[0] // 8, 8, values.shape[1]), axis=0)


def dot(a, b):
    return lax.dot_general(a, b, NN, preferred_element_type=F32)


def kernel(
    counts_ref,
    prompt_slot_ref,
    response_ref,
    len_ref,
    code_ref,
    q_ref,
    own_ref,
    cache_ref,
    go_ref,
    dq_ref,
    down_ref,
    back_ref,
    wanted,
    previous,
    last,
    q_in,
    go_in,
    own_in,
    rows_in,
    keys_in,
    values_in,
    staged,
    keys,
    values,
    q_rows,
    q_cols,
    cot_cols,
    cot_scaled_cols,
    cot_scaled_rows,
    scores,
    raw,
    top,
    delta,
    inverse,
    dq_cols,
    grads,
    terms,
    running,
    summed,
    sorted_sums,
    parts,
    final,
    own_grads,
    q_grads,
    in_sem,
    a_send,
    a_recv,
    b_send,
    b_recv,
    c_send,
    c_recv,
    rc_send,
    rc_recv,
    rb_send,
    rb_recv,
    ra_send,
    ra_recv,
):
    seq = lax.axis_index("seq")
    head = lax.axis_index("head")
    plane = seq // 2
    half = lax.rem(seq, 2)
    column = half * 8 + head

    def in_plane(other):
        return {"seq": 2 * other + half, "head": head}

    def in_column(other):
        return {"seq": 2 * plane + other // 8, "head": lax.rem(other, 8)}

    def remote(src, dst, send_sem, recv_sem, device):
        return pltpu.make_async_remote_copy(
            src_ref=src, dst_ref=dst, send_sem=send_sem, recv_sem=recv_sem, device_id=device, device_id_type=MESH
        )

    def all_at_once(buffer, sem):
        pltpu.make_async_copy(buffer.at[pl.ds(1, RING - 1)], buffer.at[pl.ds(1, RING - 1)], sem).wait()

    loads = [
        pltpu.make_async_copy(q_ref, q_in, in_sem.at[0]),
        pltpu.make_async_copy(go_ref, go_in, in_sem.at[1]),
        pltpu.make_async_copy(own_ref, own_in, in_sem.at[2]),
    ]
    for load in loads:
        load.start()

    barrier = pltpu.get_barrier_semaphore()

    def greet(step, carry):
        pl.semaphore_signal(barrier, inc=1, device_id=in_column(around(column + step)), device_id_type=MESH)
        pl.semaphore_signal(barrier, inc=1, device_id=in_plane(plus(plane, step)), device_id_type=MESH)
        return carry

    lax.fori_loop(1, RING, greet, 0)
    pl.semaphore_wait(barrier, 2 * (RING - 1))

    stays = lax.rem(column, 4) == 0

    def unit_copy(u):
        return remote(
            cache_ref.at[pl.ds(u * UNIT, UNIT)],
            rows_in.at[u],
            a_send.at[u],
            a_recv.at[u],
            in_plane(plus(plane, unit_offset(column, u))),
        )

    for u in range(1, UNITS):
        unit_copy(u).start()

    @pl.when(jnp.logical_not(stays))
    def _():
        unit_copy(0).start()

    @pl.when(stays)
    def _():
        pltpu.make_async_copy(cache_ref.at[pl.ds(0, UNIT)], rows_in.at[0], a_recv.at[0]).start()

    by_source = (keys_in, values_in)

    def column_copy(part, step):
        target = around(column + step)
        at = pl.ds(pl.multiple_of(lax.rem(target, 8) * WIDTH + part * HD, HD), HD)
        return remote(
            rows_in.at[:, :, at], by_source[part].at[column], b_send.at[part], b_recv.at[part], in_column(target)
        )

    def send_heads(part):
        def send(i, carry):
            column_copy(part, column_step(i)).start()
            return carry

        lax.fori_loop(1, RING, send, 0)
        by_source[part][column] = rows_in[:, :, pl.ds(pl.multiple_of(head * WIDTH + part * HD, HD), HD)]

    gathered = (keys, values)

    def chunk_copy(part, step):
        return remote(
            staged.at[part, step],
            gathered[part].at[chunk_rows(step)],
            c_send.at[part],
            c_recv.at[part, step],
            in_plane(plus(plane, step)),
        )

    def send_chunks(part):
        def take(step):
            prompt = wanted[step]
            units = []
            for odd in range(2):
                across = lax.rem(lax.div(plane, 4) + 4 - lax.div(prompt, 2), 4)
                along = lax.rem(plane + 4 - 2 * lax.rem(prompt, 2) - odd, 4)
                first = lax.rem(along + 4 - across, 4)
                for i in range(4):
                    units.append(by_source[part][4 * i + first, across])
            return jnp.concatenate(units, axis=0)

        all_at_once(by_source[part], b_recv.at[part])
        for step in OFFSETS:
            staged[part, step] = take(step)
            chunk_copy(part, step).start()
        gathered[part][:CHUNK] = take(0)

    ends = []
    for i in range(PROMPTS):
        ends.append(counts_ref[i] + (ends[-1] if ends else 0))
    prompts = []
    for step in range(RING):
        response = response_ref[2 * plus(plane, step) + half]
        group = jnp.int32(0)
        for end in ends[:-1]:
            group = group + (end <= response).astype(jnp.int32)
        prompts.append(prompt_slot_ref[group])
        wanted[step] = prompts[-1]
    for step in range(RING):
        found = jnp.int32(RING)
        for other in range(step):
            found = jnp.where(prompts[other] == prompts[step], other, found)
        previous[step] = found
    for prompt in range(PROMPTS):
        found = jnp.int32(RING)
        for step in range(RING):
            found = jnp.where(prompts[step] == prompt, step, found)
        last[prompt] = found

    for load in loads:
        load.wait()
    position = lax.broadcasted_iota(jnp.int32, (RLEN, HD), 0)
    factor = jnp.where(position < len_ref[0], code_ref[0].astype(F32) / 8.0, 0.0)
    for j in range(HEADS):
        query = q_in[:, head_columns(j)]
        q_rows[head_rows(j)] = query
        q_cols[:, head_rows(j)] = jnp.transpose(query)
        cotangent = go_in[:, head_columns(j)].astype(F32) * factor
        cot_cols[:, head_rows(j)] = jnp.transpose(cotangent).astype(BF16)
    keys[PLEN:] = own_in[:, :HD]
    values[PLEN:] = own_in[:, HD:]
    running[RING] = jnp.zeros((CHUNK, HD), F32)
    dq_cols[...] = jnp.zeros_like(dq_cols)

    def block_rows(b):
        return pl.ds(pl.multiple_of(b * BLOCK, BLOCK), BLOCK)

    def score(b, own):
        block = keys[block_rows(b)]
        for j in range(HEADS):
            at = head_rows(j)
            part = dot(block, q_cols[:, at])
            if own:
                key_at = lax.broadcasted_iota(jnp.int32, (BLOCK, RLEN), 0)
                seen_from = lax.broadcasted_iota(jnp.int32, (BLOCK, RLEN), 1)
                part = jnp.where(key_at <= seen_from, part, -1e30)
            scores[b, :, at] = part
            high = fold(part, jnp.max)
            top[:, at] = high if own else jnp.maximum(top[:, at], high)

    for u in range(UNITS):
        unit_copy(u).wait_recv()
    send_heads(0)
    send_heads(1)
    score(BLOCKS, True)
    send_chunks(0)
    send_chunks(1)

    def arrive(part, b):
        def one(i, carry):
            step = b * PER_BLOCK + i

            @pl.when(step > 0)
            def _():
                chunk_copy(part, step).wait_recv()

            return carry

        lax.fori_loop(0, PER_BLOCK, one, 0)

    def score_block(b, carry):
        arrive(0, b)
        score(b, False)
        return carry

    lax.fori_loop(0, BLOCKS, score_block, 0)

    for j in range(HEADS):
        at = head_rows(j)
        highest = jnp.max(top[:, at], axis=0, keepdims=True)

        def weigh(b, total):
            weights = jnp.exp2((scores[b, :, at] - highest) * (SCALE * LOG2E))
            raw[b, :, at] = weights.astype(BF16)
            return total + fold(weights, jnp.sum)

        total = lax.fori_loop(0, BLOCKS + 1, weigh, jnp.zeros((8, RLEN), F32))
        over = 1.0 / jnp.sum(total, axis=0, keepdims=True)
        inverse[:, at] = jnp.broadcast_to(over, (8, RLEN))
        scaled = cot_cols[:, at].astype(F32) * over
        cot_scaled_cols[:, at] = scaled.astype(BF16)
        cot_scaled_rows[at] = jnp.transpose(scaled).astype(BF16)

    def return_copy(part, step):
        return remote(
            grads.at[part, step],
            terms.at[part, step],
            rc_send.at[part],
            rc_recv.at[part],
            in_plane(minus(plane, step)),
        )

    def send_back(part, b, block):
        for i in range(PER_BLOCK):
            grads[part, b * PER_BLOCK + i] = block[i * CHUNK : (i + 1) * CHUNK]

        def one(i, carry):
            step = b * PER_BLOCK + i

            @pl.when(step > 0)
            def _():
                return_copy(part, step).start()

            return carry

        lax.fori_loop(0, PER_BLOCK, one, 0)

    def value_part(b, first):
        block = values[block_rows(b)]
        for j in range(HEADS):
            at = head_rows(j)
            grad = dot(block, cot_scaled_cols[:, at])
            scores[b, :, at] = grad
            term = fold(grad * raw[b, :, at].astype(F32), jnp.sum)
            delta[:, at] = term if first else delta[:, at] + term
        return dot(raw[b], cot_scaled_rows[...]).astype(BF16)

    own_grads[:, HD:] = value_part(BLOCKS, True)

    def value_block(b, carry):
        arrive(1, b)
        send_back(1, b, value_part(b, False))
        return carry

    lax.fori_loop(0, BLOCKS, value_block, 0)
    for j in range(HEADS):
        at = head_rows(j)
        delta[:, at] = jnp.sum(delta[:, at], axis=0, keepdims=True) * inverse[:, at]

    def key_part(b):
        turned = jnp.transpose(keys[block_rows(b)])
        for j in range(HEADS):
            at = head_rows(j)
            weights = raw[b, :, at].astype(F32)
            shift = delta[0:1, at]
            change = (weights * (scores[b, :, at] - shift)).astype(BF16)
            raw[b, :, at] = change
            dq_cols[:, at] += dot(turned, change)
        return (dot(raw[b], q_rows[...]) * SCALE).astype(BF16)

    def key_block(b, carry):
        send_back(0, b, key_part(b))
        return carry

    lax.fori_loop(0, 6, key_block, 0)

    def return_column(part, step):
        target = around(column + step)
        return remote(
            sorted_sums.at[part, target],
            parts.at[part, column],
            rb_send.at[part],
            rb_recv.at[part],
            in_column(target),
        )

    def add_up(part):
        all_at_once(grads.at[part], rc_recv.at[part])
        terms[part, 0] = grads[part, 0]

        def add(step, carry):
            running[step] = running[previous[step]] + terms[part, step].astype(F32)
            return carry

        lax.fori_loop(0, RING, add, 0)

        def close(prompt, carry):
            summed[prompt] = running[last[prompt]].astype(BF16)
            return carry

        lax.fori_loop(0, PROMPTS, close, 0)

        def sort(target):
            for u in range(UNITS):
                source = minus(plane, unit_offset(target, u))
                unit = lax.rem(source, 2) * 4 + target // 4
                sorted_sums[part, target, u * UNIT : (u + 1) * UNIT] = summed[
                    source // 2, pl.ds(pl.multiple_of(unit * UNIT, UNIT), UNIT)
                ]

        def send(i, carry):
            step = column_step(i)
            sort(around(column + step))
            return_column(part, step).start()
            return carry

        lax.fori_loop(1, RING, send, 0)
        sort(column)
        parts[part, column] = sorted_sums[part, column]

    def return_unit(part, u):
        return remote(
            final.at[part, pl.ds(u * UNIT, UNIT)],
            back_ref.at[part, pl.ds(u * UNIT, UNIT)],
            ra_send.at[part, u],
            ra_recv.at[part, u],
            in_plane(minus(plane, unit_offset(column, u))),
        )

    def return_stay(part):
        return pltpu.make_async_copy(
            final.at[part, pl.ds(0, UNIT)], back_ref.at[part, pl.ds(0, UNIT)], ra_recv.at[part, 0]
        )

    def return_rows(part):
        all_at_once(parts.at[part], rb_recv.at[part])
        for h in range(8):
            both = parts[part, h].astype(F32) + parts[part, 8 + h].astype(F32)
            final[part, :, head_columns(h)] = both.astype(BF16)
        for u in range(1, UNITS):
            return_unit(part, u).start()

        @pl.when(jnp.logical_not(stays))
        def _():
            return_unit(part, 0).start()

        @pl.when(stays)
        def _():
            return_stay(part).start()

    add_up(1)
    lax.fori_loop(6, BLOCKS, key_block, 0)

    own_grads[:, :HD] = key_part(BLOCKS)
    own_out = pltpu.make_async_copy(own_grads, down_ref, in_sem.at[2])
    own_out.start()
    return_rows(1)
    for j in range(HEADS):
        q_grads[:, head_columns(j)] = (jnp.transpose(dq_cols[:, head_rows(j)]) * SCALE).astype(BF16)
    q_out = pltpu.make_async_copy(q_grads, dq_ref, in_sem.at[0])
    q_out.start()
    add_up(0)
    return_rows(0)

    own_out.wait()
    q_out.wait()
    for part in range(2):
        all_at_once(by_source[part], b_send.at[part])
        all_at_once(staged.at[part], c_send.at[part])
        all_at_once(grads.at[part], rc_send.at[part])
        all_at_once(parts.at[part], rb_send.at[part])
        for u in range(UNITS):
            return_unit(part, u).wait_recv()
        for u in range(1, UNITS):
            return_unit(part, u).wait_send()
    for u in range(1, UNITS):
        unit_copy(u).wait_send()

    @pl.when(jnp.logical_not(stays))
    def _():
        unit_copy(0).wait_send()
        return_unit(0, 0).wait_send()
        return_unit(1, 0).wait_send()


def finish_kernel(dq_ref, down_ref, back_ref, dq_out, down_out, dcache_out, dq, down, back, total, get_sems, put_sems):
    gets = [
        pltpu.make_async_copy(back_ref, back, get_sems.at[0]),
        pltpu.make_async_copy(dq_ref, dq, get_sems.at[1]),
        pltpu.make_async_copy(down_ref, down, get_sems.at[2]),
    ]
    puts = [
        pltpu.make_async_copy(total, dcache_out, put_sems.at[0]),
        pltpu.make_async_copy(dq, dq_out, put_sems.at[1]),
        pltpu.make_async_copy(down, down_out, put_sems.at[2]),
    ]
    for get in gets:
        get.start()
    gets[0].wait()
    for h in range(8):
        for part in range(2):
            total[:, h * WIDTH + part * HD : h * WIDTH + (part + 1) * HD] = back[part, :, head_columns(h)]
    puts[0].start()
    for get, put in zip(gets[1:], puts[1:]):
        get.wait()
        put.start()
    for put in puts:
        put.wait()


def local(
    queries, resp_kv, prompt_cache, grad_out, group_counts, prompt_slot, slot_response, resp_len, weight_code
):
    smem = pl.BlockSpec(memory_space=pltpu.SMEM)
    hbm = pl.BlockSpec(memory_space=pltpu.HBM)
    scratch = [
        pltpu.SMEM((RING,), jnp.int32),
        pltpu.SMEM((RING,), jnp.int32),
        pltpu.SMEM((PROMPTS,), jnp.int32),
        pltpu.VMEM((RLEN, HEADS * HD), BF16),
        pltpu.VMEM((RLEN, HEADS * HD), BF16),
        pltpu.VMEM((RLEN, WIDTH), BF16),
        pltpu.VMEM((UNITS, UNIT, 8 * WIDTH), BF16),
        pltpu.VMEM((RING, UNITS, UNIT, HD), BF16),
        pltpu.VMEM((RING, UNITS, UNIT, HD), BF16),
        pltpu.VMEM((2, RING, CHUNK, HD), BF16),
        pltpu.VMEM((KEYS, HD), BF16),
        pltpu.VMEM((KEYS, HD), BF16),
        pltpu.VMEM((ROWS, HD), BF16),
        pltpu.VMEM((HD, ROWS), BF16),
        pltpu.VMEM((HD, ROWS), BF16),
        pltpu.VMEM((HD, ROWS), BF16),
        pltpu.VMEM((ROWS, HD), BF16),
        pltpu.VMEM((BLOCKS + 1, BLOCK, ROWS), F32),
        pltpu.VMEM((BLOCKS + 1, BLOCK, ROWS), BF16),
        pltpu.VMEM((8, ROWS), F32),
        pltpu.VMEM((8, ROWS), F32),
        pltpu.VMEM((8, ROWS), F32),
        pltpu.VMEM((HD, ROWS), F32),
        pltpu.VMEM((2, RING, CHUNK, HD), BF16),
        pltpu.VMEM((2, RING, CHUNK, HD), BF16),
        pltpu.VMEM((RING + 1, CHUNK, HD), F32),
        pltpu.VMEM((PROMPTS, CHUNK, HD), BF16),
        pltpu.VMEM((2, RING, UNITS * UNIT, HD), BF16),
        pltpu.VMEM((2, RING, UNITS * UNIT, HD), BF16),
        pltpu.VMEM((2, UNITS * UNIT, 8 * HD), BF16),
        pltpu.VMEM((RLEN, WIDTH), BF16),
        pltpu.VMEM((RLEN, HEADS * HD), BF16),
        pltpu.SemaphoreType.DMA((3,)),
        pltpu.SemaphoreType.DMA((UNITS,)),
        pltpu.SemaphoreType.DMA((UNITS,)),
        pltpu.SemaphoreType.DMA((2,)),
        pltpu.SemaphoreType.DMA((2,)),
        pltpu.SemaphoreType.DMA((2,)),
        pltpu.SemaphoreType.DMA((2, RING)),
        pltpu.SemaphoreType.DMA((2,)),
        pltpu.SemaphoreType.DMA((2,)),
        pltpu.SemaphoreType.DMA((2,)),
        pltpu.SemaphoreType.DMA((2,)),
        pltpu.SemaphoreType.DMA((2, UNITS)),
        pltpu.SemaphoreType.DMA((2, UNITS)),
    ]
    products = 5 * ROWS * KEYS * HD
    dq, down, back = pl.pallas_call(
        kernel,
        out_shape=[
            jax.ShapeDtypeStruct(queries.shape, BF16),
            jax.ShapeDtypeStruct(resp_kv.shape, BF16),
            jax.ShapeDtypeStruct((2, UNITS * UNIT, 8 * HD), BF16),
        ],
        in_specs=[smem] * 5 + [hbm] * 4,
        out_specs=[hbm] * 3,
        scratch_shapes=scratch,
        compiler_params=pltpu.CompilerParams(
            collective_id=0, has_side_effects=True, vmem_limit_bytes=VMEM_LIMIT
        ),
        cost_estimate=pl.CostEstimate(flops=2 * products, bytes_accessed=3 << 20, transcendentals=ROWS * KEYS),
    )(
        group_counts,
        prompt_slot,
        slot_response,
        resp_len,
        weight_code,
        queries,
        resp_kv,
        prompt_cache,
        grad_out,
    )
    return pl.pallas_call(
        finish_kernel,
        out_shape=[
            jax.ShapeDtypeStruct(queries.shape, BF16),
            jax.ShapeDtypeStruct(resp_kv.shape, BF16),
            jax.ShapeDtypeStruct(prompt_cache.shape, BF16),
        ],
        in_specs=[hbm] * 3,
        out_specs=[hbm] * 3,
        scratch_shapes=[
            pltpu.VMEM(queries.shape, BF16),
            pltpu.VMEM(resp_kv.shape, BF16),
            pltpu.VMEM((2, UNITS * UNIT, 8 * HD), BF16),
            pltpu.VMEM(prompt_cache.shape, BF16),
            pltpu.SemaphoreType.DMA((3,)),
            pltpu.SemaphoreType.DMA((3,)),
        ],
        compiler_params=pltpu.CompilerParams(vmem_limit_bytes=VMEM_LIMIT),
    )(dq, down, back)


def solution(mesh):
    placed = (
        P("seq", "head"),
        P("seq", "head"),
        P(("seq", "head"), None),
        P("seq", "head"),
        P(),
        P(),
        P(),
        P("seq"),
        P("seq"),
    )
    return jax.shard_map(
        local,
        mesh=mesh,
        in_specs=placed,
        out_specs=(P("seq", "head"), P("seq", "head"), P(("seq", "head"), None)),
        check_vma=False,
    )
```

```python
import math

import jax
import jax.numpy as jnp
from jax import lax
from jax.experimental import pallas as pl
from jax.experimental.pallas import tpu as pltpu
from jax.sharding import PartitionSpec as P

HD = 128
PLEN = 2048
RLEN = 256
HEADS = 8
PROMPTS = 8
RING = 16
CHUNK = PLEN // RING
UNITS = 4
UNIT = 16
BLOCK = 512
BLOCKS = PLEN // BLOCK
PER_BLOCK = BLOCK // CHUNK
ROWS = HEADS * RLEN
KEYS = PLEN + RLEN
WIDTH = 2 * HD
SCALE = HD**-0.5
LOG2E = math.log2(math.e)
MESH = pl.DeviceIdType.MESH
VMEM_LIMIT = 60 * 1024 * 1024
NN = (((1,), (0,)), ((), ()))
F32 = jnp.float32
BF16 = jnp.bfloat16


OFFSETS = (10, 6, 9, 14, 11, 5, 15, 7, 13, 2, 8, 1, 4, 3, 12)


def around(index):
    return lax.rem(index + 2 * RING, RING)


def plus(plane, offset):
    return lax.rem(plane // 4 + offset // 4, 4) * 4 + lax.rem(plane + lax.rem(offset, 4), 4)


def minus(plane, offset):
    return lax.rem(plane // 4 + 4 - offset // 4, 4) * 4 + lax.rem(plane + 4 - lax.rem(offset, 4), 4)


def unit_offset(column, u):
    return 4 * u + lax.rem(column + u, 4)


def column_step(i):
    return 8 + (i // 2) * (1 - 2 * lax.rem(i, 2))


def head_rows(j):
    return slice(j * RLEN, (j + 1) * RLEN)


def head_columns(j):
    return slice(j * HD, (j + 1) * HD)


def chunk_rows(step):
    return pl.ds(pl.multiple_of(step * CHUNK, CHUNK), CHUNK)


def fold(values, op):
    return op(values.reshape(values.shape[0] // 8, 8, values.shape[1]), axis=0)


def dot(a, b):
    return lax.dot_general(a, b, NN, preferred_element_type=F32)


def kernel(
    counts_ref,
    prompt_slot_ref,
    response_ref,
    len_ref,
    code_ref,
    q_ref,
    own_ref,
    cache_ref,
    go_ref,
    dq_ref,
    down_ref,
    back_ref,
    wanted,
    previous,
    last,
    q_in,
    go_in,
    own_in,
    rows_in,
    keys_in,
    values_in,
    staged,
    keys,
    values,
    q_rows,
    q_cols,
    cot_cols,
    cot_scaled_cols,
    cot_scaled_rows,
    scores,
    raw,
    top,
    delta,
    inverse,
    dq_cols,
    grads,
    terms,
    running,
    summed,
    sorted_sums,
    parts,
    final,
    own_grads,
    q_grads,
    in_sem,
    a_send,
    a_recv,
    b_send,
    b_recv,
    c_send,
    c_recv,
    rc_send,
    rc_recv,
    rb_send,
    rb_recv,
    ra_send,
    ra_recv,
):
    seq = lax.axis_index("seq")
    head = lax.axis_index("head")
    plane = seq // 2
    half = lax.rem(seq, 2)
    column = half * 8 + head

    def in_plane(other):
        return {"seq": 2 * other + half, "head": head}

    def in_column(other):
        return {"seq": 2 * plane + other // 8, "head": lax.rem(other, 8)}

    def remote(src, dst, send_sem, recv_sem, device):
        return pltpu.make_async_remote_copy(
            src_ref=src, dst_ref=dst, send_sem=send_sem, recv_sem=recv_sem, device_id=device, device_id_type=MESH
        )

    def all_at_once(buffer, sem):
        pltpu.make_async_copy(buffer.at[pl.ds(1, RING - 1)], buffer.at[pl.ds(1, RING - 1)], sem).wait()

    loads = [
        pltpu.make_async_copy(q_ref, q_in, in_sem.at[0]),
        pltpu.make_async_copy(go_ref, go_in, in_sem.at[1]),
        pltpu.make_async_copy(own_ref, own_in, in_sem.at[2]),
    ]
    for load in loads:
        load.start()

    barrier = pltpu.get_barrier_semaphore()

    def greet(step, carry):
        pl.semaphore_signal(barrier, inc=1, device_id=in_column(around(column + step)), device_id_type=MESH)
        pl.semaphore_signal(barrier, inc=1, device_id=in_plane(plus(plane, step)), device_id_type=MESH)
        return carry

    lax.fori_loop(1, RING, greet, 0)
    pl.semaphore_wait(barrier, 2 * (RING - 1))

    stays = lax.rem(column, 4) == 0

    def unit_copy(u):
        return remote(
            cache_ref.at[pl.ds(u * UNIT, UNIT)],
            rows_in.at[u],
            a_send.at[u],
            a_recv.at[u],
            in_plane(plus(plane, unit_offset(column, u))),
        )

    for u in range(1, UNITS):
        unit_copy(u).start()

    @pl.when(jnp.logical_not(stays))
    def _():
        unit_copy(0).start()

    @pl.when(stays)
    def _():
        pltpu.make_async_copy(cache_ref.at[pl.ds(0, UNIT)], rows_in.at[0], a_recv.at[0]).start()

    by_source = (keys_in, values_in)

    def column_copy(part, step):
        target = around(column + step)
        at = pl.ds(pl.multiple_of(lax.rem(target, 8) * WIDTH + part * HD, HD), HD)
        return remote(
            rows_in.at[:, :, at], by_source[part].at[column], b_send.at[part], b_recv.at[part], in_column(target)
        )

    def send_heads(part):
        def send(i, carry):
            column_copy(part, column_step(i)).start()
            return carry

        lax.fori_loop(1, RING, send, 0)
        by_source[part][column] = rows_in[:, :, pl.ds(pl.multiple_of(head * WIDTH + part * HD, HD), HD)]

    gathered = (keys, values)

    def chunk_copy(part, step):
        return remote(
            staged.at[part, step],
            gathered[part].at[chunk_rows(step)],
            c_send.at[part],
            c_recv.at[part, step],
            in_plane(plus(plane, step)),
        )

    def send_chunks(part):
        def take(step):
            prompt = wanted[step]
            units = []
            for odd in range(2):
                across = lax.rem(lax.div(plane, 4) + 4 - lax.div(prompt, 2), 4)
                along = lax.rem(plane + 4 - 2 * lax.rem(prompt, 2) - odd, 4)
                first = lax.rem(along + 4 - across, 4)
                for i in range(4):
                    units.append(by_source[part][4 * i + first, across])
            return jnp.concatenate(units, axis=0)

        all_at_once(by_source[part], b_recv.at[part])
        for step in OFFSETS:
            staged[part, step] = take(step)
            chunk_copy(part, step).start()
        gathered[part][:CHUNK] = take(0)

    ends = []
    for i in range(PROMPTS):
        ends.append(counts_ref[i] + (ends[-1] if ends else 0))
    prompts = []
    for step in range(RING):
        response = response_ref[2 * plus(plane, step) + half]
        group = jnp.int32(0)
        for end in ends[:-1]:
            group = group + (end <= response).astype(jnp.int32)
        prompts.append(prompt_slot_ref[group])
        wanted[step] = prompts[-1]
    for step in range(RING):
        found = jnp.int32(RING)
        for other in range(step):
            found = jnp.where(prompts[other] == prompts[step], other, found)
        previous[step] = found
    for prompt in range(PROMPTS):
        found = jnp.int32(RING)
        for step in range(RING):
            found = jnp.where(prompts[step] == prompt, step, found)
        last[prompt] = found

    for load in loads:
        load.wait()
    position = lax.broadcasted_iota(jnp.int32, (RLEN, HD), 0)
    factor = jnp.where(position < len_ref[0], code_ref[0].astype(F32) / 8.0, 0.0)
    for j in range(HEADS):
        query = q_in[:, head_columns(j)]
        q_rows[head_rows(j)] = query
        q_cols[:, head_rows(j)] = jnp.transpose(query)
        cotangent = go_in[:, head_columns(j)].astype(F32) * factor
        cot_cols[:, head_rows(j)] = jnp.transpose(cotangent).astype(BF16)
    keys[PLEN:] = own_in[:, :HD]
    values[PLEN:] = own_in[:, HD:]
    running[RING] = jnp.zeros((CHUNK, HD), F32)
    dq_cols[...] = jnp.zeros_like(dq_cols)

    def block_rows(b, own):
        return slice(PLEN, KEYS) if own else pl.ds(pl.multiple_of(b * BLOCK, BLOCK), BLOCK)

    def block_size(own):
        return slice(0, RLEN) if own else slice(0, BLOCK)

    def score(b, own):
        block = keys[block_rows(b, own)]
        rows = block_size(own)
        for j in range(HEADS):
            at = head_rows(j)
            part = dot(block, q_cols[:, at])
            if own:
                key_at = lax.broadcasted_iota(jnp.int32, (RLEN, RLEN), 0)
                seen_from = lax.broadcasted_iota(jnp.int32, (RLEN, RLEN), 1)
                part = jnp.where(key_at <= seen_from, part, -1e30)
            scores[b, rows, at] = part
            high = fold(part, jnp.max)
            top[:, at] = high if own else jnp.maximum(top[:, at], high)

    for u in range(UNITS):
        unit_copy(u).wait_recv()
    send_heads(0)
    send_heads(1)
    score(BLOCKS, True)
    send_chunks(0)
    send_chunks(1)

    def arrive(part, b):
        def one(i, carry):
            step = b * PER_BLOCK + i

            @pl.when(step > 0)
            def _():
                chunk_copy(part, step).wait_recv()

            return carry

        lax.fori_loop(0, PER_BLOCK, one, 0)

    def score_block(b, carry):
        arrive(0, b)
        score(b, False)
        return carry

    lax.fori_loop(0, BLOCKS, score_block, 0)

    for j in range(HEADS):
        at = head_rows(j)
        highest = jnp.max(top[:, at], axis=0, keepdims=True)

        def weigh(b, total, own=False):
            rows = block_size(own)
            weights = jnp.exp2((scores[b, rows, at] - highest) * (SCALE * LOG2E))
            raw[b, rows, at] = weights.astype(BF16)
            return total + fold(weights, jnp.sum)

        total = weigh(BLOCKS, jnp.zeros((8, RLEN), F32), True)
        total = lax.fori_loop(0, BLOCKS, weigh, total)
        over = 1.0 / jnp.sum(total, axis=0, keepdims=True)
        inverse[:, at] = jnp.broadcast_to(over, (8, RLEN))
        scaled = cot_cols[:, at].astype(F32) * over
        cot_scaled_cols[:, at] = scaled.astype(BF16)
        cot_scaled_rows[at] = jnp.transpose(scaled).astype(BF16)

    def return_copy(part, step):
        return remote(
            grads.at[part, step],
            terms.at[part, step],
            rc_send.at[part],
            rc_recv.at[part],
            in_plane(minus(plane, step)),
        )

    def send_back(part, b, block):
        for i in range(PER_BLOCK):
            grads[part, b * PER_BLOCK + i] = block[i * CHUNK : (i + 1) * CHUNK]

        def one(i, carry):
            step = b * PER_BLOCK + i

            @pl.when(step > 0)
            def _():
                return_copy(part, step).start()

            return carry

        lax.fori_loop(0, PER_BLOCK, one, 0)

    def value_part(b, own):
        block = values[block_rows(b, own)]
        rows = block_size(own)
        for j in range(HEADS):
            at = head_rows(j)
            grad = dot(block, cot_scaled_cols[:, at])
            scores[b, rows, at] = grad
            term = fold(grad * raw[b, rows, at].astype(F32), jnp.sum)
            delta[:, at] = term if own else delta[:, at] + term
        return dot(raw[b, rows], cot_scaled_rows[...]).astype(BF16)

    own_grads[:, HD:] = value_part(BLOCKS, True)

    def value_block(b, carry):
        arrive(1, b)
        send_back(1, b, value_part(b, False))
        return carry

    lax.fori_loop(0, BLOCKS, value_block, 0)
    for j in range(HEADS):
        at = head_rows(j)
        delta[:, at] = jnp.sum(delta[:, at], axis=0, keepdims=True) * inverse[:, at]

    def key_part(b, own):
        turned = jnp.transpose(keys[block_rows(b, own)])
        rows = block_size(own)
        for j in range(HEADS):
            at = head_rows(j)
            weights = raw[b, rows, at].astype(F32)
            change = (weights * (scores[b, rows, at] - delta[0:1, at])).astype(BF16)
            raw[b, rows, at] = change
            dq_cols[:, at] += dot(turned, change)
        return (dot(raw[b, rows], q_rows[...]) * SCALE).astype(BF16)

    def key_block(b, carry):
        send_back(0, b, key_part(b, False))
        return carry

    lax.fori_loop(0, 2, key_block, 0)

    def return_column(part, step):
        target = around(column + step)
        return remote(
            sorted_sums.at[part, target],
            parts.at[part, column],
            rb_send.at[part],
            rb_recv.at[part],
            in_column(target),
        )

    def add_up(part):
        all_at_once(grads.at[part], rc_recv.at[part])
        terms[part, 0] = grads[part, 0]

        def add(step, carry):
            running[step] = running[previous[step]] + terms[part, step].astype(F32)
            return carry

        lax.fori_loop(0, RING, add, 0)

        def close(prompt, carry):
            summed[prompt] = running[last[prompt]].astype(BF16)
            return carry

        lax.fori_loop(0, PROMPTS, close, 0)

        def sort(target):
            for u in range(UNITS):
                source = minus(plane, unit_offset(target, u))
                unit = lax.rem(source, 2) * 4 + target // 4
                sorted_sums[part, target, u * UNIT : (u + 1) * UNIT] = summed[
                    source // 2, pl.ds(pl.multiple_of(unit * UNIT, UNIT), UNIT)
                ]

        def send(i, carry):
            step = column_step(i)
            sort(around(column + step))
            return_column(part, step).start()
            return carry

        lax.fori_loop(1, RING, send, 0)
        sort(column)
        parts[part, column] = sorted_sums[part, column]

    def return_unit(part, u):
        return remote(
            final.at[part, pl.ds(u * UNIT, UNIT)],
            back_ref.at[part, pl.ds(u * UNIT, UNIT)],
            ra_send.at[part, u],
            ra_recv.at[part, u],
            in_plane(minus(plane, unit_offset(column, u))),
        )

    def return_stay(part):
        return pltpu.make_async_copy(
            final.at[part, pl.ds(0, UNIT)], back_ref.at[part, pl.ds(0, UNIT)], ra_recv.at[part, 0]
        )

    def return_rows(part):
        all_at_once(parts.at[part], rb_recv.at[part])
        for h in range(8):
            both = parts[part, h].astype(F32) + parts[part, 8 + h].astype(F32)
            final[part, :, head_columns(h)] = both.astype(BF16)
        for u in range(1, UNITS):
            return_unit(part, u).start()

        @pl.when(jnp.logical_not(stays))
        def _():
            return_unit(part, 0).start()

        @pl.when(stays)
        def _():
            return_stay(part).start()

    add_up(1)
    lax.fori_loop(2, BLOCKS, key_block, 0)

    own_grads[:, :HD] = key_part(BLOCKS, True)
    own_out = pltpu.make_async_copy(own_grads, down_ref, in_sem.at[2])
    own_out.start()
    return_rows(1)
    for j in range(HEADS):
        q_grads[:, head_columns(j)] = (jnp.transpose(dq_cols[:, head_rows(j)]) * SCALE).astype(BF16)
    q_out = pltpu.make_async_copy(q_grads, dq_ref, in_sem.at[0])
    q_out.start()
    add_up(0)
    return_rows(0)

    own_out.wait()
    q_out.wait()
    for part in range(2):
        all_at_once(by_source[part], b_send.at[part])
        all_at_once(staged.at[part], c_send.at[part])
        all_at_once(grads.at[part], rc_send.at[part])
        all_at_once(parts.at[part], rb_send.at[part])
        for u in range(UNITS):
            return_unit(part, u).wait_recv()
        for u in range(1, UNITS):
            return_unit(part, u).wait_send()
    for u in range(1, UNITS):
        unit_copy(u).wait_send()

    @pl.when(jnp.logical_not(stays))
    def _():
        unit_copy(0).wait_send()
        return_unit(0, 0).wait_send()
        return_unit(1, 0).wait_send()


def finish_kernel(dq_ref, down_ref, back_ref, dq_out, down_out, dcache_out, dq, down, back, total, get_sems, put_sems):
    gets = [
        pltpu.make_async_copy(back_ref, back, get_sems.at[0]),
        pltpu.make_async_copy(dq_ref, dq, get_sems.at[1]),
        pltpu.make_async_copy(down_ref, down, get_sems.at[2]),
    ]
    puts = [
        pltpu.make_async_copy(total, dcache_out, put_sems.at[0]),
        pltpu.make_async_copy(dq, dq_out, put_sems.at[1]),
        pltpu.make_async_copy(down, down_out, put_sems.at[2]),
    ]
    for get in gets:
        get.start()
    gets[0].wait()
    for h in range(8):
        for part in range(2):
            total[:, h * WIDTH + part * HD : h * WIDTH + (part + 1) * HD] = back[part, :, head_columns(h)]
    puts[0].start()
    for get, put in zip(gets[1:], puts[1:]):
        get.wait()
        put.start()
    for put in puts:
        put.wait()


def local(
    queries, resp_kv, prompt_cache, grad_out, group_counts, prompt_slot, slot_response, resp_len, weight_code
):
    smem = pl.BlockSpec(memory_space=pltpu.SMEM)
    hbm = pl.BlockSpec(memory_space=pltpu.HBM)
    scratch = [
        pltpu.SMEM((RING,), jnp.int32),
        pltpu.SMEM((RING,), jnp.int32),
        pltpu.SMEM((PROMPTS,), jnp.int32),
        pltpu.VMEM((RLEN, HEADS * HD), BF16),
        pltpu.VMEM((RLEN, HEADS * HD), BF16),
        pltpu.VMEM((RLEN, WIDTH), BF16),
        pltpu.VMEM((UNITS, UNIT, 8 * WIDTH), BF16),
        pltpu.VMEM((RING, UNITS, UNIT, HD), BF16),
        pltpu.VMEM((RING, UNITS, UNIT, HD), BF16),
        pltpu.VMEM((2, RING, CHUNK, HD), BF16),
        pltpu.VMEM((KEYS, HD), BF16),
        pltpu.VMEM((KEYS, HD), BF16),
        pltpu.VMEM((ROWS, HD), BF16),
        pltpu.VMEM((HD, ROWS), BF16),
        pltpu.VMEM((HD, ROWS), BF16),
        pltpu.VMEM((HD, ROWS), BF16),
        pltpu.VMEM((ROWS, HD), BF16),
        pltpu.VMEM((BLOCKS + 1, BLOCK, ROWS), F32),
        pltpu.VMEM((BLOCKS + 1, BLOCK, ROWS), BF16),
        pltpu.VMEM((8, ROWS), F32),
        pltpu.VMEM((8, ROWS), F32),
        pltpu.VMEM((8, ROWS), F32),
        pltpu.VMEM((HD, ROWS), F32),
        pltpu.VMEM((2, RING, CHUNK, HD), BF16),
        pltpu.VMEM((2, RING, CHUNK, HD), BF16),
        pltpu.VMEM((RING + 1, CHUNK, HD), F32),
        pltpu.VMEM((PROMPTS, CHUNK, HD), BF16),
        pltpu.VMEM((2, RING, UNITS * UNIT, HD), BF16),
        pltpu.VMEM((2, RING, UNITS * UNIT, HD), BF16),
        pltpu.VMEM((2, UNITS * UNIT, 8 * HD), BF16),
        pltpu.VMEM((RLEN, WIDTH), BF16),
        pltpu.VMEM((RLEN, HEADS * HD), BF16),
        pltpu.SemaphoreType.DMA((3,)),
        pltpu.SemaphoreType.DMA((UNITS,)),
        pltpu.SemaphoreType.DMA((UNITS,)),
        pltpu.SemaphoreType.DMA((2,)),
        pltpu.SemaphoreType.DMA((2,)),
        pltpu.SemaphoreType.DMA((2,)),
        pltpu.SemaphoreType.DMA((2, RING)),
        pltpu.SemaphoreType.DMA((2,)),
        pltpu.SemaphoreType.DMA((2,)),
        pltpu.SemaphoreType.DMA((2,)),
        pltpu.SemaphoreType.DMA((2,)),
        pltpu.SemaphoreType.DMA((2, UNITS)),
        pltpu.SemaphoreType.DMA((2, UNITS)),
    ]
    products = 5 * ROWS * KEYS * HD
    dq, down, back = pl.pallas_call(
        kernel,
        out_shape=[
            jax.ShapeDtypeStruct(queries.shape, BF16),
            jax.ShapeDtypeStruct(resp_kv.shape, BF16),
            jax.ShapeDtypeStruct((2, UNITS * UNIT, 8 * HD), BF16),
        ],
        in_specs=[smem] * 5 + [hbm] * 4,
        out_specs=[hbm] * 3,
        scratch_shapes=scratch,
        compiler_params=pltpu.CompilerParams(
            collective_id=0, has_side_effects=True, vmem_limit_bytes=VMEM_LIMIT
        ),
        cost_estimate=pl.CostEstimate(flops=2 * products, bytes_accessed=3 << 20, transcendentals=ROWS * KEYS),
    )(
        group_counts,
        prompt_slot,
        slot_response,
        resp_len,
        weight_code,
        queries,
        resp_kv,
        prompt_cache,
        grad_out,
    )
    return pl.pallas_call(
        finish_kernel,
        out_shape=[
            jax.ShapeDtypeStruct(queries.shape, BF16),
            jax.ShapeDtypeStruct(resp_kv.shape, BF16),
            jax.ShapeDtypeStruct(prompt_cache.shape, BF16),
        ],
        in_specs=[hbm] * 3,
        out_specs=[hbm] * 3,
        scratch_shapes=[
            pltpu.VMEM(queries.shape, BF16),
            pltpu.VMEM(resp_kv.shape, BF16),
            pltpu.VMEM((2, UNITS * UNIT, 8 * HD), BF16),
            pltpu.VMEM(prompt_cache.shape, BF16),
            pltpu.SemaphoreType.DMA((3,)),
            pltpu.SemaphoreType.DMA((3,)),
        ],
        compiler_params=pltpu.CompilerParams(vmem_limit_bytes=VMEM_LIMIT),
    )(dq, down, back)


def solution(mesh):
    placed = (
        P("seq", "head"),
        P("seq", "head"),
        P(("seq", "head"), None),
        P("seq", "head"),
        P(),
        P(),
        P(),
        P("seq"),
        P("seq"),
    )
    return jax.shard_map(
        local,
        mesh=mesh,
        in_specs=placed,
        out_specs=(P("seq", "head"), P("seq", "head"), P(("seq", "head"), None)),
        check_vma=False,
    )
```

```python
import math

import jax
import jax.numpy as jnp
from jax import lax
from jax.experimental import pallas as pl
from jax.experimental.pallas import tpu as pltpu
from jax.sharding import PartitionSpec as P

HD = 128
PLEN = 2048
RLEN = 256
HEADS = 8
PROMPTS = 8
RING = 16
CHUNK = PLEN // RING
UNITS = 4
UNIT = 16
BLOCK = 256
BLOCKS = (PLEN + RLEN) // BLOCK
ROWS = HEADS * RLEN
KEYS = PLEN + RLEN
WIDTH = 2 * HD
SCALE = HD**-0.5
LOG2E = math.log2(math.e)
MESH = pl.DeviceIdType.MESH
VMEM_LIMIT = 60 * 1024 * 1024
NN = (((1,), (0,)), ((), ()))
F32 = jnp.float32
BF16 = jnp.bfloat16


OFFSETS = (10, 6, 9, 14, 11, 5, 15, 7, 13, 2, 8, 1, 4, 3, 12)


def around(index):
    return lax.rem(index + 2 * RING, RING)


def plus(plane, offset):
    return lax.rem(plane // 4 + offset // 4, 4) * 4 + lax.rem(plane + lax.rem(offset, 4), 4)


def minus(plane, offset):
    return lax.rem(plane // 4 + 4 - offset // 4, 4) * 4 + lax.rem(plane + 4 - lax.rem(offset, 4), 4)


def unit_offset(column, u):
    return 4 * u + lax.rem(column + u, 4)


def column_step(i):
    return 8 + (i // 2) * (1 - 2 * lax.rem(i, 2))


def head_rows(j):
    return slice(j * RLEN, (j + 1) * RLEN)


def head_columns(j):
    return slice(j * HD, (j + 1) * HD)


def fold(values, op):
    return op(values.reshape(values.shape[0] // 8, 8, values.shape[1]), axis=0)


def dot(a, b):
    return lax.dot_general(a, b, NN, preferred_element_type=F32)


class Place:
    def __init__(self):
        seq = lax.axis_index("seq")
        self.head = lax.axis_index("head")
        self.plane = seq // 2
        self.half = lax.rem(seq, 2)
        self.column = self.half * 8 + self.head

    def in_plane(self, other):
        return {"seq": 2 * other + self.half, "head": self.head}

    def in_column(self, other):
        return {"seq": 2 * self.plane + other // 8, "head": lax.rem(other, 8)}

    def greet(self):
        barrier = pltpu.get_barrier_semaphore()

        def signal(step, carry):
            for device in (self.in_column(around(self.column + step)), self.in_plane(plus(self.plane, step))):
                pl.semaphore_signal(barrier, inc=1, device_id=device, device_id_type=MESH)
            return carry

        lax.fori_loop(1, RING, signal, 0)
        pl.semaphore_wait(barrier, 2 * (RING - 1))


def remote(src, dst, send_sem, recv_sem, device):
    return pltpu.make_async_remote_copy(
        src_ref=src, dst_ref=dst, send_sem=send_sem, recv_sem=recv_sem, device_id=device, device_id_type=MESH
    )


def all_at_once(buffer, sem):
    pltpu.make_async_copy(buffer.at[pl.ds(1, RING - 1)], buffer.at[pl.ds(1, RING - 1)], sem).wait()


def gather_kernel(
    counts_ref,
    prompt_slot_ref,
    response_ref,
    cache_ref,
    keys_ref,
    values_ref,
    wanted,
    rows_in,
    keys_in,
    values_in,
    staged,
    a_send,
    a_recv,
    b_send,
    b_recv,
    c_send,
    c_recv,
):
    here = Place()
    plane, half, head, column = here.plane, here.half, here.head, here.column
    in_plane, in_column = here.in_plane, here.in_column
    here.greet()

    stays = lax.rem(column, 4) == 0

    def unit_copy(u):
        return remote(
            cache_ref.at[pl.ds(u * UNIT, UNIT)],
            rows_in.at[u],
            a_send.at[u],
            a_recv.at[u],
            in_plane(plus(plane, unit_offset(column, u))),
        )

    for u in range(1, UNITS):
        unit_copy(u).start()

    @pl.when(jnp.logical_not(stays))
    def _():
        unit_copy(0).start()

    @pl.when(stays)
    def _():
        pltpu.make_async_copy(cache_ref.at[pl.ds(0, UNIT)], rows_in.at[0], a_recv.at[0]).start()

    by_source = (keys_in, values_in)

    def column_copy(part, step):
        target = around(column + step)
        at = pl.ds(pl.multiple_of(lax.rem(target, 8) * WIDTH + part * HD, HD), HD)
        return remote(
            rows_in.at[:, :, at], by_source[part].at[column], b_send.at[part], b_recv.at[part], in_column(target)
        )

    def send_heads(part):
        def send(i, carry):
            column_copy(part, column_step(i)).start()
            return carry

        lax.fori_loop(1, RING, send, 0)
        by_source[part][column] = rows_in[:, :, pl.ds(pl.multiple_of(head * WIDTH + part * HD, HD), HD)]

    gathered = (keys_ref, values_ref)

    def chunk_copy(part, step):
        return remote(
            staged.at[part, step],
            gathered[part].at[step],
            c_send.at[part],
            c_recv.at[part],
            in_plane(plus(plane, step)),
        )

    def send_chunks(part):
        def take(step):
            prompt = wanted[step]
            units = []
            for odd in range(2):
                across = lax.rem(lax.div(plane, 4) + 4 - lax.div(prompt, 2), 4)
                along = lax.rem(plane + 4 - 2 * lax.rem(prompt, 2) - odd, 4)
                first = lax.rem(along + 4 - across, 4)
                for i in range(4):
                    units.append(by_source[part][4 * i + first, across])
            return jnp.concatenate(units, axis=0)

        all_at_once(by_source[part], b_recv.at[part])
        for step in OFFSETS:
            staged[part, step] = take(step)
            chunk_copy(part, step).start()
        gathered[part][0] = take(0)

    ends = []
    for i in range(PROMPTS):
        ends.append(counts_ref[i] + (ends[-1] if ends else 0))
    prompts = []
    for step in range(RING):
        response = response_ref[2 * plus(plane, step) + half]
        group = jnp.int32(0)
        for end in ends[:-1]:
            group = group + (end <= response).astype(jnp.int32)
        prompts.append(prompt_slot_ref[group])
        wanted[step] = prompts[-1]

    for u in range(UNITS):
        unit_copy(u).wait_recv()
    send_heads(0)
    send_heads(1)
    send_chunks(0)
    send_chunks(1)
    for part in range(2):
        all_at_once(gathered[part], c_recv.at[part])
        all_at_once(by_source[part], b_send.at[part])
        all_at_once(staged.at[part], c_send.at[part])
    for u in range(1, UNITS):
        unit_copy(u).wait_send()

    @pl.when(jnp.logical_not(stays))
    def _():
        unit_copy(0).wait_send()


def attend_kernel(
    len_ref,
    code_ref,
    q_ref,
    go_ref,
    keys_ref,
    values_ref,
    own_ref,
    dq_ref,
    grads_ref,
    down_ref,
    q_in,
    go_in,
    own_in,
    keys,
    values,
    turned,
    q_rows,
    cot_rows,
    scores,
    changes,
    raw,
    change,
    q_grads,
    grads,
    own_grads,
    in_sem,
    out_sem,
):
    loads = [
        pltpu.make_async_copy(q_ref, q_in, in_sem.at[0]),
        pltpu.make_async_copy(go_ref, go_in, in_sem.at[1]),
        pltpu.make_async_copy(own_ref, own_in, in_sem.at[2]),
        pltpu.make_async_copy(keys_ref, keys.at[pl.ds(0, PLEN)], in_sem.at[3]),
        pltpu.make_async_copy(values_ref, values.at[pl.ds(0, PLEN)], in_sem.at[4]),
    ]
    for load in loads:
        load.start()
    for load in loads:
        load.wait()
    keys[PLEN:] = own_in[:, :HD]
    values[PLEN:] = own_in[:, HD:]
    turned[...] = jnp.transpose(keys[...])
    position = lax.broadcasted_iota(jnp.int32, (RLEN, HD), 0)
    factor = jnp.where(position < len_ref[0], code_ref[0].astype(F32) / 8.0, 0.0)
    blocks = [slice(b * BLOCK, (b + 1) * BLOCK) for b in range(BLOCKS)]

    def pair(i, carry):
        heads = []
        for way in range(2):
            j = 2 * i + way
            columns = pl.ds(pl.multiple_of(j * HD, HD), HD)
            rows = pl.ds(pl.multiple_of(j * RLEN, RLEN), RLEN)
            query = q_in[:, columns]
            q_rows[rows] = query
            cotangent = (go_in[:, columns].astype(F32) * factor).astype(BF16).astype(F32)
            heads.append((way, rows, columns, jnp.transpose(query), jnp.transpose(cotangent)))

        def score(head):
            way, _, _, q_cols, _ = head
            top = None
            for at in blocks:
                part = dot(keys[at], q_cols)
                if at is blocks[-1]:
                    key_at = lax.broadcasted_iota(jnp.int32, (BLOCK, RLEN), 0)
                    seen_from = lax.broadcasted_iota(jnp.int32, (BLOCK, RLEN), 1)
                    part = jnp.where(key_at <= seen_from, part, -1e30)
                scores[way, at] = part
                high = fold(part, jnp.max)
                top = high if top is None else jnp.maximum(top, high)
            return jnp.max(top, axis=0, keepdims=True)

        def weigh(head, highest):
            way, rows, _, _, cot_cols = head
            total = None
            for at in blocks:
                weights = jnp.exp2((scores[way, at] - highest) * (SCALE * LOG2E))
                raw[at, rows] = weights.astype(BF16)
                scores[way, at] = weights
                low = fold(weights, jnp.sum)
                total = low if total is None else total + low
            over = 1.0 / jnp.sum(total, axis=0, keepdims=True)
            scaled = cot_cols * over
            cot_rows[rows] = jnp.transpose(scaled).astype(BF16)
            return over, scaled.astype(BF16)

        def by_value(head, over, scaled):
            way = head[0]
            delta = None
            for at in blocks:
                grad = dot(values[at], scaled)
                changes[way, at] = grad
                term = fold(grad * scores[way, at], jnp.sum)
                delta = term if delta is None else delta + term
            return jnp.sum(delta, axis=0, keepdims=True) * over

        def by_key(head, delta):
            way, rows, columns, _, _ = head
            for at in blocks:
                change[at, rows] = (scores[way, at] * (changes[way, at] - delta)).astype(BF16)
            grad = dot(turned[...], change[:, rows])
            q_grads[:, columns] = (jnp.transpose(grad) * SCALE).astype(BF16)

        tops = [score(head) for head in heads]
        scaled = [weigh(head, top) for head, top in zip(heads, tops)]
        deltas = [by_value(head, over, cot) for head, (over, cot) in zip(heads, scaled)]
        for head, delta in zip(heads, deltas):
            by_key(head, delta)
        return carry

    lax.fori_loop(0, HEADS // 2, pair, 0)
    q_out = pltpu.make_async_copy(q_grads, dq_ref, out_sem.at[0])
    q_out.start()

    def block_grads(b, carry):
        at = pl.ds(pl.multiple_of(b * BLOCK, BLOCK), BLOCK)
        key_grad = (dot(change[at], q_rows[...]) * SCALE).astype(BF16)
        value_grad = dot(raw[at], cot_rows[...]).astype(BF16)
        for i in range(BLOCK // CHUNK):
            part = slice(i * CHUNK, (i + 1) * CHUNK)
            grads[0, b * (BLOCK // CHUNK) + i] = key_grad[part]
            grads[1, b * (BLOCK // CHUNK) + i] = value_grad[part]
        return carry

    lax.fori_loop(0, BLOCKS - 1, block_grads, 0)
    grads_out = pltpu.make_async_copy(grads, grads_ref, out_sem.at[1])
    grads_out.start()
    own_grads[:, :HD] = (dot(change[PLEN:], q_rows[...]) * SCALE).astype(BF16)
    own_grads[:, HD:] = dot(raw[PLEN:], cot_rows[...]).astype(BF16)
    own_out = pltpu.make_async_copy(own_grads, down_ref, out_sem.at[2])
    own_out.start()
    for out in (q_out, grads_out, own_out):
        out.wait()


def finish_kernel(back_ref, out_ref):
    for h in range(8):
        for part in range(2):
            out_ref[:, h * WIDTH + part * HD : h * WIDTH + (part + 1) * HD] = back_ref[part, :, head_columns(h)]


def return_kernel(
    counts_ref,
    prompt_slot_ref,
    response_ref,
    grads,
    back_ref,
    previous,
    last,
    terms,
    running,
    summed,
    sorted_sums,
    parts,
    final,
    rc_send,
    rc_recv,
    rb_send,
    rb_recv,
    ra_send,
    ra_recv,
):
    here = Place()
    plane, half, head, column = here.plane, here.half, here.head, here.column
    in_plane, in_column = here.in_plane, here.in_column
    here.greet()

    stays = lax.rem(column, 4) == 0

    def return_copy(part, step):
        return remote(
            grads.at[part, step], terms.at[part, step], rc_send.at[part], rc_recv.at[part], in_plane(minus(plane, step))
        )

    for part in (1, 0):
        for step in OFFSETS:
            return_copy(part, step).start()

    ends = []
    for i in range(PROMPTS):
        ends.append(counts_ref[i] + (ends[-1] if ends else 0))
    prompts = []
    for step in range(RING):
        response = response_ref[2 * plus(plane, step) + half]
        group = jnp.int32(0)
        for end in ends[:-1]:
            group = group + (end <= response).astype(jnp.int32)
        prompts.append(prompt_slot_ref[group])
    for step in range(RING):
        found = jnp.int32(RING)
        for other in range(step):
            found = jnp.where(prompts[other] == prompts[step], other, found)
        previous[step] = found
    for prompt in range(PROMPTS):
        found = jnp.int32(RING)
        for step in range(RING):
            found = jnp.where(prompts[step] == prompt, step, found)
        last[prompt] = found

    running[RING] = jnp.zeros((CHUNK, HD), F32)

    def return_column(part, step):
        target = around(column + step)
        return remote(
            sorted_sums.at[part, target],
            parts.at[part, column],
            rb_send.at[part],
            rb_recv.at[part],
            in_column(target),
        )

    def add_up(part):
        all_at_once(grads.at[part], rc_recv.at[part])
        terms[part, 0] = grads[part, 0]

        def add(step, carry):
            running[step] = running[previous[step]] + terms[part, step].astype(F32)
            return carry

        lax.fori_loop(0, RING, add, 0)

        def close(prompt, carry):
            summed[prompt] = running[last[prompt]].astype(BF16)
            return carry

        lax.fori_loop(0, PROMPTS, close, 0)

        def sort(target):
            for u in range(UNITS):
                source = minus(plane, unit_offset(target, u))
                unit = lax.rem(source, 2) * 4 + target // 4
                sorted_sums[part, target, u * UNIT : (u + 1) * UNIT] = summed[
                    source // 2, pl.ds(pl.multiple_of(unit * UNIT, UNIT), UNIT)
                ]

        def send(i, carry):
            step = column_step(i)
            sort(around(column + step))
            return_column(part, step).start()
            return carry

        lax.fori_loop(1, RING, send, 0)
        sort(column)
        parts[part, column] = sorted_sums[part, column]

    def return_unit(part, u):
        return remote(
            final.at[part, pl.ds(u * UNIT, UNIT)],
            back_ref.at[part, pl.ds(u * UNIT, UNIT)],
            ra_send.at[part, u],
            ra_recv.at[part, u],
            in_plane(minus(plane, unit_offset(column, u))),
        )

    def return_stay(part):
        return pltpu.make_async_copy(
            final.at[part, pl.ds(0, UNIT)], back_ref.at[part, pl.ds(0, UNIT)], ra_recv.at[part, 0]
        )

    def return_rows(part):
        all_at_once(parts.at[part], rb_recv.at[part])
        for h in range(8):
            both = parts[part, h].astype(F32) + parts[part, 8 + h].astype(F32)
            final[part, :, head_columns(h)] = both.astype(BF16)
        for u in range(1, UNITS):
            return_unit(part, u).start()

        @pl.when(jnp.logical_not(stays))
        def _():
            return_unit(part, 0).start()

        @pl.when(stays)
        def _():
            return_stay(part).start()

    for part in (1, 0):
        add_up(part)
    for part in (1, 0):
        return_rows(part)
    for part in range(2):
        all_at_once(grads.at[part], rc_send.at[part])
        all_at_once(parts.at[part], rb_send.at[part])
        for u in range(UNITS):
            return_unit(part, u).wait_recv()
        for u in range(1, UNITS):
            return_unit(part, u).wait_send()

    @pl.when(jnp.logical_not(stays))
    def _():
        return_unit(0, 0).wait_send()
        return_unit(1, 0).wait_send()


def local(
    queries, resp_kv, prompt_cache, grad_out, group_counts, prompt_slot, slot_response, resp_len, weight_code
):
    vmem = pl.BlockSpec(memory_space=pltpu.VMEM)
    smem = pl.BlockSpec(memory_space=pltpu.SMEM)
    hbm = pl.BlockSpec(memory_space=pltpu.HBM)

    def shape(*dims):
        return jax.ShapeDtypeStruct(dims, BF16)

    def params(number):
        return pltpu.CompilerParams(collective_id=number, has_side_effects=True, vmem_limit_bytes=VMEM_LIMIT)

    chunks = (RING, CHUNK, HD)
    rows = (RING, UNITS, UNIT, HD)
    keys, values = pl.pallas_call(
        gather_kernel,
        out_shape=[shape(*chunks)] * 2,
        in_specs=[smem] * 3 + [hbm],
        out_specs=[vmem] * 2,
        scratch_shapes=[
            pltpu.SMEM((RING,), jnp.int32),
            pltpu.VMEM((UNITS, UNIT, 8 * WIDTH), BF16),
            pltpu.VMEM(rows, BF16),
            pltpu.VMEM(rows, BF16),
            pltpu.VMEM((2,) + chunks, BF16),
            pltpu.SemaphoreType.DMA((UNITS,)),
            pltpu.SemaphoreType.DMA((UNITS,)),
        ]
        + [pltpu.SemaphoreType.DMA((2,))] * 4,
        compiler_params=params(0),
    )(group_counts, prompt_slot, slot_response, prompt_cache)

    dq, grads, down = pl.pallas_call(
        attend_kernel,
        out_shape=[shape(*queries.shape), shape(2, *chunks), shape(*resp_kv.shape)],
        in_specs=[smem] * 2 + [hbm] * 5,
        out_specs=[hbm] * 3,
        scratch_shapes=[
            pltpu.VMEM((RLEN, HEADS * HD), BF16),
            pltpu.VMEM((RLEN, HEADS * HD), BF16),
            pltpu.VMEM((RLEN, WIDTH), BF16),
            pltpu.VMEM((KEYS, HD), BF16),
            pltpu.VMEM((KEYS, HD), BF16),
            pltpu.VMEM((HD, KEYS), BF16),
            pltpu.VMEM((ROWS, HD), BF16),
            pltpu.VMEM((ROWS, HD), BF16),
            pltpu.VMEM((2, KEYS, RLEN), F32),
            pltpu.VMEM((2, KEYS, RLEN), F32),
            pltpu.VMEM((KEYS, ROWS), BF16),
            pltpu.VMEM((KEYS, ROWS), BF16),
            pltpu.VMEM((RLEN, HEADS * HD), BF16),
            pltpu.VMEM((2,) + chunks, BF16),
            pltpu.VMEM((RLEN, WIDTH), BF16),
            pltpu.SemaphoreType.DMA((5,)),
            pltpu.SemaphoreType.DMA((3,)),
        ],
        compiler_params=pltpu.CompilerParams(vmem_limit_bytes=VMEM_LIMIT),
    )(
        resp_len,
        weight_code,
        queries,
        grad_out,
        keys.reshape(PLEN, HD),
        values.reshape(PLEN, HD),
        resp_kv,
    )

    back = pl.pallas_call(
        return_kernel,
        out_shape=shape(2, UNITS * UNIT, 8 * HD),
        in_specs=[smem] * 3 + [vmem],
        out_specs=hbm,
        scratch_shapes=[
            pltpu.SMEM((RING,), jnp.int32),
            pltpu.SMEM((PROMPTS,), jnp.int32),
            pltpu.VMEM((2,) + chunks, BF16),
            pltpu.VMEM((RING + 1, CHUNK, HD), F32),
            pltpu.VMEM((PROMPTS, CHUNK, HD), BF16),
            pltpu.VMEM((2, RING, UNITS * UNIT, HD), BF16),
            pltpu.VMEM((2, RING, UNITS * UNIT, HD), BF16),
            pltpu.VMEM((2, UNITS * UNIT, 8 * HD), BF16),
        ]
        + [pltpu.SemaphoreType.DMA((2,))] * 4
        + [pltpu.SemaphoreType.DMA((2, UNITS))] * 2,
        compiler_params=params(1),
    )(group_counts, prompt_slot, slot_response, grads)
    grad_prompt_cache = pl.pallas_call(
        finish_kernel, out_shape=shape(*prompt_cache.shape), in_specs=[vmem], out_specs=vmem
    )(back)
    return dq, down, grad_prompt_cache


def solution(mesh):
    placed = (
        P("seq", "head"),
        P("seq", "head"),
        P(("seq", "head"), None),
        P("seq", "head"),
        P(),
        P(),
        P(),
        P("seq"),
        P("seq"),
    )
    return jax.shard_map(
        local,
        mesh=mesh,
        in_specs=placed,
        out_specs=(P("seq", "head"), P("seq", "head"), P(("seq", "head"), None)),
        check_vma=False,
    )
```

```python
import math

import jax
import jax.numpy as jnp
from jax import lax
from jax.experimental import pallas as pl
from jax.experimental.pallas import tpu as pltpu
from jax.sharding import PartitionSpec as P

HD = 128
PLEN = 2048
RLEN = 256
HEADS = 8
PROMPTS = 8
RING = 16
CHUNK = PLEN // RING
UNITS = 4
UNIT = 16
BLOCK = 256
BLOCKS = PLEN // BLOCK
PER_BLOCK = BLOCK // CHUNK
ROWS = HEADS * RLEN
KEYS = PLEN + RLEN
WIDTH = 2 * HD
SCALE = HD**-0.5
LOG2E = math.log2(math.e)
MESH = pl.DeviceIdType.MESH
VMEM_LIMIT = 60 * 1024 * 1024
NN = (((1,), (0,)), ((), ()))
F32 = jnp.float32
BF16 = jnp.bfloat16


OFFSETS = (10, 6, 9, 14, 11, 5, 15, 7, 13, 2, 8, 1, 4, 3, 12)


def around(index):
    return lax.rem(index + 2 * RING, RING)


def plus(plane, offset):
    return lax.rem(plane // 4 + offset // 4, 4) * 4 + lax.rem(plane + lax.rem(offset, 4), 4)


def minus(plane, offset):
    return lax.rem(plane // 4 + 4 - offset // 4, 4) * 4 + lax.rem(plane + 4 - lax.rem(offset, 4), 4)


def unit_offset(column, u):
    return 4 * u + lax.rem(column + u, 4)


def column_step(i):
    return 8 + (i // 2) * (1 - 2 * lax.rem(i, 2))


def head_rows(j):
    return slice(j * RLEN, (j + 1) * RLEN)


def head_columns(j):
    return slice(j * HD, (j + 1) * HD)


def chunk_rows(step):
    return pl.ds(pl.multiple_of(step * CHUNK, CHUNK), CHUNK)


def fold(values, op):
    return op(values.reshape(values.shape[0] // 8, 8, values.shape[1]), axis=0)


def dot(a, b):
    return lax.dot_general(a, b, NN, preferred_element_type=F32)


def kernel(
    counts_ref,
    prompt_slot_ref,
    response_ref,
    len_ref,
    code_ref,
    q_ref,
    own_ref,
    cache_ref,
    go_ref,
    dq_ref,
    down_ref,
    back_ref,
    wanted,
    previous,
    last,
    q_in,
    go_in,
    own_in,
    rows_in,
    keys_in,
    values_in,
    staged,
    keys,
    values,
    q_rows,
    q_cols,
    cot_cols,
    cot_scaled_cols,
    cot_scaled_rows,
    scores,
    raw,
    top,
    delta,
    inverse,
    dq_cols,
    grads,
    terms,
    running,
    summed,
    sorted_sums,
    parts,
    final,
    own_grads,
    q_grads,
    in_sem,
    a_send,
    a_recv,
    b_send,
    b_recv,
    c_send,
    c_recv,
    rc_send,
    rc_recv,
    rb_send,
    rb_recv,
    ra_send,
    ra_recv,
):
    seq = lax.axis_index("seq")
    head = lax.axis_index("head")
    plane = seq // 2
    half = lax.rem(seq, 2)
    column = half * 8 + head

    def in_plane(other):
        return {"seq": 2 * other + half, "head": head}

    def in_column(other):
        return {"seq": 2 * plane + other // 8, "head": lax.rem(other, 8)}

    def remote(src, dst, send_sem, recv_sem, device):
        return pltpu.make_async_remote_copy(
            src_ref=src, dst_ref=dst, send_sem=send_sem, recv_sem=recv_sem, device_id=device, device_id_type=MESH
        )

    def all_at_once(buffer, sem):
        pltpu.make_async_copy(buffer.at[pl.ds(1, RING - 1)], buffer.at[pl.ds(1, RING - 1)], sem).wait()

    loads = [
        pltpu.make_async_copy(q_ref, q_in, in_sem.at[0]),
        pltpu.make_async_copy(go_ref, go_in, in_sem.at[1]),
        pltpu.make_async_copy(own_ref, own_in, in_sem.at[2]),
    ]
    for load in loads:
        load.start()

    barrier = pltpu.get_barrier_semaphore()

    def greet(step, carry):
        pl.semaphore_signal(barrier, inc=1, device_id=in_column(around(column + step)), device_id_type=MESH)
        pl.semaphore_signal(barrier, inc=1, device_id=in_plane(plus(plane, step)), device_id_type=MESH)
        return carry

    lax.fori_loop(1, RING, greet, 0)
    pl.semaphore_wait(barrier, 2 * (RING - 1))

    stays = lax.rem(column, 4) == 0

    def unit_copy(u):
        return remote(
            cache_ref.at[pl.ds(u * UNIT, UNIT)],
            rows_in.at[u],
            a_send.at[u],
            a_recv.at[u],
            in_plane(plus(plane, unit_offset(column, u))),
        )

    for u in range(1, UNITS):
        unit_copy(u).start()

    @pl.when(jnp.logical_not(stays))
    def _():
        unit_copy(0).start()

    @pl.when(stays)
    def _():
        pltpu.make_async_copy(cache_ref.at[pl.ds(0, UNIT)], rows_in.at[0], a_recv.at[0]).start()

    by_source = (keys_in, values_in)

    def column_copy(part, step):
        target = around(column + step)
        at = pl.ds(pl.multiple_of(lax.rem(target, 8) * WIDTH + part * HD, HD), HD)
        return remote(
            rows_in.at[:, :, at], by_source[part].at[column], b_send.at[part], b_recv.at[part], in_column(target)
        )

    def send_heads(part):
        def send(i, carry):
            column_copy(part, column_step(i)).start()
            return carry

        lax.fori_loop(1, RING, send, 0)
        by_source[part][column] = rows_in[:, :, pl.ds(pl.multiple_of(head * WIDTH + part * HD, HD), HD)]

    gathered = (keys, values)

    def chunk_copy(part, step):
        return remote(
            staged.at[part, step],
            gathered[part].at[chunk_rows(step)],
            c_send.at[part],
            c_recv.at[part, step],
            in_plane(plus(plane, step)),
        )

    def send_chunks(part):
        def take(step):
            prompt = wanted[step]
            units = []
            for odd in range(2):
                across = lax.rem(lax.div(plane, 4) + 4 - lax.div(prompt, 2), 4)
                along = lax.rem(plane + 4 - 2 * lax.rem(prompt, 2) - odd, 4)
                first = lax.rem(along + 4 - across, 4)
                for i in range(4):
                    units.append(by_source[part][4 * i + first, across])
            return jnp.concatenate(units, axis=0)

        all_at_once(by_source[part], b_recv.at[part])
        for step in OFFSETS:
            staged[part, step] = take(step)
            chunk_copy(part, step).start()
        gathered[part][:CHUNK] = take(0)

    ends = []
    for i in range(PROMPTS):
        ends.append(counts_ref[i] + (ends[-1] if ends else 0))
    prompts = []
    for step in range(RING):
        response = response_ref[2 * plus(plane, step) + half]
        group = jnp.int32(0)
        for end in ends[:-1]:
            group = group + (end <= response).astype(jnp.int32)
        prompts.append(prompt_slot_ref[group])
        wanted[step] = prompts[-1]
    for step in range(RING):
        found = jnp.int32(RING)
        for other in range(step):
            found = jnp.where(prompts[other] == prompts[step], other, found)
        previous[step] = found
    for prompt in range(PROMPTS):
        found = jnp.int32(RING)
        for step in range(RING):
            found = jnp.where(prompts[step] == prompt, step, found)
        last[prompt] = found

    for load in loads:
        load.wait()
    position = lax.broadcasted_iota(jnp.int32, (RLEN, HD), 0)
    factor = jnp.where(position < len_ref[0], code_ref[0].astype(F32) / 8.0, 0.0)
    for j in range(HEADS):
        query = q_in[:, head_columns(j)]
        q_rows[head_rows(j)] = query
        q_cols[:, head_rows(j)] = jnp.transpose(query)
        cotangent = go_in[:, head_columns(j)].astype(F32) * factor
        cot_cols[:, head_rows(j)] = jnp.transpose(cotangent).astype(BF16)
    keys[PLEN:] = own_in[:, :HD]
    values[PLEN:] = own_in[:, HD:]
    running[RING] = jnp.zeros((CHUNK, HD), F32)
    dq_cols[...] = jnp.zeros_like(dq_cols)

    def block_rows(b):
        return pl.ds(pl.multiple_of(b * BLOCK, BLOCK), BLOCK)

    def score(b, own):
        block = keys[block_rows(b)]
        for j in range(HEADS):
            at = head_rows(j)
            part = dot(block, q_cols[:, at])
            if own:
                key_at = lax.broadcasted_iota(jnp.int32, (BLOCK, RLEN), 0)
                seen_from = lax.broadcasted_iota(jnp.int32, (BLOCK, RLEN), 1)
                part = jnp.where(key_at <= seen_from, part, -1e30)
            scores[b, :, at] = part
            high = fold(part, jnp.max)
            top[:, at] = high if own else jnp.maximum(top[:, at], high)

    for u in range(UNITS):
        unit_copy(u).wait_recv()
    send_heads(0)
    send_heads(1)
    score(BLOCKS, True)
    send_chunks(0)
    send_chunks(1)

    def arrive(part, b):
        def one(i, carry):
            step = b * PER_BLOCK + i

            @pl.when(step > 0)
            def _():
                chunk_copy(part, step).wait_recv()

            return carry

        lax.fori_loop(0, PER_BLOCK, one, 0)

    def score_block(b, carry):
        arrive(0, b)
        score(b, False)
        return carry

    lax.fori_loop(0, BLOCKS, score_block, 0)

    for j in range(HEADS):
        at = head_rows(j)
        highest = jnp.max(top[:, at], axis=0, keepdims=True)

        def weigh(b, total):
            weights = jnp.exp2((scores[b, :, at] - highest) * (SCALE * LOG2E))
            raw[b, :, at] = weights.astype(BF16)
            return total + fold(weights, jnp.sum)

        total = lax.fori_loop(0, BLOCKS + 1, weigh, jnp.zeros((8, RLEN), F32))
        over = 1.0 / jnp.sum(total, axis=0, keepdims=True)
        inverse[:, at] = jnp.broadcast_to(over, (8, RLEN))
        scaled = cot_cols[:, at].astype(F32) * over
        cot_scaled_cols[:, at] = scaled.astype(BF16)
        cot_scaled_rows[at] = jnp.transpose(scaled).astype(BF16)

    def return_copy(part, step):
        return remote(
            grads.at[part, step],
            terms.at[part, step],
            rc_send.at[part],
            rc_recv.at[part],
            in_plane(minus(plane, step)),
        )

    def send_back(part, b, block):
        for i in range(PER_BLOCK):
            grads[part, b * PER_BLOCK + i] = block[i * CHUNK : (i + 1) * CHUNK]

        def one(i, carry):
            step = b * PER_BLOCK + i

            @pl.when(step > 0)
            def _():
                return_copy(part, step).start()

            return carry

        lax.fori_loop(0, PER_BLOCK, one, 0)

    def value_grads(b):
        return dot(raw[b], cot_scaled_rows[...]).astype(BF16)

    def value_block(b, carry):
        send_back(1, b, value_grads(b))
        return carry

    lax.fori_loop(0, BLOCKS, value_block, 0)

    def look(b, first):
        block = values[block_rows(b)]
        for j in range(HEADS):
            at = head_rows(j)
            grad = dot(block, cot_scaled_cols[:, at])
            scores[b, :, at] = grad
            term = fold(grad * raw[b, :, at].astype(F32), jnp.sum)
            delta[:, at] = term if first else delta[:, at] + term

    def look_block(b, carry):
        arrive(1, b)
        look(b, False)
        return carry

    look(BLOCKS, True)
    lax.fori_loop(0, BLOCKS, look_block, 0)
    for j in range(HEADS):
        at = head_rows(j)
        delta[:, at] = jnp.sum(delta[:, at], axis=0, keepdims=True) * inverse[:, at]

    def key_part(b):
        turned = jnp.transpose(keys[block_rows(b)])
        for j in range(HEADS):
            at = head_rows(j)
            weights = raw[b, :, at].astype(F32)
            shift = delta[0:1, at]
            change = (weights * (scores[b, :, at] - shift)).astype(BF16)
            raw[b, :, at] = change
            dq_cols[:, at] += dot(turned, change)
        return (dot(raw[b], q_rows[...]) * SCALE).astype(BF16)

    def key_block(b, carry):
        send_back(0, b, key_part(b))
        return carry

    lax.fori_loop(0, 4, key_block, 0)

    def return_column(part, step):
        target = around(column + step)
        return remote(
            sorted_sums.at[part, target],
            parts.at[part, column],
            rb_send.at[part],
            rb_recv.at[part],
            in_column(target),
        )

    def add_up(part):
        all_at_once(grads.at[part], rc_recv.at[part])
        terms[part, 0] = grads[part, 0]

        def add(step, carry):
            running[step] = running[previous[step]] + terms[part, step].astype(F32)
            return carry

        lax.fori_loop(0, RING, add, 0)

        def close(prompt, carry):
            summed[prompt] = running[last[prompt]].astype(BF16)
            return carry

        lax.fori_loop(0, PROMPTS, close, 0)

        def sort(target):
            for u in range(UNITS):
                source = minus(plane, unit_offset(target, u))
                unit = lax.rem(source, 2) * 4 + target // 4
                sorted_sums[part, target, u * UNIT : (u + 1) * UNIT] = summed[
                    source // 2, pl.ds(pl.multiple_of(unit * UNIT, UNIT), UNIT)
                ]

        def send(i, carry):
            step = column_step(i)
            sort(around(column + step))
            return_column(part, step).start()
            return carry

        lax.fori_loop(1, RING, send, 0)
        sort(column)
        parts[part, column] = sorted_sums[part, column]

    def return_unit(part, u):
        return remote(
            final.at[part, pl.ds(u * UNIT, UNIT)],
            back_ref.at[part, pl.ds(u * UNIT, UNIT)],
            ra_send.at[part, u],
            ra_recv.at[part, u],
            in_plane(minus(plane, unit_offset(column, u))),
        )

    def return_stay(part):
        return pltpu.make_async_copy(
            final.at[part, pl.ds(0, UNIT)], back_ref.at[part, pl.ds(0, UNIT)], ra_recv.at[part, 0]
        )

    def return_rows(part):
        all_at_once(parts.at[part], rb_recv.at[part])
        for h in range(8):
            both = parts[part, h].astype(F32) + parts[part, 8 + h].astype(F32)
            final[part, :, head_columns(h)] = both.astype(BF16)
        for u in range(1, UNITS):
            return_unit(part, u).start()

        @pl.when(jnp.logical_not(stays))
        def _():
            return_unit(part, 0).start()

        @pl.when(stays)
        def _():
            return_stay(part).start()

    add_up(1)
    lax.fori_loop(4, BLOCKS, key_block, 0)

    own_grads[:, HD:] = value_grads(BLOCKS)
    own_grads[:, :HD] = key_part(BLOCKS)
    own_out = pltpu.make_async_copy(own_grads, down_ref, in_sem.at[2])
    own_out.start()
    return_rows(1)
    for j in range(HEADS):
        q_grads[:, head_columns(j)] = (jnp.transpose(dq_cols[:, head_rows(j)]) * SCALE).astype(BF16)
    q_out = pltpu.make_async_copy(q_grads, dq_ref, in_sem.at[0])
    q_out.start()
    add_up(0)
    return_rows(0)

    own_out.wait()
    q_out.wait()
    for part in range(2):
        all_at_once(by_source[part], b_send.at[part])
        all_at_once(staged.at[part], c_send.at[part])
        all_at_once(grads.at[part], rc_send.at[part])
        all_at_once(parts.at[part], rb_send.at[part])
        for u in range(UNITS):
            return_unit(part, u).wait_recv()
        for u in range(1, UNITS):
            return_unit(part, u).wait_send()
    for u in range(1, UNITS):
        unit_copy(u).wait_send()

    @pl.when(jnp.logical_not(stays))
    def _():
        unit_copy(0).wait_send()
        return_unit(0, 0).wait_send()
        return_unit(1, 0).wait_send()


def finish_kernel(dq_ref, down_ref, back_ref, dq_out, down_out, dcache_out, dq, down, back, total, get_sems, put_sems):
    gets = [
        pltpu.make_async_copy(back_ref, back, get_sems.at[0]),
        pltpu.make_async_copy(dq_ref, dq, get_sems.at[1]),
        pltpu.make_async_copy(down_ref, down, get_sems.at[2]),
    ]
    puts = [
        pltpu.make_async_copy(total, dcache_out, put_sems.at[0]),
        pltpu.make_async_copy(dq, dq_out, put_sems.at[1]),
        pltpu.make_async_copy(down, down_out, put_sems.at[2]),
    ]
    for get in gets:
        get.start()
    gets[0].wait()
    for h in range(8):
        for part in range(2):
            total[:, h * WIDTH + part * HD : h * WIDTH + (part + 1) * HD] = back[part, :, head_columns(h)]
    puts[0].start()
    for get, put in zip(gets[1:], puts[1:]):
        get.wait()
        put.start()
    for put in puts:
        put.wait()


def local(
    queries, resp_kv, prompt_cache, grad_out, group_counts, prompt_slot, slot_response, resp_len, weight_code
):
    smem = pl.BlockSpec(memory_space=pltpu.SMEM)
    hbm = pl.BlockSpec(memory_space=pltpu.HBM)
    scratch = [
        pltpu.SMEM((RING,), jnp.int32),
        pltpu.SMEM((RING,), jnp.int32),
        pltpu.SMEM((PROMPTS,), jnp.int32),
        pltpu.VMEM((RLEN, HEADS * HD), BF16),
        pltpu.VMEM((RLEN, HEADS * HD), BF16),
        pltpu.VMEM((RLEN, WIDTH), BF16),
        pltpu.VMEM((UNITS, UNIT, 8 * WIDTH), BF16),
        pltpu.VMEM((RING, UNITS, UNIT, HD), BF16),
        pltpu.VMEM((RING, UNITS, UNIT, HD), BF16),
        pltpu.VMEM((2, RING, CHUNK, HD), BF16),
        pltpu.VMEM((KEYS, HD), BF16),
        pltpu.VMEM((KEYS, HD), BF16),
        pltpu.VMEM((ROWS, HD), BF16),
        pltpu.VMEM((HD, ROWS), BF16),
        pltpu.VMEM((HD, ROWS), BF16),
        pltpu.VMEM((HD, ROWS), BF16),
        pltpu.VMEM((ROWS, HD), BF16),
        pltpu.VMEM((BLOCKS + 1, BLOCK, ROWS), F32),
        pltpu.VMEM((BLOCKS + 1, BLOCK, ROWS), BF16),
        pltpu.VMEM((8, ROWS), F32),
        pltpu.VMEM((8, ROWS), F32),
        pltpu.VMEM((8, ROWS), F32),
        pltpu.VMEM((HD, ROWS), F32),
        pltpu.VMEM((2, RING, CHUNK, HD), BF16),
        pltpu.VMEM((2, RING, CHUNK, HD), BF16),
        pltpu.VMEM((RING + 1, CHUNK, HD), F32),
        pltpu.VMEM((PROMPTS, CHUNK, HD), BF16),
        pltpu.VMEM((2, RING, UNITS * UNIT, HD), BF16),
        pltpu.VMEM((2, RING, UNITS * UNIT, HD), BF16),
        pltpu.VMEM((2, UNITS * UNIT, 8 * HD), BF16),
        pltpu.VMEM((RLEN, WIDTH), BF16),
        pltpu.VMEM((RLEN, HEADS * HD), BF16),
        pltpu.SemaphoreType.DMA((3,)),
        pltpu.SemaphoreType.DMA((UNITS,)),
        pltpu.SemaphoreType.DMA((UNITS,)),
        pltpu.SemaphoreType.DMA((2,)),
        pltpu.SemaphoreType.DMA((2,)),
        pltpu.SemaphoreType.DMA((2,)),
        pltpu.SemaphoreType.DMA((2, RING)),
        pltpu.SemaphoreType.DMA((2,)),
        pltpu.SemaphoreType.DMA((2,)),
        pltpu.SemaphoreType.DMA((2,)),
        pltpu.SemaphoreType.DMA((2,)),
        pltpu.SemaphoreType.DMA((2, UNITS)),
        pltpu.SemaphoreType.DMA((2, UNITS)),
    ]
    products = 5 * ROWS * KEYS * HD
    dq, down, back = pl.pallas_call(
        kernel,
        out_shape=[
            jax.ShapeDtypeStruct(queries.shape, BF16),
            jax.ShapeDtypeStruct(resp_kv.shape, BF16),
            jax.ShapeDtypeStruct((2, UNITS * UNIT, 8 * HD), BF16),
        ],
        in_specs=[smem] * 5 + [hbm] * 4,
        out_specs=[hbm] * 3,
        scratch_shapes=scratch,
        compiler_params=pltpu.CompilerParams(
            collective_id=0, has_side_effects=True, vmem_limit_bytes=VMEM_LIMIT
        ),
        cost_estimate=pl.CostEstimate(flops=2 * products, bytes_accessed=3 << 20, transcendentals=ROWS * KEYS),
    )(
        group_counts,
        prompt_slot,
        slot_response,
        resp_len,
        weight_code,
        queries,
        resp_kv,
        prompt_cache,
        grad_out,
    )
    return pl.pallas_call(
        finish_kernel,
        out_shape=[
            jax.ShapeDtypeStruct(queries.shape, BF16),
            jax.ShapeDtypeStruct(resp_kv.shape, BF16),
            jax.ShapeDtypeStruct(prompt_cache.shape, BF16),
        ],
        in_specs=[hbm] * 3,
        out_specs=[hbm] * 3,
        scratch_shapes=[
            pltpu.VMEM(queries.shape, BF16),
            pltpu.VMEM(resp_kv.shape, BF16),
            pltpu.VMEM((2, UNITS * UNIT, 8 * HD), BF16),
            pltpu.VMEM(prompt_cache.shape, BF16),
            pltpu.SemaphoreType.DMA((3,)),
            pltpu.SemaphoreType.DMA((3,)),
        ],
        compiler_params=pltpu.CompilerParams(vmem_limit_bytes=VMEM_LIMIT),
    )(dq, down, back)


def solution(mesh):
    placed = (
        P("seq", "head"),
        P("seq", "head"),
        P(("seq", "head"), None),
        P("seq", "head"),
        P(),
        P(),
        P(),
        P("seq"),
        P("seq"),
    )
    return jax.shard_map(
        local,
        mesh=mesh,
        in_specs=placed,
        out_specs=(P("seq", "head"), P("seq", "head"), P(("seq", "head"), None)),
        check_vma=False,
    )
```

```python
import math

import jax
import jax.numpy as jnp
from jax import lax
from jax.experimental import pallas as pl
from jax.experimental.pallas import tpu as pltpu
from jax.sharding import PartitionSpec as P

HD = 128
PLEN = 2048
RLEN = 256
HEADS = 8
PROMPTS = 8
RING = 16
CHUNK = PLEN // RING
UNITS = 4
UNIT = 16
BLOCK = 256
BLOCKS = PLEN // BLOCK
PER_BLOCK = BLOCK // CHUNK
ROWS = HEADS * RLEN
KEYS = PLEN + RLEN
WIDTH = 2 * HD
SCALE = HD**-0.5
LOG2E = math.log2(math.e)
MESH = pl.DeviceIdType.MESH
VMEM_LIMIT = 60 * 1024 * 1024
NN = (((1,), (0,)), ((), ()))
F32 = jnp.float32
BF16 = jnp.bfloat16


def around(index):
    return lax.rem(index + 2 * RING, RING)


def plus(plane, offset):
    return lax.rem(plane // 4 + offset // 4, 4) * 4 + lax.rem(plane + lax.rem(offset, 4), 4)


def minus(plane, offset):
    return lax.rem(plane // 4 + 4 - offset // 4, 4) * 4 + lax.rem(plane + 4 - lax.rem(offset, 4), 4)


def turn(place):
    return 5 * place % RING if isinstance(place, int) else lax.rem(5 * place, RING)


def unit_offset(column, u):
    return 4 * u + lax.rem(column + u, 4)


def column_step(i):
    return 8 + (i // 2) * (1 - 2 * lax.rem(i, 2))


def head_rows(j):
    return slice(j * RLEN, (j + 1) * RLEN)


def head_columns(j):
    return slice(j * HD, (j + 1) * HD)


def chunk_rows(step):
    return pl.ds(pl.multiple_of(step * CHUNK, CHUNK), CHUNK)


def fold(values, op):
    return op(values.reshape(values.shape[0] // 8, 8, values.shape[1]), axis=0)


def dot(a, b):
    return lax.dot_general(a, b, NN, preferred_element_type=F32)


def kernel(
    counts_ref,
    prompt_slot_ref,
    response_ref,
    len_ref,
    code_ref,
    q_ref,
    own_ref,
    cache_ref,
    go_ref,
    dq_ref,
    down_ref,
    back_ref,
    wanted,
    previous,
    last,
    q_in,
    go_in,
    own_in,
    rows_in,
    keys_in,
    values_in,
    staged,
    keys,
    values,
    q_rows,
    q_cols,
    cot_cols,
    cot_scaled_cols,
    cot_scaled_rows,
    scores,
    raw,
    top,
    delta,
    inverse,
    dq_cols,
    dv_sum,
    grads,
    terms,
    running,
    summed,
    sorted_sums,
    parts,
    final,
    own_grads,
    q_grads,
    in_sem,
    a_send,
    a_recv,
    b_send,
    b_recv,
    c_send,
    c_recv,
    rc_send,
    rc_recv,
    rb_send,
    rb_recv,
    ra_send,
    ra_recv,
):
    seq = lax.axis_index("seq")
    head = lax.axis_index("head")
    plane = seq // 2
    half = lax.rem(seq, 2)
    column = half * 8 + head

    def in_plane(other):
        return {"seq": 2 * other + half, "head": head}

    def in_column(other):
        return {"seq": 2 * plane + other // 8, "head": lax.rem(other, 8)}

    def remote(src, dst, send_sem, recv_sem, device):
        return pltpu.make_async_remote_copy(
            src_ref=src, dst_ref=dst, send_sem=send_sem, recv_sem=recv_sem, device_id=device, device_id_type=MESH
        )

    def all_at_once(buffer, sem):
        pltpu.make_async_copy(buffer.at[pl.ds(1, RING - 1)], buffer.at[pl.ds(1, RING - 1)], sem).wait()

    loads = [
        pltpu.make_async_copy(q_ref, q_in, in_sem.at[0]),
        pltpu.make_async_copy(go_ref, go_in, in_sem.at[1]),
        pltpu.make_async_copy(own_ref, own_in, in_sem.at[2]),
    ]
    for load in loads:
        load.start()

    barrier = pltpu.get_barrier_semaphore()

    def greet(step, carry):
        pl.semaphore_signal(barrier, inc=1, device_id=in_column(around(column + step)), device_id_type=MESH)
        pl.semaphore_signal(barrier, inc=1, device_id=in_plane(plus(plane, step)), device_id_type=MESH)
        return carry

    lax.fori_loop(1, RING, greet, 0)
    pl.semaphore_wait(barrier, 2 * (RING - 1))

    stays = lax.rem(column, 4) == 0

    def unit_copy(u):
        return remote(
            cache_ref.at[pl.ds(u * UNIT, UNIT)],
            rows_in.at[u],
            a_send.at[u],
            a_recv.at[u],
            in_plane(plus(plane, unit_offset(column, u))),
        )

    for u in range(1, UNITS):
        unit_copy(u).start()

    @pl.when(jnp.logical_not(stays))
    def _():
        unit_copy(0).start()

    @pl.when(stays)
    def _():
        pltpu.make_async_copy(cache_ref.at[pl.ds(0, UNIT)], rows_in.at[0], a_recv.at[0]).start()

    by_source = (keys_in, values_in)

    def column_copy(part, step):
        target = around(column + step)
        at = pl.ds(pl.multiple_of(lax.rem(target, 8) * WIDTH + part * HD, HD), HD)
        return remote(
            rows_in.at[:, :, at], by_source[part].at[column], b_send.at[part], b_recv.at[part], in_column(target)
        )

    def send_heads(part):
        def send(i, carry):
            column_copy(part, column_step(i)).start()
            return carry

        lax.fori_loop(1, RING, send, 0)
        by_source[part][column] = rows_in[:, :, pl.ds(pl.multiple_of(head * WIDTH + part * HD, HD), HD)]

    gathered = (keys, values)

    def chunk_copy(part, step):
        return remote(
            staged.at[part, step],
            gathered[part].at[chunk_rows(step)],
            c_send.at[part],
            c_recv.at[part, step],
            in_plane(plus(plane, turn(step))),
        )

    def send_chunks(part):
        def take(step):
            prompt = wanted[step]
            units = []
            for odd in range(2):
                across = lax.rem(lax.div(plane, 4) + 4 - lax.div(prompt, 2), 4)
                along = lax.rem(plane + 4 - 2 * lax.rem(prompt, 2) - odd, 4)
                first = lax.rem(along + 4 - across, 4)
                for i in range(4):
                    units.append(by_source[part][4 * i + first, across])
            return jnp.concatenate(units, axis=0)

        all_at_once(by_source[part], b_recv.at[part])
        for step in range(1, RING):
            staged[part, step] = take(step)
            chunk_copy(part, step).start()
        gathered[part][:CHUNK] = take(0)

    ends = []
    for i in range(PROMPTS):
        ends.append(counts_ref[i] + (ends[-1] if ends else 0))
    prompts = []
    for step in range(RING):
        response = response_ref[2 * plus(plane, turn(step)) + half]
        group = jnp.int32(0)
        for end in ends[:-1]:
            group = group + (end <= response).astype(jnp.int32)
        prompts.append(prompt_slot_ref[group])
        wanted[step] = prompts[-1]
    for step in range(RING):
        found = jnp.int32(RING)
        for other in range(step):
            found = jnp.where(prompts[other] == prompts[step], other, found)
        previous[step] = found
    for prompt in range(PROMPTS):
        found = jnp.int32(RING)
        for step in range(RING):
            found = jnp.where(prompts[step] == prompt, step, found)
        last[prompt] = found

    for load in loads:
        load.wait()
    position = lax.broadcasted_iota(jnp.int32, (RLEN, HD), 0)
    factor = jnp.where(position < len_ref[0], code_ref[0].astype(F32) / 8.0, 0.0)
    for j in range(HEADS):
        query = q_in[:, head_columns(j)]
        q_rows[head_rows(j)] = query
        q_cols[:, head_rows(j)] = jnp.transpose(query)
        cotangent = go_in[:, head_columns(j)].astype(F32) * factor
        cot_cols[:, head_rows(j)] = jnp.transpose(cotangent).astype(BF16)
    keys[PLEN:] = own_in[:, :HD]
    values[PLEN:] = own_in[:, HD:]
    running[RING] = jnp.zeros((CHUNK, HD), F32)
    dq_cols[...] = jnp.zeros_like(dq_cols)

    def block_rows(b):
        return pl.ds(pl.multiple_of(b * BLOCK, BLOCK), BLOCK)

    def score(b, own):
        block = keys[block_rows(b)]
        for j in range(HEADS):
            at = head_rows(j)
            part = dot(block, q_cols[:, at])
            if own:
                key_at = lax.broadcasted_iota(jnp.int32, (BLOCK, RLEN), 0)
                seen_from = lax.broadcasted_iota(jnp.int32, (BLOCK, RLEN), 1)
                part = jnp.where(key_at <= seen_from, part, -1e30)
            scores[b, :, at] = part
            high = fold(part, jnp.max)
            top[:, at] = high if own else jnp.maximum(top[:, at], high)

    for u in range(UNITS):
        unit_copy(u).wait_recv()
    send_heads(0)
    send_heads(1)
    score(BLOCKS, True)
    send_chunks(0)
    send_chunks(1)

    def arrive(part, b):
        def one(i, carry):
            step = b * PER_BLOCK + i

            @pl.when(step > 0)
            def _():
                chunk_copy(part, step).wait_recv()

            return carry

        lax.fori_loop(0, PER_BLOCK, one, 0)

    def score_block(b, carry):
        arrive(0, b)
        score(b, False)
        return carry

    lax.fori_loop(0, BLOCKS, score_block, 0)

    def return_copy(part, step):
        return remote(
            grads.at[part, step],
            terms.at[part, step],
            rc_send.at[part],
            rc_recv.at[part],
            in_plane(minus(plane, turn(step))),
        )

    def send_back(part, b, block):
        for i in range(PER_BLOCK):
            grads[part, b * PER_BLOCK + i] = block[i * CHUNK : (i + 1) * CHUNK]

        def one(i, carry):
            step = b * PER_BLOCK + i

            @pl.when(step > 0)
            def _():
                return_copy(part, step).start()

            return carry

        lax.fori_loop(0, PER_BLOCK, one, 0)

    def pair_rows(p):
        return slice(2 * p * RLEN, 2 * (p + 1) * RLEN)

    def pair_grads(b, p):
        return dot(raw[b, :, pair_rows(p)], cot_scaled_rows[pair_rows(p)])

    for p in range(HEADS // 2):
        heads = (2 * p, 2 * p + 1)
        highest = [jnp.max(top[:, head_rows(j)], axis=0, keepdims=True) for j in heads]

        def weigh(b, totals):
            sums = []
            for j, high, total in zip(heads, highest, totals):
                at = head_rows(j)
                weights = jnp.exp2((scores[b, :, at] - high) * (SCALE * LOG2E))
                raw[b, :, at] = weights.astype(BF16)
                sums.append(total + fold(weights, jnp.sum))
            if p == 1:
                dv_sum[b] = pair_grads(b, 0)
            elif p > 1:
                dv_sum[b] += pair_grads(b, p - 1)
            return tuple(sums)

        totals = lax.fori_loop(0, BLOCKS + 1, weigh, (jnp.zeros((8, RLEN), F32),) * 2)
        for j, total in zip(heads, totals):
            at = head_rows(j)
            over = 1.0 / jnp.sum(total, axis=0, keepdims=True)
            inverse[:, at] = jnp.broadcast_to(over, (8, RLEN))
            scaled = cot_cols[:, at].astype(F32) * over
            cot_scaled_cols[:, at] = scaled.astype(BF16)
            cot_scaled_rows[at] = jnp.transpose(scaled).astype(BF16)

    def value_grads(b):
        return (dv_sum[b] + pair_grads(b, HEADS // 2 - 1)).astype(BF16)

    def value_block(b, carry):
        send_back(1, b, value_grads(b))
        return carry

    lax.fori_loop(0, BLOCKS, value_block, 0)

    def look(b, first):
        block = values[block_rows(b)]
        for j in range(HEADS):
            at = head_rows(j)
            grad = dot(block, cot_scaled_cols[:, at])
            scores[b, :, at] = grad
            term = fold(grad * raw[b, :, at].astype(F32), jnp.sum)
            delta[:, at] = term if first else delta[:, at] + term

    def look_block(b, carry):
        arrive(1, b)
        look(b, False)
        return carry

    look(BLOCKS, True)
    lax.fori_loop(0, BLOCKS, look_block, 0)
    for j in range(HEADS):
        at = head_rows(j)
        delta[:, at] = jnp.sum(delta[:, at], axis=0, keepdims=True) * inverse[:, at]

    def key_part(b):
        turned = jnp.transpose(keys[block_rows(b)])
        for j in range(HEADS):
            at = head_rows(j)
            weights = raw[b, :, at].astype(F32)
            shift = delta[0:1, at]
            change = (weights * (scores[b, :, at] - shift)).astype(BF16)
            raw[b, :, at] = change
            dq_cols[:, at] += dot(turned, change)
        return (dot(raw[b], q_rows[...]) * SCALE).astype(BF16)

    def key_block(b, carry):
        send_back(0, b, key_part(b))
        return carry

    lax.fori_loop(0, 4, key_block, 0)

    def return_column(part, step):
        target = around(column + step)
        return remote(
            sorted_sums.at[part, target],
            parts.at[part, column],
            rb_send.at[part],
            rb_recv.at[part],
            in_column(target),
        )

    def add_up(part):
        all_at_once(grads.at[part], rc_recv.at[part])
        terms[part, 0] = grads[part, 0]

        def add(step, carry):
            running[step] = running[previous[step]] + terms[part, step].astype(F32)
            return carry

        lax.fori_loop(0, RING, add, 0)

        def close(prompt, carry):
            summed[prompt] = running[last[prompt]].astype(BF16)
            return carry

        lax.fori_loop(0, PROMPTS, close, 0)

        def sort(target):
            for u in range(UNITS):
                source = minus(plane, unit_offset(target, u))
                unit = lax.rem(source, 2) * 4 + target // 4
                sorted_sums[part, target, u * UNIT : (u + 1) * UNIT] = summed[
                    source // 2, pl.ds(pl.multiple_of(unit * UNIT, UNIT), UNIT)
                ]

        def send(i, carry):
            step = column_step(i)
            sort(around(column + step))
            return_column(part, step).start()
            return carry

        lax.fori_loop(1, RING, send, 0)
        sort(column)
        parts[part, column] = sorted_sums[part, column]

    def return_unit(part, u):
        return remote(
            final.at[part, pl.ds(u * UNIT, UNIT)],
            back_ref.at[part, pl.ds(u * UNIT, UNIT)],
            ra_send.at[part, u],
            ra_recv.at[part, u],
            in_plane(minus(plane, unit_offset(column, u))),
        )

    def return_stay(part):
        return pltpu.make_async_copy(
            final.at[part, pl.ds(0, UNIT)], back_ref.at[part, pl.ds(0, UNIT)], ra_recv.at[part, 0]
        )

    def return_rows(part):
        all_at_once(parts.at[part], rb_recv.at[part])
        for h in range(8):
            both = parts[part, h].astype(F32) + parts[part, 8 + h].astype(F32)
            final[part, :, head_columns(h)] = both.astype(BF16)
        for u in range(1, UNITS):
            return_unit(part, u).start()

        @pl.when(jnp.logical_not(stays))
        def _():
            return_unit(part, 0).start()

        @pl.when(stays)
        def _():
            return_stay(part).start()

    add_up(1)
    lax.fori_loop(4, BLOCKS, key_block, 0)

    own_grads[:, HD:] = value_grads(BLOCKS)
    own_grads[:, :HD] = key_part(BLOCKS)
    own_out = pltpu.make_async_copy(own_grads, down_ref, in_sem.at[2])
    own_out.start()
    return_rows(1)
    for j in range(HEADS):
        q_grads[:, head_columns(j)] = (jnp.transpose(dq_cols[:, head_rows(j)]) * SCALE).astype(BF16)
    q_out = pltpu.make_async_copy(q_grads, dq_ref, in_sem.at[0])
    q_out.start()
    add_up(0)
    return_rows(0)

    own_out.wait()
    q_out.wait()
    for part in range(2):
        all_at_once(by_source[part], b_send.at[part])
        all_at_once(staged.at[part], c_send.at[part])
        all_at_once(grads.at[part], rc_send.at[part])
        all_at_once(parts.at[part], rb_send.at[part])
        for u in range(UNITS):
            return_unit(part, u).wait_recv()
        for u in range(1, UNITS):
            return_unit(part, u).wait_send()
    for u in range(1, UNITS):
        unit_copy(u).wait_send()

    @pl.when(jnp.logical_not(stays))
    def _():
        unit_copy(0).wait_send()
        return_unit(0, 0).wait_send()
        return_unit(1, 0).wait_send()


def finish_kernel(dq_ref, down_ref, back_ref, dq_out, down_out, dcache_out, dq, down, back, total, get_sems, put_sems):
    gets = [
        pltpu.make_async_copy(back_ref, back, get_sems.at[0]),
        pltpu.make_async_copy(dq_ref, dq, get_sems.at[1]),
        pltpu.make_async_copy(down_ref, down, get_sems.at[2]),
    ]
    puts = [
        pltpu.make_async_copy(total, dcache_out, put_sems.at[0]),
        pltpu.make_async_copy(dq, dq_out, put_sems.at[1]),
        pltpu.make_async_copy(down, down_out, put_sems.at[2]),
    ]
    for get in gets:
        get.start()
    gets[0].wait()
    for h in range(8):
        for part in range(2):
            total[:, h * WIDTH + part * HD : h * WIDTH + (part + 1) * HD] = back[part, :, head_columns(h)]
    puts[0].start()
    for get, put in zip(gets[1:], puts[1:]):
        get.wait()
        put.start()
    for put in puts:
        put.wait()


def local(
    queries, resp_kv, prompt_cache, grad_out, group_counts, prompt_slot, slot_response, resp_len, weight_code
):
    smem = pl.BlockSpec(memory_space=pltpu.SMEM)
    hbm = pl.BlockSpec(memory_space=pltpu.HBM)
    scratch = [
        pltpu.SMEM((RING,), jnp.int32),
        pltpu.SMEM((RING,), jnp.int32),
        pltpu.SMEM((PROMPTS,), jnp.int32),
        pltpu.VMEM((RLEN, HEADS * HD), BF16),
        pltpu.VMEM((RLEN, HEADS * HD), BF16),
        pltpu.VMEM((RLEN, WIDTH), BF16),
        pltpu.VMEM((UNITS, UNIT, 8 * WIDTH), BF16),
        pltpu.VMEM((RING, UNITS, UNIT, HD), BF16),
        pltpu.VMEM((RING, UNITS, UNIT, HD), BF16),
        pltpu.VMEM((2, RING, CHUNK, HD), BF16),
        pltpu.VMEM((KEYS, HD), BF16),
        pltpu.VMEM((KEYS, HD), BF16),
        pltpu.VMEM((ROWS, HD), BF16),
        pltpu.VMEM((HD, ROWS), BF16),
        pltpu.VMEM((HD, ROWS), BF16),
        pltpu.VMEM((HD, ROWS), BF16),
        pltpu.VMEM((ROWS, HD), BF16),
        pltpu.VMEM((BLOCKS + 1, BLOCK, ROWS), F32),
        pltpu.VMEM((BLOCKS + 1, BLOCK, ROWS), BF16),
        pltpu.VMEM((8, ROWS), F32),
        pltpu.VMEM((8, ROWS), F32),
        pltpu.VMEM((8, ROWS), F32),
        pltpu.VMEM((HD, ROWS), F32),
        pltpu.VMEM((BLOCKS + 1, BLOCK, HD), F32),
        pltpu.VMEM((2, RING, CHUNK, HD), BF16),
        pltpu.VMEM((2, RING, CHUNK, HD), BF16),
        pltpu.VMEM((RING + 1, CHUNK, HD), F32),
        pltpu.VMEM((PROMPTS, CHUNK, HD), BF16),
        pltpu.VMEM((2, RING, UNITS * UNIT, HD), BF16),
        pltpu.VMEM((2, RING, UNITS * UNIT, HD), BF16),
        pltpu.VMEM((2, UNITS * UNIT, 8 * HD), BF16),
        pltpu.VMEM((RLEN, WIDTH), BF16),
        pltpu.VMEM((RLEN, HEADS * HD), BF16),
        pltpu.SemaphoreType.DMA((3,)),
        pltpu.SemaphoreType.DMA((UNITS,)),
        pltpu.SemaphoreType.DMA((UNITS,)),
        pltpu.SemaphoreType.DMA((2,)),
        pltpu.SemaphoreType.DMA((2,)),
        pltpu.SemaphoreType.DMA((2,)),
        pltpu.SemaphoreType.DMA((2, RING)),
        pltpu.SemaphoreType.DMA((2,)),
        pltpu.SemaphoreType.DMA((2,)),
        pltpu.SemaphoreType.DMA((2,)),
        pltpu.SemaphoreType.DMA((2,)),
        pltpu.SemaphoreType.DMA((2, UNITS)),
        pltpu.SemaphoreType.DMA((2, UNITS)),
    ]
    products = 5 * ROWS * KEYS * HD
    dq, down, back = pl.pallas_call(
        kernel,
        out_shape=[
            jax.ShapeDtypeStruct(queries.shape, BF16),
            jax.ShapeDtypeStruct(resp_kv.shape, BF16),
            jax.ShapeDtypeStruct((2, UNITS * UNIT, 8 * HD), BF16),
        ],
        in_specs=[smem] * 5 + [hbm] * 4,
        out_specs=[hbm] * 3,
        scratch_shapes=scratch,
        compiler_params=pltpu.CompilerParams(
            collective_id=0, has_side_effects=True, vmem_limit_bytes=VMEM_LIMIT
        ),
        cost_estimate=pl.CostEstimate(flops=2 * products, bytes_accessed=3 << 20, transcendentals=ROWS * KEYS),
    )(
        group_counts,
        prompt_slot,
        slot_response,
        resp_len,
        weight_code,
        queries,
        resp_kv,
        prompt_cache,
        grad_out,
    )
    return pl.pallas_call(
        finish_kernel,
        out_shape=[
            jax.ShapeDtypeStruct(queries.shape, BF16),
            jax.ShapeDtypeStruct(resp_kv.shape, BF16),
            jax.ShapeDtypeStruct(prompt_cache.shape, BF16),
        ],
        in_specs=[hbm] * 3,
        out_specs=[hbm] * 3,
        scratch_shapes=[
            pltpu.VMEM(queries.shape, BF16),
            pltpu.VMEM(resp_kv.shape, BF16),
            pltpu.VMEM((2, UNITS * UNIT, 8 * HD), BF16),
            pltpu.VMEM(prompt_cache.shape, BF16),
            pltpu.SemaphoreType.DMA((3,)),
            pltpu.SemaphoreType.DMA((3,)),
        ],
        compiler_params=pltpu.CompilerParams(vmem_limit_bytes=VMEM_LIMIT),
    )(dq, down, back)


def solution(mesh):
    placed = (
        P("seq", "head"),
        P("seq", "head"),
        P(("seq", "head"), None),
        P("seq", "head"),
        P(),
        P(),
        P(),
        P("seq"),
        P("seq"),
    )
    return jax.shard_map(
        local,
        mesh=mesh,
        in_specs=placed,
        out_specs=(P("seq", "head"), P("seq", "head"), P(("seq", "head"), None)),
        check_vma=False,
    )
```

```python
import math

import jax
import jax.numpy as jnp
from jax import lax
from jax.experimental import pallas as pl
from jax.experimental.pallas import tpu as pltpu
from jax.sharding import PartitionSpec as P

HD = 128
PLEN = 2048
RLEN = 256
HEADS = 8
PROMPTS = 8
RING = 16
CHUNK = PLEN // RING
UNITS = 4
UNIT = 16
BLOCK = 256
BLOCKS = PLEN // BLOCK
PER_BLOCK = BLOCK // CHUNK
ROWS = HEADS * RLEN
KEYS = PLEN + RLEN
WIDTH = 2 * HD
SCALE = HD**-0.5
LOG2E = math.log2(math.e)
MESH = pl.DeviceIdType.MESH
VMEM_LIMIT = 60 * 1024 * 1024
NN = (((1,), (0,)), ((), ()))
F32 = jnp.float32
BF16 = jnp.bfloat16


def around(index):
    return lax.rem(index + 2 * RING, RING)


def plus(plane, offset):
    return lax.rem(plane // 4 + offset // 4, 4) * 4 + lax.rem(plane + lax.rem(offset, 4), 4)


def minus(plane, offset):
    return lax.rem(plane // 4 + 4 - offset // 4, 4) * 4 + lax.rem(plane + 4 - lax.rem(offset, 4), 4)


def turn(place):
    return 5 * place % RING if isinstance(place, int) else lax.rem(5 * place, RING)


def unit_offset(column, u):
    return 4 * u + lax.rem(column + u, 4)


def column_step(i):
    return 8 + (i // 2) * (1 - 2 * lax.rem(i, 2))


def head_rows(j):
    return slice(j * RLEN, (j + 1) * RLEN)


def head_columns(j):
    return slice(j * HD, (j + 1) * HD)


def chunk_rows(step):
    return pl.ds(pl.multiple_of(step * CHUNK, CHUNK), CHUNK)


def fold(values, op):
    return op(values.reshape(values.shape[0] // 8, 8, values.shape[1]), axis=0)


def dot(a, b):
    return lax.dot_general(a, b, NN, preferred_element_type=F32)


def kernel(
    counts_ref,
    prompt_slot_ref,
    response_ref,
    len_ref,
    code_ref,
    q_ref,
    own_ref,
    cache_ref,
    go_ref,
    dq_ref,
    down_ref,
    back_ref,
    wanted,
    previous,
    last,
    q_in,
    go_in,
    own_in,
    rows_in,
    keys_in,
    values_in,
    staged,
    keys,
    values,
    q_rows,
    q_cols,
    cot_cols,
    cot_scaled_cols,
    cot_scaled_rows,
    scores,
    raw,
    top,
    delta,
    inverse,
    turned,
    dv_sum,
    grads,
    terms,
    running,
    summed,
    sorted_sums,
    parts,
    final,
    own_grads,
    q_grads,
    in_sem,
    a_send,
    a_recv,
    b_send,
    b_recv,
    c_send,
    c_recv,
    rc_send,
    rc_recv,
    rb_send,
    rb_recv,
    ra_send,
    ra_recv,
):
    seq = lax.axis_index("seq")
    head = lax.axis_index("head")
    plane = seq // 2
    half = lax.rem(seq, 2)
    column = half * 8 + head

    def in_plane(other):
        return {"seq": 2 * other + half, "head": head}

    def in_column(other):
        return {"seq": 2 * plane + other // 8, "head": lax.rem(other, 8)}

    def remote(src, dst, send_sem, recv_sem, device):
        return pltpu.make_async_remote_copy(
            src_ref=src, dst_ref=dst, send_sem=send_sem, recv_sem=recv_sem, device_id=device, device_id_type=MESH
        )

    def all_at_once(buffer, sem):
        pltpu.make_async_copy(buffer.at[pl.ds(1, RING - 1)], buffer.at[pl.ds(1, RING - 1)], sem).wait()

    loads = [
        pltpu.make_async_copy(q_ref, q_in, in_sem.at[0]),
        pltpu.make_async_copy(go_ref, go_in, in_sem.at[1]),
        pltpu.make_async_copy(own_ref, own_in, in_sem.at[2]),
    ]
    for load in loads:
        load.start()

    barrier = pltpu.get_barrier_semaphore()

    def greet(step, carry):
        pl.semaphore_signal(barrier, inc=1, device_id=in_column(around(column + step)), device_id_type=MESH)
        pl.semaphore_signal(barrier, inc=1, device_id=in_plane(plus(plane, step)), device_id_type=MESH)
        return carry

    lax.fori_loop(1, RING, greet, 0)
    pl.semaphore_wait(barrier, 2 * (RING - 1))

    stays = lax.rem(column, 4) == 0

    def unit_copy(u):
        return remote(
            cache_ref.at[pl.ds(u * UNIT, UNIT)],
            rows_in.at[u],
            a_send.at[u],
            a_recv.at[u],
            in_plane(plus(plane, unit_offset(column, u))),
        )

    for u in range(1, UNITS):
        unit_copy(u).start()

    @pl.when(jnp.logical_not(stays))
    def _():
        unit_copy(0).start()

    @pl.when(stays)
    def _():
        pltpu.make_async_copy(cache_ref.at[pl.ds(0, UNIT)], rows_in.at[0], a_recv.at[0]).start()

    by_source = (keys_in, values_in)

    def column_copy(part, step):
        target = around(column + step)
        at = pl.ds(pl.multiple_of(lax.rem(target, 8) * WIDTH + part * HD, HD), HD)
        return remote(
            rows_in.at[:, :, at], by_source[part].at[column], b_send.at[part], b_recv.at[part], in_column(target)
        )

    def send_heads(part):
        def send(i, carry):
            column_copy(part, column_step(i)).start()
            return carry

        lax.fori_loop(1, RING, send, 0)
        by_source[part][column] = rows_in[:, :, pl.ds(pl.multiple_of(head * WIDTH + part * HD, HD), HD)]

    gathered = (keys, values)

    def chunk_copy(part, step):
        return remote(
            staged.at[part, step],
            gathered[part].at[chunk_rows(step)],
            c_send.at[part],
            c_recv.at[part, step],
            in_plane(plus(plane, turn(step))),
        )

    def send_chunks(part):
        def take(step):
            prompt = wanted[step]
            units = []
            for odd in range(2):
                across = lax.rem(lax.div(plane, 4) + 4 - lax.div(prompt, 2), 4)
                along = lax.rem(plane + 4 - 2 * lax.rem(prompt, 2) - odd, 4)
                first = lax.rem(along + 4 - across, 4)
                for i in range(4):
                    units.append(by_source[part][4 * i + first, across])
            return jnp.concatenate(units, axis=0)

        all_at_once(by_source[part], b_recv.at[part])
        for step in range(1, RING):
            staged[part, step] = take(step)
            chunk_copy(part, step).start()
        gathered[part][:CHUNK] = take(0)

    ends = []
    for i in range(PROMPTS):
        ends.append(counts_ref[i] + (ends[-1] if ends else 0))
    prompts = []
    for step in range(RING):
        response = response_ref[2 * plus(plane, turn(step)) + half]
        group = jnp.int32(0)
        for end in ends[:-1]:
            group = group + (end <= response).astype(jnp.int32)
        prompts.append(prompt_slot_ref[group])
        wanted[step] = prompts[-1]
    for step in range(RING):
        found = jnp.int32(RING)
        for other in range(step):
            found = jnp.where(prompts[other] == prompts[step], other, found)
        previous[step] = found
    for prompt in range(PROMPTS):
        found = jnp.int32(RING)
        for step in range(RING):
            found = jnp.where(prompts[step] == prompt, step, found)
        last[prompt] = found

    for load in loads:
        load.wait()
    position = lax.broadcasted_iota(jnp.int32, (RLEN, HD), 0)
    factor = jnp.where(position < len_ref[0], code_ref[0].astype(F32) / 8.0, 0.0)
    for j in range(HEADS):
        query = q_in[:, head_columns(j)]
        q_rows[head_rows(j)] = query
        q_cols[:, head_rows(j)] = jnp.transpose(query)
        cotangent = go_in[:, head_columns(j)].astype(F32) * factor
        cot_cols[:, head_rows(j)] = jnp.transpose(cotangent).astype(BF16)
    keys[PLEN:] = own_in[:, :HD]
    values[PLEN:] = own_in[:, HD:]
    running[RING] = jnp.zeros((CHUNK, HD), F32)

    def block_rows(b):
        return pl.ds(pl.multiple_of(b * BLOCK, BLOCK), BLOCK)

    def score(b, own):
        block = keys[block_rows(b)]
        for j in range(HEADS):
            at = head_rows(j)
            part = dot(block, q_cols[:, at])
            if own:
                key_at = lax.broadcasted_iota(jnp.int32, (BLOCK, RLEN), 0)
                seen_from = lax.broadcasted_iota(jnp.int32, (BLOCK, RLEN), 1)
                part = jnp.where(key_at <= seen_from, part, -1e30)
            scores[b, :, at] = part
            high = fold(part, jnp.max)
            top[:, at] = high if own else jnp.maximum(top[:, at], high)

    for u in range(UNITS):
        unit_copy(u).wait_recv()
    send_heads(0)
    send_heads(1)
    score(BLOCKS, True)
    send_chunks(0)
    send_chunks(1)

    def arrive(part, b):
        def one(i, carry):
            step = b * PER_BLOCK + i

            @pl.when(step > 0)
            def _():
                chunk_copy(part, step).wait_recv()

            return carry

        lax.fori_loop(0, PER_BLOCK, one, 0)

    def score_block(b, carry):
        arrive(0, b)
        score(b, False)
        return carry

    lax.fori_loop(0, BLOCKS, score_block, 0)

    def return_copy(part, step):
        return remote(
            grads.at[part, step],
            terms.at[part, step],
            rc_send.at[part],
            rc_recv.at[part],
            in_plane(minus(plane, turn(step))),
        )

    def send_back(part, b, block):
        for i in range(PER_BLOCK):
            grads[part, b * PER_BLOCK + i] = block[i * CHUNK : (i + 1) * CHUNK]

        def one(i, carry):
            step = b * PER_BLOCK + i

            @pl.when(step > 0)
            def _():
                return_copy(part, step).start()

            return carry

        lax.fori_loop(0, PER_BLOCK, one, 0)

    def pair_rows(p):
        return slice(2 * p * RLEN, 2 * (p + 1) * RLEN)

    def pair_grads(b, p):
        return dot(raw[b, :, pair_rows(p)], cot_scaled_rows[pair_rows(p)])

    for p in range(HEADS // 2):
        heads = (2 * p, 2 * p + 1)
        highest = [jnp.max(top[:, head_rows(j)], axis=0, keepdims=True) for j in heads]

        def weigh(b, totals):
            sums = []
            for j, high, total in zip(heads, highest, totals):
                at = head_rows(j)
                weights = jnp.exp2((scores[b, :, at] - high) * (SCALE * LOG2E))
                raw[b, :, at] = weights.astype(BF16)
                sums.append(total + fold(weights, jnp.sum))
            if p == 1:
                dv_sum[b] = pair_grads(b, 0)
            elif p > 1:
                dv_sum[b] += pair_grads(b, p - 1)
            return tuple(sums)

        totals = lax.fori_loop(0, BLOCKS + 1, weigh, (jnp.zeros((8, RLEN), F32),) * 2)
        for j, total in zip(heads, totals):
            at = head_rows(j)
            over = 1.0 / jnp.sum(total, axis=0, keepdims=True)
            inverse[:, at] = jnp.broadcast_to(over, (8, RLEN))
            scaled = cot_cols[:, at].astype(F32) * over
            cot_scaled_cols[:, at] = scaled.astype(BF16)
            cot_scaled_rows[at] = jnp.transpose(scaled).astype(BF16)

    def value_grads(b):
        return (dv_sum[b] + pair_grads(b, HEADS // 2 - 1)).astype(BF16)

    def value_block(b, carry):
        send_back(1, b, value_grads(b))
        return carry

    lax.fori_loop(0, BLOCKS, value_block, 0)

    def look(b, first):
        block = values[block_rows(b)]
        for j in range(HEADS):
            at = head_rows(j)
            grad = dot(block, cot_scaled_cols[:, at])
            scores[b, :, at] = grad
            term = fold(grad * raw[b, :, at].astype(F32), jnp.sum)
            delta[:, at] = term if first else delta[:, at] + term

    def look_block(b, carry):
        arrive(1, b)
        look(b, False)
        return carry

    look(BLOCKS, True)
    lax.fori_loop(0, BLOCKS, look_block, 0)
    for j in range(HEADS):
        at = head_rows(j)
        delta[:, at] = jnp.sum(delta[:, at], axis=0, keepdims=True) * inverse[:, at]

    def key_part(b):
        for j in range(HEADS):
            at = head_rows(j)
            weights = raw[b, :, at].astype(F32)
            shift = delta[0:1, at]
            change = (weights * (scores[b, :, at] - shift)).astype(BF16)
            raw[b, :, at] = change
        return (dot(raw[b], q_rows[...]) * SCALE).astype(BF16)

    def key_block(b, carry):
        send_back(0, b, key_part(b))
        return carry

    lax.fori_loop(0, BLOCKS, key_block, 0)

    def return_column(part, step):
        target = around(column + step)
        return remote(
            sorted_sums.at[part, target],
            parts.at[part, column],
            rb_send.at[part],
            rb_recv.at[part],
            in_column(target),
        )

    def add_up(part):
        all_at_once(grads.at[part], rc_recv.at[part])
        terms[part, 0] = grads[part, 0]

        def add(step, carry):
            running[step] = running[previous[step]] + terms[part, step].astype(F32)
            return carry

        lax.fori_loop(0, RING, add, 0)

        def close(prompt, carry):
            summed[prompt] = running[last[prompt]].astype(BF16)
            return carry

        lax.fori_loop(0, PROMPTS, close, 0)

        def sort(target):
            for u in range(UNITS):
                source = minus(plane, unit_offset(target, u))
                unit = lax.rem(source, 2) * 4 + target // 4
                sorted_sums[part, target, u * UNIT : (u + 1) * UNIT] = summed[
                    source // 2, pl.ds(pl.multiple_of(unit * UNIT, UNIT), UNIT)
                ]

        def send(i, carry):
            step = column_step(i)
            sort(around(column + step))
            return_column(part, step).start()
            return carry

        lax.fori_loop(1, RING, send, 0)
        sort(column)
        parts[part, column] = sorted_sums[part, column]

    def return_unit(part, u):
        return remote(
            final.at[part, pl.ds(u * UNIT, UNIT)],
            back_ref.at[part, pl.ds(u * UNIT, UNIT)],
            ra_send.at[part, u],
            ra_recv.at[part, u],
            in_plane(minus(plane, unit_offset(column, u))),
        )

    def return_stay(part):
        return pltpu.make_async_copy(
            final.at[part, pl.ds(0, UNIT)], back_ref.at[part, pl.ds(0, UNIT)], ra_recv.at[part, 0]
        )

    def return_rows(part):
        all_at_once(parts.at[part], rb_recv.at[part])
        for h in range(8):
            both = parts[part, h].astype(F32) + parts[part, 8 + h].astype(F32)
            final[part, :, head_columns(h)] = both.astype(BF16)
        for u in range(1, UNITS):
            return_unit(part, u).start()

        @pl.when(jnp.logical_not(stays))
        def _():
            return_unit(part, 0).start()

        @pl.when(stays)
        def _():
            return_stay(part).start()

    add_up(1)

    own_grads[:, HD:] = value_grads(BLOCKS)
    own_grads[:, :HD] = key_part(BLOCKS)
    own_out = pltpu.make_async_copy(own_grads, down_ref, in_sem.at[2])
    own_out.start()
    turned[...] = jnp.transpose(keys[...])

    def query_grads(first, end):
        for j in range(first, end):
            grad = dot(turned[...], raw[:, :, head_rows(j)].reshape(KEYS, RLEN))
            q_grads[:, head_columns(j)] = (jnp.transpose(grad) * SCALE).astype(BF16)

    query_grads(0, 2)
    add_up(0)
    query_grads(2, HEADS)
    q_out = pltpu.make_async_copy(q_grads, dq_ref, in_sem.at[0])
    q_out.start()
    return_rows(1)
    return_rows(0)

    own_out.wait()
    q_out.wait()
    for part in range(2):
        all_at_once(by_source[part], b_send.at[part])
        all_at_once(staged.at[part], c_send.at[part])
        all_at_once(grads.at[part], rc_send.at[part])
        all_at_once(parts.at[part], rb_send.at[part])
        for u in range(UNITS):
            return_unit(part, u).wait_recv()
        for u in range(1, UNITS):
            return_unit(part, u).wait_send()
    for u in range(1, UNITS):
        unit_copy(u).wait_send()

    @pl.when(jnp.logical_not(stays))
    def _():
        unit_copy(0).wait_send()
        return_unit(0, 0).wait_send()
        return_unit(1, 0).wait_send()


def finish_kernel(dq_ref, down_ref, back_ref, dq_out, down_out, dcache_out, dq, down, back, total, get_sems, put_sems):
    gets = [
        pltpu.make_async_copy(back_ref, back, get_sems.at[0]),
        pltpu.make_async_copy(dq_ref, dq, get_sems.at[1]),
        pltpu.make_async_copy(down_ref, down, get_sems.at[2]),
    ]
    puts = [
        pltpu.make_async_copy(total, dcache_out, put_sems.at[0]),
        pltpu.make_async_copy(dq, dq_out, put_sems.at[1]),
        pltpu.make_async_copy(down, down_out, put_sems.at[2]),
    ]
    for get in gets:
        get.start()
    gets[0].wait()
    for h in range(8):
        for part in range(2):
            total[:, h * WIDTH + part * HD : h * WIDTH + (part + 1) * HD] = back[part, :, head_columns(h)]
    puts[0].start()
    for get, put in zip(gets[1:], puts[1:]):
        get.wait()
        put.start()
    for put in puts:
        put.wait()


def local(
    queries, resp_kv, prompt_cache, grad_out, group_counts, prompt_slot, slot_response, resp_len, weight_code
):
    smem = pl.BlockSpec(memory_space=pltpu.SMEM)
    hbm = pl.BlockSpec(memory_space=pltpu.HBM)
    scratch = [
        pltpu.SMEM((RING,), jnp.int32),
        pltpu.SMEM((RING,), jnp.int32),
        pltpu.SMEM((PROMPTS,), jnp.int32),
        pltpu.VMEM((RLEN, HEADS * HD), BF16),
        pltpu.VMEM((RLEN, HEADS * HD), BF16),
        pltpu.VMEM((RLEN, WIDTH), BF16),
        pltpu.VMEM((UNITS, UNIT, 8 * WIDTH), BF16),
        pltpu.VMEM((RING, UNITS, UNIT, HD), BF16),
        pltpu.VMEM((RING, UNITS, UNIT, HD), BF16),
        pltpu.VMEM((2, RING, CHUNK, HD), BF16),
        pltpu.VMEM((KEYS, HD), BF16),
        pltpu.VMEM((KEYS, HD), BF16),
        pltpu.VMEM((ROWS, HD), BF16),
        pltpu.VMEM((HD, ROWS), BF16),
        pltpu.VMEM((HD, ROWS), BF16),
        pltpu.VMEM((HD, ROWS), BF16),
        pltpu.VMEM((ROWS, HD), BF16),
        pltpu.VMEM((BLOCKS + 1, BLOCK, ROWS), F32),
        pltpu.VMEM((BLOCKS + 1, BLOCK, ROWS), BF16),
        pltpu.VMEM((8, ROWS), F32),
        pltpu.VMEM((8, ROWS), F32),
        pltpu.VMEM((8, ROWS), F32),
        pltpu.VMEM((HD, KEYS), BF16),
        pltpu.VMEM((BLOCKS + 1, BLOCK, HD), F32),
        pltpu.VMEM((2, RING, CHUNK, HD), BF16),
        pltpu.VMEM((2, RING, CHUNK, HD), BF16),
        pltpu.VMEM((RING + 1, CHUNK, HD), F32),
        pltpu.VMEM((PROMPTS, CHUNK, HD), BF16),
        pltpu.VMEM((2, RING, UNITS * UNIT, HD), BF16),
        pltpu.VMEM((2, RING, UNITS * UNIT, HD), BF16),
        pltpu.VMEM((2, UNITS * UNIT, 8 * HD), BF16),
        pltpu.VMEM((RLEN, WIDTH), BF16),
        pltpu.VMEM((RLEN, HEADS * HD), BF16),
        pltpu.SemaphoreType.DMA((3,)),
        pltpu.SemaphoreType.DMA((UNITS,)),
        pltpu.SemaphoreType.DMA((UNITS,)),
        pltpu.SemaphoreType.DMA((2,)),
        pltpu.SemaphoreType.DMA((2,)),
        pltpu.SemaphoreType.DMA((2,)),
        pltpu.SemaphoreType.DMA((2, RING)),
        pltpu.SemaphoreType.DMA((2,)),
        pltpu.SemaphoreType.DMA((2,)),
        pltpu.SemaphoreType.DMA((2,)),
        pltpu.SemaphoreType.DMA((2,)),
        pltpu.SemaphoreType.DMA((2, UNITS)),
        pltpu.SemaphoreType.DMA((2, UNITS)),
    ]
    products = 5 * ROWS * KEYS * HD
    dq, down, back = pl.pallas_call(
        kernel,
        out_shape=[
            jax.ShapeDtypeStruct(queries.shape, BF16),
            jax.ShapeDtypeStruct(resp_kv.shape, BF16),
            jax.ShapeDtypeStruct((2, UNITS * UNIT, 8 * HD), BF16),
        ],
        in_specs=[smem] * 5 + [hbm] * 4,
        out_specs=[hbm] * 3,
        scratch_shapes=scratch,
        compiler_params=pltpu.CompilerParams(
            collective_id=0, has_side_effects=True, vmem_limit_bytes=VMEM_LIMIT
        ),
        cost_estimate=pl.CostEstimate(flops=2 * products, bytes_accessed=3 << 20, transcendentals=ROWS * KEYS),
    )(
        group_counts,
        prompt_slot,
        slot_response,
        resp_len,
        weight_code,
        queries,
        resp_kv,
        prompt_cache,
        grad_out,
    )
    return pl.pallas_call(
        finish_kernel,
        out_shape=[
            jax.ShapeDtypeStruct(queries.shape, BF16),
            jax.ShapeDtypeStruct(resp_kv.shape, BF16),
            jax.ShapeDtypeStruct(prompt_cache.shape, BF16),
        ],
        in_specs=[hbm] * 3,
        out_specs=[hbm] * 3,
        scratch_shapes=[
            pltpu.VMEM(queries.shape, BF16),
            pltpu.VMEM(resp_kv.shape, BF16),
            pltpu.VMEM((2, UNITS * UNIT, 8 * HD), BF16),
            pltpu.VMEM(prompt_cache.shape, BF16),
            pltpu.SemaphoreType.DMA((3,)),
            pltpu.SemaphoreType.DMA((3,)),
        ],
        compiler_params=pltpu.CompilerParams(vmem_limit_bytes=VMEM_LIMIT),
    )(dq, down, back)


def solution(mesh):
    placed = (
        P("seq", "head"),
        P("seq", "head"),
        P(("seq", "head"), None),
        P("seq", "head"),
        P(),
        P(),
        P(),
        P("seq"),
        P("seq"),
    )
    return jax.shard_map(
        local,
        mesh=mesh,
        in_specs=placed,
        out_specs=(P("seq", "head"), P("seq", "head"), P(("seq", "head"), None)),
        check_vma=False,
    )
```

```python
import math

import jax
import jax.numpy as jnp
from jax import lax
from jax.experimental import pallas as pl
from jax.experimental.pallas import tpu as pltpu
from jax.sharding import PartitionSpec as P

HD = 128
PLEN = 2048
RLEN = 256
HEADS = 8
PROMPTS = 8
RING = 16
CHUNK = PLEN // RING
UNITS = 4
UNIT = 16
BLOCK = 256
BLOCKS = PLEN // BLOCK
PER_BLOCK = BLOCK // CHUNK
ROWS = HEADS * RLEN
KEYS = PLEN + RLEN
WIDTH = 2 * HD
SCALE = HD**-0.5
LOG2E = math.log2(math.e)
MESH = pl.DeviceIdType.MESH
VMEM_LIMIT = 60 * 1024 * 1024
NN = (((1,), (0,)), ((), ()))
F32 = jnp.float32
BF16 = jnp.bfloat16


def around(index):
    return lax.rem(index + 2 * RING, RING)


def plus(plane, offset):
    return lax.rem(plane // 4 + offset // 4, 4) * 4 + lax.rem(plane + lax.rem(offset, 4), 4)


def minus(plane, offset):
    return lax.rem(plane // 4 + 4 - offset // 4, 4) * 4 + lax.rem(plane + 4 - lax.rem(offset, 4), 4)


def turn(place):
    return 5 * place % RING if isinstance(place, int) else lax.rem(5 * place, RING)


def unit_offset(column, u):
    return 4 * u + lax.rem(column + u, 4)


def column_step(i):
    return 8 + (i // 2) * (1 - 2 * lax.rem(i, 2))


def head_rows(j):
    return slice(j * RLEN, (j + 1) * RLEN)


def head_columns(j):
    return slice(j * HD, (j + 1) * HD)


def chunk_rows(step):
    return pl.ds(pl.multiple_of(step * CHUNK, CHUNK), CHUNK)


def fold(values, op):
    return op(values.reshape(values.shape[0] // 8, 8, values.shape[1]), axis=0)


def dot(a, b):
    return lax.dot_general(a, b, NN, preferred_element_type=F32)


def kernel(
    counts_ref,
    prompt_slot_ref,
    response_ref,
    len_ref,
    code_ref,
    q_ref,
    own_ref,
    cache_ref,
    go_ref,
    dq_ref,
    down_ref,
    back_ref,
    wanted,
    previous,
    last,
    q_in,
    go_in,
    own_in,
    rows_in,
    keys_in,
    values_in,
    staged,
    keys,
    values,
    q_rows,
    q_cols,
    cot_cols,
    cot_scaled_cols,
    cot_scaled_rows,
    scores,
    raw,
    top,
    delta,
    inverse,
    turned,
    dv_sum,
    grads,
    terms,
    running,
    summed,
    own_grads,
    q_grads,
    in_sem,
    a_send,
    a_recv,
    b_send,
    b_recv,
    c_send,
    c_recv,
    rc_send,
    rc_recv,
    rb_send,
    rb_recv,
    stay_sem,
):
    seq = lax.axis_index("seq")
    head = lax.axis_index("head")
    plane = seq // 2
    half = lax.rem(seq, 2)
    column = half * 8 + head

    def in_plane(other):
        return {"seq": 2 * other + half, "head": head}

    def in_column(other):
        return {"seq": 2 * plane + other // 8, "head": lax.rem(other, 8)}

    def remote(src, dst, send_sem, recv_sem, device):
        return pltpu.make_async_remote_copy(
            src_ref=src, dst_ref=dst, send_sem=send_sem, recv_sem=recv_sem, device_id=device, device_id_type=MESH
        )

    def all_at_once(buffer, sem):
        pltpu.make_async_copy(buffer.at[pl.ds(1, RING - 1)], buffer.at[pl.ds(1, RING - 1)], sem).wait()

    loads = [
        pltpu.make_async_copy(q_ref, q_in, in_sem.at[0]),
        pltpu.make_async_copy(go_ref, go_in, in_sem.at[1]),
        pltpu.make_async_copy(own_ref, own_in, in_sem.at[2]),
    ]
    for load in loads:
        load.start()

    barrier = pltpu.get_barrier_semaphore()

    def greet(step, carry):
        pl.semaphore_signal(barrier, inc=1, device_id=in_column(around(column + step)), device_id_type=MESH)
        pl.semaphore_signal(barrier, inc=1, device_id=in_plane(plus(plane, step)), device_id_type=MESH)
        return carry

    lax.fori_loop(1, RING, greet, 0)
    pl.semaphore_wait(barrier, 2 * (RING - 1))

    stays = lax.rem(column, 4) == 0

    def unit_copy(u):
        return remote(
            cache_ref.at[pl.ds(u * UNIT, UNIT)],
            rows_in.at[u],
            a_send.at[u],
            a_recv.at[u],
            in_plane(plus(plane, unit_offset(column, u))),
        )

    for u in range(1, UNITS):
        unit_copy(u).start()

    @pl.when(jnp.logical_not(stays))
    def _():
        unit_copy(0).start()

    @pl.when(stays)
    def _():
        pltpu.make_async_copy(cache_ref.at[pl.ds(0, UNIT)], rows_in.at[0], a_recv.at[0]).start()

    by_source = (keys_in, values_in)

    def column_copy(part, step):
        target = around(column + step)
        at = pl.ds(pl.multiple_of(lax.rem(target, 8) * WIDTH + part * HD, HD), HD)
        return remote(
            rows_in.at[:, :, at], by_source[part].at[column], b_send.at[part], b_recv.at[part], in_column(target)
        )

    def send_heads(part):
        def send(i, carry):
            column_copy(part, column_step(i)).start()
            return carry

        lax.fori_loop(1, RING, send, 0)
        by_source[part][column] = rows_in[:, :, pl.ds(pl.multiple_of(head * WIDTH + part * HD, HD), HD)]

    gathered = (keys, values)

    def chunk_copy(part, step):
        return remote(
            staged.at[part, step],
            gathered[part].at[chunk_rows(step)],
            c_send.at[part],
            c_recv.at[part, step],
            in_plane(plus(plane, turn(step))),
        )

    def send_chunks(part):
        def take(step):
            prompt = wanted[step]
            units = []
            for odd in range(2):
                across = lax.rem(lax.div(plane, 4) + 4 - lax.div(prompt, 2), 4)
                along = lax.rem(plane + 4 - 2 * lax.rem(prompt, 2) - odd, 4)
                first = lax.rem(along + 4 - across, 4)
                for i in range(4):
                    units.append(by_source[part][4 * i + first, across])
            return jnp.concatenate(units, axis=0)

        all_at_once(by_source[part], b_recv.at[part])
        for step in range(1, RING):
            staged[part, step] = take(step)
            chunk_copy(part, step).start()
        gathered[part][:CHUNK] = take(0)

    ends = []
    for i in range(PROMPTS):
        ends.append(counts_ref[i] + (ends[-1] if ends else 0))
    prompts = []
    for step in range(RING):
        response = response_ref[2 * plus(plane, turn(step)) + half]
        group = jnp.int32(0)
        for end in ends[:-1]:
            group = group + (end <= response).astype(jnp.int32)
        prompts.append(prompt_slot_ref[group])
        wanted[step] = prompts[-1]
    for step in range(RING):
        found = jnp.int32(RING)
        for other in range(step):
            found = jnp.where(prompts[other] == prompts[step], other, found)
        previous[step] = found
    for prompt in range(PROMPTS):
        found = jnp.int32(RING)
        for step in range(RING):
            found = jnp.where(prompts[step] == prompt, step, found)
        last[prompt] = found

    for load in loads:
        load.wait()
    position = lax.broadcasted_iota(jnp.int32, (RLEN, HD), 0)
    factor = jnp.where(position < len_ref[0], code_ref[0].astype(F32) / 8.0, 0.0)
    for j in range(HEADS):
        query = q_in[:, head_columns(j)]
        q_rows[head_rows(j)] = query
        q_cols[:, head_rows(j)] = jnp.transpose(query)
        cotangent = go_in[:, head_columns(j)].astype(F32) * factor
        cot_cols[:, head_rows(j)] = jnp.transpose(cotangent).astype(BF16)
    keys[PLEN:] = own_in[:, :HD]
    values[PLEN:] = own_in[:, HD:]
    running[RING] = jnp.zeros((CHUNK, HD), F32)

    def block_rows(b):
        return pl.ds(pl.multiple_of(b * BLOCK, BLOCK), BLOCK)

    def score(b, own):
        block = keys[block_rows(b)]
        for j in range(HEADS):
            at = head_rows(j)
            part = dot(block, q_cols[:, at])
            if own:
                key_at = lax.broadcasted_iota(jnp.int32, (BLOCK, RLEN), 0)
                seen_from = lax.broadcasted_iota(jnp.int32, (BLOCK, RLEN), 1)
                part = jnp.where(key_at <= seen_from, part, -1e30)
            scores[b, :, at] = part
            high = fold(part, jnp.max)
            top[:, at] = high if own else jnp.maximum(top[:, at], high)

    for u in range(UNITS):
        unit_copy(u).wait_recv()
    send_heads(0)
    send_heads(1)
    score(BLOCKS, True)
    send_chunks(0)
    send_chunks(1)

    def arrive(part, b):
        def one(i, carry):
            step = b * PER_BLOCK + i

            @pl.when(step > 0)
            def _():
                chunk_copy(part, step).wait_recv()

            return carry

        lax.fori_loop(0, PER_BLOCK, one, 0)

    def score_block(b, carry):
        arrive(0, b)
        score(b, False)
        return carry

    lax.fori_loop(0, BLOCKS, score_block, 0)

    def return_copy(part, step):
        return remote(
            grads.at[part, step],
            terms.at[part, step],
            rc_send.at[part],
            rc_recv.at[part],
            in_plane(minus(plane, turn(step))),
        )

    def send_back(part, b, block):
        for i in range(PER_BLOCK):
            grads[part, b * PER_BLOCK + i] = block[i * CHUNK : (i + 1) * CHUNK]

        def one(i, carry):
            step = b * PER_BLOCK + i

            @pl.when(step > 0)
            def _():
                return_copy(part, step).start()

            return carry

        lax.fori_loop(0, PER_BLOCK, one, 0)

    def pair_rows(p):
        return slice(2 * p * RLEN, 2 * (p + 1) * RLEN)

    def pair_grads(b, p):
        return dot(raw[b, :, pair_rows(p)], cot_scaled_rows[pair_rows(p)])

    for p in range(HEADS // 2):
        heads = (2 * p, 2 * p + 1)
        highest = [jnp.max(top[:, head_rows(j)], axis=0, keepdims=True) for j in heads]

        def weigh(b, totals):
            sums = []
            for j, high, total in zip(heads, highest, totals):
                at = head_rows(j)
                weights = jnp.exp2((scores[b, :, at] - high) * (SCALE * LOG2E))
                raw[b, :, at] = weights.astype(BF16)
                sums.append(total + fold(weights, jnp.sum))
            if p == 1:
                dv_sum[b] = pair_grads(b, 0)
            elif p > 1:
                dv_sum[b] += pair_grads(b, p - 1)
            return tuple(sums)

        totals = lax.fori_loop(0, BLOCKS + 1, weigh, (jnp.zeros((8, RLEN), F32),) * 2)
        for j, total in zip(heads, totals):
            at = head_rows(j)
            over = 1.0 / jnp.sum(total, axis=0, keepdims=True)
            inverse[:, at] = jnp.broadcast_to(over, (8, RLEN))
            scaled = cot_cols[:, at].astype(F32) * over
            cot_scaled_cols[:, at] = scaled.astype(BF16)
            cot_scaled_rows[at] = jnp.transpose(scaled).astype(BF16)

    def value_grads(b):
        return (dv_sum[b] + pair_grads(b, HEADS // 2 - 1)).astype(BF16)

    def value_block(b, carry):
        send_back(1, b, value_grads(b))
        return carry

    lax.fori_loop(0, BLOCKS, value_block, 0)

    def look(b, first):
        block = values[block_rows(b)]
        for j in range(HEADS):
            at = head_rows(j)
            grad = dot(block, cot_scaled_cols[:, at])
            scores[b, :, at] = grad
            term = fold(grad * raw[b, :, at].astype(F32), jnp.sum)
            delta[:, at] = term if first else delta[:, at] + term

    def look_block(b, carry):
        arrive(1, b)
        look(b, False)
        return carry

    look(BLOCKS, True)
    lax.fori_loop(0, BLOCKS, look_block, 0)
    for j in range(HEADS):
        at = head_rows(j)
        delta[:, at] = jnp.sum(delta[:, at], axis=0, keepdims=True) * inverse[:, at]

    def key_part(b):
        for j in range(HEADS):
            at = head_rows(j)
            weights = raw[b, :, at].astype(F32)
            shift = delta[0:1, at]
            change = (weights * (scores[b, :, at] - shift)).astype(BF16)
            raw[b, :, at] = change
        return (dot(raw[b], q_rows[...]) * SCALE).astype(BF16)

    def key_block(b, carry):
        send_back(0, b, key_part(b))
        return carry

    lax.fori_loop(0, BLOCKS, key_block, 0)

    def home_copy(part, target, u):
        source = minus(plane, unit_offset(target, u))
        unit = lax.rem(source, 2) * 4 + target // 4
        return remote(
            summed.at[part, source // 2, unit],
            back_ref.at[part, 4 * column + u],
            rb_send.at[part],
            rb_recv.at[part],
            {"seq": 2 * source + target // 8, "head": lax.rem(target, 8)},
        )

    def home_stay(part):
        return pltpu.make_async_copy(
            summed.at[part, plane // 2, lax.rem(plane, 2) * 4 + column // 4],
            back_ref.at[part, 4 * column],
            stay_sem.at[part],
        )

    def add_up(part):
        all_at_once(grads.at[part], rc_recv.at[part])
        terms[part, 0] = grads[part, 0]

        def add(step, carry):
            running[step] = running[previous[step]] + terms[part, step].astype(F32)
            return carry

        lax.fori_loop(0, RING, add, 0)

        def close(prompt, carry):
            summed[part, prompt] = running[last[prompt]].astype(BF16).reshape(CHUNK // UNIT, UNIT, HD)
            return carry

        lax.fori_loop(0, PROMPTS, close, 0)

        def send(i, carry):
            target = around(column + column_step(i))
            for u in range(UNITS):
                home_copy(part, target, u).start()
            return carry

        lax.fori_loop(1, RING, send, 0)
        for u in range(1, UNITS):
            home_copy(part, column, u).start()

        @pl.when(jnp.logical_not(stays))
        def _():
            home_copy(part, column, 0).start()

        @pl.when(stays)
        def _():
            home_stay(part).start()

    def home_wait(part, sem):
        @pl.when(jnp.logical_not(stays))
        def _():
            pltpu.make_async_copy(back_ref.at[part], back_ref.at[part], sem).wait()

        @pl.when(stays)
        def _():
            rest = back_ref.at[part, pl.ds(1, RING * UNITS - 1)]
            pltpu.make_async_copy(rest, rest, sem).wait()

    add_up(1)

    own_grads[:, HD:] = value_grads(BLOCKS)
    own_grads[:, :HD] = key_part(BLOCKS)
    own_out = pltpu.make_async_copy(own_grads, down_ref, in_sem.at[2])
    own_out.start()
    turned[...] = jnp.transpose(keys[...])

    def query_grads(first, end):
        for j in range(first, end):
            grad = dot(turned[...], raw[:, :, head_rows(j)].reshape(KEYS, RLEN))
            q_grads[:, head_columns(j)] = (jnp.transpose(grad) * SCALE).astype(BF16)

    query_grads(0, 2)
    add_up(0)
    query_grads(2, HEADS)
    q_out = pltpu.make_async_copy(q_grads, dq_ref, in_sem.at[0])
    q_out.start()

    own_out.wait()
    q_out.wait()
    for u in range(1, UNITS):
        unit_copy(u).wait_send()

    @pl.when(jnp.logical_not(stays))
    def _():
        unit_copy(0).wait_send()

    for part in range(2):
        all_at_once(by_source[part], b_send.at[part])
        all_at_once(staged.at[part], c_send.at[part])
        all_at_once(grads.at[part], rc_send.at[part])
    for part in (1, 0):
        home_wait(part, rb_send.at[part])
        home_wait(part, rb_recv.at[part])

        @pl.when(stays)
        def _():
            home_stay(part).wait()


def finish_kernel(dq_ref, down_ref, back_ref, dq_out, down_out, dcache_out, dq, down, back, total, get_sems, put_sems):
    gets = [
        pltpu.make_async_copy(back_ref, back, get_sems.at[0]),
        pltpu.make_async_copy(dq_ref, dq, get_sems.at[1]),
        pltpu.make_async_copy(down_ref, down, get_sems.at[2]),
    ]
    puts = [
        pltpu.make_async_copy(total, dcache_out, put_sems.at[0]),
        pltpu.make_async_copy(dq, dq_out, put_sems.at[1]),
        pltpu.make_async_copy(down, down_out, put_sems.at[2]),
    ]
    for get in gets:
        get.start()
    gets[0].wait()
    for h in range(8):
        for part in range(2):
            first = back[part, UNITS * h : UNITS * (h + 1)].astype(F32)
            second = back[part, UNITS * (8 + h) : UNITS * (9 + h)].astype(F32)
            both = (first + second).astype(BF16).reshape(UNITS * UNIT, HD)
            total[:, h * WIDTH + part * HD : h * WIDTH + (part + 1) * HD] = both
    puts[0].start()
    for get, put in zip(gets[1:], puts[1:]):
        get.wait()
        put.start()
    for put in puts:
        put.wait()


def local(
    queries, resp_kv, prompt_cache, grad_out, group_counts, prompt_slot, slot_response, resp_len, weight_code
):
    smem = pl.BlockSpec(memory_space=pltpu.SMEM)
    hbm = pl.BlockSpec(memory_space=pltpu.HBM)
    scratch = [
        pltpu.SMEM((RING,), jnp.int32),
        pltpu.SMEM((RING,), jnp.int32),
        pltpu.SMEM((PROMPTS,), jnp.int32),
        pltpu.VMEM((RLEN, HEADS * HD), BF16),
        pltpu.VMEM((RLEN, HEADS * HD), BF16),
        pltpu.VMEM((RLEN, WIDTH), BF16),
        pltpu.VMEM((UNITS, UNIT, 8 * WIDTH), BF16),
        pltpu.VMEM((RING, UNITS, UNIT, HD), BF16),
        pltpu.VMEM((RING, UNITS, UNIT, HD), BF16),
        pltpu.VMEM((2, RING, CHUNK, HD), BF16),
        pltpu.VMEM((KEYS, HD), BF16),
        pltpu.VMEM((KEYS, HD), BF16),
        pltpu.VMEM((ROWS, HD), BF16),
        pltpu.VMEM((HD, ROWS), BF16),
        pltpu.VMEM((HD, ROWS), BF16),
        pltpu.VMEM((HD, ROWS), BF16),
        pltpu.VMEM((ROWS, HD), BF16),
        pltpu.VMEM((BLOCKS + 1, BLOCK, ROWS), F32),
        pltpu.VMEM((BLOCKS + 1, BLOCK, ROWS), BF16),
        pltpu.VMEM((8, ROWS), F32),
        pltpu.VMEM((8, ROWS), F32),
        pltpu.VMEM((8, ROWS), F32),
        pltpu.VMEM((HD, KEYS), BF16),
        pltpu.VMEM((BLOCKS + 1, BLOCK, HD), F32),
        pltpu.VMEM((2, RING, CHUNK, HD), BF16),
        pltpu.VMEM((2, RING, CHUNK, HD), BF16),
        pltpu.VMEM((RING + 1, CHUNK, HD), F32),
        pltpu.VMEM((2, PROMPTS, CHUNK // UNIT, UNIT, HD), BF16),
        pltpu.VMEM((RLEN, WIDTH), BF16),
        pltpu.VMEM((RLEN, HEADS * HD), BF16),
        pltpu.SemaphoreType.DMA((3,)),
        pltpu.SemaphoreType.DMA((UNITS,)),
        pltpu.SemaphoreType.DMA((UNITS,)),
        pltpu.SemaphoreType.DMA((2,)),
        pltpu.SemaphoreType.DMA((2,)),
        pltpu.SemaphoreType.DMA((2,)),
        pltpu.SemaphoreType.DMA((2, RING)),
        pltpu.SemaphoreType.DMA((2,)),
        pltpu.SemaphoreType.DMA((2,)),
        pltpu.SemaphoreType.DMA((2,)),
        pltpu.SemaphoreType.DMA((2,)),
        pltpu.SemaphoreType.DMA((2,)),
    ]
    products = 5 * ROWS * KEYS * HD
    dq, down, back = pl.pallas_call(
        kernel,
        out_shape=[
            jax.ShapeDtypeStruct(queries.shape, BF16),
            jax.ShapeDtypeStruct(resp_kv.shape, BF16),
            jax.ShapeDtypeStruct((2, RING * UNITS, UNIT, HD), BF16),
        ],
        in_specs=[smem] * 5 + [hbm] * 4,
        out_specs=[hbm] * 3,
        scratch_shapes=scratch,
        compiler_params=pltpu.CompilerParams(
            collective_id=0, has_side_effects=True, vmem_limit_bytes=VMEM_LIMIT
        ),
        cost_estimate=pl.CostEstimate(flops=2 * products, bytes_accessed=3 << 20, transcendentals=ROWS * KEYS),
    )(
        group_counts,
        prompt_slot,
        slot_response,
        resp_len,
        weight_code,
        queries,
        resp_kv,
        prompt_cache,
        grad_out,
    )
    return pl.pallas_call(
        finish_kernel,
        out_shape=[
            jax.ShapeDtypeStruct(queries.shape, BF16),
            jax.ShapeDtypeStruct(resp_kv.shape, BF16),
            jax.ShapeDtypeStruct(prompt_cache.shape, BF16),
        ],
        in_specs=[hbm] * 3,
        out_specs=[hbm] * 3,
        scratch_shapes=[
            pltpu.VMEM(queries.shape, BF16),
            pltpu.VMEM(resp_kv.shape, BF16),
            pltpu.VMEM((2, RING * UNITS, UNIT, HD), BF16),
            pltpu.VMEM(prompt_cache.shape, BF16),
            pltpu.SemaphoreType.DMA((3,)),
            pltpu.SemaphoreType.DMA((3,)),
        ],
        compiler_params=pltpu.CompilerParams(vmem_limit_bytes=VMEM_LIMIT),
    )(dq, down, back)


def solution(mesh):
    placed = (
        P("seq", "head"),
        P("seq", "head"),
        P(("seq", "head"), None),
        P("seq", "head"),
        P(),
        P(),
        P(),
        P("seq"),
        P("seq"),
    )
    return jax.shard_map(
        local,
        mesh=mesh,
        in_specs=placed,
        out_specs=(P("seq", "head"), P("seq", "head"), P(("seq", "head"), None)),
        check_vma=False,
    )
```

```python
import math

import jax
import jax.numpy as jnp
from jax import lax
from jax.experimental import pallas as pl
from jax.experimental.pallas import tpu as pltpu
from jax.sharding import PartitionSpec as P

HD = 128
PLEN = 2048
RLEN = 256
HEADS = 8
PROMPTS = 8
RING = 16
CHUNK = PLEN // RING
UNITS = 4
UNIT = 16
BLOCK = 256
BLOCKS = PLEN // BLOCK
PER_BLOCK = BLOCK // CHUNK
ROWS = HEADS * RLEN
KEYS = PLEN + RLEN
WIDTH = 2 * HD
SCALE = HD**-0.5
LOG2E = math.log2(math.e)
MESH = pl.DeviceIdType.MESH
VMEM_LIMIT = 60 * 1024 * 1024
NN = (((1,), (0,)), ((), ()))
F32 = jnp.float32
BF16 = jnp.bfloat16


def around(index):
    return lax.rem(index + 2 * RING, RING)


def div(a, b):
    return a // b if isinstance(a, int) else lax.div(a, b)


def rem(a, b):
    return a % b if isinstance(a, int) else lax.rem(a, b)


def plus(plane, offset):
    return 4 * rem(div(plane, 4) + div(offset, 4), 4) + rem(plane + rem(offset, 4), 4)


def minus(plane, offset):
    return 4 * rem(div(plane, 4) + 4 - div(offset, 4), 4) + rem(plane + 4 - rem(offset, 4), 4)


def turn(place):
    return rem(5 * place, RING)


def unit_offset(column, u):
    return 4 * u + lax.rem(column + u, 4)


def column_step(i):
    return 8 + div(i, 2) * (1 - 2 * rem(i, 2))


def head_rows(j):
    return slice(j * RLEN, (j + 1) * RLEN)


def head_columns(j):
    return slice(j * HD, (j + 1) * HD)


def chunk_rows(step):
    return pl.ds(pl.multiple_of(step * CHUNK, CHUNK), CHUNK)


def fold(values, op):
    return op(values.reshape(values.shape[0] // 8, 8, values.shape[1]), axis=0)


def dot(a, b):
    return lax.dot_general(a, b, NN, preferred_element_type=F32)


def kernel(
    counts_ref,
    prompt_slot_ref,
    response_ref,
    len_ref,
    code_ref,
    q_ref,
    own_ref,
    cache_ref,
    go_ref,
    dq_ref,
    down_ref,
    back_ref,
    across,
    first,
    previous,
    last,
    q_in,
    go_in,
    own_in,
    rows_in,
    keys_in,
    values_in,
    staged,
    keys,
    values,
    q_rows,
    q_cols,
    cot_cols,
    cot_scaled_cols,
    cot_scaled_rows,
    scores,
    raw,
    top,
    delta,
    inverse,
    turned,
    dv_sum,
    grads,
    terms,
    running,
    summed,
    own_grads,
    q_grads,
    in_sem,
    a_send,
    a_recv,
    b_send,
    b_recv,
    c_send,
    c_recv,
    rc_send,
    rc_recv,
    rb_send,
    rb_recv,
    stay_sem,
):
    seq = lax.axis_index("seq")
    head = lax.axis_index("head")
    plane = div(seq, 2)
    half = lax.rem(seq, 2)
    column = half * 8 + head

    def in_plane(other):
        return {"seq": 2 * other + half, "head": head}

    def in_column(other):
        return {"seq": 2 * plane + div(other, 8), "head": lax.rem(other, 8)}

    def remote(src, dst, send_sem, recv_sem, device):
        return pltpu.make_async_remote_copy(
            src_ref=src, dst_ref=dst, send_sem=send_sem, recv_sem=recv_sem, device_id=device, device_id_type=MESH
        )

    def all_at_once(buffer, sem):
        pltpu.make_async_copy(buffer.at[pl.ds(1, RING - 1)], buffer.at[pl.ds(1, RING - 1)], sem).wait()

    loads = [
        pltpu.make_async_copy(q_ref, q_in, in_sem.at[0]),
        pltpu.make_async_copy(go_ref, go_in, in_sem.at[1]),
        pltpu.make_async_copy(own_ref, own_in, in_sem.at[2]),
    ]
    for load in loads:
        load.start()

    barrier = pltpu.get_barrier_semaphore()
    stays = rem(column, 4) == 0

    def greet(device):
        pl.semaphore_signal(barrier, inc=1, device_id=device, device_id_type=MESH)

    def greet_column(step, carry):
        greet(in_column(around(column + step)))
        return carry

    def greet_unit(u):
        greet(in_plane(plus(plane, unit_offset(column, u))))
        greet(in_plane(minus(plane, unit_offset(column, u))))

    lax.fori_loop(1, RING, greet_column, 0)
    for u in range(1, UNITS):
        greet_unit(u)

    @pl.when(stays)
    def _():
        pl.semaphore_wait(barrier, RING - 1 + 2 * (UNITS - 1))

    @pl.when(jnp.logical_not(stays))
    def _():
        greet_unit(0)
        pl.semaphore_wait(barrier, RING - 1 + 2 * UNITS)

    def unit_copy(u):
        return remote(
            cache_ref.at[pl.ds(u * UNIT, UNIT)],
            rows_in.at[u],
            a_send.at[u],
            a_recv.at[u],
            in_plane(plus(plane, unit_offset(column, u))),
        )

    for u in range(1, UNITS):
        unit_copy(u).start()

    @pl.when(jnp.logical_not(stays))
    def _():
        unit_copy(0).start()

    @pl.when(stays)
    def _():
        pltpu.make_async_copy(cache_ref.at[pl.ds(0, UNIT)], rows_in.at[0], a_recv.at[0]).start()

    by_source = (keys_in, values_in)

    def column_copy(part, step):
        target = around(column + step)
        at = pl.ds(pl.multiple_of(lax.rem(target, 8) * WIDTH + part * HD, HD), HD)
        return remote(
            rows_in.at[:, :, at], by_source[part].at[column], b_send.at[part], b_recv.at[part], in_column(target)
        )

    def send_heads(part):
        def send(i, carry):
            column_copy(part, column_step(i)).start()
            return carry

        lax.fori_loop(1, RING, send, 0)
        by_source[part][column] = rows_in[:, :, pl.ds(pl.multiple_of(head * WIDTH + part * HD, HD), HD)]

    gathered = (keys, values)

    def chunk_copy(part, step):
        return remote(
            staged.at[part, step],
            gathered[part].at[chunk_rows(step)],
            c_send.at[part],
            c_recv.at[part, step],
            in_plane(plus(plane, turn(step))),
        )

    def send_chunks(part):
        def take(place):
            units = [by_source[part][4 * i + first[odd, place], across[place]] for odd in range(2) for i in range(4)]
            return jnp.concatenate(units, axis=0)

        all_at_once(by_source[part], b_recv.at[part])
        for step in range(1, RING):
            staged[part, step] = take(step)
            chunk_copy(part, step).start()
        gathered[part][:CHUNK] = take(0)

    ends = []
    for i in range(PROMPTS):
        ends.append(counts_ref[i] + (ends[-1] if ends else 0))
    prompts = []
    for step in range(RING):
        response = response_ref[2 * plus(plane, turn(step)) + half]
        group = jnp.int32(0)
        for end in ends[:-1]:
            group = group + (end <= response).astype(jnp.int32)
        prompt = prompt_slot_ref[group]
        prompts.append(prompt)
        way = rem(div(plane, 4) + 4 - div(prompt, 2), 4)
        across[step] = way
        for odd in range(2):
            first[odd, step] = rem(plane + 8 - 2 * rem(prompt, 2) - odd - way, 4)
    for step in range(RING):
        found = jnp.int32(RING)
        for other in range(step):
            found = jnp.where(prompts[other] == prompts[step], other, found)
        previous[step] = found
    for prompt in range(PROMPTS):
        found = jnp.int32(RING)
        for step in range(RING):
            found = jnp.where(prompts[step] == prompt, step, found)
        last[prompt] = found

    for load in loads:
        load.wait()
    position = lax.broadcasted_iota(jnp.int32, (RLEN, HD), 0)
    factor = jnp.where(position < len_ref[0], code_ref[0].astype(F32) / 8.0, 0.0)
    for j in range(HEADS):
        query = q_in[:, head_columns(j)]
        q_rows[head_rows(j)] = query
        q_cols[:, head_rows(j)] = jnp.transpose(query)
        cotangent = go_in[:, head_columns(j)].astype(F32) * factor
        cot_cols[:, head_rows(j)] = jnp.transpose(cotangent).astype(BF16)
    keys[PLEN:] = own_in[:, :HD]
    values[PLEN:] = own_in[:, HD:]
    running[RING] = jnp.zeros((CHUNK, HD), F32)

    def block_rows(b):
        return pl.ds(pl.multiple_of(b * BLOCK, BLOCK), BLOCK)

    def score(b, own):
        block = keys[block_rows(b)]
        for j in range(HEADS):
            at = head_rows(j)
            part = dot(block, q_cols[:, at])
            if own:
                key_at = lax.broadcasted_iota(jnp.int32, (BLOCK, RLEN), 0)
                seen_from = lax.broadcasted_iota(jnp.int32, (BLOCK, RLEN), 1)
                part = jnp.where(key_at <= seen_from, part, -1e30)
            scores[b, :, at] = part
            high = fold(part, jnp.max)
            top[:, at] = high if own else jnp.maximum(top[:, at], high)

    for u in range(UNITS):
        unit_copy(u).wait_recv()
    send_heads(0)
    send_heads(1)
    score(BLOCKS, True)
    send_chunks(0)
    send_chunks(1)

    def arrive(part, b):
        def one(i, carry):
            step = b * PER_BLOCK + i

            @pl.when(step > 0)
            def _():
                chunk_copy(part, step).wait_recv()

            return carry

        lax.fori_loop(0, PER_BLOCK, one, 0)

    def score_block(b, carry):
        arrive(0, b)
        score(b, False)
        return carry

    lax.fori_loop(0, BLOCKS, score_block, 0)

    def return_copy(part, step):
        return remote(
            grads.at[part, step],
            terms.at[part, step],
            rc_send.at[part],
            rc_recv.at[part],
            in_plane(minus(plane, turn(step))),
        )

    def send_back(part, b, block):
        for i in range(PER_BLOCK):
            grads[part, b * PER_BLOCK + i] = block[i * CHUNK : (i + 1) * CHUNK]

        def one(i, carry):
            step = b * PER_BLOCK + i

            @pl.when(step > 0)
            def _():
                return_copy(part, step).start()

            return carry

        lax.fori_loop(0, PER_BLOCK, one, 0)

    def pair_rows(p):
        return slice(2 * p * RLEN, 2 * (p + 1) * RLEN)

    def pair_grads(b, p):
        return dot(raw[b, :, pair_rows(p)], cot_scaled_rows[pair_rows(p)])

    for p in range(HEADS // 2):
        heads = (2 * p, 2 * p + 1)
        highest = [jnp.max(top[:, head_rows(j)], axis=0, keepdims=True) for j in heads]

        def weigh(b, totals):
            sums = []
            for j, high, total in zip(heads, highest, totals):
                at = head_rows(j)
                weights = jnp.exp2((scores[b, :, at] - high) * (SCALE * LOG2E))
                raw[b, :, at] = weights.astype(BF16)
                sums.append(total + fold(weights, jnp.sum))
            if p == 1:
                dv_sum[b] = pair_grads(b, 0)
            elif p > 1:
                dv_sum[b] += pair_grads(b, p - 1)
            return tuple(sums)

        totals = lax.fori_loop(0, BLOCKS + 1, weigh, (jnp.zeros((8, RLEN), F32),) * 2)
        for j, total in zip(heads, totals):
            at = head_rows(j)
            over = 1.0 / jnp.sum(total, axis=0, keepdims=True)
            inverse[:, at] = jnp.broadcast_to(over, (8, RLEN))
            scaled = cot_cols[:, at].astype(F32) * over
            cot_scaled_cols[:, at] = scaled.astype(BF16)
            cot_scaled_rows[at] = jnp.transpose(scaled).astype(BF16)

    def value_grads(b):
        return (dv_sum[b] + pair_grads(b, HEADS // 2 - 1)).astype(BF16)

    def value_block(b, carry):
        send_back(1, b, value_grads(b))
        return carry

    lax.fori_loop(0, BLOCKS, value_block, 0)

    def look(b, first):
        block = values[block_rows(b)]
        for j in range(HEADS):
            at = head_rows(j)
            grad = dot(block, cot_scaled_cols[:, at])
            scores[b, :, at] = grad
            term = fold(grad * raw[b, :, at].astype(F32), jnp.sum)
            delta[:, at] = term if first else delta[:, at] + term

    def look_block(b, carry):
        arrive(1, b)
        look(b, False)
        return carry

    look(BLOCKS, True)
    lax.fori_loop(0, BLOCKS, look_block, 0)
    for j in range(HEADS):
        at = head_rows(j)
        delta[:, at] = jnp.sum(delta[:, at], axis=0, keepdims=True) * inverse[:, at]

    def key_part(b):
        for j in range(HEADS):
            at = head_rows(j)
            weights = raw[b, :, at].astype(F32)
            shift = delta[0:1, at]
            change = (weights * (scores[b, :, at] - shift)).astype(BF16)
            raw[b, :, at] = change
        return (dot(raw[b], q_rows[...]) * SCALE).astype(BF16)

    def key_block(b, carry):
        send_back(0, b, key_part(b))
        return carry

    lax.fori_loop(0, BLOCKS, key_block, 0)

    def home_copy(part, target, u):
        x = rem(div(plane, 4) + 4 - u, 4)
        y = rem(plane + 20 - target - u, 4)
        source = 4 * x + y
        return remote(
            summed.at[part, 4 * source + div(target, 4)],
            back_ref.at[part, 4 * column + u],
            rb_send.at[part],
            rb_recv.at[part],
            {"seq": 2 * source + div(target, 8), "head": rem(target, 8)},
        )

    def home_stay(part):
        return pltpu.make_async_copy(
            summed.at[part, 4 * plane + div(column, 4)],
            back_ref.at[part, 4 * column],
            stay_sem.at[part],
        )

    def add_up(part):
        all_at_once(grads.at[part], rc_recv.at[part])
        terms[part, 0] = grads[part, 0]

        def add(step, carry):
            running[step] = running[previous[step]] + terms[part, step].astype(F32)
            return carry

        lax.fori_loop(0, RING, add, 0)

        def close(prompt, carry):
            units = running[last[prompt]].astype(BF16).reshape(CHUNK // UNIT, UNIT, HD)
            summed[part, pl.ds(prompt * (CHUNK // UNIT), CHUNK // UNIT)] = units
            return carry

        lax.fori_loop(0, PROMPTS, close, 0)

        def send(i, carry):
            target = around(column + column_step(i))
            for u in range(UNITS):
                home_copy(part, target, u).start()
            return carry

        lax.fori_loop(1, RING, send, 0)
        for u in range(1, UNITS):
            home_copy(part, column, u).start()

        @pl.when(jnp.logical_not(stays))
        def _():
            home_copy(part, column, 0).start()

        @pl.when(stays)
        def _():
            home_stay(part).start()

    def home_wait(part, sem):
        @pl.when(jnp.logical_not(stays))
        def _():
            pltpu.make_async_copy(back_ref.at[part], back_ref.at[part], sem).wait()

        @pl.when(stays)
        def _():
            rest = back_ref.at[part, pl.ds(1, RING * UNITS - 1)]
            pltpu.make_async_copy(rest, rest, sem).wait()

    add_up(1)

    own_grads[:, HD:] = value_grads(BLOCKS)
    own_grads[:, :HD] = key_part(BLOCKS)
    own_out = pltpu.make_async_copy(own_grads, down_ref, in_sem.at[2])
    own_out.start()
    turned[...] = jnp.transpose(keys[...])

    def query_grads(first, end):
        for j in range(first, end):
            grad = dot(turned[...], raw[:, :, head_rows(j)].reshape(KEYS, RLEN))
            q_grads[:, head_columns(j)] = (jnp.transpose(grad) * SCALE).astype(BF16)

    query_grads(0, 2)
    add_up(0)
    query_grads(2, HEADS)
    q_out = pltpu.make_async_copy(q_grads, dq_ref, in_sem.at[0])
    q_out.start()

    own_out.wait()
    q_out.wait()
    for u in range(1, UNITS):
        unit_copy(u).wait_send()

    @pl.when(jnp.logical_not(stays))
    def _():
        unit_copy(0).wait_send()

    for part in range(2):
        all_at_once(by_source[part], b_send.at[part])
        all_at_once(staged.at[part], c_send.at[part])
        all_at_once(grads.at[part], rc_send.at[part])
    for part in (1, 0):
        home_wait(part, rb_send.at[part])
        home_wait(part, rb_recv.at[part])

        @pl.when(stays)
        def _():
            home_stay(part).wait()


def finish_kernel(dq_ref, down_ref, back_ref, dq_out, down_out, dcache_out, dq, down, back, total, get_sems, put_sems):
    gets = [
        pltpu.make_async_copy(back_ref, back, get_sems.at[0]),
        pltpu.make_async_copy(dq_ref, dq, get_sems.at[1]),
        pltpu.make_async_copy(down_ref, down, get_sems.at[2]),
    ]
    puts = [
        pltpu.make_async_copy(total, dcache_out, put_sems.at[0]),
        pltpu.make_async_copy(dq, dq_out, put_sems.at[1]),
        pltpu.make_async_copy(down, down_out, put_sems.at[2]),
    ]
    for get in gets:
        get.start()
    gets[0].wait()
    for h in range(8):
        for part in range(2):
            first = back[part, UNITS * h : UNITS * (h + 1)].astype(F32)
            second = back[part, UNITS * (8 + h) : UNITS * (9 + h)].astype(F32)
            both = (first + second).astype(BF16).reshape(UNITS * UNIT, HD)
            total[:, h * WIDTH + part * HD : h * WIDTH + (part + 1) * HD] = both
    puts[0].start()
    for get, put in zip(gets[1:], puts[1:]):
        get.wait()
        put.start()
    for put in puts:
        put.wait()


def local(
    queries, resp_kv, prompt_cache, grad_out, group_counts, prompt_slot, slot_response, resp_len, weight_code
):
    smem = pl.BlockSpec(memory_space=pltpu.SMEM)
    hbm = pl.BlockSpec(memory_space=pltpu.HBM)
    scratch = [
        pltpu.SMEM((RING,), jnp.int32),
        pltpu.SMEM((2, RING), jnp.int32),
        pltpu.SMEM((RING,), jnp.int32),
        pltpu.SMEM((PROMPTS,), jnp.int32),
        pltpu.VMEM((RLEN, HEADS * HD), BF16),
        pltpu.VMEM((RLEN, HEADS * HD), BF16),
        pltpu.VMEM((RLEN, WIDTH), BF16),
        pltpu.VMEM((UNITS, UNIT, 8 * WIDTH), BF16),
        pltpu.VMEM((RING, UNITS, UNIT, HD), BF16),
        pltpu.VMEM((RING, UNITS, UNIT, HD), BF16),
        pltpu.VMEM((2, RING, CHUNK, HD), BF16),
        pltpu.VMEM((KEYS, HD), BF16),
        pltpu.VMEM((KEYS, HD), BF16),
        pltpu.VMEM((ROWS, HD), BF16),
        pltpu.VMEM((HD, ROWS), BF16),
        pltpu.VMEM((HD, ROWS), BF16),
        pltpu.VMEM((HD, ROWS), BF16),
        pltpu.VMEM((ROWS, HD), BF16),
        pltpu.VMEM((BLOCKS + 1, BLOCK, ROWS), F32),
        pltpu.VMEM((BLOCKS + 1, BLOCK, ROWS), BF16),
        pltpu.VMEM((8, ROWS), F32),
        pltpu.VMEM((8, ROWS), F32),
        pltpu.VMEM((8, ROWS), F32),
        pltpu.VMEM((HD, KEYS), BF16),
        pltpu.VMEM((BLOCKS + 1, BLOCK, HD), F32),
        pltpu.VMEM((2, RING, CHUNK, HD), BF16),
        pltpu.VMEM((2, RING, CHUNK, HD), BF16),
        pltpu.VMEM((RING + 1, CHUNK, HD), F32),
        pltpu.VMEM((2, RING * UNITS, UNIT, HD), BF16),
        pltpu.VMEM((RLEN, WIDTH), BF16),
        pltpu.VMEM((RLEN, HEADS * HD), BF16),
        pltpu.SemaphoreType.DMA((3,)),
        pltpu.SemaphoreType.DMA((UNITS,)),
        pltpu.SemaphoreType.DMA((UNITS,)),
        pltpu.SemaphoreType.DMA((2,)),
        pltpu.SemaphoreType.DMA((2,)),
        pltpu.SemaphoreType.DMA((2,)),
        pltpu.SemaphoreType.DMA((2, RING)),
        pltpu.SemaphoreType.DMA((2,)),
        pltpu.SemaphoreType.DMA((2,)),
        pltpu.SemaphoreType.DMA((2,)),
        pltpu.SemaphoreType.DMA((2,)),
        pltpu.SemaphoreType.DMA((2,)),
    ]
    products = 5 * ROWS * KEYS * HD
    dq, down, back = pl.pallas_call(
        kernel,
        out_shape=[
            jax.ShapeDtypeStruct(queries.shape, BF16),
            jax.ShapeDtypeStruct(resp_kv.shape, BF16),
            jax.ShapeDtypeStruct((2, RING * UNITS, UNIT, HD), BF16),
        ],
        in_specs=[smem] * 5 + [hbm] * 4,
        out_specs=[hbm] * 3,
        scratch_shapes=scratch,
        compiler_params=pltpu.CompilerParams(
            collective_id=0, has_side_effects=True, vmem_limit_bytes=VMEM_LIMIT
        ),
        cost_estimate=pl.CostEstimate(flops=2 * products, bytes_accessed=3 << 20, transcendentals=ROWS * KEYS),
    )(
        group_counts,
        prompt_slot,
        slot_response,
        resp_len,
        weight_code,
        queries,
        resp_kv,
        prompt_cache,
        grad_out,
    )
    return pl.pallas_call(
        finish_kernel,
        out_shape=[
            jax.ShapeDtypeStruct(queries.shape, BF16),
            jax.ShapeDtypeStruct(resp_kv.shape, BF16),
            jax.ShapeDtypeStruct(prompt_cache.shape, BF16),
        ],
        in_specs=[hbm] * 3,
        out_specs=[hbm] * 3,
        scratch_shapes=[
            pltpu.VMEM(queries.shape, BF16),
            pltpu.VMEM(resp_kv.shape, BF16),
            pltpu.VMEM((2, RING * UNITS, UNIT, HD), BF16),
            pltpu.VMEM(prompt_cache.shape, BF16),
            pltpu.SemaphoreType.DMA((3,)),
            pltpu.SemaphoreType.DMA((3,)),
        ],
        compiler_params=pltpu.CompilerParams(vmem_limit_bytes=VMEM_LIMIT),
    )(dq, down, back)


def solution(mesh):
    placed = (
        P("seq", "head"),
        P("seq", "head"),
        P(("seq", "head"), None),
        P("seq", "head"),
        P(),
        P(),
        P(),
        P("seq"),
        P("seq"),
    )
    return jax.shard_map(
        local,
        mesh=mesh,
        in_specs=placed,
        out_specs=(P("seq", "head"), P("seq", "head"), P(("seq", "head"), None)),
        check_vma=False,
    )
```

```python
import math

import jax
import jax.numpy as jnp
from jax import lax
from jax.experimental import pallas as pl
from jax.experimental.pallas import tpu as pltpu
from jax.sharding import PartitionSpec as P

HD = 128
PLEN = 2048
RLEN = 256
HEADS = 8
PROMPTS = 8
RING = 16
CHUNK = PLEN // RING
UNITS = 4
UNIT = 16
BLOCK = 256
BLOCKS = PLEN // BLOCK
PER_BLOCK = BLOCK // CHUNK
ROWS = HEADS * RLEN
KEYS = PLEN + RLEN
WIDTH = 2 * HD
SCALE = HD**-0.5
LOG2E = math.log2(math.e)
MESH = pl.DeviceIdType.MESH
VMEM_LIMIT = 60 * 1024 * 1024
NN = (((1,), (0,)), ((), ()))
F32 = jnp.float32
BF16 = jnp.bfloat16


def around(index):
    return lax.rem(index + 2 * RING, RING)


def div(a, b):
    return a // b if isinstance(a, int) else lax.div(a, b)


def rem(a, b):
    return a % b if isinstance(a, int) else lax.rem(a, b)


def plus(plane, offset):
    return 4 * rem(div(plane, 4) + div(offset, 4), 4) + rem(plane + rem(offset, 4), 4)


def minus(plane, offset):
    return 4 * rem(div(plane, 4) + 4 - div(offset, 4), 4) + rem(plane + 4 - rem(offset, 4), 4)


def turn(place):
    return rem(5 * place, RING)


def unit_offset(column, u):
    return 4 * u + lax.rem(column + u, 4)


def column_step(i):
    return 8 + div(i, 2) * (1 - 2 * rem(i, 2))


def head_rows(j):
    return slice(j * RLEN, (j + 1) * RLEN)


def head_columns(j):
    return slice(j * HD, (j + 1) * HD)


def chunk_rows(step):
    return pl.ds(pl.multiple_of(step * CHUNK, CHUNK), CHUNK)


def fold(values, op):
    return op(values.reshape(values.shape[0] // 8, 8, values.shape[1]), axis=0)


def dot(a, b):
    return lax.dot_general(a, b, NN, preferred_element_type=F32)


def kernel(
    counts_ref,
    prompt_slot_ref,
    response_ref,
    len_ref,
    code_ref,
    q_ref,
    own_ref,
    cache_ref,
    go_ref,
    dq_ref,
    down_ref,
    back_ref,
    across,
    first,
    previous,
    last,
    q_in,
    go_in,
    own_in,
    rows_in,
    keys_in,
    values_in,
    staged,
    keys,
    values,
    q_rows,
    q_cols,
    cot_cols,
    cot_scaled_cols,
    cot_scaled_rows,
    scores,
    raw,
    top,
    delta,
    inverse,
    turned,
    dv_sum,
    grads,
    terms,
    running,
    summed,
    own_grads,
    q_grads,
    in_sem,
    a_send,
    a_recv,
    b_send,
    b_recv,
    c_send,
    c_recv,
    rc_send,
    rc_recv,
    rb_send,
    rb_recv,
    stay_sem,
):
    seq = lax.axis_index("seq")
    head = lax.axis_index("head")
    plane = div(seq, 2)
    half = lax.rem(seq, 2)
    column = half * 8 + head

    def in_plane(other):
        return {"seq": 2 * other + half, "head": head}

    def in_column(other):
        return {"seq": 2 * plane + div(other, 8), "head": lax.rem(other, 8)}

    def remote(src, dst, send_sem, recv_sem, device):
        return pltpu.make_async_remote_copy(
            src_ref=src, dst_ref=dst, send_sem=send_sem, recv_sem=recv_sem, device_id=device, device_id_type=MESH
        )

    def all_at_once(buffer, sem):
        pltpu.make_async_copy(buffer.at[pl.ds(1, RING - 1)], buffer.at[pl.ds(1, RING - 1)], sem).wait()

    loads = [
        pltpu.make_async_copy(q_ref, q_in, in_sem.at[0]),
        pltpu.make_async_copy(go_ref, go_in, in_sem.at[1]),
        pltpu.make_async_copy(own_ref, own_in, in_sem.at[2]),
    ]
    for load in loads:
        load.start()

    barrier = pltpu.get_barrier_semaphore()
    stays = rem(column, 4) == 0

    def greet(device):
        pl.semaphore_signal(barrier, inc=1, device_id=device, device_id_type=MESH)

    def greet_column(step, carry):
        greet(in_column(around(column + step)))
        return carry

    def greet_unit(u):
        greet(in_plane(plus(plane, unit_offset(column, u))))
        greet(in_plane(minus(plane, unit_offset(column, u))))

    lax.fori_loop(1, RING, greet_column, 0)
    for u in range(1, UNITS):
        greet_unit(u)

    @pl.when(stays)
    def _():
        pl.semaphore_wait(barrier, RING - 1 + 2 * (UNITS - 1))

    @pl.when(jnp.logical_not(stays))
    def _():
        greet_unit(0)
        pl.semaphore_wait(barrier, RING - 1 + 2 * UNITS)

    def unit_copy(u):
        return remote(
            cache_ref.at[pl.ds(u * UNIT, UNIT)],
            rows_in.at[u],
            a_send.at[u],
            a_recv.at[u],
            in_plane(plus(plane, unit_offset(column, u))),
        )

    for u in range(1, UNITS):
        unit_copy(u).start()

    @pl.when(jnp.logical_not(stays))
    def _():
        unit_copy(0).start()

    @pl.when(stays)
    def _():
        pltpu.make_async_copy(cache_ref.at[pl.ds(0, UNIT)], rows_in.at[0], a_recv.at[0]).start()

    by_source = (keys_in, values_in)

    def column_copy(part, step):
        target = around(column + step)
        at = pl.ds(pl.multiple_of(lax.rem(target, 8) * WIDTH + part * HD, HD), HD)
        return remote(
            rows_in.at[:, :, at], by_source[part].at[column], b_send.at[part], b_recv.at[part], in_column(target)
        )

    def send_heads(part):
        def send(i, carry):
            column_copy(part, column_step(i)).start()
            return carry

        lax.fori_loop(1, RING, send, 0)
        by_source[part][column] = rows_in[:, :, pl.ds(pl.multiple_of(head * WIDTH + part * HD, HD), HD)]

    gathered = (keys, values)

    def chunk_copy(part, step):
        return remote(
            staged.at[part, step],
            gathered[part].at[chunk_rows(step)],
            c_send.at[part],
            c_recv.at[part, step],
            in_plane(plus(plane, turn(step))),
        )

    def send_chunks(part):
        def take(place):
            units = [by_source[part][4 * i + first[odd, place], across[place]] for odd in range(2) for i in range(4)]
            return jnp.concatenate(units, axis=0)

        all_at_once(by_source[part], b_recv.at[part])
        for step in range(1, RING):
            staged[part, step] = take(step)
            chunk_copy(part, step).start()
        gathered[part][:CHUNK] = take(0)

    ends = []
    for i in range(PROMPTS):
        ends.append(counts_ref[i] + (ends[-1] if ends else 0))
    prompts = []
    for step in range(RING):
        response = response_ref[2 * plus(plane, turn(step)) + half]
        group = jnp.int32(0)
        for end in ends[:-1]:
            group = group + (end <= response).astype(jnp.int32)
        prompt = prompt_slot_ref[group]
        prompts.append(prompt)
        way = rem(div(plane, 4) + 4 - div(prompt, 2), 4)
        across[step] = way
        for odd in range(2):
            first[odd, step] = rem(plane + 8 - 2 * rem(prompt, 2) - odd - way, 4)
    for step in range(RING):
        found = jnp.int32(RING)
        for other in range(step):
            found = jnp.where(prompts[other] == prompts[step], other, found)
        previous[step] = found
    for prompt in range(PROMPTS):
        found = jnp.int32(RING)
        for step in range(RING):
            found = jnp.where(prompts[step] == prompt, step, found)
        last[prompt] = found

    for load in loads:
        load.wait()
    position = lax.broadcasted_iota(jnp.int32, (RLEN, HD), 0)
    factor = jnp.where(position < len_ref[0], code_ref[0].astype(F32) / 8.0, 0.0)
    for j in range(HEADS):
        query = q_in[:, head_columns(j)]
        q_rows[head_rows(j)] = query
        q_cols[:, head_rows(j)] = jnp.transpose(query)
        cotangent = go_in[:, head_columns(j)].astype(F32) * factor
        cot_cols[:, head_rows(j)] = jnp.transpose(cotangent).astype(BF16)
    keys[PLEN:] = own_in[:, :HD]
    values[PLEN:] = own_in[:, HD:]
    running[RING] = jnp.zeros((CHUNK, HD), F32)

    def block_rows(b):
        return pl.ds(pl.multiple_of(b * BLOCK, BLOCK), BLOCK)

    def score(b, own):
        block = keys[block_rows(b)]
        for j in range(HEADS):
            at = head_rows(j)
            part = dot(block, q_cols[:, at])
            if own:
                key_at = lax.broadcasted_iota(jnp.int32, (BLOCK, RLEN), 0)
                seen_from = lax.broadcasted_iota(jnp.int32, (BLOCK, RLEN), 1)
                part = jnp.where(key_at <= seen_from, part, -1e30)
            scores[b, :, at] = part
            high = fold(part, jnp.max)
            top[:, at] = high if own else jnp.maximum(top[:, at], high)

    for u in range(UNITS):
        unit_copy(u).wait_recv()
    send_heads(0)
    send_heads(1)
    score(BLOCKS, True)
    send_chunks(0)
    send_chunks(1)

    def arrive(part, b):
        def one(i, carry):
            step = b * PER_BLOCK + i

            @pl.when(step > 0)
            def _():
                chunk_copy(part, step).wait_recv()

            return carry

        lax.fori_loop(0, PER_BLOCK, one, 0)

    def score_block(b, carry):
        arrive(0, b)
        score(b, False)
        return carry

    lax.fori_loop(0, BLOCKS, score_block, 0)

    def return_copy(part, step):
        return remote(
            grads.at[part, step],
            terms.at[part, step],
            rc_send.at[part],
            rc_recv.at[part],
            in_plane(minus(plane, turn(step))),
        )

    def send_back(part, b, block):
        for i in range(PER_BLOCK):
            grads[part, b * PER_BLOCK + i] = block[i * CHUNK : (i + 1) * CHUNK]

        def one(i, carry):
            step = b * PER_BLOCK + i

            @pl.when(step > 0)
            def _():
                return_copy(part, step).start()

            return carry

        lax.fori_loop(0, PER_BLOCK, one, 0)

    def pair_rows(p):
        return slice(2 * p * RLEN, 2 * (p + 1) * RLEN)

    def pair_grads(b, p):
        return dot(raw[b, :, pair_rows(p)], cot_scaled_rows[pair_rows(p)])

    for p in range(HEADS // 2):
        heads = (2 * p, 2 * p + 1)
        highest = [jnp.max(top[:, head_rows(j)], axis=0, keepdims=True) for j in heads]

        def weigh(b, totals):
            sums = []
            for j, high, total in zip(heads, highest, totals):
                at = head_rows(j)
                weights = jnp.exp2((scores[b, :, at] - high) * (SCALE * LOG2E))
                raw[b, :, at] = weights.astype(BF16)
                sums.append(total + fold(weights, jnp.sum))
            if p == 1:
                dv_sum[b] = pair_grads(b, 0)
            elif p > 1:
                dv_sum[b] += pair_grads(b, p - 1)
            return tuple(sums)

        totals = lax.fori_loop(0, BLOCKS + 1, weigh, (jnp.zeros((8, RLEN), F32),) * 2)
        for j, total in zip(heads, totals):
            at = head_rows(j)
            over = 1.0 / jnp.sum(total, axis=0, keepdims=True)
            inverse[:, at] = jnp.broadcast_to(over, (8, RLEN))
            scaled = cot_cols[:, at].astype(F32) * over
            cot_scaled_cols[:, at] = scaled.astype(BF16)
            cot_scaled_rows[at] = jnp.transpose(scaled).astype(BF16)

    def value_grads(b):
        return (dv_sum[b] + pair_grads(b, HEADS // 2 - 1)).astype(BF16)

    def value_block(b, carry):
        send_back(1, b, value_grads(b))
        return carry

    lax.fori_loop(0, BLOCKS, value_block, 0)

    def look(b, first):
        block = values[block_rows(b)]
        for j in range(HEADS):
            at = head_rows(j)
            grad = dot(block, cot_scaled_cols[:, at])
            scores[b, :, at] = grad
            term = fold(grad * raw[b, :, at].astype(F32), jnp.sum)
            delta[:, at] = term if first else delta[:, at] + term

    def look_block(b, carry):
        arrive(1, b)
        look(b, False)
        return carry

    look(BLOCKS, True)
    lax.fori_loop(0, BLOCKS, look_block, 0)
    for j in range(HEADS):
        at = head_rows(j)
        delta[:, at] = jnp.sum(delta[:, at], axis=0, keepdims=True) * inverse[:, at]

    def key_part(b):
        for j in range(HEADS):
            at = head_rows(j)
            weights = raw[b, :, at].astype(F32)
            shift = delta[0:1, at]
            change = (weights * (scores[b, :, at] - shift)).astype(BF16)
            raw[b, :, at] = change
        return (dot(raw[b], q_rows[...]) * SCALE).astype(BF16)

    def key_block(b, carry):
        send_back(0, b, key_part(b))
        return carry

    lax.fori_loop(0, BLOCKS, key_block, 0)

    def add_up(part):
        all_at_once(grads.at[part], rc_recv.at[part])
        terms[part, 0] = grads[part, 0]

        def add(step, carry):
            running[step] = running[previous[step]] + terms[part, step].astype(F32)
            return carry

        lax.fori_loop(0, RING, add, 0)

        def close(prompt, carry):
            units = running[last[prompt]].astype(BF16).reshape(CHUNK // UNIT, UNIT, HD)
            summed[pl.ds(prompt * (CHUNK // UNIT), CHUNK // UNIT), part] = units
            return carry

        lax.fori_loop(0, PROMPTS, close, 0)

    def home_copy(target, u):
        x = rem(div(plane, 4) + 4 - u, 4)
        y = rem(plane + 20 - target - u, 4)
        source = 4 * x + y
        return remote(
            summed.at[4 * source + div(target, 4)],
            back_ref.at[4 * column + u],
            rb_send,
            rb_recv,
            {"seq": 2 * source + div(target, 8), "head": rem(target, 8)},
        )

    home_stay = pltpu.make_async_copy(
        summed.at[4 * plane + div(column, 4)], back_ref.at[4 * column], stay_sem
    )

    def send_home():
        def send(i, carry):
            target = around(column + column_step(i))
            for u in range(UNITS):
                home_copy(target, u).start()
            return carry

        lax.fori_loop(1, RING, send, 0)
        for u in range(1, UNITS):
            home_copy(column, u).start()

        @pl.when(jnp.logical_not(stays))
        def _():
            home_copy(column, 0).start()

        @pl.when(stays)
        def _():
            home_stay.start()

    def home_wait(sem):
        @pl.when(jnp.logical_not(stays))
        def _():
            pltpu.make_async_copy(back_ref, back_ref, sem).wait()

        @pl.when(stays)
        def _():
            rest = back_ref.at[pl.ds(1, RING * UNITS - 1)]
            pltpu.make_async_copy(rest, rest, sem).wait()

    add_up(1)

    own_grads[:, HD:] = value_grads(BLOCKS)
    own_grads[:, :HD] = key_part(BLOCKS)
    own_out = pltpu.make_async_copy(own_grads, down_ref, in_sem.at[2])
    own_out.start()
    def query_grads(first, end):
        turned[...] = jnp.transpose(keys[...])
        for j in range(first, end):
            grad = dot(turned[...], raw[:, :, head_rows(j)].reshape(KEYS, RLEN))
            q_grads[:, head_columns(j)] = (jnp.transpose(grad) * SCALE).astype(BF16)

    add_up(0)
    send_home()
    query_grads(0, HEADS)
    q_out = pltpu.make_async_copy(q_grads, dq_ref, in_sem.at[0])
    q_out.start()

    own_out.wait()
    q_out.wait()
    for u in range(1, UNITS):
        unit_copy(u).wait_send()

    @pl.when(jnp.logical_not(stays))
    def _():
        unit_copy(0).wait_send()

    for part in range(2):
        all_at_once(by_source[part], b_send.at[part])
        all_at_once(staged.at[part], c_send.at[part])
        all_at_once(grads.at[part], rc_send.at[part])
    home_wait(rb_send)
    home_wait(rb_recv)

    @pl.when(stays)
    def _():
        home_stay.wait()


def finish_kernel(dq_ref, down_ref, back_ref, dq_out, down_out, dcache_out, dq, down, back, total, get_sems, put_sems):
    gets = [
        pltpu.make_async_copy(back_ref, back, get_sems.at[0]),
        pltpu.make_async_copy(dq_ref, dq, get_sems.at[1]),
        pltpu.make_async_copy(down_ref, down, get_sems.at[2]),
    ]
    puts = [
        pltpu.make_async_copy(total, dcache_out, put_sems.at[0]),
        pltpu.make_async_copy(dq, dq_out, put_sems.at[1]),
        pltpu.make_async_copy(down, down_out, put_sems.at[2]),
    ]
    for get in gets:
        get.start()
    gets[0].wait()
    for h in range(8):
        for part in range(2):
            first = back[UNITS * h : UNITS * (h + 1), part].astype(F32)
            second = back[UNITS * (8 + h) : UNITS * (9 + h), part].astype(F32)
            both = (first + second).astype(BF16).reshape(UNITS * UNIT, HD)
            total[:, h * WIDTH + part * HD : h * WIDTH + (part + 1) * HD] = both
    puts[0].start()
    for get, put in zip(gets[1:], puts[1:]):
        get.wait()
        put.start()
    for put in puts:
        put.wait()


def local(
    queries, resp_kv, prompt_cache, grad_out, group_counts, prompt_slot, slot_response, resp_len, weight_code
):
    smem = pl.BlockSpec(memory_space=pltpu.SMEM)
    hbm = pl.BlockSpec(memory_space=pltpu.HBM)
    scratch = [
        pltpu.SMEM((RING,), jnp.int32),
        pltpu.SMEM((2, RING), jnp.int32),
        pltpu.SMEM((RING,), jnp.int32),
        pltpu.SMEM((PROMPTS,), jnp.int32),
        pltpu.VMEM((RLEN, HEADS * HD), BF16),
        pltpu.VMEM((RLEN, HEADS * HD), BF16),
        pltpu.VMEM((RLEN, WIDTH), BF16),
        pltpu.VMEM((UNITS, UNIT, 8 * WIDTH), BF16),
        pltpu.VMEM((RING, UNITS, UNIT, HD), BF16),
        pltpu.VMEM((RING, UNITS, UNIT, HD), BF16),
        pltpu.VMEM((2, RING, CHUNK, HD), BF16),
        pltpu.VMEM((KEYS, HD), BF16),
        pltpu.VMEM((KEYS, HD), BF16),
        pltpu.VMEM((ROWS, HD), BF16),
        pltpu.VMEM((HD, ROWS), BF16),
        pltpu.VMEM((HD, ROWS), BF16),
        pltpu.VMEM((HD, ROWS), BF16),
        pltpu.VMEM((ROWS, HD), BF16),
        pltpu.VMEM((BLOCKS + 1, BLOCK, ROWS), F32),
        pltpu.VMEM((BLOCKS + 1, BLOCK, ROWS), BF16),
        pltpu.VMEM((8, ROWS), F32),
        pltpu.VMEM((8, ROWS), F32),
        pltpu.VMEM((8, ROWS), F32),
        pltpu.VMEM((HD, KEYS), BF16),
        pltpu.VMEM((BLOCKS + 1, BLOCK, HD), F32),
        pltpu.VMEM((2, RING, CHUNK, HD), BF16),
        pltpu.VMEM((2, RING, CHUNK, HD), BF16),
        pltpu.VMEM((RING + 1, CHUNK, HD), F32),
        pltpu.VMEM((RING * UNITS, 2, UNIT, HD), BF16),
        pltpu.VMEM((RLEN, WIDTH), BF16),
        pltpu.VMEM((RLEN, HEADS * HD), BF16),
        pltpu.SemaphoreType.DMA((3,)),
        pltpu.SemaphoreType.DMA((UNITS,)),
        pltpu.SemaphoreType.DMA((UNITS,)),
        pltpu.SemaphoreType.DMA((2,)),
        pltpu.SemaphoreType.DMA((2,)),
        pltpu.SemaphoreType.DMA((2,)),
        pltpu.SemaphoreType.DMA((2, RING)),
        pltpu.SemaphoreType.DMA((2,)),
        pltpu.SemaphoreType.DMA((2,)),
        pltpu.SemaphoreType.DMA,
        pltpu.SemaphoreType.DMA,
        pltpu.SemaphoreType.DMA,
    ]
    products = 5 * ROWS * KEYS * HD
    dq, down, back = pl.pallas_call(
        kernel,
        out_shape=[
            jax.ShapeDtypeStruct(queries.shape, BF16),
            jax.ShapeDtypeStruct(resp_kv.shape, BF16),
            jax.ShapeDtypeStruct((RING * UNITS, 2, UNIT, HD), BF16),
        ],
        in_specs=[smem] * 5 + [hbm] * 4,
        out_specs=[hbm] * 3,
        scratch_shapes=scratch,
        compiler_params=pltpu.CompilerParams(
            collective_id=0, has_side_effects=True, vmem_limit_bytes=VMEM_LIMIT
        ),
        cost_estimate=pl.CostEstimate(flops=2 * products, bytes_accessed=3 << 20, transcendentals=ROWS * KEYS),
    )(
        group_counts,
        prompt_slot,
        slot_response,
        resp_len,
        weight_code,
        queries,
        resp_kv,
        prompt_cache,
        grad_out,
    )
    return pl.pallas_call(
        finish_kernel,
        out_shape=[
            jax.ShapeDtypeStruct(queries.shape, BF16),
            jax.ShapeDtypeStruct(resp_kv.shape, BF16),
            jax.ShapeDtypeStruct(prompt_cache.shape, BF16),
        ],
        in_specs=[hbm] * 3,
        out_specs=[hbm] * 3,
        scratch_shapes=[
            pltpu.VMEM(queries.shape, BF16),
            pltpu.VMEM(resp_kv.shape, BF16),
            pltpu.VMEM((RING * UNITS, 2, UNIT, HD), BF16),
            pltpu.VMEM(prompt_cache.shape, BF16),
            pltpu.SemaphoreType.DMA((3,)),
            pltpu.SemaphoreType.DMA((3,)),
        ],
        compiler_params=pltpu.CompilerParams(vmem_limit_bytes=VMEM_LIMIT),
    )(dq, down, back)


def solution(mesh):
    placed = (
        P("seq", "head"),
        P("seq", "head"),
        P(("seq", "head"), None),
        P("seq", "head"),
        P(),
        P(),
        P(),
        P("seq"),
        P("seq"),
    )
    return jax.shard_map(
        local,
        mesh=mesh,
        in_specs=placed,
        out_specs=(P("seq", "head"), P("seq", "head"), P(("seq", "head"), None)),
        check_vma=False,
    )
```

```python
import math

import jax
import jax.numpy as jnp
from jax import lax
from jax.experimental import pallas as pl
from jax.experimental.pallas import tpu as pltpu
from jax.sharding import PartitionSpec as P

HD = 128
PLEN = 2048
RLEN = 256
HEADS = 8
PROMPTS = 8
RING = 16
CHUNK = PLEN // RING
UNITS = 4
UNIT = 16
BLOCK = 256
BLOCKS = PLEN // BLOCK
PER_BLOCK = BLOCK // CHUNK
ROWS = HEADS * RLEN
KEYS = PLEN + RLEN
WIDTH = 2 * HD
SCALE = HD**-0.5
LOG2E = math.log2(math.e)
MESH = pl.DeviceIdType.MESH
VMEM_LIMIT = 60 * 1024 * 1024
NN = (((1,), (0,)), ((), ()))
F32 = jnp.float32
BF16 = jnp.bfloat16


def around(index):
    return lax.rem(index + 2 * RING, RING)


def div(a, b):
    return a // b if isinstance(a, int) else lax.div(a, b)


def rem(a, b):
    return a % b if isinstance(a, int) else lax.rem(a, b)


def plus(plane, offset):
    return 4 * rem(div(plane, 4) + div(offset, 4), 4) + rem(plane + rem(offset, 4), 4)


def minus(plane, offset):
    return 4 * rem(div(plane, 4) + 4 - div(offset, 4), 4) + rem(plane + 4 - rem(offset, 4), 4)


def turn(place):
    return rem(5 * place, RING)


def unit_offset(column, u):
    return 4 * u + lax.rem(column + u, 4)


def column_step(i):
    return 8 + div(i, 2) * (1 - 2 * rem(i, 2))


def head_rows(j):
    return slice(j * RLEN, (j + 1) * RLEN)


def head_columns(j):
    return slice(j * HD, (j + 1) * HD)


def chunk_rows(step):
    return pl.ds(pl.multiple_of(step * CHUNK, CHUNK), CHUNK)


def fold(values, op):
    return op(values.reshape(values.shape[0] // 8, 8, values.shape[1]), axis=0)


def dot(a, b):
    return lax.dot_general(a, b, NN, preferred_element_type=F32)


def kernel(
    counts_ref,
    prompt_slot_ref,
    response_ref,
    len_ref,
    code_ref,
    q_ref,
    own_ref,
    cache_ref,
    go_ref,
    dq_ref,
    down_ref,
    back_ref,
    across,
    first,
    previous,
    last,
    q_in,
    go_in,
    own_in,
    rows_in,
    keys_in,
    values_in,
    staged,
    keys,
    values,
    q_rows,
    q_cols,
    cot_cols,
    cot_scaled_cols,
    cot_scaled_rows,
    scores,
    raw,
    top,
    delta,
    inverse,
    turned,
    dv_sum,
    grads,
    terms,
    running,
    summed,
    own_grads,
    q_grads,
    in_sem,
    a_send,
    a_recv,
    b_send,
    b_recv,
    c_send,
    c_recv,
    rc_send,
    rc_recv,
    rb_send,
    rb_recv,
    stay_sem,
):
    seq = lax.axis_index("seq")
    head = lax.axis_index("head")
    plane = div(seq, 2)
    half = lax.rem(seq, 2)
    column = half * 8 + head

    def in_plane(other):
        return {"seq": 2 * other + half, "head": head}

    def in_column(other):
        return {"seq": 2 * plane + div(other, 8), "head": lax.rem(other, 8)}

    def remote(src, dst, send_sem, recv_sem, device):
        return pltpu.make_async_remote_copy(
            src_ref=src, dst_ref=dst, send_sem=send_sem, recv_sem=recv_sem, device_id=device, device_id_type=MESH
        )

    def all_at_once(buffer, sem):
        pltpu.make_async_copy(buffer.at[pl.ds(1, RING - 1)], buffer.at[pl.ds(1, RING - 1)], sem).wait()

    loads = [
        pltpu.make_async_copy(q_ref, q_in, in_sem.at[0]),
        pltpu.make_async_copy(go_ref, go_in, in_sem.at[1]),
        pltpu.make_async_copy(own_ref, own_in, in_sem.at[2]),
    ]
    for load in loads:
        load.start()

    barrier = pltpu.get_barrier_semaphore()
    stays = rem(column, 4) == 0

    def greet(device):
        pl.semaphore_signal(barrier, inc=1, device_id=device, device_id_type=MESH)

    def greet_column(step, carry):
        greet(in_column(around(column + step)))
        return carry

    def greet_unit(u):
        greet(in_plane(plus(plane, unit_offset(column, u))))
        greet(in_plane(minus(plane, unit_offset(column, u))))

    lax.fori_loop(1, RING, greet_column, 0)
    for u in range(1, UNITS):
        greet_unit(u)

    @pl.when(stays)
    def _():
        pl.semaphore_wait(barrier, RING - 1 + 2 * (UNITS - 1))

    @pl.when(jnp.logical_not(stays))
    def _():
        greet_unit(0)
        pl.semaphore_wait(barrier, RING - 1 + 2 * UNITS)

    def unit_copy(u):
        return remote(
            cache_ref.at[pl.ds(u * UNIT, UNIT)],
            rows_in.at[u],
            a_send.at[u],
            a_recv.at[u],
            in_plane(plus(plane, unit_offset(column, u))),
        )

    for u in range(1, UNITS):
        unit_copy(u).start()

    @pl.when(jnp.logical_not(stays))
    def _():
        unit_copy(0).start()

    @pl.when(stays)
    def _():
        pltpu.make_async_copy(cache_ref.at[pl.ds(0, UNIT)], rows_in.at[0], a_recv.at[0]).start()

    by_source = (keys_in, values_in)

    def column_copy(part, step):
        target = around(column + step)
        at = pl.ds(pl.multiple_of(lax.rem(target, 8) * WIDTH + part * HD, HD), HD)
        return remote(
            rows_in.at[:, :, at], by_source[part].at[column], b_send.at[part], b_recv.at[part], in_column(target)
        )

    def send_heads(part):
        def send(i, carry):
            column_copy(part, column_step(i)).start()
            return carry

        lax.fori_loop(1, RING, send, 0)
        by_source[part][column] = rows_in[:, :, pl.ds(pl.multiple_of(head * WIDTH + part * HD, HD), HD)]

    gathered = (keys, values)

    def chunk_copy(part, step):
        return remote(
            staged.at[part, step],
            gathered[part].at[chunk_rows(step)],
            c_send.at[part],
            c_recv.at[part, step],
            in_plane(plus(plane, turn(step))),
        )

    def send_chunks(part):
        def take(place):
            units = [by_source[part][4 * i + first[odd, place], across[place]] for odd in range(2) for i in range(4)]
            return jnp.concatenate(units, axis=0)

        all_at_once(by_source[part], b_recv.at[part])
        for step in range(1, RING):
            staged[part, step] = take(step)
            chunk_copy(part, step).start()
        gathered[part][:CHUNK] = take(0)

    ends = []
    for i in range(PROMPTS):
        ends.append(counts_ref[i] + (ends[-1] if ends else 0))
    prompts = []
    for step in range(RING):
        response = response_ref[2 * plus(plane, turn(step)) + half]
        group = jnp.int32(0)
        for end in ends[:-1]:
            group = group + (end <= response).astype(jnp.int32)
        prompt = prompt_slot_ref[group]
        prompts.append(prompt)
        way = rem(div(plane, 4) + 4 - div(prompt, 2), 4)
        across[step] = way
        for odd in range(2):
            first[odd, step] = rem(plane + 8 - 2 * rem(prompt, 2) - odd - way, 4)
    for step in range(RING):
        found = jnp.int32(RING)
        for other in range(step):
            found = jnp.where(prompts[other] == prompts[step], other, found)
        previous[step] = found
    for prompt in range(PROMPTS):
        found = jnp.int32(RING)
        for step in range(RING):
            found = jnp.where(prompts[step] == prompt, step, found)
        last[prompt] = found

    for load in loads:
        load.wait()
    position = lax.broadcasted_iota(jnp.int32, (RLEN, HD), 0)
    factor = jnp.where(position < len_ref[0], code_ref[0].astype(F32) / 8.0, 0.0)
    for j in range(HEADS):
        query = q_in[:, head_columns(j)]
        q_rows[head_rows(j)] = query
        q_cols[:, head_rows(j)] = jnp.transpose(query)
        cotangent = go_in[:, head_columns(j)].astype(F32) * factor
        cot_cols[:, head_rows(j)] = jnp.transpose(cotangent).astype(BF16)
    keys[PLEN:] = own_in[:, :HD]
    values[PLEN:] = own_in[:, HD:]
    running[RING] = jnp.zeros((CHUNK, HD), F32)

    def block_rows(b):
        return pl.ds(pl.multiple_of(b * BLOCK, BLOCK), BLOCK)

    def score(b, own):
        block = keys[block_rows(b)]
        for j in range(HEADS):
            at = head_rows(j)
            part = dot(block, q_cols[:, at])
            if own:
                key_at = lax.broadcasted_iota(jnp.int32, (BLOCK, RLEN), 0)
                seen_from = lax.broadcasted_iota(jnp.int32, (BLOCK, RLEN), 1)
                part = jnp.where(key_at <= seen_from, part, -1e30)
            scores[b, :, at] = part
            high = fold(part, jnp.max)
            top[:, at] = high if own else jnp.maximum(top[:, at], high)

    for u in range(UNITS):
        unit_copy(u).wait_recv()
    send_heads(0)
    send_heads(1)
    score(BLOCKS, True)
    send_chunks(0)
    send_chunks(1)

    def arrive(part, b):
        def one(i, carry):
            step = b * PER_BLOCK + i

            @pl.when(step > 0)
            def _():
                chunk_copy(part, step).wait_recv()

            return carry

        lax.fori_loop(0, PER_BLOCK, one, 0)

    def score_block(b, carry):
        arrive(0, b)
        score(b, False)
        return carry

    lax.fori_loop(0, BLOCKS, score_block, 0)

    def return_copy(part, step):
        return remote(
            grads.at[part, step],
            terms.at[part, step],
            rc_send.at[part],
            rc_recv.at[part],
            in_plane(minus(plane, turn(step))),
        )

    def send_back(part, b, block):
        for i in range(PER_BLOCK):
            grads[part, b * PER_BLOCK + i] = block[i * CHUNK : (i + 1) * CHUNK]

        def one(i, carry):
            step = b * PER_BLOCK + i

            @pl.when(step > 0)
            def _():
                return_copy(part, step).start()

            return carry

        lax.fori_loop(0, PER_BLOCK, one, 0)

    def pair_rows(p):
        return slice(2 * p * RLEN, 2 * (p + 1) * RLEN)

    def pair_grads(b, p):
        return dot(raw[b, :, pair_rows(p)], cot_scaled_rows[pair_rows(p)])

    for p in range(HEADS // 2):
        heads = (2 * p, 2 * p + 1)
        highest = [jnp.max(top[:, head_rows(j)], axis=0, keepdims=True) for j in heads]

        def weigh(b, totals):
            sums = []
            for j, high, total in zip(heads, highest, totals):
                at = head_rows(j)
                weights = jnp.exp2((scores[b, :, at] - high) * (SCALE * LOG2E))
                raw[b, :, at] = weights.astype(BF16)
                sums.append(total + fold(weights, jnp.sum))
            if p == 1:
                dv_sum[b] = pair_grads(b, 0)
            elif p > 1:
                dv_sum[b] += pair_grads(b, p - 1)
            return tuple(sums)

        totals = lax.fori_loop(0, BLOCKS + 1, weigh, (jnp.zeros((8, RLEN), F32),) * 2)
        for j, total in zip(heads, totals):
            at = head_rows(j)
            over = 1.0 / jnp.sum(total, axis=0, keepdims=True)
            inverse[:, at] = jnp.broadcast_to(over, (8, RLEN))
            scaled = cot_cols[:, at].astype(F32) * over
            cot_scaled_cols[:, at] = scaled.astype(BF16)
            cot_scaled_rows[at] = jnp.transpose(scaled).astype(BF16)

    def value_grads(b):
        return (dv_sum[b] + pair_grads(b, HEADS // 2 - 1)).astype(BF16)

    def value_block(b, carry):
        send_back(1, b, value_grads(b))
        return carry

    lax.fori_loop(0, BLOCKS, value_block, 0)

    def look(b, first):
        block = values[block_rows(b)]
        for j in range(HEADS):
            at = head_rows(j)
            grad = dot(block, cot_scaled_cols[:, at])
            scores[b, :, at] = grad
            term = fold(grad * raw[b, :, at].astype(F32), jnp.sum)
            delta[:, at] = term if first else delta[:, at] + term

    def look_block(b, carry):
        arrive(1, b)
        look(b, False)
        return carry

    look(BLOCKS, True)
    lax.fori_loop(0, BLOCKS, look_block, 0)
    for j in range(HEADS):
        at = head_rows(j)
        delta[:, at] = jnp.sum(delta[:, at], axis=0, keepdims=True) * inverse[:, at]

    def key_part(b):
        for j in range(HEADS):
            at = head_rows(j)
            weights = raw[b, :, at].astype(F32)
            shift = delta[0:1, at]
            change = (weights * (scores[b, :, at] - shift)).astype(BF16)
            raw[b, :, at] = change
        return (dot(raw[b], q_rows[...]) * SCALE).astype(BF16)

    def key_block(b, carry):
        send_back(0, b, key_part(b))
        return carry


    def home_copy(part, target, u):
        x = rem(div(plane, 4) + 4 - u, 4)
        y = rem(plane + 20 - target - u, 4)
        source = 4 * x + y
        return remote(
            summed.at[part, 4 * source + div(target, 4)],
            back_ref.at[part, 4 * column + u],
            rb_send.at[part],
            rb_recv.at[part],
            {"seq": 2 * source + div(target, 8), "head": rem(target, 8)},
        )

    def home_stay(part):
        return pltpu.make_async_copy(
            summed.at[part, 4 * plane + div(column, 4)],
            back_ref.at[part, 4 * column],
            stay_sem.at[part],
        )

    def add_up(part):
        all_at_once(grads.at[part], rc_recv.at[part])
        terms[part, 0] = grads[part, 0]

        def add(step, carry):
            running[step] = running[previous[step]] + terms[part, step].astype(F32)
            return carry

        lax.fori_loop(0, RING, add, 0)

        def close(prompt, carry):
            units = running[last[prompt]].astype(BF16).reshape(CHUNK // UNIT, UNIT, HD)
            summed[part, pl.ds(prompt * (CHUNK // UNIT), CHUNK // UNIT)] = units
            return carry

        lax.fori_loop(0, PROMPTS, close, 0)

        def send(i, carry):
            target = around(column + column_step(i))
            for u in range(UNITS):
                home_copy(part, target, u).start()
            return carry

        lax.fori_loop(1, RING, send, 0)
        for u in range(1, UNITS):
            home_copy(part, column, u).start()

        @pl.when(jnp.logical_not(stays))
        def _():
            home_copy(part, column, 0).start()

        @pl.when(stays)
        def _():
            home_stay(part).start()

    def home_wait(part, sem):
        @pl.when(jnp.logical_not(stays))
        def _():
            pltpu.make_async_copy(back_ref.at[part], back_ref.at[part], sem).wait()

        @pl.when(stays)
        def _():
            rest = back_ref.at[part, pl.ds(1, RING * UNITS - 1)]
            pltpu.make_async_copy(rest, rest, sem).wait()

    lax.fori_loop(0, 5, key_block, 0)
    add_up(1)
    lax.fori_loop(5, BLOCKS, key_block, 0)

    own_grads[:, HD:] = value_grads(BLOCKS)
    own_grads[:, :HD] = key_part(BLOCKS)
    own_out = pltpu.make_async_copy(own_grads, down_ref, in_sem.at[2])
    own_out.start()
    turned[...] = jnp.transpose(keys[...])

    def query_grads(first, end):
        for j in range(first, end):
            grad = dot(turned[...], raw[:, :, head_rows(j)].reshape(KEYS, RLEN))
            q_grads[:, head_columns(j)] = (jnp.transpose(grad) * SCALE).astype(BF16)

    add_up(0)
    query_grads(0, HEADS)
    q_out = pltpu.make_async_copy(q_grads, dq_ref, in_sem.at[0])
    q_out.start()

    own_out.wait()
    q_out.wait()
    for u in range(1, UNITS):
        unit_copy(u).wait_send()

    @pl.when(jnp.logical_not(stays))
    def _():
        unit_copy(0).wait_send()

    for part in range(2):
        all_at_once(by_source[part], b_send.at[part])
        all_at_once(staged.at[part], c_send.at[part])
        all_at_once(grads.at[part], rc_send.at[part])
    for part in (1, 0):
        home_wait(part, rb_send.at[part])
        home_wait(part, rb_recv.at[part])

        @pl.when(stays)
        def _():
            home_stay(part).wait()


def finish_kernel(dq_ref, down_ref, back_ref, dq_out, down_out, dcache_out, dq, down, back, total, get_sems, put_sems):
    gets = [
        pltpu.make_async_copy(back_ref, back, get_sems.at[0]),
        pltpu.make_async_copy(dq_ref, dq, get_sems.at[1]),
        pltpu.make_async_copy(down_ref, down, get_sems.at[2]),
    ]
    puts = [
        pltpu.make_async_copy(total, dcache_out, put_sems.at[0]),
        pltpu.make_async_copy(dq, dq_out, put_sems.at[1]),
        pltpu.make_async_copy(down, down_out, put_sems.at[2]),
    ]
    for get in gets:
        get.start()
    gets[0].wait()
    for h in range(8):
        for part in range(2):
            first = back[part, UNITS * h : UNITS * (h + 1)].astype(F32)
            second = back[part, UNITS * (8 + h) : UNITS * (9 + h)].astype(F32)
            both = (first + second).astype(BF16).reshape(UNITS * UNIT, HD)
            total[:, h * WIDTH + part * HD : h * WIDTH + (part + 1) * HD] = both
    puts[0].start()
    for get, put in zip(gets[1:], puts[1:]):
        get.wait()
        put.start()
    for put in puts:
        put.wait()


def local(
    queries, resp_kv, prompt_cache, grad_out, group_counts, prompt_slot, slot_response, resp_len, weight_code
):
    smem = pl.BlockSpec(memory_space=pltpu.SMEM)
    hbm = pl.BlockSpec(memory_space=pltpu.HBM)
    scratch = [
        pltpu.SMEM((RING,), jnp.int32),
        pltpu.SMEM((2, RING), jnp.int32),
        pltpu.SMEM((RING,), jnp.int32),
        pltpu.SMEM((PROMPTS,), jnp.int32),
        pltpu.VMEM((RLEN, HEADS * HD), BF16),
        pltpu.VMEM((RLEN, HEADS * HD), BF16),
        pltpu.VMEM((RLEN, WIDTH), BF16),
        pltpu.VMEM((UNITS, UNIT, 8 * WIDTH), BF16),
        pltpu.VMEM((RING, UNITS, UNIT, HD), BF16),
        pltpu.VMEM((RING, UNITS, UNIT, HD), BF16),
        pltpu.VMEM((2, RING, CHUNK, HD), BF16),
        pltpu.VMEM((KEYS, HD), BF16),
        pltpu.VMEM((KEYS, HD), BF16),
        pltpu.VMEM((ROWS, HD), BF16),
        pltpu.VMEM((HD, ROWS), BF16),
        pltpu.VMEM((HD, ROWS), BF16),
        pltpu.VMEM((HD, ROWS), BF16),
        pltpu.VMEM((ROWS, HD), BF16),
        pltpu.VMEM((BLOCKS + 1, BLOCK, ROWS), F32),
        pltpu.VMEM((BLOCKS + 1, BLOCK, ROWS), BF16),
        pltpu.VMEM((8, ROWS), F32),
        pltpu.VMEM((8, ROWS), F32),
        pltpu.VMEM((8, ROWS), F32),
        pltpu.VMEM((HD, KEYS), BF16),
        pltpu.VMEM((BLOCKS + 1, BLOCK, HD), F32),
        pltpu.VMEM((2, RING, CHUNK, HD), BF16),
        pltpu.VMEM((2, RING, CHUNK, HD), BF16),
        pltpu.VMEM((RING + 1, CHUNK, HD), F32),
        pltpu.VMEM((2, RING * UNITS, UNIT, HD), BF16),
        pltpu.VMEM((RLEN, WIDTH), BF16),
        pltpu.VMEM((RLEN, HEADS * HD), BF16),
        pltpu.SemaphoreType.DMA((3,)),
        pltpu.SemaphoreType.DMA((UNITS,)),
        pltpu.SemaphoreType.DMA((UNITS,)),
        pltpu.SemaphoreType.DMA((2,)),
        pltpu.SemaphoreType.DMA((2,)),
        pltpu.SemaphoreType.DMA((2,)),
        pltpu.SemaphoreType.DMA((2, RING)),
        pltpu.SemaphoreType.DMA((2,)),
        pltpu.SemaphoreType.DMA((2,)),
        pltpu.SemaphoreType.DMA((2,)),
        pltpu.SemaphoreType.DMA((2,)),
        pltpu.SemaphoreType.DMA((2,)),
    ]
    products = 5 * ROWS * KEYS * HD
    dq, down, back = pl.pallas_call(
        kernel,
        out_shape=[
            jax.ShapeDtypeStruct(queries.shape, BF16),
            jax.ShapeDtypeStruct(resp_kv.shape, BF16),
            jax.ShapeDtypeStruct((2, RING * UNITS, UNIT, HD), BF16),
        ],
        in_specs=[smem] * 5 + [hbm] * 4,
        out_specs=[hbm] * 3,
        scratch_shapes=scratch,
        compiler_params=pltpu.CompilerParams(
            collective_id=0, has_side_effects=True, vmem_limit_bytes=VMEM_LIMIT
        ),
        cost_estimate=pl.CostEstimate(flops=2 * products, bytes_accessed=3 << 20, transcendentals=ROWS * KEYS),
    )(
        group_counts,
        prompt_slot,
        slot_response,
        resp_len,
        weight_code,
        queries,
        resp_kv,
        prompt_cache,
        grad_out,
    )
    return pl.pallas_call(
        finish_kernel,
        out_shape=[
            jax.ShapeDtypeStruct(queries.shape, BF16),
            jax.ShapeDtypeStruct(resp_kv.shape, BF16),
            jax.ShapeDtypeStruct(prompt_cache.shape, BF16),
        ],
        in_specs=[hbm] * 3,
        out_specs=[hbm] * 3,
        scratch_shapes=[
            pltpu.VMEM(queries.shape, BF16),
            pltpu.VMEM(resp_kv.shape, BF16),
            pltpu.VMEM((2, RING * UNITS, UNIT, HD), BF16),
            pltpu.VMEM(prompt_cache.shape, BF16),
            pltpu.SemaphoreType.DMA((3,)),
            pltpu.SemaphoreType.DMA((3,)),
        ],
        compiler_params=pltpu.CompilerParams(vmem_limit_bytes=VMEM_LIMIT),
    )(dq, down, back)


def solution(mesh):
    placed = (
        P("seq", "head"),
        P("seq", "head"),
        P(("seq", "head"), None),
        P("seq", "head"),
        P(),
        P(),
        P(),
        P("seq"),
        P("seq"),
    )
    return jax.shard_map(
        local,
        mesh=mesh,
        in_specs=placed,
        out_specs=(P("seq", "head"), P("seq", "head"), P(("seq", "head"), None)),
        check_vma=False,
    )
```

```python
import math

import jax
import jax.numpy as jnp
from jax import lax
from jax.experimental import pallas as pl
from jax.experimental.pallas import tpu as pltpu
from jax.sharding import PartitionSpec as P

HD = 128
PLEN = 2048
RLEN = 256
HEADS = 8
PROMPTS = 8
RING = 16
CHUNK = PLEN // RING
UNITS = 4
UNIT = 16
BLOCK = 256
BLOCKS = PLEN // BLOCK
PER_BLOCK = BLOCK // CHUNK
ROWS = HEADS * RLEN
KEYS = PLEN + RLEN
WIDTH = 2 * HD
SCALE = HD**-0.5
LOG2E = math.log2(math.e)
MESH = pl.DeviceIdType.MESH
VMEM_LIMIT = 60 * 1024 * 1024
NN = (((1,), (0,)), ((), ()))
F32 = jnp.float32
BF16 = jnp.bfloat16


def around(index):
    return lax.rem(index + 2 * RING, RING)


def div(a, b):
    return a // b if isinstance(a, int) else lax.div(a, b)


def rem(a, b):
    return a % b if isinstance(a, int) else lax.rem(a, b)


def plus(plane, offset):
    return 4 * rem(div(plane, 4) + div(offset, 4), 4) + rem(plane + rem(offset, 4), 4)


def minus(plane, offset):
    return 4 * rem(div(plane, 4) + 4 - div(offset, 4), 4) + rem(plane + 4 - rem(offset, 4), 4)


def turn(place):
    return rem(5 * place, RING)


def unit_offset(column, u):
    return 4 * u + lax.rem(column + u, 4)


def column_step(i):
    return 8 + div(i, 2) * (1 - 2 * rem(i, 2))


def head_rows(j):
    return slice(j * RLEN, (j + 1) * RLEN)


def head_columns(j):
    return slice(j * HD, (j + 1) * HD)


def chunk_rows(step):
    return pl.ds(pl.multiple_of(step * CHUNK, CHUNK), CHUNK)


def fold(values, op):
    return op(values.reshape(values.shape[0] // 8, 8, values.shape[1]), axis=0)


def dot(a, b):
    return lax.dot_general(a, b, NN, preferred_element_type=F32)


def kernel(
    counts_ref,
    prompt_slot_ref,
    response_ref,
    len_ref,
    code_ref,
    q_ref,
    own_ref,
    cache_ref,
    go_ref,
    dq_ref,
    down_ref,
    back_ref,
    across,
    first,
    previous,
    last,
    q_in,
    go_in,
    own_in,
    rows_in,
    keys_in,
    values_in,
    staged,
    keys,
    values,
    q_rows,
    q_cols,
    cot_cols,
    cot_scaled_cols,
    cot_scaled_rows,
    scores,
    raw,
    top,
    delta,
    inverse,
    turned,
    dv_sum,
    grads,
    terms,
    running,
    summed,
    own_grads,
    q_grads,
    in_sem,
    a_send,
    a_recv,
    b_send,
    b_recv,
    c_send,
    c_recv,
    rc_send,
    rc_recv,
    rb_send,
    rb_recv,
    stay_sem,
):
    seq = lax.axis_index("seq")
    head = lax.axis_index("head")
    plane = div(seq, 2)
    half = lax.rem(seq, 2)
    column = half * 8 + head

    def in_plane(other):
        return {"seq": 2 * other + half, "head": head}

    def in_column(other):
        return {"seq": 2 * plane + div(other, 8), "head": lax.rem(other, 8)}

    def remote(src, dst, send_sem, recv_sem, device):
        return pltpu.make_async_remote_copy(
            src_ref=src, dst_ref=dst, send_sem=send_sem, recv_sem=recv_sem, device_id=device, device_id_type=MESH
        )

    def all_at_once(buffer, sem):
        pltpu.make_async_copy(buffer.at[pl.ds(1, RING - 1)], buffer.at[pl.ds(1, RING - 1)], sem).wait()

    loads = [
        pltpu.make_async_copy(q_ref, q_in, in_sem.at[0]),
        pltpu.make_async_copy(go_ref, go_in, in_sem.at[1]),
        pltpu.make_async_copy(own_ref, own_in, in_sem.at[2]),
    ]
    for load in loads:
        load.start()

    barrier = pltpu.get_barrier_semaphore()
    stays = rem(column, 4) == 0

    def greet(device):
        pl.semaphore_signal(barrier, inc=1, device_id=device, device_id_type=MESH)

    def greet_column(step, carry):
        greet(in_column(around(column + step)))
        return carry

    def greet_unit(u):
        greet(in_plane(plus(plane, unit_offset(column, u))))
        greet(in_plane(minus(plane, unit_offset(column, u))))

    lax.fori_loop(1, RING, greet_column, 0)
    for u in range(1, UNITS):
        greet_unit(u)

    @pl.when(stays)
    def _():
        pl.semaphore_wait(barrier, RING - 1 + 2 * (UNITS - 1))

    @pl.when(jnp.logical_not(stays))
    def _():
        greet_unit(0)
        pl.semaphore_wait(barrier, RING - 1 + 2 * UNITS)

    def unit_copy(u):
        return remote(
            cache_ref.at[pl.ds(u * UNIT, UNIT)],
            rows_in.at[u],
            a_send.at[u],
            a_recv.at[u],
            in_plane(plus(plane, unit_offset(column, u))),
        )

    for u in range(1, UNITS):
        unit_copy(u).start()

    @pl.when(jnp.logical_not(stays))
    def _():
        unit_copy(0).start()

    @pl.when(stays)
    def _():
        pltpu.make_async_copy(cache_ref.at[pl.ds(0, UNIT)], rows_in.at[0], a_recv.at[0]).start()

    by_source = (keys_in, values_in)

    def column_copy(part, step):
        target = around(column + step)
        at = pl.ds(pl.multiple_of(lax.rem(target, 8) * WIDTH + part * HD, HD), HD)
        return remote(
            rows_in.at[:, :, at], by_source[part].at[column], b_send.at[part], b_recv.at[part], in_column(target)
        )

    def send_heads(part):
        def send(i, carry):
            column_copy(part, column_step(i)).start()
            return carry

        lax.fori_loop(1, RING, send, 0)
        by_source[part][column] = rows_in[:, :, pl.ds(pl.multiple_of(head * WIDTH + part * HD, HD), HD)]

    gathered = (keys, values)

    def chunk_copy(part, step):
        return remote(
            staged.at[part, step],
            gathered[part].at[chunk_rows(step)],
            c_send.at[part],
            c_recv.at[part, step],
            in_plane(plus(plane, turn(step))),
        )

    def send_chunks(part):
        def take(place):
            units = [by_source[part][4 * i + first[odd, place], across[place]] for odd in range(2) for i in range(4)]
            return jnp.concatenate(units, axis=0)

        all_at_once(by_source[part], b_recv.at[part])
        for step in range(1, RING):
            staged[part, step] = take(step)
            chunk_copy(part, step).start()
        gathered[part][:CHUNK] = take(0)

    ends = []
    for i in range(PROMPTS):
        ends.append(counts_ref[i] + (ends[-1] if ends else 0))
    prompts = []
    for step in range(RING):
        response = response_ref[2 * plus(plane, turn(step)) + half]
        group = jnp.int32(0)
        for end in ends[:-1]:
            group = group + (end <= response).astype(jnp.int32)
        prompt = prompt_slot_ref[group]
        prompts.append(prompt)
        way = rem(div(plane, 4) + 4 - div(prompt, 2), 4)
        across[step] = way
        for odd in range(2):
            first[odd, step] = rem(plane + 8 - 2 * rem(prompt, 2) - odd - way, 4)
    for step in range(RING):
        found = jnp.int32(RING)
        for other in range(step):
            found = jnp.where(prompts[other] == prompts[step], other, found)
        previous[step] = found
    for prompt in range(PROMPTS):
        found = jnp.int32(RING)
        for step in range(RING):
            found = jnp.where(prompts[step] == prompt, step, found)
        last[prompt] = found

    for load in loads:
        load.wait()
    position = lax.broadcasted_iota(jnp.int32, (RLEN, HD), 0)
    factor = jnp.where(position < len_ref[0], code_ref[0].astype(F32) / 8.0, 0.0)
    for j in range(HEADS):
        query = q_in[:, head_columns(j)]
        q_rows[head_rows(j)] = query
        q_cols[:, head_rows(j)] = jnp.transpose(query)
        cotangent = go_in[:, head_columns(j)].astype(F32) * factor
        cot_cols[:, head_rows(j)] = jnp.transpose(cotangent).astype(BF16)
    keys[PLEN:] = own_in[:, :HD]
    values[PLEN:] = own_in[:, HD:]
    running[RING] = jnp.zeros((CHUNK, HD), F32)

    def block_rows(b):
        return pl.ds(pl.multiple_of(b * BLOCK, BLOCK), BLOCK)

    def score(b, own):
        block = keys[block_rows(b)]
        for j in range(HEADS):
            at = head_rows(j)
            part = dot(block, q_cols[:, at])
            if own:
                key_at = lax.broadcasted_iota(jnp.int32, (BLOCK, RLEN), 0)
                seen_from = lax.broadcasted_iota(jnp.int32, (BLOCK, RLEN), 1)
                part = jnp.where(key_at <= seen_from, part, -1e30)
            scores[b, :, at] = part
            high = fold(part, jnp.max)
            top[:, at] = high if own else jnp.maximum(top[:, at], high)

    for u in range(UNITS):
        unit_copy(u).wait_recv()
    send_heads(0)
    send_heads(1)
    score(BLOCKS, True)
    send_chunks(0)
    send_chunks(1)

    def arrive(part, b):
        def one(i, carry):
            step = b * PER_BLOCK + i

            @pl.when(step > 0)
            def _():
                chunk_copy(part, step).wait_recv()

            return carry

        lax.fori_loop(0, PER_BLOCK, one, 0)

    def score_block(b, carry):
        arrive(0, b)
        score(b, False)
        return carry

    lax.fori_loop(0, BLOCKS, score_block, 0)

    def return_copy(part, step):
        return remote(
            grads.at[part, step],
            terms.at[part, step],
            rc_send.at[part],
            rc_recv.at[part],
            in_plane(minus(plane, turn(step))),
        )

    def send_back(part, b, block):
        for i in range(PER_BLOCK):
            grads[part, b * PER_BLOCK + i] = block[i * CHUNK : (i + 1) * CHUNK]

        def one(i, carry):
            step = b * PER_BLOCK + i

            @pl.when(step > 0)
            def _():
                return_copy(part, step).start()

            return carry

        lax.fori_loop(0, PER_BLOCK, one, 0)

    def pair_rows(p):
        return slice(2 * p * RLEN, 2 * (p + 1) * RLEN)

    def pair_grads(b, p):
        return dot(raw[b, :, pair_rows(p)], cot_scaled_rows[pair_rows(p)])

    for p in range(HEADS // 2):
        heads = (2 * p, 2 * p + 1)
        highest = [jnp.max(top[:, head_rows(j)], axis=0, keepdims=True) for j in heads]

        def weigh(b, totals):
            sums = []
            for j, high, total in zip(heads, highest, totals):
                at = head_rows(j)
                weights = jnp.exp2((scores[b, :, at] - high) * (SCALE * LOG2E))
                raw[b, :, at] = weights.astype(BF16)
                sums.append(total + fold(weights, jnp.sum))
            if p == 1:
                dv_sum[b] = pair_grads(b, 0)
            elif p > 1:
                dv_sum[b] += pair_grads(b, p - 1)
            return tuple(sums)

        totals = lax.fori_loop(0, BLOCKS + 1, weigh, (jnp.zeros((8, RLEN), F32),) * 2)
        for j, total in zip(heads, totals):
            at = head_rows(j)
            over = 1.0 / jnp.sum(total, axis=0, keepdims=True)
            inverse[:, at] = jnp.broadcast_to(over, (8, RLEN))
            scaled = cot_cols[:, at].astype(F32) * over
            cot_scaled_cols[:, at] = scaled.astype(BF16)
            cot_scaled_rows[at] = jnp.transpose(scaled).astype(BF16)

    def value_grads(b):
        return (dv_sum[b] + pair_grads(b, HEADS // 2 - 1)).astype(BF16)

    def value_block(b, carry):
        send_back(1, b, value_grads(b))
        return carry

    lax.fori_loop(0, BLOCKS, value_block, 0)

    def look(b, first):
        block = values[block_rows(b)]
        for j in range(HEADS):
            at = head_rows(j)
            grad = dot(block, cot_scaled_cols[:, at])
            scores[b, :, at] = grad
            term = fold(grad * raw[b, :, at].astype(F32), jnp.sum)
            delta[:, at] = term if first else delta[:, at] + term

    def look_block(b, carry):
        arrive(1, b)
        look(b, False)
        return carry

    look(BLOCKS, True)
    lax.fori_loop(0, BLOCKS, look_block, 0)
    for j in range(HEADS):
        at = head_rows(j)
        delta[:, at] = jnp.sum(delta[:, at], axis=0, keepdims=True) * inverse[:, at]

    def key_part(b):
        for j in range(HEADS):
            at = head_rows(j)
            weights = raw[b, :, at].astype(F32)
            shift = delta[0:1, at]
            change = (weights * (scores[b, :, at] - shift)).astype(BF16)
            raw[b, :, at] = change
        return (dot(raw[b], q_rows[...]) * SCALE).astype(BF16)

    def key_block(b, carry):
        send_back(0, b, key_part(b))
        return carry


    def home_copy(part, target, u):
        x = rem(div(plane, 4) + 4 - u, 4)
        y = rem(plane + 20 - target - u, 4)
        source = 4 * x + y
        return remote(
            summed.at[part, 4 * source + div(target, 4)],
            back_ref.at[part, 4 * column + u],
            rb_send.at[part],
            rb_recv.at[part],
            {"seq": 2 * source + div(target, 8), "head": rem(target, 8)},
        )

    def home_stay(part):
        return pltpu.make_async_copy(
            summed.at[part, 4 * plane + div(column, 4)],
            back_ref.at[part, 4 * column],
            stay_sem.at[part],
        )

    def add_up(part):
        all_at_once(grads.at[part], rc_recv.at[part])
        terms[part, 0] = grads[part, 0]

        def add(step, carry):
            running[step] = running[previous[step]] + terms[part, step].astype(F32)
            return carry

        lax.fori_loop(0, RING, add, 0)

        def close(prompt, carry):
            units = running[last[prompt]].astype(BF16).reshape(CHUNK // UNIT, UNIT, HD)
            summed[part, pl.ds(prompt * (CHUNK // UNIT), CHUNK // UNIT)] = units
            return carry

        lax.fori_loop(0, PROMPTS, close, 0)

    def send_home(part, begin, end):
        def send(i, carry):
            target = around(column + column_step(i))
            for u in range(UNITS):
                home_copy(part, target, u).start()
            return carry

        lax.fori_loop(begin, end, send, 0)

    def send_own(part):
        for u in range(1, UNITS):
            home_copy(part, column, u).start()

        @pl.when(jnp.logical_not(stays))
        def _():
            home_copy(part, column, 0).start()

        @pl.when(stays)
        def _():
            home_stay(part).start()

    def home_wait(part, sem):
        @pl.when(jnp.logical_not(stays))
        def _():
            pltpu.make_async_copy(back_ref.at[part], back_ref.at[part], sem).wait()

        @pl.when(stays)
        def _():
            rest = back_ref.at[part, pl.ds(1, RING * UNITS - 1)]
            pltpu.make_async_copy(rest, rest, sem).wait()

    lax.fori_loop(0, 5, key_block, 0)
    add_up(1)
    for b in range(5, BLOCKS):
        send_home(1, 5 * b - 24, 5 * b - 19)
        key_block(b, 0)
    send_own(1)

    own_grads[:, HD:] = value_grads(BLOCKS)
    own_grads[:, :HD] = key_part(BLOCKS)
    own_out = pltpu.make_async_copy(own_grads, down_ref, in_sem.at[2])
    own_out.start()
    turned[...] = jnp.transpose(keys[...])

    add_up(0)
    for j in range(HEADS):
        if j < 5:
            send_home(0, 3 * j + 1, 3 * j + 4)
        elif j == 5:
            send_own(0)
        grad = dot(turned[...], raw[:, :, head_rows(j)].reshape(KEYS, RLEN))
        q_grads[:, head_columns(j)] = (jnp.transpose(grad) * SCALE).astype(BF16)
    q_out = pltpu.make_async_copy(q_grads, dq_ref, in_sem.at[0])
    q_out.start()

    own_out.wait()
    q_out.wait()
    for u in range(1, UNITS):
        unit_copy(u).wait_send()

    @pl.when(jnp.logical_not(stays))
    def _():
        unit_copy(0).wait_send()

    for part in range(2):
        all_at_once(by_source[part], b_send.at[part])
        all_at_once(staged.at[part], c_send.at[part])
        all_at_once(grads.at[part], rc_send.at[part])
    for part in (1, 0):
        home_wait(part, rb_send.at[part])
        home_wait(part, rb_recv.at[part])

        @pl.when(stays)
        def _():
            home_stay(part).wait()


def finish_kernel(dq_ref, down_ref, back_ref, dq_out, down_out, dcache_out, dq, down, back, total, get_sems, put_sems):
    gets = [
        pltpu.make_async_copy(back_ref, back, get_sems.at[0]),
        pltpu.make_async_copy(dq_ref, dq, get_sems.at[1]),
        pltpu.make_async_copy(down_ref, down, get_sems.at[2]),
    ]
    puts = [
        pltpu.make_async_copy(total, dcache_out, put_sems.at[0]),
        pltpu.make_async_copy(dq, dq_out, put_sems.at[1]),
        pltpu.make_async_copy(down, down_out, put_sems.at[2]),
    ]
    for get in gets:
        get.start()
    gets[0].wait()
    for h in range(8):
        for part in range(2):
            first = back[part, UNITS * h : UNITS * (h + 1)].astype(F32)
            second = back[part, UNITS * (8 + h) : UNITS * (9 + h)].astype(F32)
            both = (first + second).astype(BF16).reshape(UNITS * UNIT, HD)
            total[:, h * WIDTH + part * HD : h * WIDTH + (part + 1) * HD] = both
    puts[0].start()
    for get, put in zip(gets[1:], puts[1:]):
        get.wait()
        put.start()
    for put in puts:
        put.wait()


def local(
    queries, resp_kv, prompt_cache, grad_out, group_counts, prompt_slot, slot_response, resp_len, weight_code
):
    smem = pl.BlockSpec(memory_space=pltpu.SMEM)
    hbm = pl.BlockSpec(memory_space=pltpu.HBM)
    scratch = [
        pltpu.SMEM((RING,), jnp.int32),
        pltpu.SMEM((2, RING), jnp.int32),
        pltpu.SMEM((RING,), jnp.int32),
        pltpu.SMEM((PROMPTS,), jnp.int32),
        pltpu.VMEM((RLEN, HEADS * HD), BF16),
        pltpu.VMEM((RLEN, HEADS * HD), BF16),
        pltpu.VMEM((RLEN, WIDTH), BF16),
        pltpu.VMEM((UNITS, UNIT, 8 * WIDTH), BF16),
        pltpu.VMEM((RING, UNITS, UNIT, HD), BF16),
        pltpu.VMEM((RING, UNITS, UNIT, HD), BF16),
        pltpu.VMEM((2, RING, CHUNK, HD), BF16),
        pltpu.VMEM((KEYS, HD), BF16),
        pltpu.VMEM((KEYS, HD), BF16),
        pltpu.VMEM((ROWS, HD), BF16),
        pltpu.VMEM((HD, ROWS), BF16),
        pltpu.VMEM((HD, ROWS), BF16),
        pltpu.VMEM((HD, ROWS), BF16),
        pltpu.VMEM((ROWS, HD), BF16),
        pltpu.VMEM((BLOCKS + 1, BLOCK, ROWS), F32),
        pltpu.VMEM((BLOCKS + 1, BLOCK, ROWS), BF16),
        pltpu.VMEM((8, ROWS), F32),
        pltpu.VMEM((8, ROWS), F32),
        pltpu.VMEM((8, ROWS), F32),
        pltpu.VMEM((HD, KEYS), BF16),
        pltpu.VMEM((BLOCKS + 1, BLOCK, HD), F32),
        pltpu.VMEM((2, RING, CHUNK, HD), BF16),
        pltpu.VMEM((2, RING, CHUNK, HD), BF16),
        pltpu.VMEM((RING + 1, CHUNK, HD), F32),
        pltpu.VMEM((2, RING * UNITS, UNIT, HD), BF16),
        pltpu.VMEM((RLEN, WIDTH), BF16),
        pltpu.VMEM((RLEN, HEADS * HD), BF16),
        pltpu.SemaphoreType.DMA((3,)),
        pltpu.SemaphoreType.DMA((UNITS,)),
        pltpu.SemaphoreType.DMA((UNITS,)),
        pltpu.SemaphoreType.DMA((2,)),
        pltpu.SemaphoreType.DMA((2,)),
        pltpu.SemaphoreType.DMA((2,)),
        pltpu.SemaphoreType.DMA((2, RING)),
        pltpu.SemaphoreType.DMA((2,)),
        pltpu.SemaphoreType.DMA((2,)),
        pltpu.SemaphoreType.DMA((2,)),
        pltpu.SemaphoreType.DMA((2,)),
        pltpu.SemaphoreType.DMA((2,)),
    ]
    products = 5 * ROWS * KEYS * HD
    dq, down, back = pl.pallas_call(
        kernel,
        out_shape=[
            jax.ShapeDtypeStruct(queries.shape, BF16),
            jax.ShapeDtypeStruct(resp_kv.shape, BF16),
            jax.ShapeDtypeStruct((2, RING * UNITS, UNIT, HD), BF16),
        ],
        in_specs=[smem] * 5 + [hbm] * 4,
        out_specs=[hbm] * 3,
        scratch_shapes=scratch,
        compiler_params=pltpu.CompilerParams(
            collective_id=0, has_side_effects=True, vmem_limit_bytes=VMEM_LIMIT
        ),
        cost_estimate=pl.CostEstimate(flops=2 * products, bytes_accessed=3 << 20, transcendentals=ROWS * KEYS),
    )(
        group_counts,
        prompt_slot,
        slot_response,
        resp_len,
        weight_code,
        queries,
        resp_kv,
        prompt_cache,
        grad_out,
    )
    return pl.pallas_call(
        finish_kernel,
        out_shape=[
            jax.ShapeDtypeStruct(queries.shape, BF16),
            jax.ShapeDtypeStruct(resp_kv.shape, BF16),
            jax.ShapeDtypeStruct(prompt_cache.shape, BF16),
        ],
        in_specs=[hbm] * 3,
        out_specs=[hbm] * 3,
        scratch_shapes=[
            pltpu.VMEM(queries.shape, BF16),
            pltpu.VMEM(resp_kv.shape, BF16),
            pltpu.VMEM((2, RING * UNITS, UNIT, HD), BF16),
            pltpu.VMEM(prompt_cache.shape, BF16),
            pltpu.SemaphoreType.DMA((3,)),
            pltpu.SemaphoreType.DMA((3,)),
        ],
        compiler_params=pltpu.CompilerParams(vmem_limit_bytes=VMEM_LIMIT),
    )(dq, down, back)


def solution(mesh):
    placed = (
        P("seq", "head"),
        P("seq", "head"),
        P(("seq", "head"), None),
        P("seq", "head"),
        P(),
        P(),
        P(),
        P("seq"),
        P("seq"),
    )
    return jax.shard_map(
        local,
        mesh=mesh,
        in_specs=placed,
        out_specs=(P("seq", "head"), P("seq", "head"), P(("seq", "head"), None)),
        check_vma=False,
    )
```

```python
import math

import jax
import jax.numpy as jnp
from jax import lax
from jax.experimental import pallas as pl
from jax.experimental.pallas import tpu as pltpu
from jax.sharding import PartitionSpec as P

HD = 128
PLEN = 2048
RLEN = 256
HEADS = 8
PROMPTS = 8
RING = 16
CHUNK = PLEN // RING
UNITS = 4
UNIT = 16
BLOCK = 256
BLOCKS = PLEN // BLOCK
PER_BLOCK = BLOCK // CHUNK
ROWS = HEADS * RLEN
KEYS = PLEN + RLEN
WIDTH = 2 * HD
SCALE = HD**-0.5
LOG2E = math.log2(math.e)
MESH = pl.DeviceIdType.MESH
VMEM_LIMIT = 60 * 1024 * 1024
NN = (((1,), (0,)), ((), ()))
F32 = jnp.float32
BF16 = jnp.bfloat16


def around(index):
    return lax.rem(index + 2 * RING, RING)


def div(a, b):
    return a // b if isinstance(a, int) else lax.div(a, b)


def rem(a, b):
    return a % b if isinstance(a, int) else lax.rem(a, b)


def plus(plane, offset):
    return 4 * rem(div(plane, 4) + div(offset, 4), 4) + rem(plane + rem(offset, 4), 4)


def minus(plane, offset):
    return 4 * rem(div(plane, 4) + 4 - div(offset, 4), 4) + rem(plane + 4 - rem(offset, 4), 4)


def turn(place):
    return rem(5 * place, RING)


def unit_offset(column, u):
    return 4 * u + lax.rem(column + u, 4)


def column_step(i):
    return 8 + div(i, 2) * (1 - 2 * rem(i, 2))


def head_rows(j):
    return slice(j * RLEN, (j + 1) * RLEN)


def head_columns(j):
    return slice(j * HD, (j + 1) * HD)


def chunk_rows(step):
    return pl.ds(pl.multiple_of(step * CHUNK, CHUNK), CHUNK)


def fold(values, op):
    return op(values.reshape(values.shape[0] // 8, 8, values.shape[1]), axis=0)


def dot(a, b):
    return lax.dot_general(a, b, NN, preferred_element_type=F32)


def kernel(
    counts_ref,
    prompt_slot_ref,
    response_ref,
    len_ref,
    code_ref,
    q_ref,
    own_ref,
    cache_ref,
    go_ref,
    dq_ref,
    down_ref,
    back_ref,
    across,
    first,
    previous,
    last,
    q_in,
    go_in,
    own_in,
    rows_in,
    keys_in,
    values_in,
    staged,
    keys,
    values,
    q_rows,
    q_cols,
    cot_cols,
    cot_scaled_cols,
    cot_scaled_rows,
    scores,
    raw,
    top,
    delta,
    inverse,
    turned,
    dv_sum,
    grads,
    terms,
    running,
    summed,
    own_grads,
    q_grads,
    in_sem,
    a_send,
    a_recv,
    b_send,
    b_recv,
    c_send,
    c_recv,
    rc_send,
    rc_recv,
    rb_send,
    rb_recv,
    stay_sem,
):
    seq = lax.axis_index("seq")
    head = lax.axis_index("head")
    plane = div(seq, 2)
    half = lax.rem(seq, 2)
    column = half * 8 + head

    def in_plane(other):
        return {"seq": 2 * other + half, "head": head}

    def in_column(other):
        return {"seq": 2 * plane + div(other, 8), "head": lax.rem(other, 8)}

    def remote(src, dst, send_sem, recv_sem, device):
        return pltpu.make_async_remote_copy(
            src_ref=src, dst_ref=dst, send_sem=send_sem, recv_sem=recv_sem, device_id=device, device_id_type=MESH
        )

    def all_at_once(buffer, sem):
        pltpu.make_async_copy(buffer.at[pl.ds(1, RING - 1)], buffer.at[pl.ds(1, RING - 1)], sem).wait()

    loads = [
        pltpu.make_async_copy(q_ref, q_in, in_sem.at[0]),
        pltpu.make_async_copy(go_ref, go_in, in_sem.at[1]),
        pltpu.make_async_copy(own_ref, own_in, in_sem.at[2]),
    ]
    for load in loads:
        load.start()

    barrier = pltpu.get_barrier_semaphore()
    stays = rem(column, 4) == 0

    def greet(device):
        pl.semaphore_signal(barrier, inc=1, device_id=device, device_id_type=MESH)

    def greet_column(step, carry):
        greet(in_column(around(column + step)))
        return carry

    def greet_unit(u):
        greet(in_plane(plus(plane, unit_offset(column, u))))
        greet(in_plane(minus(plane, unit_offset(column, u))))

    lax.fori_loop(1, RING, greet_column, 0)
    for u in range(1, UNITS):
        greet_unit(u)

    @pl.when(stays)
    def _():
        pl.semaphore_wait(barrier, RING - 1 + 2 * (UNITS - 1))

    @pl.when(jnp.logical_not(stays))
    def _():
        greet_unit(0)
        pl.semaphore_wait(barrier, RING - 1 + 2 * UNITS)

    def unit_copy(u):
        return remote(
            cache_ref.at[pl.ds(u * UNIT, UNIT)],
            rows_in.at[u],
            a_send.at[u],
            a_recv.at[u],
            in_plane(plus(plane, unit_offset(column, u))),
        )

    for u in range(1, UNITS):
        unit_copy(u).start()

    @pl.when(jnp.logical_not(stays))
    def _():
        unit_copy(0).start()

    @pl.when(stays)
    def _():
        pltpu.make_async_copy(cache_ref.at[pl.ds(0, UNIT)], rows_in.at[0], a_recv.at[0]).start()

    by_source = (keys_in, values_in)

    def column_copy(part, step):
        target = around(column + step)
        at = pl.ds(pl.multiple_of(lax.rem(target, 8) * WIDTH + part * HD, HD), HD)
        return remote(
            rows_in.at[:, :, at], by_source[part].at[column], b_send.at[part], b_recv.at[part], in_column(target)
        )

    def send_heads(part):
        def send(i, carry):
            column_copy(part, column_step(i)).start()
            return carry

        lax.fori_loop(1, RING, send, 0)
        by_source[part][column] = rows_in[:, :, pl.ds(pl.multiple_of(head * WIDTH + part * HD, HD), HD)]

    gathered = (keys, values)

    def chunk_copy(part, step):
        return remote(
            staged.at[part, step],
            gathered[part].at[chunk_rows(step)],
            c_send.at[part],
            c_recv.at[part, step],
            in_plane(plus(plane, turn(step))),
        )

    def send_chunks(part):
        def take(place):
            units = [by_source[part][4 * i + first[odd, place], across[place]] for odd in range(2) for i in range(4)]
            return jnp.concatenate(units, axis=0)

        all_at_once(by_source[part], b_recv.at[part])
        for step in range(1, RING):
            staged[part, step] = take(step)
            chunk_copy(part, step).start()
        gathered[part][:CHUNK] = take(0)

    ends = []
    for i in range(PROMPTS):
        ends.append(counts_ref[i] + (ends[-1] if ends else 0))
    prompts = []
    for step in range(RING):
        response = response_ref[2 * plus(plane, turn(step)) + half]
        group = jnp.int32(0)
        for end in ends[:-1]:
            group = group + (end <= response).astype(jnp.int32)
        prompt = prompt_slot_ref[group]
        prompts.append(prompt)
        way = rem(div(plane, 4) + 4 - div(prompt, 2), 4)
        across[step] = way
        for odd in range(2):
            first[odd, step] = rem(plane + 8 - 2 * rem(prompt, 2) - odd - way, 4)
    for step in range(RING):
        found = jnp.int32(RING)
        for other in range(step):
            found = jnp.where(prompts[other] == prompts[step], other, found)
        previous[step] = found
    for prompt in range(PROMPTS):
        found = jnp.int32(RING)
        for step in range(RING):
            found = jnp.where(prompts[step] == prompt, step, found)
        last[prompt] = found

    for load in loads:
        load.wait()
    position = lax.broadcasted_iota(jnp.int32, (RLEN, HD), 0)
    factor = jnp.where(position < len_ref[0], code_ref[0].astype(F32) / 8.0, 0.0)
    for j in range(HEADS):
        query = q_in[:, head_columns(j)]
        q_rows[head_rows(j)] = query
        q_cols[:, head_rows(j)] = jnp.transpose(query)
        cotangent = go_in[:, head_columns(j)].astype(F32) * factor
        cot_cols[:, head_rows(j)] = jnp.transpose(cotangent).astype(BF16)
    keys[PLEN:] = own_in[:, :HD]
    values[PLEN:] = own_in[:, HD:]
    running[RING] = jnp.zeros((CHUNK, HD), F32)

    def block_rows(b):
        return pl.ds(pl.multiple_of(b * BLOCK, BLOCK), BLOCK)

    def score(b, own):
        block = keys[block_rows(b)]
        for j in range(HEADS):
            at = head_rows(j)
            part = dot(block, q_cols[:, at])
            if own:
                key_at = lax.broadcasted_iota(jnp.int32, (BLOCK, RLEN), 0)
                seen_from = lax.broadcasted_iota(jnp.int32, (BLOCK, RLEN), 1)
                part = jnp.where(key_at <= seen_from, part, -1e30)
            scores[b, :, at] = part
            high = fold(part, jnp.max)
            top[:, at] = high if own else jnp.maximum(top[:, at], high)

    for u in range(UNITS):
        unit_copy(u).wait_recv()
    send_heads(0)
    send_heads(1)
    score(BLOCKS, True)
    send_chunks(0)
    send_chunks(1)

    def arrive(part, b):
        def one(i, carry):
            step = b * PER_BLOCK + i

            @pl.when(step > 0)
            def _():
                chunk_copy(part, step).wait_recv()

            return carry

        lax.fori_loop(0, PER_BLOCK, one, 0)

    def score_block(b, carry):
        arrive(0, b)
        score(b, False)
        return carry

    lax.fori_loop(0, BLOCKS, score_block, 0)

    def return_copy(part, step):
        return remote(
            grads.at[part, step],
            terms.at[part, step],
            rc_send.at[part],
            rc_recv.at[part],
            in_plane(minus(plane, turn(step))),
        )

    def send_back(part, b, block):
        for i in range(PER_BLOCK):
            grads[part, b * PER_BLOCK + i] = block[i * CHUNK : (i + 1) * CHUNK]

        def one(i, carry):
            step = b * PER_BLOCK + i

            @pl.when(step > 0)
            def _():
                return_copy(part, step).start()

            return carry

        lax.fori_loop(0, PER_BLOCK, one, 0)

    def pair_rows(p):
        return slice(2 * p * RLEN, 2 * (p + 1) * RLEN)

    def pair_grads(b, p):
        return dot(raw[b, :, pair_rows(p)], cot_scaled_rows[pair_rows(p)])

    for p in range(HEADS // 2):
        heads = (2 * p, 2 * p + 1)
        highest = [jnp.max(top[:, head_rows(j)], axis=0, keepdims=True) for j in heads]

        def weigh(b, totals):
            sums = []
            for j, high, total in zip(heads, highest, totals):
                at = head_rows(j)
                weights = jnp.exp2((scores[b, :, at] - high) * (SCALE * LOG2E))
                raw[b, :, at] = weights.astype(BF16)
                sums.append(total + fold(weights, jnp.sum))
            if p == 1:
                dv_sum[b] = pair_grads(b, 0)
            elif p > 1:
                dv_sum[b] += pair_grads(b, p - 1)
            return tuple(sums)

        totals = lax.fori_loop(0, BLOCKS + 1, weigh, (jnp.zeros((8, RLEN), F32),) * 2, unroll=3)
        for j, total in zip(heads, totals):
            at = head_rows(j)
            over = 1.0 / jnp.sum(total, axis=0, keepdims=True)
            inverse[:, at] = jnp.broadcast_to(over, (8, RLEN))
            scaled = cot_cols[:, at].astype(F32) * over
            cot_scaled_cols[:, at] = scaled.astype(BF16)
            cot_scaled_rows[at] = jnp.transpose(scaled).astype(BF16)

    def value_grads(b):
        return (dv_sum[b] + pair_grads(b, HEADS // 2 - 1)).astype(BF16)

    def value_block(b, carry):
        send_back(1, b, value_grads(b))
        return carry

    lax.fori_loop(0, BLOCKS, value_block, 0)

    def look(b, first):
        block = values[block_rows(b)]
        for j in range(HEADS):
            at = head_rows(j)
            grad = dot(block, cot_scaled_cols[:, at])
            scores[b, :, at] = grad
            term = fold(grad * raw[b, :, at].astype(F32), jnp.sum)
            delta[:, at] = term if first else delta[:, at] + term

    look(BLOCKS, True)
    for b in range(0, BLOCKS, 2):
        arrive(1, b)
        arrive(1, b + 1)
        look(b, False)
        look(b + 1, False)
    for j in range(HEADS):
        at = head_rows(j)
        delta[:, at] = jnp.sum(delta[:, at], axis=0, keepdims=True) * inverse[:, at]

    def key_part(b):
        for j in range(HEADS):
            at = head_rows(j)
            weights = raw[b, :, at].astype(F32)
            shift = delta[0:1, at]
            change = (weights * (scores[b, :, at] - shift)).astype(BF16)
            raw[b, :, at] = change
        return (dot(raw[b], q_rows[...]) * SCALE).astype(BF16)

    for b in range(0, BLOCKS, 2):
        key_grads = [key_part(b), key_part(b + 1)]
        send_back(0, b, key_grads[0])
        send_back(0, b + 1, key_grads[1])

    def home_copy(part, target, u):
        x = rem(div(plane, 4) + 4 - u, 4)
        y = rem(plane + 20 - target - u, 4)
        source = 4 * x + y
        return remote(
            summed.at[part, 4 * source + div(target, 4)],
            back_ref.at[part, 4 * column + u],
            rb_send.at[part],
            rb_recv.at[part],
            {"seq": 2 * source + div(target, 8), "head": rem(target, 8)},
        )

    def home_stay(part):
        return pltpu.make_async_copy(
            summed.at[part, 4 * plane + div(column, 4)],
            back_ref.at[part, 4 * column],
            stay_sem.at[part],
        )

    def add_up(part):
        all_at_once(grads.at[part], rc_recv.at[part])
        terms[part, 0] = grads[part, 0]

        def add(step, carry):
            running[step] = running[previous[step]] + terms[part, step].astype(F32)
            return carry

        lax.fori_loop(0, RING, add, 0)

        def close(prompt, carry):
            units = running[last[prompt]].astype(BF16).reshape(CHUNK // UNIT, UNIT, HD)
            summed[part, pl.ds(prompt * (CHUNK // UNIT), CHUNK // UNIT)] = units
            return carry

        lax.fori_loop(0, PROMPTS, close, 0)

        def send(i, carry):
            target = around(column + column_step(i))
            for u in range(UNITS):
                home_copy(part, target, u).start()
            return carry

        lax.fori_loop(1, RING, send, 0)
        for u in range(1, UNITS):
            home_copy(part, column, u).start()

        @pl.when(jnp.logical_not(stays))
        def _():
            home_copy(part, column, 0).start()

        @pl.when(stays)
        def _():
            home_stay(part).start()

    def home_wait(part, sem):
        @pl.when(jnp.logical_not(stays))
        def _():
            pltpu.make_async_copy(back_ref.at[part], back_ref.at[part], sem).wait()

        @pl.when(stays)
        def _():
            rest = back_ref.at[part, pl.ds(1, RING * UNITS - 1)]
            pltpu.make_async_copy(rest, rest, sem).wait()

    add_up(1)

    own_grads[:, HD:] = value_grads(BLOCKS)
    own_grads[:, :HD] = key_part(BLOCKS)
    own_out = pltpu.make_async_copy(own_grads, down_ref, in_sem.at[2])
    own_out.start()
    turned[...] = jnp.transpose(keys[...])

    def query_grads(first, end):
        for j in range(first, end):
            grad = dot(turned[...], raw[:, :, head_rows(j)].reshape(KEYS, RLEN))
            q_grads[:, head_columns(j)] = (jnp.transpose(grad) * SCALE).astype(BF16)

    query_grads(0, 2)
    add_up(0)
    query_grads(2, HEADS)
    q_out = pltpu.make_async_copy(q_grads, dq_ref, in_sem.at[0])
    q_out.start()

    own_out.wait()
    q_out.wait()
    for u in range(1, UNITS):
        unit_copy(u).wait_send()

    @pl.when(jnp.logical_not(stays))
    def _():
        unit_copy(0).wait_send()

    for part in range(2):
        all_at_once(by_source[part], b_send.at[part])
        all_at_once(staged.at[part], c_send.at[part])
        all_at_once(grads.at[part], rc_send.at[part])
    for part in (1, 0):
        home_wait(part, rb_send.at[part])
        home_wait(part, rb_recv.at[part])

        @pl.when(stays)
        def _():
            home_stay(part).wait()


def finish_kernel(dq_ref, down_ref, back_ref, dq_out, down_out, dcache_out, dq, down, back, total, get_sems, put_sems):
    gets = [
        pltpu.make_async_copy(back_ref, back, get_sems.at[0]),
        pltpu.make_async_copy(dq_ref, dq, get_sems.at[1]),
        pltpu.make_async_copy(down_ref, down, get_sems.at[2]),
    ]
    puts = [
        pltpu.make_async_copy(total, dcache_out, put_sems.at[0]),
        pltpu.make_async_copy(dq, dq_out, put_sems.at[1]),
        pltpu.make_async_copy(down, down_out, put_sems.at[2]),
    ]
    for get in gets:
        get.start()
    gets[0].wait()
    for h in range(8):
        for part in range(2):
            first = back[part, UNITS * h : UNITS * (h + 1)].astype(F32)
            second = back[part, UNITS * (8 + h) : UNITS * (9 + h)].astype(F32)
            both = (first + second).astype(BF16).reshape(UNITS * UNIT, HD)
            total[:, h * WIDTH + part * HD : h * WIDTH + (part + 1) * HD] = both
    puts[0].start()
    for get, put in zip(gets[1:], puts[1:]):
        get.wait()
        put.start()
    for put in puts:
        put.wait()


def local(
    queries, resp_kv, prompt_cache, grad_out, group_counts, prompt_slot, slot_response, resp_len, weight_code
):
    smem = pl.BlockSpec(memory_space=pltpu.SMEM)
    hbm = pl.BlockSpec(memory_space=pltpu.HBM)
    scratch = [
        pltpu.SMEM((RING,), jnp.int32),
        pltpu.SMEM((2, RING), jnp.int32),
        pltpu.SMEM((RING,), jnp.int32),
        pltpu.SMEM((PROMPTS,), jnp.int32),
        pltpu.VMEM((RLEN, HEADS * HD), BF16),
        pltpu.VMEM((RLEN, HEADS * HD), BF16),
        pltpu.VMEM((RLEN, WIDTH), BF16),
        pltpu.VMEM((UNITS, UNIT, 8 * WIDTH), BF16),
        pltpu.VMEM((RING, UNITS, UNIT, HD), BF16),
        pltpu.VMEM((RING, UNITS, UNIT, HD), BF16),
        pltpu.VMEM((2, RING, CHUNK, HD), BF16),
        pltpu.VMEM((KEYS, HD), BF16),
        pltpu.VMEM((KEYS, HD), BF16),
        pltpu.VMEM((ROWS, HD), BF16),
        pltpu.VMEM((HD, ROWS), BF16),
        pltpu.VMEM((HD, ROWS), BF16),
        pltpu.VMEM((HD, ROWS), BF16),
        pltpu.VMEM((ROWS, HD), BF16),
        pltpu.VMEM((BLOCKS + 1, BLOCK, ROWS), F32),
        pltpu.VMEM((BLOCKS + 1, BLOCK, ROWS), BF16),
        pltpu.VMEM((8, ROWS), F32),
        pltpu.VMEM((8, ROWS), F32),
        pltpu.VMEM((8, ROWS), F32),
        pltpu.VMEM((HD, KEYS), BF16),
        pltpu.VMEM((BLOCKS + 1, BLOCK, HD), F32),
        pltpu.VMEM((2, RING, CHUNK, HD), BF16),
        pltpu.VMEM((2, RING, CHUNK, HD), BF16),
        pltpu.VMEM((RING + 1, CHUNK, HD), F32),
        pltpu.VMEM((2, RING * UNITS, UNIT, HD), BF16),
        pltpu.VMEM((RLEN, WIDTH), BF16),
        pltpu.VMEM((RLEN, HEADS * HD), BF16),
        pltpu.SemaphoreType.DMA((3,)),
        pltpu.SemaphoreType.DMA((UNITS,)),
        pltpu.SemaphoreType.DMA((UNITS,)),
        pltpu.SemaphoreType.DMA((2,)),
        pltpu.SemaphoreType.DMA((2,)),
        pltpu.SemaphoreType.DMA((2,)),
        pltpu.SemaphoreType.DMA((2, RING)),
        pltpu.SemaphoreType.DMA((2,)),
        pltpu.SemaphoreType.DMA((2,)),
        pltpu.SemaphoreType.DMA((2,)),
        pltpu.SemaphoreType.DMA((2,)),
        pltpu.SemaphoreType.DMA((2,)),
    ]
    products = 5 * ROWS * KEYS * HD
    dq, down, back = pl.pallas_call(
        kernel,
        out_shape=[
            jax.ShapeDtypeStruct(queries.shape, BF16),
            jax.ShapeDtypeStruct(resp_kv.shape, BF16),
            jax.ShapeDtypeStruct((2, RING * UNITS, UNIT, HD), BF16),
        ],
        in_specs=[smem] * 5 + [hbm] * 4,
        out_specs=[hbm] * 3,
        scratch_shapes=scratch,
        compiler_params=pltpu.CompilerParams(
            collective_id=0, has_side_effects=True, vmem_limit_bytes=VMEM_LIMIT
        ),
        cost_estimate=pl.CostEstimate(flops=2 * products, bytes_accessed=3 << 20, transcendentals=ROWS * KEYS),
    )(
        group_counts,
        prompt_slot,
        slot_response,
        resp_len,
        weight_code,
        queries,
        resp_kv,
        prompt_cache,
        grad_out,
    )
    return pl.pallas_call(
        finish_kernel,
        out_shape=[
            jax.ShapeDtypeStruct(queries.shape, BF16),
            jax.ShapeDtypeStruct(resp_kv.shape, BF16),
            jax.ShapeDtypeStruct(prompt_cache.shape, BF16),
        ],
        in_specs=[hbm] * 3,
        out_specs=[hbm] * 3,
        scratch_shapes=[
            pltpu.VMEM(queries.shape, BF16),
            pltpu.VMEM(resp_kv.shape, BF16),
            pltpu.VMEM((2, RING * UNITS, UNIT, HD), BF16),
            pltpu.VMEM(prompt_cache.shape, BF16),
            pltpu.SemaphoreType.DMA((3,)),
            pltpu.SemaphoreType.DMA((3,)),
        ],
        compiler_params=pltpu.CompilerParams(vmem_limit_bytes=VMEM_LIMIT),
    )(dq, down, back)


def solution(mesh):
    placed = (
        P("seq", "head"),
        P("seq", "head"),
        P(("seq", "head"), None),
        P("seq", "head"),
        P(),
        P(),
        P(),
        P("seq"),
        P("seq"),
    )
    return jax.shard_map(
        local,
        mesh=mesh,
        in_specs=placed,
        out_specs=(P("seq", "head"), P("seq", "head"), P(("seq", "head"), None)),
        check_vma=False,
    )
```

```python
import math

import jax
import jax.numpy as jnp
from jax import lax
from jax.experimental import pallas as pl
from jax.experimental.pallas import tpu as pltpu
from jax.sharding import PartitionSpec as P

HD = 128
PLEN = 2048
RLEN = 256
HEADS = 8
PROMPTS = 8
RING = 16
CHUNK = PLEN // RING
UNITS = 4
UNIT = 16
BLOCK = 256
BLOCKS = PLEN // BLOCK
PER_BLOCK = BLOCK // CHUNK
ROWS = HEADS * RLEN
KEYS = PLEN + RLEN
WIDTH = 2 * HD
SCALE = HD**-0.5
LOG2E = math.log2(math.e)
MESH = pl.DeviceIdType.MESH
VMEM_LIMIT = 60 * 1024 * 1024
NN = (((1,), (0,)), ((), ()))
F32 = jnp.float32
BF16 = jnp.bfloat16


def around(index):
    return lax.rem(index + 2 * RING, RING)


def div(a, b):
    return a // b if isinstance(a, int) else lax.div(a, b)


def rem(a, b):
    return a % b if isinstance(a, int) else lax.rem(a, b)


def plus(plane, offset):
    return 4 * rem(div(plane, 4) + div(offset, 4), 4) + rem(plane + rem(offset, 4), 4)


def minus(plane, offset):
    return 4 * rem(div(plane, 4) + 4 - div(offset, 4), 4) + rem(plane + 4 - rem(offset, 4), 4)


def turn(place):
    return rem(5 * place, RING)


def unit_offset(column, u):
    return 4 * u + lax.rem(column + u, 4)


def column_step(i):
    return 8 + div(i, 2) * (1 - 2 * rem(i, 2))


def head_rows(j):
    return slice(j * RLEN, (j + 1) * RLEN)


def head_columns(j):
    return slice(j * HD, (j + 1) * HD)


def chunk_rows(step):
    return pl.ds(pl.multiple_of(step * CHUNK, CHUNK), CHUNK)


def fold(values, op):
    return op(values.reshape(values.shape[0] // 8, 8, values.shape[1]), axis=0)


def dot(a, b):
    return lax.dot_general(a, b, NN, preferred_element_type=F32)


def kernel(
    counts_ref,
    prompt_slot_ref,
    response_ref,
    len_ref,
    code_ref,
    q_ref,
    own_ref,
    cache_ref,
    go_ref,
    dq_ref,
    down_ref,
    back_ref,
    across,
    first,
    previous,
    last,
    q_in,
    go_in,
    own_in,
    rows_in,
    keys_in,
    values_in,
    staged,
    keys,
    values,
    q_rows,
    q_cols,
    cot_cols,
    cot_scaled_cols,
    cot_scaled_rows,
    scores,
    raw,
    top,
    delta,
    inverse,
    turned,
    dv_sum,
    grads,
    terms,
    running,
    summed,
    own_grads,
    q_grads,
    in_sem,
    a_send,
    a_recv,
    b_send,
    b_recv,
    c_send,
    c_recv,
    rc_send,
    rc_recv,
    rb_send,
    rb_recv,
    stay_sem,
):
    seq = lax.axis_index("seq")
    head = lax.axis_index("head")
    plane = div(seq, 2)
    half = lax.rem(seq, 2)
    column = half * 8 + head

    def in_plane(other):
        return {"seq": 2 * other + half, "head": head}

    def in_column(other):
        return {"seq": 2 * plane + div(other, 8), "head": lax.rem(other, 8)}

    def remote(src, dst, send_sem, recv_sem, device):
        return pltpu.make_async_remote_copy(
            src_ref=src, dst_ref=dst, send_sem=send_sem, recv_sem=recv_sem, device_id=device, device_id_type=MESH
        )

    def all_at_once(buffer, sem):
        pltpu.make_async_copy(buffer.at[pl.ds(1, RING - 1)], buffer.at[pl.ds(1, RING - 1)], sem).wait()

    loads = [
        pltpu.make_async_copy(q_ref, q_in, in_sem.at[0]),
        pltpu.make_async_copy(go_ref, go_in, in_sem.at[1]),
        pltpu.make_async_copy(own_ref, own_in, in_sem.at[2]),
    ]
    for load in loads:
        load.start()

    barrier = pltpu.get_barrier_semaphore()
    stays = rem(column, 4) == 0

    def greet(device):
        pl.semaphore_signal(barrier, inc=1, device_id=device, device_id_type=MESH)

    def greet_column(step, carry):
        greet(in_column(around(column + step)))
        return carry

    def greet_unit(u):
        greet(in_plane(plus(plane, unit_offset(column, u))))
        greet(in_plane(minus(plane, unit_offset(column, u))))

    lax.fori_loop(1, RING, greet_column, 0)
    for u in range(1, UNITS):
        greet_unit(u)

    @pl.when(stays)
    def _():
        pl.semaphore_wait(barrier, RING - 1 + 2 * (UNITS - 1))

    @pl.when(jnp.logical_not(stays))
    def _():
        greet_unit(0)
        pl.semaphore_wait(barrier, RING - 1 + 2 * UNITS)

    def unit_copy(u):
        return remote(
            cache_ref.at[pl.ds(u * UNIT, UNIT)],
            rows_in.at[u],
            a_send.at[u],
            a_recv.at[u],
            in_plane(plus(plane, unit_offset(column, u))),
        )

    for u in range(1, UNITS):
        unit_copy(u).start()

    @pl.when(jnp.logical_not(stays))
    def _():
        unit_copy(0).start()

    @pl.when(stays)
    def _():
        pltpu.make_async_copy(cache_ref.at[pl.ds(0, UNIT)], rows_in.at[0], a_recv.at[0]).start()

    by_source = (keys_in, values_in)

    def column_copy(part, step):
        target = around(column + step)
        at = pl.ds(pl.multiple_of(lax.rem(target, 8) * WIDTH + part * HD, HD), HD)
        return remote(
            rows_in.at[:, :, at], by_source[part].at[column], b_send.at[part], b_recv.at[part], in_column(target)
        )

    def send_heads(part):
        def send(i, carry):
            column_copy(part, column_step(i)).start()
            return carry

        lax.fori_loop(1, RING, send, 0)
        by_source[part][column] = rows_in[:, :, pl.ds(pl.multiple_of(head * WIDTH + part * HD, HD), HD)]

    gathered = (keys, values)

    def chunk_copy(part, step):
        return remote(
            staged.at[part, step],
            gathered[part].at[chunk_rows(step)],
            c_send.at[part],
            c_recv.at[part, step],
            in_plane(plus(plane, turn(step))),
        )

    def send_chunks(part):
        def take(place):
            units = [by_source[part][4 * i + first[odd, place], across[place]] for odd in range(2) for i in range(4)]
            return jnp.concatenate(units, axis=0)

        all_at_once(by_source[part], b_recv.at[part])
        for step in range(1, RING):
            staged[part, step] = take(step)
            chunk_copy(part, step).start()
        gathered[part][:CHUNK] = take(0)

    ends = []
    for i in range(PROMPTS):
        ends.append(counts_ref[i] + (ends[-1] if ends else 0))
    prompts = []
    for step in range(RING):
        response = response_ref[2 * plus(plane, turn(step)) + half]
        group = jnp.int32(0)
        for end in ends[:-1]:
            group = group + (end <= response).astype(jnp.int32)
        prompt = prompt_slot_ref[group]
        prompts.append(prompt)
        way = rem(div(plane, 4) + 4 - div(prompt, 2), 4)
        across[step] = way
        for odd in range(2):
            first[odd, step] = rem(plane + 8 - 2 * rem(prompt, 2) - odd - way, 4)
    for step in range(RING):
        found = jnp.int32(RING)
        for other in range(step):
            found = jnp.where(prompts[other] == prompts[step], other, found)
        previous[step] = found
    for prompt in range(PROMPTS):
        found = jnp.int32(RING)
        for step in range(RING):
            found = jnp.where(prompts[step] == prompt, step, found)
        last[prompt] = found

    for load in loads:
        load.wait()
    position = lax.broadcasted_iota(jnp.int32, (RLEN, HD), 0)
    factor = jnp.where(position < len_ref[0], code_ref[0].astype(F32) / 8.0, 0.0)
    for j in range(HEADS):
        query = q_in[:, head_columns(j)]
        q_rows[head_rows(j)] = query
        q_cols[:, head_rows(j)] = jnp.transpose(query)
        cotangent = go_in[:, head_columns(j)].astype(F32) * factor
        cot_cols[:, head_rows(j)] = jnp.transpose(cotangent).astype(BF16)
    keys[PLEN:] = own_in[:, :HD]
    values[PLEN:] = own_in[:, HD:]
    running[RING] = jnp.zeros((CHUNK, HD), F32)

    def block_rows(b):
        return pl.ds(pl.multiple_of(b * BLOCK, BLOCK), BLOCK)

    def score(b, own):
        block = keys[block_rows(b)]
        for j in range(HEADS):
            at = head_rows(j)
            part = dot(block, q_cols[:, at])
            if own:
                key_at = lax.broadcasted_iota(jnp.int32, (BLOCK, RLEN), 0)
                seen_from = lax.broadcasted_iota(jnp.int32, (BLOCK, RLEN), 1)
                part = jnp.where(key_at <= seen_from, part, -1e30)
            scores[b, :, at] = part
            high = fold(part, jnp.max)
            top[:, at] = high if own else jnp.maximum(top[:, at], high)

    for u in range(UNITS):
        unit_copy(u).wait_recv()
    send_heads(0)
    send_heads(1)
    score(BLOCKS, True)
    send_chunks(0)
    send_chunks(1)

    def arrive(part, b):
        def one(i, carry):
            step = b * PER_BLOCK + i

            @pl.when(step > 0)
            def _():
                chunk_copy(part, step).wait_recv()

            return carry

        lax.fori_loop(0, PER_BLOCK, one, 0)

    for b in range(0, BLOCKS, 2):
        arrive(0, b)
        arrive(0, b + 1)
        score(b, False)
        score(b + 1, False)

    def return_copy(part, step):
        return remote(
            grads.at[part, step],
            terms.at[part, step],
            rc_send.at[part],
            rc_recv.at[part],
            in_plane(minus(plane, turn(step))),
        )

    def send_back(part, b, block):
        for i in range(PER_BLOCK):
            grads[part, b * PER_BLOCK + i] = block[i * CHUNK : (i + 1) * CHUNK]

        def one(i, carry):
            step = b * PER_BLOCK + i

            @pl.when(step > 0)
            def _():
                return_copy(part, step).start()

            return carry

        lax.fori_loop(0, PER_BLOCK, one, 0)

    def pair_rows(p):
        return slice(2 * p * RLEN, 2 * (p + 1) * RLEN)

    def pair_grads(b, p):
        return dot(raw[b, :, pair_rows(p)], cot_scaled_rows[pair_rows(p)])

    for p in range(HEADS // 2):
        heads = (2 * p, 2 * p + 1)
        highest = [jnp.max(top[:, head_rows(j)], axis=0, keepdims=True) for j in heads]

        def weigh(b, totals):
            sums = []
            for j, high, total in zip(heads, highest, totals):
                at = head_rows(j)
                weights = jnp.exp2((scores[b, :, at] - high) * (SCALE * LOG2E))
                raw[b, :, at] = weights.astype(BF16)
                sums.append(total + fold(weights, jnp.sum))
            if p == 1:
                dv_sum[b] = pair_grads(b, 0)
            elif p > 1:
                dv_sum[b] += pair_grads(b, p - 1)
            return tuple(sums)

        totals = (jnp.zeros((8, RLEN), F32),) * 2
        for b in range(BLOCKS + 1):
            totals = weigh(b, totals)
        for j, total in zip(heads, totals):
            at = head_rows(j)
            over = 1.0 / jnp.sum(total, axis=0, keepdims=True)
            inverse[:, at] = jnp.broadcast_to(over, (8, RLEN))
            scaled = cot_cols[:, at].astype(F32) * over
            cot_scaled_cols[:, at] = scaled.astype(BF16)
            cot_scaled_rows[at] = jnp.transpose(scaled).astype(BF16)

    def value_grads(b):
        return (dv_sum[b] + pair_grads(b, HEADS // 2 - 1)).astype(BF16)

    for b in range(0, BLOCKS, 2):
        block_grads = [value_grads(b), value_grads(b + 1)]
        send_back(1, b, block_grads[0])
        send_back(1, b + 1, block_grads[1])

    def look(b, first):
        block = values[block_rows(b)]
        for j in range(HEADS):
            at = head_rows(j)
            grad = dot(block, cot_scaled_cols[:, at])
            scores[b, :, at] = grad
            term = fold(grad * raw[b, :, at].astype(F32), jnp.sum)
            delta[:, at] = term if first else delta[:, at] + term

    look(BLOCKS, True)
    for b in range(0, BLOCKS, 2):
        arrive(1, b)
        arrive(1, b + 1)
        look(b, False)
        look(b + 1, False)
    for j in range(HEADS):
        at = head_rows(j)
        delta[:, at] = jnp.sum(delta[:, at], axis=0, keepdims=True) * inverse[:, at]

    def key_part(b):
        for j in range(HEADS):
            at = head_rows(j)
            weights = raw[b, :, at].astype(F32)
            shift = delta[0:1, at]
            change = (weights * (scores[b, :, at] - shift)).astype(BF16)
            raw[b, :, at] = change
        return (dot(raw[b], q_rows[...]) * SCALE).astype(BF16)

    for b in range(0, BLOCKS, 2):
        key_grads = [key_part(b), key_part(b + 1)]
        send_back(0, b, key_grads[0])
        send_back(0, b + 1, key_grads[1])

    def home_copy(part, target, u):
        x = rem(div(plane, 4) + 4 - u, 4)
        y = rem(plane + 20 - target - u, 4)
        source = 4 * x + y
        return remote(
            summed.at[part, 4 * source + div(target, 4)],
            back_ref.at[part, 4 * column + u],
            rb_send.at[part],
            rb_recv.at[part],
            {"seq": 2 * source + div(target, 8), "head": rem(target, 8)},
        )

    def home_stay(part):
        return pltpu.make_async_copy(
            summed.at[part, 4 * plane + div(column, 4)],
            back_ref.at[part, 4 * column],
            stay_sem.at[part],
        )

    def add_up(part):
        all_at_once(grads.at[part], rc_recv.at[part])
        terms[part, 0] = grads[part, 0]

        def add(step, carry):
            running[step] = running[previous[step]] + terms[part, step].astype(F32)
            return carry

        lax.fori_loop(0, RING, add, 0)

        def close(prompt, carry):
            units = running[last[prompt]].astype(BF16).reshape(CHUNK // UNIT, UNIT, HD)
            summed[part, pl.ds(prompt * (CHUNK // UNIT), CHUNK // UNIT)] = units
            return carry

        lax.fori_loop(0, PROMPTS, close, 0)

        def send(i, carry):
            target = around(column + column_step(i))
            for u in range(UNITS):
                home_copy(part, target, u).start()
            return carry

        lax.fori_loop(1, RING, send, 0)
        for u in range(1, UNITS):
            home_copy(part, column, u).start()

        @pl.when(jnp.logical_not(stays))
        def _():
            home_copy(part, column, 0).start()

        @pl.when(stays)
        def _():
            home_stay(part).start()

    def home_wait(part, sem):
        @pl.when(jnp.logical_not(stays))
        def _():
            pltpu.make_async_copy(back_ref.at[part], back_ref.at[part], sem).wait()

        @pl.when(stays)
        def _():
            rest = back_ref.at[part, pl.ds(1, RING * UNITS - 1)]
            pltpu.make_async_copy(rest, rest, sem).wait()

    add_up(1)

    own_grads[:, HD:] = value_grads(BLOCKS)
    own_grads[:, :HD] = key_part(BLOCKS)
    own_out = pltpu.make_async_copy(own_grads, down_ref, in_sem.at[2])
    own_out.start()
    turned[...] = jnp.transpose(keys[...])

    def query_grads(first, end):
        for j in range(first, end):
            grad = dot(turned[...], raw[:, :, head_rows(j)].reshape(KEYS, RLEN))
            q_grads[:, head_columns(j)] = (jnp.transpose(grad) * SCALE).astype(BF16)

    query_grads(0, 2)
    add_up(0)
    query_grads(2, HEADS)
    q_out = pltpu.make_async_copy(q_grads, dq_ref, in_sem.at[0])
    q_out.start()

    own_out.wait()
    q_out.wait()
    for u in range(1, UNITS):
        unit_copy(u).wait_send()

    @pl.when(jnp.logical_not(stays))
    def _():
        unit_copy(0).wait_send()

    for part in range(2):
        all_at_once(by_source[part], b_send.at[part])
        all_at_once(staged.at[part], c_send.at[part])
        all_at_once(grads.at[part], rc_send.at[part])
    for part in (1, 0):
        home_wait(part, rb_send.at[part])
        home_wait(part, rb_recv.at[part])

        @pl.when(stays)
        def _():
            home_stay(part).wait()


def finish_kernel(dq_ref, down_ref, back_ref, dq_out, down_out, dcache_out, dq, down, back, total, get_sems, put_sems):
    gets = [
        pltpu.make_async_copy(back_ref, back, get_sems.at[0]),
        pltpu.make_async_copy(dq_ref, dq, get_sems.at[1]),
        pltpu.make_async_copy(down_ref, down, get_sems.at[2]),
    ]
    puts = [
        pltpu.make_async_copy(total, dcache_out, put_sems.at[0]),
        pltpu.make_async_copy(dq, dq_out, put_sems.at[1]),
        pltpu.make_async_copy(down, down_out, put_sems.at[2]),
    ]
    for get in gets:
        get.start()
    gets[0].wait()
    for h in range(8):
        for part in range(2):
            first = back[part, UNITS * h : UNITS * (h + 1)].astype(F32)
            second = back[part, UNITS * (8 + h) : UNITS * (9 + h)].astype(F32)
            both = (first + second).astype(BF16).reshape(UNITS * UNIT, HD)
            total[:, h * WIDTH + part * HD : h * WIDTH + (part + 1) * HD] = both
    puts[0].start()
    for get, put in zip(gets[1:], puts[1:]):
        get.wait()
        put.start()
    for put in puts:
        put.wait()


def local(
    queries, resp_kv, prompt_cache, grad_out, group_counts, prompt_slot, slot_response, resp_len, weight_code
):
    smem = pl.BlockSpec(memory_space=pltpu.SMEM)
    hbm = pl.BlockSpec(memory_space=pltpu.HBM)
    scratch = [
        pltpu.SMEM((RING,), jnp.int32),
        pltpu.SMEM((2, RING), jnp.int32),
        pltpu.SMEM((RING,), jnp.int32),
        pltpu.SMEM((PROMPTS,), jnp.int32),
        pltpu.VMEM((RLEN, HEADS * HD), BF16),
        pltpu.VMEM((RLEN, HEADS * HD), BF16),
        pltpu.VMEM((RLEN, WIDTH), BF16),
        pltpu.VMEM((UNITS, UNIT, 8 * WIDTH), BF16),
        pltpu.VMEM((RING, UNITS, UNIT, HD), BF16),
        pltpu.VMEM((RING, UNITS, UNIT, HD), BF16),
        pltpu.VMEM((2, RING, CHUNK, HD), BF16),
        pltpu.VMEM((KEYS, HD), BF16),
        pltpu.VMEM((KEYS, HD), BF16),
        pltpu.VMEM((ROWS, HD), BF16),
        pltpu.VMEM((HD, ROWS), BF16),
        pltpu.VMEM((HD, ROWS), BF16),
        pltpu.VMEM((HD, ROWS), BF16),
        pltpu.VMEM((ROWS, HD), BF16),
        pltpu.VMEM((BLOCKS + 1, BLOCK, ROWS), F32),
        pltpu.VMEM((BLOCKS + 1, BLOCK, ROWS), BF16),
        pltpu.VMEM((8, ROWS), F32),
        pltpu.VMEM((8, ROWS), F32),
        pltpu.VMEM((8, ROWS), F32),
        pltpu.VMEM((HD, KEYS), BF16),
        pltpu.VMEM((BLOCKS + 1, BLOCK, HD), F32),
        pltpu.VMEM((2, RING, CHUNK, HD), BF16),
        pltpu.VMEM((2, RING, CHUNK, HD), BF16),
        pltpu.VMEM((RING + 1, CHUNK, HD), F32),
        pltpu.VMEM((2, RING * UNITS, UNIT, HD), BF16),
        pltpu.VMEM((RLEN, WIDTH), BF16),
        pltpu.VMEM((RLEN, HEADS * HD), BF16),
        pltpu.SemaphoreType.DMA((3,)),
        pltpu.SemaphoreType.DMA((UNITS,)),
        pltpu.SemaphoreType.DMA((UNITS,)),
        pltpu.SemaphoreType.DMA((2,)),
        pltpu.SemaphoreType.DMA((2,)),
        pltpu.SemaphoreType.DMA((2,)),
        pltpu.SemaphoreType.DMA((2, RING)),
        pltpu.SemaphoreType.DMA((2,)),
        pltpu.SemaphoreType.DMA((2,)),
        pltpu.SemaphoreType.DMA((2,)),
        pltpu.SemaphoreType.DMA((2,)),
        pltpu.SemaphoreType.DMA((2,)),
    ]
    products = 5 * ROWS * KEYS * HD
    dq, down, back = pl.pallas_call(
        kernel,
        out_shape=[
            jax.ShapeDtypeStruct(queries.shape, BF16),
            jax.ShapeDtypeStruct(resp_kv.shape, BF16),
            jax.ShapeDtypeStruct((2, RING * UNITS, UNIT, HD), BF16),
        ],
        in_specs=[smem] * 5 + [hbm] * 4,
        out_specs=[hbm] * 3,
        scratch_shapes=scratch,
        compiler_params=pltpu.CompilerParams(
            collective_id=0, has_side_effects=True, vmem_limit_bytes=VMEM_LIMIT
        ),
        cost_estimate=pl.CostEstimate(flops=2 * products, bytes_accessed=3 << 20, transcendentals=ROWS * KEYS),
    )(
        group_counts,
        prompt_slot,
        slot_response,
        resp_len,
        weight_code,
        queries,
        resp_kv,
        prompt_cache,
        grad_out,
    )
    return pl.pallas_call(
        finish_kernel,
        out_shape=[
            jax.ShapeDtypeStruct(queries.shape, BF16),
            jax.ShapeDtypeStruct(resp_kv.shape, BF16),
            jax.ShapeDtypeStruct(prompt_cache.shape, BF16),
        ],
        in_specs=[hbm] * 3,
        out_specs=[hbm] * 3,
        scratch_shapes=[
            pltpu.VMEM(queries.shape, BF16),
            pltpu.VMEM(resp_kv.shape, BF16),
            pltpu.VMEM((2, RING * UNITS, UNIT, HD), BF16),
            pltpu.VMEM(prompt_cache.shape, BF16),
            pltpu.SemaphoreType.DMA((3,)),
            pltpu.SemaphoreType.DMA((3,)),
        ],
        compiler_params=pltpu.CompilerParams(vmem_limit_bytes=VMEM_LIMIT),
    )(dq, down, back)


def solution(mesh):
    placed = (
        P("seq", "head"),
        P("seq", "head"),
        P(("seq", "head"), None),
        P("seq", "head"),
        P(),
        P(),
        P(),
        P("seq"),
        P("seq"),
    )
    return jax.shard_map(
        local,
        mesh=mesh,
        in_specs=placed,
        out_specs=(P("seq", "head"), P("seq", "head"), P(("seq", "head"), None)),
        check_vma=False,
    )
```

```python
import math

import jax
import jax.numpy as jnp
from jax import lax
from jax.experimental import pallas as pl
from jax.experimental.pallas import tpu as pltpu
from jax.sharding import PartitionSpec as P

HD = 128
PLEN = 2048
RLEN = 256
HEADS = 8
PROMPTS = 8
RING = 16
CHUNK = PLEN // RING
UNITS = 4
UNIT = 16
BLOCK = 256
BLOCKS = PLEN // BLOCK
PER_BLOCK = BLOCK // CHUNK
ROWS = HEADS * RLEN
KEYS = PLEN + RLEN
WIDTH = 2 * HD
SCALE = HD**-0.5
LOG2E = math.log2(math.e)
MESH = pl.DeviceIdType.MESH
VMEM_LIMIT = 60 * 1024 * 1024
NN = (((1,), (0,)), ((), ()))
F32 = jnp.float32
BF16 = jnp.bfloat16


def around(index):
    return lax.rem(index + 2 * RING, RING)


def div(a, b):
    return a // b if isinstance(a, int) else lax.div(a, b)


def rem(a, b):
    return a % b if isinstance(a, int) else lax.rem(a, b)


def plus(plane, offset):
    return 4 * rem(div(plane, 4) + div(offset, 4), 4) + rem(plane + rem(offset, 4), 4)


def minus(plane, offset):
    return 4 * rem(div(plane, 4) + 4 - div(offset, 4), 4) + rem(plane + 4 - rem(offset, 4), 4)


def turn(place):
    return rem(5 * place, RING)


def unit_offset(column, u):
    return 4 * u + lax.rem(column + u, 4)


def column_step(i):
    return 8 + div(i, 2) * (1 - 2 * rem(i, 2))


def head_rows(j):
    return slice(j * RLEN, (j + 1) * RLEN)


def head_columns(j):
    return slice(j * HD, (j + 1) * HD)


def chunk_rows(step):
    return pl.ds(pl.multiple_of(step * CHUNK, CHUNK), CHUNK)


def fold(values, op):
    return op(values.reshape(values.shape[0] // 8, 8, values.shape[1]), axis=0)


def dot(a, b):
    return lax.dot_general(a, b, NN, preferred_element_type=F32)


def kernel(
    counts_ref,
    prompt_slot_ref,
    response_ref,
    len_ref,
    code_ref,
    q_ref,
    own_ref,
    cache_ref,
    go_ref,
    dq_ref,
    down_ref,
    back_ref,
    across,
    first,
    previous,
    last,
    q_in,
    go_in,
    own_in,
    rows_in,
    keys_in,
    values_in,
    staged,
    keys,
    values,
    q_rows,
    q_cols,
    cot_cols,
    cot_scaled_cols,
    cot_scaled_rows,
    scores,
    raw,
    top,
    delta,
    inverse,
    turned,
    dv_sum,
    grads,
    terms,
    running,
    summed,
    own_grads,
    q_grads,
    in_sem,
    a_send,
    a_recv,
    b_send,
    b_recv,
    c_send,
    c_recv,
    rc_send,
    rc_recv,
    rb_send,
    rb_recv,
    stay_sem,
):
    seq = lax.axis_index("seq")
    head = lax.axis_index("head")
    plane = div(seq, 2)
    half = lax.rem(seq, 2)
    column = half * 8 + head

    def in_plane(other):
        return {"seq": 2 * other + half, "head": head}

    def in_column(other):
        return {"seq": 2 * plane + div(other, 8), "head": lax.rem(other, 8)}

    def remote(src, dst, send_sem, recv_sem, device):
        return pltpu.make_async_remote_copy(
            src_ref=src, dst_ref=dst, send_sem=send_sem, recv_sem=recv_sem, device_id=device, device_id_type=MESH
        )

    def all_at_once(buffer, sem):
        pltpu.make_async_copy(buffer.at[pl.ds(1, RING - 1)], buffer.at[pl.ds(1, RING - 1)], sem).wait()

    loads = [
        pltpu.make_async_copy(q_ref, q_in, in_sem.at[0]),
        pltpu.make_async_copy(go_ref, go_in, in_sem.at[1]),
        pltpu.make_async_copy(own_ref, own_in, in_sem.at[2]),
    ]
    for load in loads:
        load.start()

    barrier = pltpu.get_barrier_semaphore()
    stays = rem(column, 4) == 0

    def greet(device):
        pl.semaphore_signal(barrier, inc=1, device_id=device, device_id_type=MESH)

    def greet_column(step, carry):
        greet(in_column(around(column + step)))
        return carry

    def greet_unit(u):
        greet(in_plane(plus(plane, unit_offset(column, u))))
        greet(in_plane(minus(plane, unit_offset(column, u))))

    lax.fori_loop(1, RING, greet_column, 0)
    for u in range(1, UNITS):
        greet_unit(u)

    @pl.when(stays)
    def _():
        pl.semaphore_wait(barrier, RING - 1 + 2 * (UNITS - 1))

    @pl.when(jnp.logical_not(stays))
    def _():
        greet_unit(0)
        pl.semaphore_wait(barrier, RING - 1 + 2 * UNITS)

    def unit_copy(u):
        return remote(
            cache_ref.at[pl.ds(u * UNIT, UNIT)],
            rows_in.at[u],
            a_send.at[u],
            a_recv.at[u],
            in_plane(plus(plane, unit_offset(column, u))),
        )

    for u in range(1, UNITS):
        unit_copy(u).start()

    @pl.when(jnp.logical_not(stays))
    def _():
        unit_copy(0).start()

    @pl.when(stays)
    def _():
        pltpu.make_async_copy(cache_ref.at[pl.ds(0, UNIT)], rows_in.at[0], a_recv.at[0]).start()

    by_source = (keys_in, values_in)

    def column_copy(part, step):
        target = around(column + step)
        at = pl.ds(pl.multiple_of(lax.rem(target, 8) * WIDTH + part * HD, HD), HD)
        return remote(
            rows_in.at[:, :, at], by_source[part].at[column], b_send.at[part], b_recv.at[part], in_column(target)
        )

    def send_heads(part):
        def send(i, carry):
            column_copy(part, column_step(i)).start()
            return carry

        lax.fori_loop(1, RING, send, 0)
        by_source[part][column] = rows_in[:, :, pl.ds(pl.multiple_of(head * WIDTH + part * HD, HD), HD)]

    gathered = (keys, values)

    def chunk_copy(part, step):
        return remote(
            staged.at[part, step],
            gathered[part].at[chunk_rows(step)],
            c_send.at[part],
            c_recv.at[part, step],
            in_plane(plus(plane, turn(step))),
        )

    def send_chunks(part):
        def take(place):
            units = [by_source[part][4 * i + first[odd, place], across[place]] for odd in range(2) for i in range(4)]
            return jnp.concatenate(units, axis=0)

        all_at_once(by_source[part], b_recv.at[part])
        for step in range(1, RING):
            staged[part, step] = take(step)
            chunk_copy(part, step).start()
        gathered[part][:CHUNK] = take(0)

    ends = []
    for i in range(PROMPTS):
        ends.append(counts_ref[i] + (ends[-1] if ends else 0))
    prompts = []
    for step in range(RING):
        response = response_ref[2 * plus(plane, turn(step)) + half]
        group = jnp.int32(0)
        for end in ends[:-1]:
            group = group + (end <= response).astype(jnp.int32)
        prompt = prompt_slot_ref[group]
        prompts.append(prompt)
        way = rem(div(plane, 4) + 4 - div(prompt, 2), 4)
        across[step] = way
        for odd in range(2):
            first[odd, step] = rem(plane + 8 - 2 * rem(prompt, 2) - odd - way, 4)
    for step in range(RING):
        found = jnp.int32(RING)
        for other in range(step):
            found = jnp.where(prompts[other] == prompts[step], other, found)
        previous[step] = found
    for prompt in range(PROMPTS):
        found = jnp.int32(RING)
        for step in range(RING):
            found = jnp.where(prompts[step] == prompt, step, found)
        last[prompt] = found

    for load in loads:
        load.wait()
    position = lax.broadcasted_iota(jnp.int32, (RLEN, HD), 0)
    factor = jnp.where(position < len_ref[0], code_ref[0].astype(F32) / 8.0, 0.0)
    for j in range(HEADS):
        query = q_in[:, head_columns(j)]
        q_rows[head_rows(j)] = query
        q_cols[:, head_rows(j)] = jnp.transpose(query)
        cotangent = go_in[:, head_columns(j)].astype(F32) * factor
        cot_cols[:, head_rows(j)] = jnp.transpose(cotangent).astype(BF16)
    keys[PLEN:] = own_in[:, :HD]
    values[PLEN:] = own_in[:, HD:]
    running[RING] = jnp.zeros((CHUNK, HD), F32)

    def block_rows(b):
        return pl.ds(pl.multiple_of(b * BLOCK, BLOCK), BLOCK)

    def score(b, own):
        block = keys[block_rows(b)]
        for j in range(HEADS):
            at = head_rows(j)
            part = dot(block, q_cols[:, at])
            if own:
                key_at = lax.broadcasted_iota(jnp.int32, (BLOCK, RLEN), 0)
                seen_from = lax.broadcasted_iota(jnp.int32, (BLOCK, RLEN), 1)
                part = jnp.where(key_at <= seen_from, part, -1e30)
            scores[b, :, at] = part
            high = fold(part, jnp.max)
            top[:, at] = high if own else jnp.maximum(top[:, at], high)

    for u in range(UNITS):
        unit_copy(u).wait_recv()
    send_heads(0)
    send_heads(1)
    score(BLOCKS, True)
    send_chunks(0)
    send_chunks(1)

    def arrive(part, b):
        def one(i, carry):
            step = b * PER_BLOCK + i

            @pl.when(step > 0)
            def _():
                chunk_copy(part, step).wait_recv()

            return carry

        lax.fori_loop(0, PER_BLOCK, one, 0)

    for b in range(0, BLOCKS, 2):
        arrive(0, b)
        arrive(0, b + 1)
        score(b, False)
        score(b + 1, False)

    def return_copy(part, step):
        return remote(
            grads.at[part, step],
            terms.at[part, step],
            rc_send.at[part],
            rc_recv.at[part],
            in_plane(minus(plane, turn(step))),
        )

    def send_back(part, b, block):
        for i in range(PER_BLOCK):
            grads[part, b * PER_BLOCK + i] = block[i * CHUNK : (i + 1) * CHUNK]

        def one(i, carry):
            step = b * PER_BLOCK + i

            @pl.when(step > 0)
            def _():
                return_copy(part, step).start()

            return carry

        lax.fori_loop(0, PER_BLOCK, one, 0)

    def pair_rows(p):
        return slice(2 * p * RLEN, 2 * (p + 1) * RLEN)

    def pair_grads(b, p):
        return dot(raw[b, :, pair_rows(p)], cot_scaled_rows[pair_rows(p)])

    for p in range(HEADS // 2):
        heads = (2 * p, 2 * p + 1)
        highest = [jnp.max(top[:, head_rows(j)], axis=0, keepdims=True) for j in heads]

        def weigh(b, totals):
            sums = []
            for j, high, total in zip(heads, highest, totals):
                at = head_rows(j)
                weights = jnp.exp2((scores[b, :, at] - high) * (SCALE * LOG2E))
                raw[b, :, at] = weights.astype(BF16)
                sums.append(total + fold(weights, jnp.sum))
            if p == 1:
                dv_sum[b] = pair_grads(b, 0)
            elif p > 1:
                dv_sum[b] += pair_grads(b, p - 1)
            return tuple(sums)

        totals = (jnp.zeros((8, RLEN), F32),) * 2
        for b in range(BLOCKS + 1):
            totals = weigh(b, totals)
        for j, total in zip(heads, totals):
            at = head_rows(j)
            over = 1.0 / jnp.sum(total, axis=0, keepdims=True)
            inverse[:, at] = jnp.broadcast_to(over, (8, RLEN))
            scaled = cot_cols[:, at].astype(F32) * over
            cot_scaled_cols[:, at] = scaled.astype(BF16)
            cot_scaled_rows[at] = jnp.transpose(scaled).astype(BF16)

    def value_grads(b):
        return (dv_sum[b] + pair_grads(b, HEADS // 2 - 1)).astype(BF16)

    for b in range(0, BLOCKS, 2):
        block_grads = [value_grads(b), value_grads(b + 1)]
        send_back(1, b, block_grads[0])
        send_back(1, b + 1, block_grads[1])

    def look(b, first):
        block = values[block_rows(b)]
        for j in range(HEADS):
            at = head_rows(j)
            grad = dot(block, cot_scaled_cols[:, at])
            scores[b, :, at] = grad
            term = fold(grad * raw[b, :, at].astype(F32), jnp.sum)
            delta[:, at] = term if first else delta[:, at] + term

    look(BLOCKS, True)
    for b in range(0, BLOCKS, 4):
        for i in range(4):
            arrive(1, b + i)
        for i in range(4):
            look(b + i, False)
    for j in range(HEADS):
        at = head_rows(j)
        delta[:, at] = jnp.sum(delta[:, at], axis=0, keepdims=True) * inverse[:, at]

    def key_part(b):
        for j in range(HEADS):
            at = head_rows(j)
            weights = raw[b, :, at].astype(F32)
            shift = delta[0:1, at]
            change = (weights * (scores[b, :, at] - shift)).astype(BF16)
            raw[b, :, at] = change
        return (dot(raw[b], q_rows[...]) * SCALE).astype(BF16)

    for b in range(0, BLOCKS, 2):
        key_grads = [key_part(b), key_part(b + 1)]
        send_back(0, b, key_grads[0])
        send_back(0, b + 1, key_grads[1])

    def home_copy(part, target, u):
        x = rem(div(plane, 4) + 4 - u, 4)
        y = rem(plane + 20 - target - u, 4)
        source = 4 * x + y
        return remote(
            summed.at[part, 4 * source + div(target, 4)],
            back_ref.at[part, 4 * column + u],
            rb_send.at[part],
            rb_recv.at[part],
            {"seq": 2 * source + div(target, 8), "head": rem(target, 8)},
        )

    def home_stay(part):
        return pltpu.make_async_copy(
            summed.at[part, 4 * plane + div(column, 4)],
            back_ref.at[part, 4 * column],
            stay_sem.at[part],
        )

    def add_up(part):
        all_at_once(grads.at[part], rc_recv.at[part])
        terms[part, 0] = grads[part, 0]

        def add(step, carry):
            running[step] = running[previous[step]] + terms[part, step].astype(F32)
            return carry

        lax.fori_loop(0, RING, add, 0, unroll=4)

        def close(prompt, carry):
            units = running[last[prompt]].astype(BF16).reshape(CHUNK // UNIT, UNIT, HD)
            summed[part, pl.ds(prompt * (CHUNK // UNIT), CHUNK // UNIT)] = units
            return carry

        lax.fori_loop(0, PROMPTS, close, 0, unroll=4)

        def send(i, carry):
            target = around(column + column_step(i))
            for u in range(UNITS):
                home_copy(part, target, u).start()
            return carry

        lax.fori_loop(1, RING, send, 0)
        for u in range(1, UNITS):
            home_copy(part, column, u).start()

        @pl.when(jnp.logical_not(stays))
        def _():
            home_copy(part, column, 0).start()

        @pl.when(stays)
        def _():
            home_stay(part).start()

    def home_wait(part, sem):
        @pl.when(jnp.logical_not(stays))
        def _():
            pltpu.make_async_copy(back_ref.at[part], back_ref.at[part], sem).wait()

        @pl.when(stays)
        def _():
            rest = back_ref.at[part, pl.ds(1, RING * UNITS - 1)]
            pltpu.make_async_copy(rest, rest, sem).wait()

    add_up(1)

    own_grads[:, HD:] = value_grads(BLOCKS)
    own_grads[:, :HD] = key_part(BLOCKS)
    own_out = pltpu.make_async_copy(own_grads, down_ref, in_sem.at[2])
    own_out.start()
    turned[...] = jnp.transpose(keys[...])

    def query_grads(first, end):
        for j in range(first, end):
            grad = dot(turned[...], raw[:, :, head_rows(j)].reshape(KEYS, RLEN))
            q_grads[:, head_columns(j)] = (jnp.transpose(grad) * SCALE).astype(BF16)

    query_grads(0, 2)
    add_up(0)
    query_grads(2, HEADS)
    q_out = pltpu.make_async_copy(q_grads, dq_ref, in_sem.at[0])
    q_out.start()

    own_out.wait()
    q_out.wait()
    for u in range(1, UNITS):
        unit_copy(u).wait_send()

    @pl.when(jnp.logical_not(stays))
    def _():
        unit_copy(0).wait_send()

    for part in range(2):
        all_at_once(by_source[part], b_send.at[part])
        all_at_once(staged.at[part], c_send.at[part])
        all_at_once(grads.at[part], rc_send.at[part])
    for part in (1, 0):
        home_wait(part, rb_send.at[part])
        home_wait(part, rb_recv.at[part])

        @pl.when(stays)
        def _():
            home_stay(part).wait()


def finish_kernel(dq_ref, down_ref, back_ref, dq_out, down_out, dcache_out, dq, down, back, total, get_sems, put_sems):
    gets = [
        pltpu.make_async_copy(back_ref, back, get_sems.at[0]),
        pltpu.make_async_copy(dq_ref, dq, get_sems.at[1]),
        pltpu.make_async_copy(down_ref, down, get_sems.at[2]),
    ]
    puts = [
        pltpu.make_async_copy(total, dcache_out, put_sems.at[0]),
        pltpu.make_async_copy(dq, dq_out, put_sems.at[1]),
        pltpu.make_async_copy(down, down_out, put_sems.at[2]),
    ]
    for get in gets:
        get.start()
    gets[0].wait()
    for h in range(8):
        for part in range(2):
            first = back[part, UNITS * h : UNITS * (h + 1)].astype(F32)
            second = back[part, UNITS * (8 + h) : UNITS * (9 + h)].astype(F32)
            both = (first + second).astype(BF16).reshape(UNITS * UNIT, HD)
            total[:, h * WIDTH + part * HD : h * WIDTH + (part + 1) * HD] = both
    puts[0].start()
    for get, put in zip(gets[1:], puts[1:]):
        get.wait()
        put.start()
    for put in puts:
        put.wait()


def local(
    queries, resp_kv, prompt_cache, grad_out, group_counts, prompt_slot, slot_response, resp_len, weight_code
):
    smem = pl.BlockSpec(memory_space=pltpu.SMEM)
    hbm = pl.BlockSpec(memory_space=pltpu.HBM)
    scratch = [
        pltpu.SMEM((RING,), jnp.int32),
        pltpu.SMEM((2, RING), jnp.int32),
        pltpu.SMEM((RING,), jnp.int32),
        pltpu.SMEM((PROMPTS,), jnp.int32),
        pltpu.VMEM((RLEN, HEADS * HD), BF16),
        pltpu.VMEM((RLEN, HEADS * HD), BF16),
        pltpu.VMEM((RLEN, WIDTH), BF16),
        pltpu.VMEM((UNITS, UNIT, 8 * WIDTH), BF16),
        pltpu.VMEM((RING, UNITS, UNIT, HD), BF16),
        pltpu.VMEM((RING, UNITS, UNIT, HD), BF16),
        pltpu.VMEM((2, RING, CHUNK, HD), BF16),
        pltpu.VMEM((KEYS, HD), BF16),
        pltpu.VMEM((KEYS, HD), BF16),
        pltpu.VMEM((ROWS, HD), BF16),
        pltpu.VMEM((HD, ROWS), BF16),
        pltpu.VMEM((HD, ROWS), BF16),
        pltpu.VMEM((HD, ROWS), BF16),
        pltpu.VMEM((ROWS, HD), BF16),
        pltpu.VMEM((BLOCKS + 1, BLOCK, ROWS), F32),
        pltpu.VMEM((BLOCKS + 1, BLOCK, ROWS), BF16),
        pltpu.VMEM((8, ROWS), F32),
        pltpu.VMEM((8, ROWS), F32),
        pltpu.VMEM((8, ROWS), F32),
        pltpu.VMEM((HD, KEYS), BF16),
        pltpu.VMEM((BLOCKS + 1, BLOCK, HD), F32),
        pltpu.VMEM((2, RING, CHUNK, HD), BF16),
        pltpu.VMEM((2, RING, CHUNK, HD), BF16),
        pltpu.VMEM((RING + 1, CHUNK, HD), F32),
        pltpu.VMEM((2, RING * UNITS, UNIT, HD), BF16),
        pltpu.VMEM((RLEN, WIDTH), BF16),
        pltpu.VMEM((RLEN, HEADS * HD), BF16),
        pltpu.SemaphoreType.DMA((3,)),
        pltpu.SemaphoreType.DMA((UNITS,)),
        pltpu.SemaphoreType.DMA((UNITS,)),
        pltpu.SemaphoreType.DMA((2,)),
        pltpu.SemaphoreType.DMA((2,)),
        pltpu.SemaphoreType.DMA((2,)),
        pltpu.SemaphoreType.DMA((2, RING)),
        pltpu.SemaphoreType.DMA((2,)),
        pltpu.SemaphoreType.DMA((2,)),
        pltpu.SemaphoreType.DMA((2,)),
        pltpu.SemaphoreType.DMA((2,)),
        pltpu.SemaphoreType.DMA((2,)),
    ]
    products = 5 * ROWS * KEYS * HD
    dq, down, back = pl.pallas_call(
        kernel,
        out_shape=[
            jax.ShapeDtypeStruct(queries.shape, BF16),
            jax.ShapeDtypeStruct(resp_kv.shape, BF16),
            jax.ShapeDtypeStruct((2, RING * UNITS, UNIT, HD), BF16),
        ],
        in_specs=[smem] * 5 + [hbm] * 4,
        out_specs=[hbm] * 3,
        scratch_shapes=scratch,
        compiler_params=pltpu.CompilerParams(
            collective_id=0, has_side_effects=True, vmem_limit_bytes=VMEM_LIMIT
        ),
        cost_estimate=pl.CostEstimate(flops=2 * products, bytes_accessed=3 << 20, transcendentals=ROWS * KEYS),
    )(
        group_counts,
        prompt_slot,
        slot_response,
        resp_len,
        weight_code,
        queries,
        resp_kv,
        prompt_cache,
        grad_out,
    )
    return pl.pallas_call(
        finish_kernel,
        out_shape=[
            jax.ShapeDtypeStruct(queries.shape, BF16),
            jax.ShapeDtypeStruct(resp_kv.shape, BF16),
            jax.ShapeDtypeStruct(prompt_cache.shape, BF16),
        ],
        in_specs=[hbm] * 3,
        out_specs=[hbm] * 3,
        scratch_shapes=[
            pltpu.VMEM(queries.shape, BF16),
            pltpu.VMEM(resp_kv.shape, BF16),
            pltpu.VMEM((2, RING * UNITS, UNIT, HD), BF16),
            pltpu.VMEM(prompt_cache.shape, BF16),
            pltpu.SemaphoreType.DMA((3,)),
            pltpu.SemaphoreType.DMA((3,)),
        ],
        compiler_params=pltpu.CompilerParams(vmem_limit_bytes=VMEM_LIMIT),
    )(dq, down, back)


def solution(mesh):
    placed = (
        P("seq", "head"),
        P("seq", "head"),
        P(("seq", "head"), None),
        P("seq", "head"),
        P(),
        P(),
        P(),
        P("seq"),
        P("seq"),
    )
    return jax.shard_map(
        local,
        mesh=mesh,
        in_specs=placed,
        out_specs=(P("seq", "head"), P("seq", "head"), P(("seq", "head"), None)),
        check_vma=False,
    )
```
